32 devices in a mesh: dp: 2 (over core), ctx: 4 (over y, x), ulysses: 4 (over z).
Axes of the slice: x: 2, y: 2, z: 4, core: 2. Of those that a mesh axis runs over, the one named last changes fastest.
Arguments:
- hidden_in: bfloat16 [2, 2048, 2048], P('dp', ('ctx', 'ulysses')), may hold values from -6 to 6
- cotangent: bfloat16 [2, 2048, 2048], P('dp', ('ctx', 'ulysses')), may hold values from -6 to 6
- log_decay: float32 [2, 8, 2048], P('dp', 'ulysses', 'ctx'), may hold values from -1 to 0, as said below
- w_query: bfloat16 [2048, 2048], P(('dp', 'ctx', 'ulysses')), may hold values from -0.125 to 0.125
- w_key: bfloat16 [2048, 2048], P(('dp', 'ctx', 'ulysses')), may hold values from -0.125 to 0.125
- w_value: bfloat16 [2048, 3456], P(('dp', 'ctx', 'ulysses')), may hold values from -0.125 to 0.125
- w_swish: bfloat16 [2048, 3456], P(('dp', 'ctx', 'ulysses')), may hold values from -0.125 to 0.125
- w_output: bfloat16 [3456, 2048], P(('dp', 'ctx', 'ulysses')), may hold values from -0.21875 to 0.21875
- w_gate: bfloat16 [2048, 3456], P(('dp', 'ctx', 'ulysses')), may hold values from -0.125 to 0.125
- w_up: bfloat16 [2048, 3456], P(('dp', 'ctx', 'ulysses')), may hold values from -0.125 to 0.125
- w_down: bfloat16 [3456, 2048], P(('dp', 'ctx', 'ulysses')), may hold values from -0.21875 to 0.21875
- gain_attn: bfloat16 [2048], P(('dp', 'ctx', 'ulysses')), may hold values from 0.5 to 1.5
- gain_ffn: bfloat16 [2048], P(('dp', 'ctx', 'ulysses')), may hold values from 0.5 to 1.5
Outputs:
- layer_out: float32 [2, 2048, 2048], P('dp', ('ctx', 'ulysses'))
- grad_input: float32 [2, 2048, 2048], P('dp', ('ctx', 'ulysses'))
- grad_query: float32 [2048, 2048], P(('dp', 'ctx', 'ulysses'))
- grad_key: float32 [2048, 2048], P(('dp', 'ctx', 'ulysses'))
- grad_value: float32 [2048, 3456], P(('dp', 'ctx', 'ulysses'))
- grad_swish: float32 [2048, 3456], P(('dp', 'ctx', 'ulysses'))
- grad_output: float32 [3456, 2048], P(('dp', 'ctx', 'ulysses'))
- grad_gate: float32 [2048, 3456], P(('dp', 'ctx', 'ulysses'))
- grad_up: float32 [2048, 3456], P(('dp', 'ctx', 'ulysses'))
- grad_down: float32 [3456, 2048], P(('dp', 'ctx', 'ulysses'))
- grad_gain_attn: float32 [2048], P(('dp', 'ctx', 'ulysses'))
- grad_gain_ffn: float32 [2048], P(('dp', 'ctx', 'ulysses'))
The draws below stay inside these ranges and needn't reach their ends.
Inputs may be any that keep to these rules, and one draw needn't show every extreme that they name: log_decay is strictly negative.
All inputs are finite; a program needn't handle non-finite values.
Results may differ from the reference program's by a relative error of at most 0.015.
The reference program's roundings to bfloat16 on the way count: a program that leaves them out, or rounds other values in their place, can miss the bound.
Values may be sent and summed in bfloat16 or wider, within the bound.
A program may use at most 384 MiB of HBM per device.

```python
import math
import jax
import jax.numpy as jnp
from jax import lax

D = 2048
RETENTION_HEADS = 8
KEY_DIM = 256
VALUE_DIM = 432
FF = 3456
BLOCK = 512
SEQUENCE_LENGTH = 2048
SEQUENCE_COUNT = 2


def draw_log_decay(key, part):
    every_key_rows = jax.random.split(jax.random.fold_in(key, 7), 7)
    shape_head = (SEQUENCE_COUNT, RETENTION_HEADS, 1)
    picks = jax.random.randint(every_key_rows[0], shape_head, 0, 8)
    fast = picks < 4
    fast_rate = 1.0 / jax.random.uniform(every_key_rows[1], shape_head, jnp.float32, 30.0, 50.0)
    slow_rate = jax.random.uniform(every_key_rows[2], shape_head, jnp.float32, 0.2, 0.6) / SEQUENCE_LENGTH
    baseline_decay_rate = jnp.where(fast, fast_rate, slow_rate)
    rough = jax.random.uniform(every_key_rows[3], (SEQUENCE_COUNT, RETENTION_HEADS, SEQUENCE_LENGTH // BLOCK, BLOCK), jnp.float32, 0.5, 2.0)
    block_factor = jax.random.uniform(every_key_rows[4], (SEQUENCE_COUNT, RETENTION_HEADS, SEQUENCE_LENGTH // BLOCK, 1), jnp.float32, 0.5, 2.0)
    multiplier_value = (rough * block_factor).reshape(SEQUENCE_COUNT, RETENTION_HEADS, SEQUENCE_LENGTH)
    spike_positions = jax.random.randint(every_key_rows[5], (SEQUENCE_COUNT, RETENTION_HEADS, 2), 0, SEQUENCE_LENGTH)
    token_location = lax_iota(SEQUENCE_LENGTH)
    match_count = jnp.any(token_location[None, None, :, None] == spike_positions[:, :, None, :], axis=-1)
    spike_loss_value = jax.random.uniform(every_key_rows[6], (SEQUENCE_COUNT, RETENTION_HEADS, SEQUENCE_LENGTH), jnp.float32, 0.22, 0.69)
    return -(baseline_decay_rate * multiplier_value) - jnp.where(match_count, spike_loss_value, 0.0)


def lax_iota(count):
    return jnp.arange(count, dtype=jnp.int32)


def levels(own_key, shape, shards, low, largest):
    loudness, own = 1.0, jax.random.fold_in(own_key, 6)
    for axis_at, parts in shards:
        heights = jnp.exp(jax.random.uniform(jax.random.fold_in(own, axis_at), (parts,), jnp.float32, low / len(shards), largest / len(shards)))
        loudness = loudness * jnp.repeat(heights, shape[axis_at] // parts).reshape([-1 if axis == axis_at else 1 for axis in range(len(shape))])
    return loudness


def normal_values(stream_key, dims, scale, bound, cuts=(), kind=jnp.bfloat16):
    array = jax.random.normal(stream_key, dims, jnp.float32) * scale
    if len(cuts) > 0:
        array = levels(stream_key, dims, cuts, -0.22, 0.18) * array
    return jnp.clip(array, min=-bound, max=bound).astype(kind)


def setup_inputs(seed: int = 0) -> dict:
    seeds = jax.random.split(jax.random.key(seed), 14)
    hidden_in = normal_values(seeds[0], (SEQUENCE_COUNT, SEQUENCE_LENGTH, D), 1.0, 6.0, ((0, 2), (1, 16)))
    cotangent = normal_values(seeds[1], (SEQUENCE_COUNT, SEQUENCE_LENGTH, D), 1.0, 6.0, ((0, 2), (1, 16)))
    log_decay = draw_log_decay(jax.random.fold_in(seeds[13], 71), 0)
    w_query = normal_values(seeds[3], (D, RETENTION_HEADS * KEY_DIM), D ** -0.5, 0.125, ((0, 32),))
    w_key = normal_values(seeds[4], (D, RETENTION_HEADS * KEY_DIM), D ** -0.5, 0.125, ((0, 32),))
    w_value = normal_values(seeds[5], (D, RETENTION_HEADS * VALUE_DIM), D ** -0.5, 0.125, ((0, 32),))
    w_swish = normal_values(seeds[6], (D, RETENTION_HEADS * VALUE_DIM), D ** -0.5, 0.125, ((0, 32),))
    w_output = normal_values(seeds[7], (RETENTION_HEADS * VALUE_DIM, D), (RETENTION_HEADS * VALUE_DIM // 4) ** -0.5, 0.21875, ((0, 32),))
    w_gate = normal_values(seeds[8], (D, FF), D ** -0.5, 0.125, ((0, 32),))
    w_up = normal_values(seeds[9], (D, FF), D ** -0.5, 0.125, ((0, 32),))
    w_down = normal_values(seeds[10], (FF, D), (FF // 4) ** -0.5, 0.21875, ((0, 32),))
    gain_attn = jnp.clip(1.0 + 0.1 * jax.random.normal(seeds[11], (D,), jnp.float32), 0.5, 1.5).astype(jnp.bfloat16)
    gain_ffn = jnp.clip(1.0 + 0.1 * jax.random.normal(seeds[12], (D,), jnp.float32), 0.5, 1.5).astype(jnp.bfloat16)
    return {"hidden_in": hidden_in, "cotangent": cotangent, "log_decay": log_decay, "w_query": w_query, "w_key": w_key, "w_value": w_value, "w_swish": w_swish, "w_output": w_output, "w_gate": w_gate, "w_up": w_up, "w_down": w_down, "gain_attn": gain_attn, "gain_ffn": gain_ffn}


@jax.custom_vjp
def low(v):
    return lax.optimization_barrier(v.astype(jnp.bfloat16)).astype(jnp.float32)

@jax.custom_vjp
def low_back(v):
    return v

def low_keep(v):
    return (low(v), None)

def low_pass(kept, grad):
    return (grad,)

def back_keep(v):
    return (v, None)

def back_low(kept, grad):
    return (low(grad),)
low.defvjp(low_keep, low_pass)
low_back.defvjp(back_keep, back_low)

def matmul(left, right):
    return jnp.dot(left, right, precision=lax.Precision.HIGHEST)

def normalize(values):
    return values * lax.rsqrt(lax.optimization_barrier(jnp.mean(values * values, axis=-1, keepdims=True)) + 1e-06)

def retention_block(state, block_items):
    queries, keys_in, values, decay = block_items
    scale = 1.0 / math.sqrt(KEY_DIM)
    cumulative = jnp.cumsum(decay, axis=1)
    width = queries.shape[0]
    later = lax.broadcasted_iota(jnp.int32, (width, width), 0) >= lax.broadcasted_iota(jnp.int32, (width, width), 1)
    gap = cumulative[:, :, None] - cumulative[:, None, :]
    mask = jnp.where(later[None], jnp.exp(jnp.minimum(gap, 0.0)), 0.0) * scale
    scores = low_back(jnp.einsum('thd,shd->hts', queries, keys_in, precision=lax.Precision.HIGHEST))
    weights = low(scores * mask)
    intra = jnp.einsum('hts,she->the', weights, values, precision=lax.Precision.HIGHEST)
    reach = jnp.exp(cumulative).T[:, :, None]
    inter = scale * reach * jnp.einsum('thd,hde->the', queries, state, precision=lax.Precision.HIGHEST)
    tail = jnp.exp(cumulative[:, -1:] - cumulative).T[:, :, None]
    update = jnp.einsum('shd,she->hde', keys_in * tail, values, precision=lax.Precision.HIGHEST)
    state_next = jnp.exp(cumulative[:, -1])[:, None, None] * state + update
    return (state_next, intra + inter)

def one_sequence(inputs, decay, weights_all):
    w_query, w_key, w_value, w_swish, w_output, w_gate, w_up, w_down, gain_attn, gain_ffn = weights_all
    scaled_one = low(normalize(inputs) * gain_attn)
    queries = low_back(low(matmul(scaled_one, w_query))).reshape(SEQUENCE_LENGTH, RETENTION_HEADS, KEY_DIM)
    keys_in = low_back(low(matmul(scaled_one, w_key))).reshape(SEQUENCE_LENGTH, RETENTION_HEADS, KEY_DIM)
    values = low_back(low(matmul(scaled_one, w_value))).reshape(SEQUENCE_LENGTH, RETENTION_HEADS, VALUE_DIM)
    blocks = SEQUENCE_LENGTH // BLOCK
    query_blocks = queries.reshape(blocks, BLOCK, RETENTION_HEADS, KEY_DIM)
    key_blocks = keys_in.reshape(blocks, BLOCK, RETENTION_HEADS, KEY_DIM)
    value_blocks = values.reshape(blocks, BLOCK, RETENTION_HEADS, VALUE_DIM)
    decay_blocks = decay.reshape(RETENTION_HEADS, blocks, BLOCK).transpose(1, 0, 2)
    start = jnp.zeros((RETENTION_HEADS, KEY_DIM, VALUE_DIM), jnp.float32)
    _, retained = lax.scan(jax.checkpoint(retention_block), start, (query_blocks, key_blocks, value_blocks, decay_blocks))
    retained = low_back(retained.reshape(SEQUENCE_LENGTH, RETENTION_HEADS, VALUE_DIM))
    head_out = low_back(low(normalize(retained))).reshape(SEQUENCE_LENGTH, RETENTION_HEADS * VALUE_DIM)
    swish_pre = low_back(matmul(scaled_one, w_swish))
    gated = low(jax.nn.silu(swish_pre) * head_out)
    residual = inputs + low_back(matmul(gated, w_output))
    scaled_two = low(normalize(residual) * gain_ffn)
    gate_pre = low_back(matmul(scaled_two, w_gate))
    up_pre = low_back(matmul(scaled_two, w_up))
    product = low(jax.nn.silu(gate_pre) * up_pre)
    return residual + low_back(matmul(product, w_down))

def reference(hidden_in, cotangent, log_decay, w_query, w_key, w_value, w_swish, w_output, w_gate, w_up, w_down, gain_attn, gain_ffn):
    params = tuple((item.astype(jnp.float32) for item in (w_query, w_key, w_value, w_swish, w_output, w_gate, w_up, w_down, gain_attn, gain_ffn)))

    def forward(inputs_all, *weights_all):
        return lax.map(lambda paired: one_sequence(paired[0], paired[1], weights_all), (inputs_all, log_decay))
    layer_out, pullback = jax.vjp(forward, hidden_in.astype(jnp.float32), *params)
    grads = pullback(cotangent.astype(jnp.float32))
    return (layer_out, grads[0], grads[1], grads[2], grads[3], grads[4], grads[5], grads[6], grads[7], grads[8], grads[9], grads[10])
```

```python
import math

import jax
import jax.numpy as jnp
from jax import lax
from jax.sharding import PartitionSpec as P

RETENTION_HEADS = 8
KEY_DIM = 256
VALUE_DIM = 432


EPSILON = 1e-06


def entering(value, axis, join, neutral, backward):
    count, mine = (lax.axis_size(axis), lax.axis_index(axis))
    pieces = jax.tree.map(lambda part: lax.all_gather(part, axis), value)
    if backward:
        pieces = jax.tree.map(lambda part: part[::-1], pieces)
        mine = count - 1 - mine
    subtotal = jax.tree.map(
        lambda part, zero: jnp.full_like(part, 0) + jnp.asarray(zero, part.dtype), value, neutral
    )

    def step(position, subtotal):
        longer = join(subtotal, jax.tree.map(lambda part: part[position], pieces))
        return jax.tree.map(lambda new, old: jnp.where(position < mine, new, old), longer, subtotal)

    return lax.fori_loop(0, count - 1, step, subtotal)


def normalize(values):
    inverse = lax.rsqrt(jnp.mean(values * values, axis=-1, keepdims=True) + EPSILON)
    return (values * inverse, inverse)


def norm_back(grad_normed, normed, inverse):
    return inverse * (grad_normed - normed * jnp.mean(grad_normed * normed, axis=-1, keepdims=True))


def swish_slope(values):
    sigma = jax.nn.sigmoid(values)
    return sigma * (1.0 + values * (1.0 - sigma))


def carry_forward(earlier, later):
    return (earlier[0] * later[0], later[0][:, None, None] * earlier[1] + later[1])


def carry_backward(earlier, later):
    return (earlier[0] * later[0], later[1] + later[0][:, None, None] * earlier[1])


def running_sum(values):
    size = values.shape[-1]
    upper = lax.broadcasted_iota(jnp.int32, (size, size), 0) <= lax.broadcasted_iota(
        jnp.int32, (size, size), 1
    )
    return jnp.dot(values, upper.astype(jnp.float32), precision=lax.Precision.HIGHEST)


def matmul(left, right):
    return jnp.dot(left, right, preferred_element_type=jnp.float32)


def local_any(
    hidden_in,
    cotangent,
    log_decay,
    w_query,
    w_key,
    w_value,
    w_swish,
    w_output,
    w_gate,
    w_up,
    w_down,
    gain_attn,
    gain_ffn,
):
    highest = lax.Precision.HIGHEST
    query_full, key_full, value_full, swish_full, output_full, gain_one = (
        lax.all_gather(w_query, ("dp", "ctx", "ulysses"), axis=0, tiled=True),
        lax.all_gather(w_key, ("dp", "ctx", "ulysses"), axis=0, tiled=True),
        lax.all_gather(w_value, ("dp", "ctx", "ulysses"), axis=0, tiled=True),
        lax.all_gather(w_swish, ("dp", "ctx", "ulysses"), axis=0, tiled=True),
        lax.all_gather(w_output, ("dp", "ctx", "ulysses"), axis=0, tiled=True),
        lax.all_gather(gain_attn, ("dp", "ctx", "ulysses"), axis=0, tiled=True),
    )
    inputs = hidden_in[0].astype(jnp.float32)
    tokens = inputs.shape[0]
    normed_one, inverse_one = normalize(inputs)
    scaled_one = (normed_one * gain_one.astype(jnp.float32)).astype(jnp.bfloat16)
    queries = (
        matmul(scaled_one, query_full)
        .astype(jnp.bfloat16)
        .reshape(tokens, RETENTION_HEADS, KEY_DIM)
    )
    keys_tok = (
        matmul(scaled_one, key_full).astype(jnp.bfloat16).reshape(tokens, RETENTION_HEADS, KEY_DIM)
    )
    values_tok = (
        matmul(scaled_one, value_full)
        .astype(jnp.bfloat16)
        .reshape(tokens, RETENTION_HEADS, VALUE_DIM)
    )
    swish_pre = matmul(scaled_one, swish_full)
    head_q, head_k, head_v = (
        lax.all_to_all(queries, "ulysses", split_axis=1, concat_axis=0, tiled=True),
        lax.all_to_all(keys_tok, "ulysses", split_axis=1, concat_axis=0, tiled=True),
        lax.all_to_all(values_tok, "ulysses", split_axis=1, concat_axis=0, tiled=True),
    )
    block = head_q.shape[0]
    scale = 1.0 / math.sqrt(KEY_DIM)
    cumulative = running_sum(log_decay[0])
    later = lax.broadcasted_iota(jnp.int32, (block, block), 0) >= lax.broadcasted_iota(
        jnp.int32, (block, block), 1
    )
    gap = cumulative[:, :, None] - cumulative[:, None, :]
    mask = jnp.where(later[None], jnp.exp(jnp.minimum(gap, 0.0)), 0.0) * scale
    scores = jnp.einsum("thd,shd->hts", head_q, head_k, preferred_element_type=jnp.float32)
    weights = (scores * mask).astype(jnp.bfloat16)
    intra = jnp.einsum("hts,she->the", weights, head_v, preferred_element_type=jnp.float32)
    query_f = head_q.astype(jnp.float32)
    key_f = head_k.astype(jnp.float32)
    value_f = head_v.astype(jnp.float32)
    tail = jnp.exp(cumulative[:, -1:] - cumulative).T[:, :, None]
    reach = jnp.exp(cumulative).T[:, :, None]
    update = jnp.einsum("shd,she->hde", key_f * tail, value_f, precision=highest)
    block_decay = jnp.exp(cumulative[:, -1])
    identity = (jnp.ones_like(block_decay), jnp.zeros_like(update))
    _, state_in = entering((block_decay, update), "ctx", carry_forward, identity, False)
    retained = intra + scale * reach * jnp.einsum(
        "thd,hde->the", query_f, state_in, precision=highest
    )
    head_normed, head_inverse = normalize(retained)
    head_out = head_normed.astype(jnp.bfloat16)
    token_out = lax.all_to_all(
        head_out, "ulysses", split_axis=0, concat_axis=1, tiled=True
    ).reshape(tokens, RETENTION_HEADS * VALUE_DIM)
    token_out_f = token_out.astype(jnp.float32)
    swish_act = jax.nn.silu(swish_pre)
    gated = (swish_act * token_out_f).astype(jnp.bfloat16)
    residual = inputs + matmul(gated, output_full)
    gate_full, up_full, down_full, gain_two = (
        lax.all_gather(w_gate, ("dp", "ctx", "ulysses"), axis=0, tiled=True),
        lax.all_gather(w_up, ("dp", "ctx", "ulysses"), axis=0, tiled=True),
        lax.all_gather(w_down, ("dp", "ctx", "ulysses"), axis=0, tiled=True),
        lax.all_gather(gain_ffn, ("dp", "ctx", "ulysses"), axis=0, tiled=True),
    )
    normed_two, inverse_two = normalize(residual)
    scaled_two = (normed_two * gain_two.astype(jnp.float32)).astype(jnp.bfloat16)
    gate_pre = matmul(scaled_two, gate_full)
    up_pre = matmul(scaled_two, up_full)
    product = (jax.nn.silu(gate_pre) * up_pre).astype(jnp.bfloat16)
    layer_out = residual + matmul(product, down_full)
    grad_top = cotangent[0].astype(jnp.float32)
    grad_top_low = grad_top.astype(jnp.bfloat16)
    grad_product = matmul(grad_top_low, down_full.T)
    grad_down_term = matmul(product.T, grad_top_low)
    grad_gate_pre = (grad_product * up_pre * swish_slope(gate_pre)).astype(jnp.bfloat16)
    grad_up_pre = (grad_product * jax.nn.silu(gate_pre)).astype(jnp.bfloat16)
    grad_gate_term = matmul(scaled_two.T, grad_gate_pre)
    grad_up_term = matmul(scaled_two.T, grad_up_pre)
    grad_scaled_two = matmul(grad_gate_pre, gate_full.T) + matmul(grad_up_pre, up_full.T)
    grad_gain_two = jnp.sum(grad_scaled_two * normed_two, axis=0)
    grad_residual = grad_top + norm_back(
        grad_scaled_two * gain_two.astype(jnp.float32), normed_two, inverse_two
    )
    grad_gate, grad_up, grad_down, grad_gain_ffn = (
        lax.psum_scatter(grad_gate_term, ("dp", "ctx", "ulysses"), scatter_dimension=0, tiled=True),
        lax.psum_scatter(grad_up_term, ("dp", "ctx", "ulysses"), scatter_dimension=0, tiled=True),
        lax.psum_scatter(grad_down_term, ("dp", "ctx", "ulysses"), scatter_dimension=0, tiled=True),
        lax.psum_scatter(grad_gain_two, ("dp", "ctx", "ulysses"), scatter_dimension=0, tiled=True),
    )
    grad_y = grad_residual.astype(jnp.bfloat16)
    grad_output_term = matmul(gated.T, grad_y)
    grad_gated = matmul(grad_y, output_full.T)
    grad_swish_pre = (grad_gated * token_out_f * swish_slope(swish_pre)).astype(jnp.bfloat16)
    grad_token_out = (
        (grad_gated * swish_act).astype(jnp.bfloat16).reshape(tokens, RETENTION_HEADS, VALUE_DIM)
    )
    grad_swish_term = matmul(scaled_one.T, grad_swish_pre)
    grad_head_out = lax.all_to_all(
        grad_token_out, "ulysses", split_axis=1, concat_axis=0, tiled=True
    ).astype(jnp.float32)
    grad_retained = norm_back(grad_head_out, head_normed, head_inverse).astype(jnp.bfloat16)
    grad_retained_f = grad_retained.astype(jnp.float32)
    grad_weights = jnp.einsum(
        "the,she->hts", grad_retained, head_v, preferred_element_type=jnp.float32
    )
    grad_scores = (grad_weights * mask).astype(jnp.bfloat16)
    grad_state_in = scale * jnp.einsum(
        "thd,the->hde", query_f * reach, grad_retained_f, precision=highest
    )
    _, grad_update = entering((block_decay, grad_state_in), "ctx", carry_backward, identity, True)
    grad_head_q = jnp.einsum(
        "hts,shd->thd", grad_scores, head_k, preferred_element_type=jnp.float32
    ) + scale * reach * jnp.einsum("the,hde->thd", grad_retained_f, state_in, precision=highest)
    grad_head_k = jnp.einsum(
        "hts,thd->shd", grad_scores, head_q, preferred_element_type=jnp.float32
    ) + tail * jnp.einsum("she,hde->shd", value_f, grad_update, precision=highest)
    grad_head_v = jnp.einsum(
        "hts,the->she", weights, grad_retained, preferred_element_type=jnp.float32
    ) + tail * jnp.einsum("shd,hde->she", key_f, grad_update, precision=highest)
    grad_queries, grad_keys, grad_values = (
        lax.all_to_all(
            grad_head_q.astype(jnp.bfloat16), "ulysses", split_axis=0, concat_axis=1, tiled=True
        ),
        lax.all_to_all(
            grad_head_k.astype(jnp.bfloat16), "ulysses", split_axis=0, concat_axis=1, tiled=True
        ),
        lax.all_to_all(
            grad_head_v.astype(jnp.bfloat16), "ulysses", split_axis=0, concat_axis=1, tiled=True
        ),
    )
    grad_queries = grad_queries.reshape(tokens, RETENTION_HEADS * KEY_DIM)
    grad_keys = grad_keys.reshape(tokens, RETENTION_HEADS * KEY_DIM)
    grad_values = grad_values.reshape(tokens, RETENTION_HEADS * VALUE_DIM)
    grad_query_term = matmul(scaled_one.T, grad_queries)
    grad_key_term = matmul(scaled_one.T, grad_keys)
    grad_value_term = matmul(scaled_one.T, grad_values)
    grad_scaled_one = (
        matmul(grad_queries, query_full.T)
        + matmul(grad_keys, key_full.T)
        + matmul(grad_values, value_full.T)
        + matmul(grad_swish_pre, swish_full.T)
    )
    grad_gain_one = jnp.sum(grad_scaled_one * normed_one, axis=0)
    grad_input = grad_residual + norm_back(
        grad_scaled_one * gain_one.astype(jnp.float32), normed_one, inverse_one
    )
    grad_query, grad_key, grad_value, grad_swish, grad_output, grad_gain_attn = (
        lax.psum_scatter(
            grad_query_term, ("dp", "ctx", "ulysses"), scatter_dimension=0, tiled=True
        ),
        lax.psum_scatter(grad_key_term, ("dp", "ctx", "ulysses"), scatter_dimension=0, tiled=True),
        lax.psum_scatter(
            grad_value_term, ("dp", "ctx", "ulysses"), scatter_dimension=0, tiled=True
        ),
        lax.psum_scatter(
            grad_swish_term, ("dp", "ctx", "ulysses"), scatter_dimension=0, tiled=True
        ),
        lax.psum_scatter(
            grad_output_term, ("dp", "ctx", "ulysses"), scatter_dimension=0, tiled=True
        ),
        lax.psum_scatter(grad_gain_one, ("dp", "ctx", "ulysses"), scatter_dimension=0, tiled=True),
    )
    return (
        layer_out[None],
        grad_input[None],
        grad_query,
        grad_key,
        grad_value,
        grad_swish,
        grad_output,
        grad_gate,
        grad_up,
        grad_down,
        grad_gain_attn,
        grad_gain_ffn,
    )


HEAD_AXES = ("dp", "ulysses")
FF_AXES = ("dp", "ctx")


def dot_t(left, right):
    return lax.dot_general(left, right, (((0,), (0,)), ((), ())), preferred_element_type=jnp.float32)


def dot_nt(left, right):
    return lax.dot_general(left, right, (((1,), (1,)), ((), ())), preferred_element_type=jnp.float32)


def by_head(weight, width):
    rows = weight.shape[0]
    return (
        weight.reshape(rows, 4, 2, width).transpose(2, 1, 0, 3).reshape(8, rows, width)
    )


def from_heads(parts, width):
    rows = parts.shape[1]
    return parts.reshape(2, 4, rows, width).transpose(2, 1, 0, 3).reshape(rows, 8 * width)


def local(
    hidden_in,
    cotangent,
    log_decay,
    w_query,
    w_key,
    w_value,
    w_swish,
    w_output,
    w_gate,
    w_up,
    w_down,
    gain_attn,
    gain_ffn,
):
    bf16, f32 = jnp.bfloat16, jnp.float32
    everywhere = ("dp", "ctx", "ulysses")
    dp, ctx, uly = (lax.axis_index(a) for a in everywhere)
    tokens = hidden_in.shape[1]
    width = hidden_in.shape[2]
    rows = w_query.shape[0]
    out_rows = w_output.shape[0]
    key, val, ff = KEY_DIM, VALUE_DIM, w_gate.shape[1] // 8

    packed = jnp.concatenate(
        [by_head(w_query, key), by_head(w_key, key), by_head(w_value, val), by_head(w_swish, val)],
        axis=2,
    )
    attn_cols = packed.shape[2]
    packed = lax.all_to_all(packed, HEAD_AXES, split_axis=0, concat_axis=0, tiled=True)
    packed = lax.all_gather(packed, "ctx", axis=0)
    w_attn = (
        packed.reshape(4, 2, 4, rows, attn_cols)
        .transpose(1, 0, 2, 3, 4)
        .reshape(32 * rows, attn_cols)
    )
    quarter = width // 4
    pieces = []
    for shift in range(4):
        piece = lax.dynamic_slice_in_dim(w_output, (uly + shift) % 4 * quarter, quarter, axis=1)
        perm = []
        for d in range(2):
            for c in range(4):
                for u in range(4):
                    h = d * 4 + c
                    perm.append((d * 16 + c * 4 + u, (h % 2) * 16 + (u + shift) % 4 * 4 + h // 2))
        pieces.append(lax.ppermute(piece, everywhere, perm))
    mine = jnp.zeros((4, out_rows, quarter), bf16)
    for shift in range(4):
        mine = lax.dynamic_update_index_in_dim(mine, pieces[shift], (ctx - shift) % 4, 0)
    w_out = (
        lax.all_gather(mine, "ctx", axis=0).transpose(1, 2, 0, 3).reshape(4 * out_rows, width)
    )
    gate_up = jnp.concatenate(
        [
            w_gate.reshape(rows, 8, ff).transpose(1, 0, 2),
            w_up.reshape(rows, 8, ff).transpose(1, 0, 2),
        ],
        axis=2,
    )
    gate_up = lax.all_to_all(gate_up, FF_AXES, split_axis=0, concat_axis=0, tiled=True)
    gate_up = lax.all_gather(gate_up, "ulysses", axis=0)
    w_gu = (
        gate_up.reshape(4, 8, rows, 2 * ff).transpose(1, 0, 2, 3).reshape(32 * rows, 2 * ff)
    )
    w_dn = lax.all_gather(w_down, "ulysses", axis=0, tiled=True)

    gain_one = lax.all_gather(gain_attn, everywhere, axis=0, tiled=True).astype(f32)
    gain_two = lax.all_gather(gain_ffn, everywhere, axis=0, tiled=True).astype(f32)

    top_all = lax.all_gather(cotangent[0], FF_AXES, axis=0, tiled=True)
    hidden_all = lax.all_gather(hidden_in[0], HEAD_AXES, axis=0, tiled=True)
    normed_all, _ = normalize(hidden_all.astype(f32))
    scaled_one = (normed_all * gain_one).astype(bf16)
    qkvs = matmul(scaled_one, w_attn)
    block = 4 * tokens
    q = qkvs[:, :key].astype(bf16).reshape(2, block, key)
    k = qkvs[:, key : 2 * key].astype(bf16).reshape(2, block, key)
    v = qkvs[:, 2 * key : 2 * key + val].astype(bf16).reshape(2, block, val)
    swish_pre = qkvs[:, 2 * key + val :]

    own = lax.dynamic_slice_in_dim(log_decay[0], dp, 1, axis=0)
    other = lax.ppermute(
        lax.dynamic_slice_in_dim(log_decay[0], 1 - dp, 1, axis=0), "dp", [(0, 1), (1, 0)]
    )
    decay = jnp.where(
        dp == 0, jnp.concatenate([own, other]), jnp.concatenate([other, own])
    )
    scale = 1.0 / math.sqrt(KEY_DIM)
    cumulative = running_sum(decay)
    later = lax.broadcasted_iota(jnp.int32, (block, block), 0) >= lax.broadcasted_iota(
        jnp.int32, (block, block), 1
    )
    gap = cumulative[:, :, None] - cumulative[:, None, :]
    mask = jnp.where(later[None], jnp.exp(jnp.minimum(gap, 0.0)), 0.0) * scale
    last = cumulative[:, -1:]
    tail = jnp.exp(last - cumulative)[:, :, None]
    reach = jnp.exp(cumulative)[:, :, None]

    def bdot(pattern, a, b):
        return jnp.einsum(pattern, a, b, preferred_element_type=f32)

    weights = (bdot("btd,bsd->bts", q, k) * mask).astype(bf16)
    k_tail = (k.astype(f32) * tail).astype(bf16)
    update = bdot("bsd,bse->bde", k_tail, v)
    lasts = lax.all_gather(last[:, 0], "ctx", axis=0)
    spots = jnp.arange(4)
    before = jnp.stack(
        [
            jnp.where(
                j < ctx,
                jnp.exp(jnp.sum(jnp.where(((spots > j) & (spots < ctx))[:, None], lasts, 0.0), 0)),
                0.0,
            )
            for j in range(4)
        ]
    )
    after = jnp.stack(
        [
            jnp.where(
                j > ctx,
                jnp.exp(jnp.sum(jnp.where(((spots < j) & (spots > ctx))[:, None], lasts, 0.0), 0)),
                0.0,
            )
            for j in range(4)
        ]
    )
    updates = lax.all_gather(update.astype(bf16), "ctx", axis=0).astype(f32)
    state_in = jnp.sum(before[:, :, None, None] * updates, axis=0).astype(bf16)
    retained = bdot("bts,bse->bte", weights, v) + scale * reach * bdot("btd,bde->bte", q, state_in)
    head_normed, head_inverse = normalize(retained)
    head_out = head_normed.astype(bf16).reshape(2 * block, val).astype(f32)
    swish_act = jax.nn.silu(swish_pre)
    gated = (swish_act * head_out).astype(bf16)
    attn = lax.psum_scatter(
        matmul(gated, w_out).astype(bf16), HEAD_AXES, scatter_dimension=0, tiled=True
    )
    inputs = hidden_in[0].astype(f32)
    residual = inputs + attn.astype(f32)

    normed_two, inverse_two = normalize(residual)
    scaled_two = lax.all_gather(
        (normed_two * gain_two).astype(bf16), FF_AXES, axis=0, tiled=True
    )
    gu = matmul(scaled_two, w_gu)
    gate_pre, up_pre = gu[:, :ff], gu[:, ff:]
    gate_act = jax.nn.silu(gate_pre)
    product = (gate_act * up_pre).astype(bf16)
    grad_product = dot_nt(top_all, w_dn)
    grad_gu = jnp.concatenate(
        [
            (grad_product * up_pre * swish_slope(gate_pre)).astype(bf16),
            (grad_product * gate_act).astype(bf16),
        ],
        axis=1,
    )
    gs2 = lax.psum_scatter(
        dot_nt(grad_gu, w_gu).astype(bf16), FF_AXES, scatter_dimension=0, tiled=True
    ).astype(f32)
    out_part = lax.psum_scatter(
        matmul(product, w_dn).astype(bf16), FF_AXES, scatter_dimension=0, tiled=True
    )
    layer_out = residual + out_part.astype(f32)
    grad_top = cotangent[0].astype(f32)
    gain_two_term = jnp.sum(gs2 * normed_two, axis=0)
    grad_residual = grad_top + norm_back(gs2 * gain_two, normed_two, inverse_two)
    grad_y = lax.all_gather(grad_residual.astype(bf16), HEAD_AXES, axis=0, tiled=True)

    grad_down = lax.psum_scatter(
        dot_t(product, top_all).astype(bf16).reshape(4, out_rows, width),
        "ulysses",
        scatter_dimension=0,
        tiled=True,
    )[0].astype(f32)
    ggu = dot_t(scaled_two, grad_gu).astype(bf16).reshape(8, 4, rows, 2 * ff).transpose(1, 0, 2, 3)
    ggu = lax.psum_scatter(ggu, "ulysses", scatter_dimension=0, tiled=True)[0]
    ggu = lax.all_to_all(ggu, FF_AXES, split_axis=0, concat_axis=0, tiled=True).astype(f32)
    grad_gate = ggu[:, :, :ff].transpose(1, 0, 2).reshape(rows, 8 * ff)
    grad_up = ggu[:, :, ff:].transpose(1, 0, 2).reshape(rows, 8 * ff)

    grad_gated = dot_nt(grad_y, w_out)
    g_out = dot_t(gated, grad_y).astype(bf16)
    grad_swish_pre = (grad_gated * head_out * swish_slope(swish_pre)).astype(bf16)
    grad_head = (grad_gated * swish_act).astype(bf16).astype(f32).reshape(2, block, val)
    grad_retained = norm_back(grad_head, head_normed, head_inverse).astype(bf16)
    grad_scores = (bdot("bte,bse->bts", grad_retained, v) * mask).astype(bf16)
    q_reach = (q.astype(f32) * (reach * scale)).astype(bf16)
    grad_state = bdot("btd,bte->bde", q_reach, grad_retained)
    grad_states = lax.all_gather(grad_state.astype(bf16), "ctx", axis=0).astype(f32)
    grad_update = jnp.sum(after[:, :, None, None] * grad_states, axis=0).astype(bf16)
    grad_q = bdot("bts,bsd->btd", grad_scores, k) + scale * reach * bdot(
        "bte,bde->btd", grad_retained, state_in
    )
    grad_k = bdot("bts,btd->bsd", grad_scores, q) + tail * bdot("bse,bde->bsd", v, grad_update)
    grad_v = bdot("bts,bte->bse", weights, grad_retained) + tail * bdot(
        "bsd,bde->bse", k, grad_update
    )
    grad_cat = jnp.concatenate(
        [
            grad_q.astype(bf16).reshape(2 * block, key),
            grad_k.astype(bf16).reshape(2 * block, key),
            grad_v.astype(bf16).reshape(2 * block, val),
            grad_swish_pre,
        ],
        axis=1,
    )
    gs1 = lax.psum_scatter(
        dot_nt(grad_cat, w_attn).astype(bf16), HEAD_AXES, scatter_dimension=0, tiled=True
    ).astype(f32)
    normed_one, inverse_one = normalize(inputs)
    gain_one_term = jnp.sum(gs1 * normed_one, axis=0)
    grad_input = grad_residual + norm_back(gs1 * gain_one, normed_one, inverse_one)

    gcat = dot_t(scaled_one, grad_cat).astype(bf16).reshape(2, 4, 4, rows, attn_cols)
    gcat = lax.psum_scatter(
        gcat.transpose(1, 0, 2, 3, 4), "ctx", scatter_dimension=0, tiled=True
    )
    gcat = lax.all_to_all(
        gcat.reshape(8, rows, attn_cols), HEAD_AXES, split_axis=0, concat_axis=0, tiled=True
    ).astype(f32)
    grad_query = from_heads(gcat[:, :, :key], key)
    grad_key = from_heads(gcat[:, :, key : 2 * key], key)
    grad_value = from_heads(gcat[:, :, 2 * key : 2 * key + val], val)
    grad_swish = from_heads(gcat[:, :, 2 * key + val :], val)

    g_out = g_out.reshape(4, out_rows, 4, quarter).transpose(2, 0, 1, 3)
    g_out = lax.psum_scatter(g_out, "ctx", scatter_dimension=0, tiled=True)[0]
    grad_output = jnp.zeros((4, out_rows, quarter), bf16)
    for shift in range(4):
        piece = lax.dynamic_index_in_dim(g_out, (ctx - shift) % 4, 0, keepdims=False)
        perm = []
        for d in range(2):
            for c in range(4):
                for u in range(4):
                    h = d * 4 + c
                    perm.append(((h % 2) * 16 + (u + shift) % 4 * 4 + h // 2, d * 16 + c * 4 + u))
        got = lax.ppermute(piece, everywhere, perm)
        grad_output = lax.dynamic_update_index_in_dim(grad_output, got, (uly + shift) % 4, 0)
    grad_output = grad_output.astype(f32).transpose(1, 0, 2).reshape(out_rows, width)

    gain_terms = lax.psum_scatter(
        jnp.stack([gain_one_term, gain_two_term]), everywhere, scatter_dimension=1, tiled=True
    )
    return (
        layer_out[None],
        grad_input[None],
        grad_query,
        grad_key,
        grad_value,
        grad_swish,
        grad_output,
        grad_gate,
        grad_up,
        grad_down,
        gain_terms[0],
        gain_terms[1],
    )


def solution(mesh):
    planned = (mesh.shape["dp"], mesh.shape["ctx"], mesh.shape["ulysses"]) == (2, 4, 4)
    placed = (
        P("dp", ("ctx", "ulysses"), None),
        P("dp", ("ctx", "ulysses"), None),
        P("dp", "ulysses", "ctx"),
        P(("dp", "ctx", "ulysses"), None),
        P(("dp", "ctx", "ulysses"), None),
        P(("dp", "ctx", "ulysses"), None),
        P(("dp", "ctx", "ulysses"), None),
        P(("dp", "ctx", "ulysses"), None),
        P(("dp", "ctx", "ulysses"), None),
        P(("dp", "ctx", "ulysses"), None),
        P(("dp", "ctx", "ulysses"), None),
        P(("dp", "ctx", "ulysses")),
        P(("dp", "ctx", "ulysses")),
    )
    return jax.shard_map(
        local if planned else local_any,
        mesh=mesh,
        in_specs=placed,
        out_specs=(
            P("dp", ("ctx", "ulysses"), None),
            P("dp", ("ctx", "ulysses"), None),
            P(("dp", "ctx", "ulysses"), None),
            P(("dp", "ctx", "ulysses"), None),
            P(("dp", "ctx", "ulysses"), None),
            P(("dp", "ctx", "ulysses"), None),
            P(("dp", "ctx", "ulysses"), None),
            P(("dp", "ctx", "ulysses"), None),
            P(("dp", "ctx", "ulysses"), None),
            P(("dp", "ctx", "ulysses"), None),
            P(("dp", "ctx", "ulysses")),
            P(("dp", "ctx", "ulysses")),
        ),
        check_vma=False,
    )
```

```python
import functools
import math

import jax
import jax.numpy as jnp
from jax import lax
from jax.experimental import pallas as pl
from jax.experimental.pallas import tpu as pltpu
from jax.sharding import PartitionSpec as P

RETENTION_HEADS = 8
KEY_DIM = 256
VALUE_DIM = 432


EPSILON = 1e-06
DP, CTX, ULY = "dp", "ctx", "ulysses"
EVERYWHERE = (DP, CTX, ULY)


def entering(value, axis, join, neutral, backward):
    count, mine = (lax.axis_size(axis), lax.axis_index(axis))
    pieces = jax.tree.map(lambda part: lax.all_gather(part, axis), value)
    if backward:
        pieces = jax.tree.map(lambda part: part[::-1], pieces)
        mine = count - 1 - mine
    subtotal = jax.tree.map(
        lambda part, zero: jnp.full_like(part, 0) + jnp.asarray(zero, part.dtype), value, neutral
    )

    def step(position, subtotal):
        longer = join(subtotal, jax.tree.map(lambda part: part[position], pieces))
        return jax.tree.map(lambda new, old: jnp.where(position < mine, new, old), longer, subtotal)

    return lax.fori_loop(0, count - 1, step, subtotal)


def normalize(values):
    inverse = lax.rsqrt(jnp.mean(values * values, axis=-1, keepdims=True) + EPSILON)
    return (values * inverse, inverse)


def norm_back(grad_normed, normed, inverse):
    return inverse * (grad_normed - normed * jnp.mean(grad_normed * normed, axis=-1, keepdims=True))


def swish_slope(values):
    sigma = jax.nn.sigmoid(values)
    return sigma * (1.0 + values * (1.0 - sigma))


def carry_forward(earlier, later):
    return (earlier[0] * later[0], later[0][:, None, None] * earlier[1] + later[1])


def carry_backward(earlier, later):
    return (earlier[0] * later[0], later[1] + later[0][:, None, None] * earlier[1])


def running_sum(values):
    size = values.shape[-1]
    upper = lax.broadcasted_iota(jnp.int32, (size, size), 0) <= lax.broadcasted_iota(
        jnp.int32, (size, size), 1
    )
    return jnp.dot(values, upper.astype(jnp.float32), precision=lax.Precision.HIGHEST)


def matmul(left, right):
    return jnp.dot(left, right, preferred_element_type=jnp.float32)


def local_any(
    hidden_in,
    cotangent,
    log_decay,
    w_query,
    w_key,
    w_value,
    w_swish,
    w_output,
    w_gate,
    w_up,
    w_down,
    gain_attn,
    gain_ffn,
):
    highest = lax.Precision.HIGHEST
    query_full, key_full, value_full, swish_full, output_full, gain_one = (
        lax.all_gather(w_query, EVERYWHERE, axis=0, tiled=True),
        lax.all_gather(w_key, EVERYWHERE, axis=0, tiled=True),
        lax.all_gather(w_value, EVERYWHERE, axis=0, tiled=True),
        lax.all_gather(w_swish, EVERYWHERE, axis=0, tiled=True),
        lax.all_gather(w_output, EVERYWHERE, axis=0, tiled=True),
        lax.all_gather(gain_attn, EVERYWHERE, axis=0, tiled=True),
    )
    inputs = hidden_in[0].astype(jnp.float32)
    tokens = inputs.shape[0]
    normed_one, inverse_one = normalize(inputs)
    scaled_one = (normed_one * gain_one.astype(jnp.float32)).astype(jnp.bfloat16)
    queries = (
        matmul(scaled_one, query_full)
        .astype(jnp.bfloat16)
        .reshape(tokens, RETENTION_HEADS, KEY_DIM)
    )
    keys_tok = (
        matmul(scaled_one, key_full).astype(jnp.bfloat16).reshape(tokens, RETENTION_HEADS, KEY_DIM)
    )
    values_tok = (
        matmul(scaled_one, value_full)
        .astype(jnp.bfloat16)
        .reshape(tokens, RETENTION_HEADS, VALUE_DIM)
    )
    swish_pre = matmul(scaled_one, swish_full)
    head_q, head_k, head_v = (
        lax.all_to_all(queries, ULY, split_axis=1, concat_axis=0, tiled=True),
        lax.all_to_all(keys_tok, ULY, split_axis=1, concat_axis=0, tiled=True),
        lax.all_to_all(values_tok, ULY, split_axis=1, concat_axis=0, tiled=True),
    )
    block = head_q.shape[0]
    scale = 1.0 / math.sqrt(KEY_DIM)
    cumulative = running_sum(log_decay[0])
    later = lax.broadcasted_iota(jnp.int32, (block, block), 0) >= lax.broadcasted_iota(
        jnp.int32, (block, block), 1
    )
    gap = cumulative[:, :, None] - cumulative[:, None, :]
    mask = jnp.where(later[None], jnp.exp(jnp.minimum(gap, 0.0)), 0.0) * scale
    scores = jnp.einsum("thd,shd->hts", head_q, head_k, preferred_element_type=jnp.float32)
    weights = (scores * mask).astype(jnp.bfloat16)
    intra = jnp.einsum("hts,she->the", weights, head_v, preferred_element_type=jnp.float32)
    query_f = head_q.astype(jnp.float32)
    key_f = head_k.astype(jnp.float32)
    value_f = head_v.astype(jnp.float32)
    tail = jnp.exp(cumulative[:, -1:] - cumulative).T[:, :, None]
    reach = jnp.exp(cumulative).T[:, :, None]
    update = jnp.einsum("shd,she->hde", key_f * tail, value_f, precision=highest)
    block_decay = jnp.exp(cumulative[:, -1])
    identity = (jnp.ones_like(block_decay), jnp.zeros_like(update))
    _, state_in = entering((block_decay, update), CTX, carry_forward, identity, False)
    retained = intra + scale * reach * jnp.einsum(
        "thd,hde->the", query_f, state_in, precision=highest
    )
    head_normed, head_inverse = normalize(retained)
    head_out = head_normed.astype(jnp.bfloat16)
    token_out = lax.all_to_all(
        head_out, ULY, split_axis=0, concat_axis=1, tiled=True
    ).reshape(tokens, RETENTION_HEADS * VALUE_DIM)
    token_out_f = token_out.astype(jnp.float32)
    swish_act = jax.nn.silu(swish_pre)
    gated = (swish_act * token_out_f).astype(jnp.bfloat16)
    residual = inputs + matmul(gated, output_full)
    gate_full, up_full, down_full, gain_two = (
        lax.all_gather(w_gate, EVERYWHERE, axis=0, tiled=True),
        lax.all_gather(w_up, EVERYWHERE, axis=0, tiled=True),
        lax.all_gather(w_down, EVERYWHERE, axis=0, tiled=True),
        lax.all_gather(gain_ffn, EVERYWHERE, axis=0, tiled=True),
    )
    normed_two, inverse_two = normalize(residual)
    scaled_two = (normed_two * gain_two.astype(jnp.float32)).astype(jnp.bfloat16)
    gate_pre = matmul(scaled_two, gate_full)
    up_pre = matmul(scaled_two, up_full)
    product = (jax.nn.silu(gate_pre) * up_pre).astype(jnp.bfloat16)
    layer_out = residual + matmul(product, down_full)
    grad_top = cotangent[0].astype(jnp.float32)
    grad_top_low = grad_top.astype(jnp.bfloat16)
    grad_product = matmul(grad_top_low, down_full.T)
    grad_down_term = matmul(product.T, grad_top_low)
    grad_gate_pre = (grad_product * up_pre * swish_slope(gate_pre)).astype(jnp.bfloat16)
    grad_up_pre = (grad_product * jax.nn.silu(gate_pre)).astype(jnp.bfloat16)
    grad_gate_term = matmul(scaled_two.T, grad_gate_pre)
    grad_up_term = matmul(scaled_two.T, grad_up_pre)
    grad_scaled_two = matmul(grad_gate_pre, gate_full.T) + matmul(grad_up_pre, up_full.T)
    grad_gain_two = jnp.sum(grad_scaled_two * normed_two, axis=0)
    grad_residual = grad_top + norm_back(
        grad_scaled_two * gain_two.astype(jnp.float32), normed_two, inverse_two
    )
    grad_gate, grad_up, grad_down, grad_gain_ffn = (
        lax.psum_scatter(grad_gate_term, EVERYWHERE, scatter_dimension=0, tiled=True),
        lax.psum_scatter(grad_up_term, EVERYWHERE, scatter_dimension=0, tiled=True),
        lax.psum_scatter(grad_down_term, EVERYWHERE, scatter_dimension=0, tiled=True),
        lax.psum_scatter(grad_gain_two, EVERYWHERE, scatter_dimension=0, tiled=True),
    )
    grad_y = grad_residual.astype(jnp.bfloat16)
    grad_output_term = matmul(gated.T, grad_y)
    grad_gated = matmul(grad_y, output_full.T)
    grad_swish_pre = (grad_gated * token_out_f * swish_slope(swish_pre)).astype(jnp.bfloat16)
    grad_token_out = (
        (grad_gated * swish_act).astype(jnp.bfloat16).reshape(tokens, RETENTION_HEADS, VALUE_DIM)
    )
    grad_swish_term = matmul(scaled_one.T, grad_swish_pre)
    grad_head_out = lax.all_to_all(
        grad_token_out, ULY, split_axis=1, concat_axis=0, tiled=True
    ).astype(jnp.float32)
    grad_retained = norm_back(grad_head_out, head_normed, head_inverse).astype(jnp.bfloat16)
    grad_retained_f = grad_retained.astype(jnp.float32)
    grad_weights = jnp.einsum(
        "the,she->hts", grad_retained, head_v, preferred_element_type=jnp.float32
    )
    grad_scores = (grad_weights * mask).astype(jnp.bfloat16)
    grad_state_in = scale * jnp.einsum(
        "thd,the->hde", query_f * reach, grad_retained_f, precision=highest
    )
    _, grad_update = entering((block_decay, grad_state_in), CTX, carry_backward, identity, True)
    grad_head_q = jnp.einsum(
        "hts,shd->thd", grad_scores, head_k, preferred_element_type=jnp.float32
    ) + scale * reach * jnp.einsum("the,hde->thd", grad_retained_f, state_in, precision=highest)
    grad_head_k = jnp.einsum(
        "hts,thd->shd", grad_scores, head_q, preferred_element_type=jnp.float32
    ) + tail * jnp.einsum("she,hde->shd", value_f, grad_update, precision=highest)
    grad_head_v = jnp.einsum(
        "hts,the->she", weights, grad_retained, preferred_element_type=jnp.float32
    ) + tail * jnp.einsum("shd,hde->she", key_f, grad_update, precision=highest)
    grad_queries, grad_keys, grad_values = (
        lax.all_to_all(
            grad_head_q.astype(jnp.bfloat16), ULY, split_axis=0, concat_axis=1, tiled=True
        ),
        lax.all_to_all(
            grad_head_k.astype(jnp.bfloat16), ULY, split_axis=0, concat_axis=1, tiled=True
        ),
        lax.all_to_all(
            grad_head_v.astype(jnp.bfloat16), ULY, split_axis=0, concat_axis=1, tiled=True
        ),
    )
    grad_queries = grad_queries.reshape(tokens, RETENTION_HEADS * KEY_DIM)
    grad_keys = grad_keys.reshape(tokens, RETENTION_HEADS * KEY_DIM)
    grad_values = grad_values.reshape(tokens, RETENTION_HEADS * VALUE_DIM)
    grad_query_term = matmul(scaled_one.T, grad_queries)
    grad_key_term = matmul(scaled_one.T, grad_keys)
    grad_value_term = matmul(scaled_one.T, grad_values)
    grad_scaled_one = (
        matmul(grad_queries, query_full.T)
        + matmul(grad_keys, key_full.T)
        + matmul(grad_values, value_full.T)
        + matmul(grad_swish_pre, swish_full.T)
    )
    grad_gain_one = jnp.sum(grad_scaled_one * normed_one, axis=0)
    grad_input = grad_residual + norm_back(
        grad_scaled_one * gain_one.astype(jnp.float32), normed_one, inverse_one
    )
    grad_query, grad_key, grad_value, grad_swish, grad_output, grad_gain_attn = (
        lax.psum_scatter(
            grad_query_term, EVERYWHERE, scatter_dimension=0, tiled=True
        ),
        lax.psum_scatter(grad_key_term, EVERYWHERE, scatter_dimension=0, tiled=True),
        lax.psum_scatter(
            grad_value_term, EVERYWHERE, scatter_dimension=0, tiled=True
        ),
        lax.psum_scatter(
            grad_swish_term, EVERYWHERE, scatter_dimension=0, tiled=True
        ),
        lax.psum_scatter(
            grad_output_term, EVERYWHERE, scatter_dimension=0, tiled=True
        ),
        lax.psum_scatter(grad_gain_one, EVERYWHERE, scatter_dimension=0, tiled=True),
    )
    return (
        layer_out[None],
        grad_input[None],
        grad_query,
        grad_key,
        grad_value,
        grad_swish,
        grad_output,
        grad_gate,
        grad_up,
        grad_down,
        grad_gain_attn,
        grad_gain_ffn,
    )


MESH = pl.DeviceIdType.MESH
BF16, F32 = jnp.bfloat16, jnp.float32
HBM, VMEM = pltpu.HBM, pltpu.VMEM
N_SEMS = 160


def dot_t(left, right):
    return lax.dot_general(left, right, (((0,), (0,)), ((), ())), preferred_element_type=F32)


def dot_nt(left, right):
    return lax.dot_general(left, right, (((1,), (1,)), ((), ())), preferred_element_type=F32)


def pair_dot(left_axis, right_axis, left, right):
    dims = (((left_axis,), (right_axis,)), ((0,), (0,)))
    return lax.dot_general(left, right, dims, preferred_element_type=F32)


class Place:
    def __init__(self, uly):
        self.dp, self.ctx, self.uly = lax.axis_index(DP), lax.axis_index(CTX), uly
        odd = lax.rem(self.ctx, 2)
        self.xn = self.ctx + 1 - 2 * odd
        self.yn = lax.rem(self.ctx + 2, 4)
        self.dg = self.yn + 1 - 2 * odd
        self.other = 1 - self.dp

    def at(self, dp=None, ctx=None, uly=None):
        return (
            self.dp if dp is None else dp,
            self.ctx if ctx is None else ctx,
            self.uly if uly is None else uly,
        )


class Mover:
    def __init__(self, place, names, send, recv):
        self.place, self.names, self.send_sems, self.recv_sems = place, names, send, recv
        self.sent = []

    def number(self, name):
        return self.names.setdefault(name, len(self.names))

    def remote(self, name, src, dst, device):
        k = self.number(name)
        return pltpu.make_async_remote_copy(
            src_ref=src,
            dst_ref=dst,
            send_sem=self.send_sems.at[k],
            recv_sem=self.recv_sems.at[k],
            device_id=device,
            device_id_type=MESH,
        )

    def send(self, name, src, dst, device):
        copy = self.remote(name, src, dst, device)
        copy.start()
        self.sent.append(copy)

    def arrive(self, name, dst):
        self.remote(name, dst, dst, self.place.at(dp=self.place.other)).wait_recv()

    def local(self, name, src, dst):
        copy = pltpu.make_async_copy(src, dst, self.send_sems.at[self.number(name)])
        copy.start()
        return copy

    def finish(self):
        for copy in self.sent:
            copy.wait_send()


def greet(devices):
    barrier = pltpu.get_barrier_semaphore()
    for device in devices:
        pl.semaphore_signal(barrier, inc=1, device_id=device, device_id_type=MESH)
    pl.semaphore_wait(barrier, len(devices))


def together(streams):
    streams = list(streams)
    while streams:
        left = []
        for stream in streams:
            if next(stream, 0) is None:
                left.append(stream)
        streams = left


def later(stream, stages):
    for _ in range(stages):
        yield
    yield from stream


def add_up(dst, sources, step=32):
    rows, columns = dst.shape
    by_rows = rows % step == 0
    step = step if by_rows else 256

    def body(i, carry):
        part = pl.ds(pl.multiple_of(i * step, step), step)
        at = (part, slice(None)) if by_rows else (slice(None), part)
        total = sources[0][at].astype(F32)
        for source in sources[1:]:
            total = total + source[at].astype(F32)
        dst[at] = total.astype(dst.dtype)
        return carry

    lax.fori_loop(0, (rows if by_rows else columns) // step, body, 0)


def line_gather(m, tag, own, out, pause=1):
    p = m.place
    u = p.uly
    copy = m.local(tag + "=", own, out.at[p.dp * 4 + u])
    if u < 3:
        m.send((tag, "r", u), own, out.at[p.dp * 4 + u], p.at(uly=u + 1))
    if u > 0:
        m.send((tag, "l", u), own, out.at[p.dp * 4 + u], p.at(uly=u - 1))
    m.send((tag, "c", u), own, out.at[p.dp * 4 + u], p.at(dp=p.other))
    for _ in range(pause):
        yield
    for d in range(1, 4):
        for way, b, onward in (("r", u - d, u + 1), ("l", u + d, u - 1)):
            if 0 <= b <= 3:
                block = out.at[p.dp * 4 + b]
                m.arrive((tag, way, b), block)
                if 0 <= onward <= 3:
                    m.send((tag, way, b), block, block, p.at(uly=onward))
                m.send((tag, "c", b), block, block, p.at(dp=p.other))
        yield
    for b in range(4):
        m.arrive((tag, "c", b), out.at[p.other * 4 + b])
    copy.wait()


def plane_gather(m, tag, own, out, slot, halves, pair=True):
    p = m.place

    def half(c, i):
        return slot(out, p.dp, c, halves[i])

    mine = slot(out, p.dp, p.ctx, None)
    copy = m.local(tag + "=", own, mine)
    m.send((tag, "x"), own, mine, p.at(ctx=p.xn))
    m.send((tag, "y"), own, mine, p.at(ctx=p.yn))
    if pair:
        m.send((tag, "c", 0), own, mine, p.at(dp=p.other))
    yield
    block = slot(out, p.dp, p.xn, None)
    m.arrive((tag, "x"), block)
    m.send((tag, "z", 0), half(p.xn, 0), half(p.xn, 0), p.at(ctx=p.yn))
    if pair:
        m.send((tag, "c", 1), block, block, p.at(dp=p.other))
    block = slot(out, p.dp, p.yn, None)
    m.arrive((tag, "y"), block)
    m.send((tag, "z", 1), half(p.yn, 1), half(p.yn, 1), p.at(ctx=p.xn))
    if pair:
        m.send((tag, "c", 2), block, block, p.at(dp=p.other))
    yield
    for i in range(2):
        block = half(p.dg, i)
        m.arrive((tag, "z", i), block)
        if pair:
            m.send((tag, "c", 3 + i), block, block, p.at(dp=p.other))
    yield
    if pair:
        for i, c in enumerate((p.ctx, p.xn, p.yn)):
            m.arrive((tag, "c", i), slot(out, p.other, c, None))
        for i in range(2):
            m.arrive((tag, "c", 3 + i), slot(out, p.other, p.dg, halves[i]))
    copy.wait()


def line_reduce(m, tag, part, out, sib, right, left, sums):
    p = m.place
    u = p.uly
    order = (3, 0, 2, 1) if u < 2 else (0, 3, 1, 2)
    for b in order if sib is not None else ():
        m.send((tag, "c", b), part.at[p.other * 4 + b], sib.at[b], p.at(dp=p.other))
    met = set()

    def meet(b):
        if sib is None:
            return [part.at[b]]
        if b not in met:
            met.add(b)
            m.arrive((tag, "c", b), sib.at[b])
        return [part.at[p.dp * 4 + b], sib.at[b]]

    for slot in range(3):
        for b in range(1, 4):
            if u < b and u + 3 - b == slot:
                terms = meet(b)
                if u > 0:
                    m.arrive((tag, "r", b), right.at[b])
                    terms.append(right.at[b])
                add_up(sums.at[b], terms)
                m.send((tag, "r", b), sums.at[b], right.at[b], p.at(uly=u + 1))
        for b in range(3):
            if u > b and 3 - u + b == slot:
                terms = meet(b)
                if u < 3:
                    m.arrive((tag, "l", b), left.at[b])
                    terms.append(left.at[b])
                add_up(sums.at[b], terms)
                m.send((tag, "l", b), sums.at[b], left.at[b], p.at(uly=u - 1))
        yield
    terms = meet(u)
    if u > 0:
        m.arrive((tag, "r", u), right.at[u])
        terms.append(right.at[u])
    if u < 3:
        m.arrive((tag, "l", u), left.at[u])
        terms.append(left.at[u])
    add_up(out, terms)


def plane_reduce(m, tag, part, out, sib, sums, got, got2):
    p = m.place
    rows = out.shape[0]
    halves = (pl.ds(0, rows // 2), pl.ds(rows // 2, rows // 2))
    order = (p.dg, p.xn, p.yn, p.ctx)
    for i, c in enumerate(order):
        m.send((tag, "c", i), part.at[p.other * 4 + c], sib.at[c], p.at(dp=p.other))
    yield
    for i, c in enumerate(order):
        m.arrive((tag, "c", i), sib.at[c])
        add_up(sums.at[c], [part.at[p.dp * 4 + c], sib.at[c]])
        if i == 0:
            m.send((tag, "x", 1), sums.at[c, halves[0]], got.at[1, halves[0]], p.at(ctx=p.xn))
            m.send((tag, "y", 1), sums.at[c, halves[1]], got.at[1, halves[1]], p.at(ctx=p.yn))
        if i == 1:
            m.send((tag, "x", 0), sums.at[c, halves[0]], got.at[0, halves[0]], p.at(ctx=p.xn))
        if i == 2:
            m.send((tag, "y", 0), sums.at[c, halves[1]], got.at[0, halves[1]], p.at(ctx=p.yn))
    yield
    m.arrive((tag, "x", 1), got.at[1, halves[0]])
    add_up(got.at[1, halves[0]], [sums.at[p.yn, halves[0]], got.at[1, halves[0]]])
    m.send((tag, "y2"), got.at[1, halves[0]], got2.at[halves[0]], p.at(ctx=p.yn))
    m.arrive((tag, "y", 1), got.at[1, halves[1]])
    add_up(got.at[1, halves[1]], [sums.at[p.xn, halves[1]], got.at[1, halves[1]]])
    m.send((tag, "x2"), got.at[1, halves[1]], got2.at[halves[1]], p.at(ctx=p.xn))
    yield
    m.arrive((tag, "x", 0), got.at[0, halves[0]])
    m.arrive((tag, "y", 0), got.at[0, halves[1]])
    yield
    m.arrive((tag, "y2"), got2.at[halves[0]])
    m.arrive((tag, "x2"), got2.at[halves[1]])
    add_up(out, [sums.at[p.ctx], got.at[0], got2])


def run_kernel(name, number, branches, partners, streams, outs, ins, scratch=(), vmem=48, time=40):
    def kernel(*refs):
        send, recv = refs[-2:]
        refs = refs[:-2]
        uly = lax.axis_index(ULY)
        names = {}
        greet(partners(Place(uly)) if partners else [])

        def body(u):
            m = Mover(Place(u), names, send, recv)
            together(streams(m, *refs))
            m.finish()

        if branches == 1:
            body(uly)
        else:
            for u in range(4):
                pl.when(uly == u)(functools.partial(body, u))
        assert len(names) <= N_SEMS

    return pl.pallas_call(
        kernel,
        out_shape=[jax.ShapeDtypeStruct(*o[:2]) for o in outs],
        in_specs=[pl.BlockSpec(memory_space=s) for _, s in ins],
        out_specs=[pl.BlockSpec(memory_space=o[2]) for o in outs],
        scratch_shapes=[
            *[pltpu.VMEM(shape, dtype) for shape, dtype in scratch],
            pltpu.SemaphoreType.DMA((N_SEMS,)),
            pltpu.SemaphoreType.DMA((N_SEMS,)),
        ],
        name=name,
        cost_estimate=pl.CostEstimate(
            flops=0, bytes_accessed=time * 3_700_000, transcendentals=0
        ),
        compiler_params=pltpu.CompilerParams(
            collective_id=number, has_side_effects=True, vmem_limit_bytes=vmem << 20
        ),
    )(*[a for a, _ in ins])


def everyone(p):
    me = p.dp * 16 + p.ctx * 4 + p.uly
    found = []
    for k in range(1, 32):
        there = lax.rem(me + k, 32)
        found.append((lax.div(there, 16), lax.rem(lax.div(there, 4), 4), lax.rem(there, 4)))
    return found


def line_partners(p):
    found = [p.at(dp=p.other)]
    for d in range(1, 4):
        there = lax.rem(p.uly + d, 4)
        found += [p.at(uly=there), p.at(dp=p.other, uly=there)]
    return found


def plane_partners(p):
    return [p.at(dp=p.other), p.at(ctx=p.xn), p.at(ctx=p.yn)]


def token_slot(out, dp, c, part):
    view = out.at[dp * 4 + c]
    return view if part is None else view.at[part]


def state_slot(out, dp, c, part):
    view = out.at[c]
    return view if part is None else view.at[part]


def pack(w_query, w_key, w_value, w_swish, w_output, w_gate, w_up, gains):
    rows, (out_rows, width) = w_query.shape[0], w_output.shape
    key, val, ff, quarter = KEY_DIM, VALUE_DIM, w_gate.shape[1] // 8, width // 4
    cols = 2 * key + 2 * val + 32

    def kernel(q, k, v, s, o, g, u, n, packed, outw, gu):
        for d in range(2):
            for z in range(4):
                h, i = 2 * z + d, 4 * d + z
                at = 0
                for ref, w in ((q, key), (k, key), (v, val), (s, val)):
                    packed[i, :, at : at + w] = ref[:, h * w : (h + 1) * w]
                    at += w
                packed[i, :, at : at + 32] = n[...]
        for i in range(8):
            gu[i, :, :ff] = g[:, i * ff : (i + 1) * ff]
            gu[i, :, ff:] = u[:, i * ff : (i + 1) * ff]
        for j in range(4):
            outw[j] = o[:, j * quarter : (j + 1) * quarter]

    return pl.pallas_call(
        kernel,
        out_shape=[
            jax.ShapeDtypeStruct((8, rows, cols), BF16),
            jax.ShapeDtypeStruct((4, out_rows, quarter), BF16),
            jax.ShapeDtypeStruct((8, rows, 2 * ff), BF16),
        ],
        name="pack",
        compiler_params=pltpu.CompilerParams(vmem_limit_bytes=32 << 20),
    )(w_query, w_key, w_value, w_swish, w_output, w_gate, w_up, gains)


def unpack(heads, outg, slices):
    rows, (_, out_rows, quarter) = heads.shape[1], outg.shape
    key, val, ff = KEY_DIM, VALUE_DIM, slices.shape[2] // 2

    def kernel(hs, og, sl, q, k, v, s, o, g, u):
        for d in range(2):
            for z in range(4):
                h, i = 2 * z + d, 4 * d + z
                at = 0
                for ref, w in ((q, key), (k, key), (v, val), (s, val)):
                    ref[:, h * w : (h + 1) * w] = hs[i, :, at : at + w].astype(F32)
                    at += w
        for i in range(8):
            g[:, i * ff : (i + 1) * ff] = sl[i, :, :ff].astype(F32)
            u[:, i * ff : (i + 1) * ff] = sl[i, :, ff:].astype(F32)
        for j in range(4):
            o[:, j * quarter : (j + 1) * quarter] = og[j].astype(F32)

    wide = jax.ShapeDtypeStruct((rows, 8 * key), F32)
    wider = jax.ShapeDtypeStruct((rows, 8 * val), F32)
    ffs = jax.ShapeDtypeStruct((rows, 8 * ff), F32)
    return pl.pallas_call(
        kernel,
        out_shape=[
            wide, wide, wider, wider,
            jax.ShapeDtypeStruct((out_rows, 4 * quarter), F32),
            ffs, ffs,
        ],
        name="unpack",
        compiler_params=pltpu.CompilerParams(vmem_limit_bytes=32 << 20),
    )(heads, outg, slices)


def start_exchange(hidden, decay, packed, outw, gu):
    tokens, width = hidden.shape
    rows, cols = packed.shape[1:]
    out_rows, quarter = outw.shape[1:]
    ff2 = gu.shape[2]

    def streams(m, hid_ref, dec_ref, pk_ref, ow_ref, gu_ref, hall, dall, wall, oall, gall):
        p = m.place
        u = p.uly

        def row(q, c, us):
            dp = p.dp if q == 0 else p.other
            return wall.at[dp * 16 + c * 4 + us]

        def attn():
            sources = sorted(
                ((q, us) for q in range(2) for us in range(4)), key=lambda s: (abs(s[1] - u), s[0])
            )
            copy = None
            for q, to in sources:
                dp = p.dp if q == 0 else p.other
                mine = row(0, p.ctx, u)
                src = pk_ref.at[dp * 4 + to]
                if (q, to) == (0, u):
                    copy = m.local("T", src, mine)
                else:
                    m.send(("t", q, u), src, mine, p.at(dp=dp, uly=to))
            yield
            relays = []
            for n, (q, us) in enumerate(sources):
                tile = row(q, p.ctx, us)
                if (q, us) == (0, u):
                    copy.wait()
                else:
                    m.arrive(("t", q, us), tile)
                m.send(("X", q, us), tile, tile, p.at(ctx=p.xn))
                m.send(("Y", q, us), tile, tile, p.at(ctx=p.yn))
                relays.append((q, us))
                if n >= 2:
                    yield
                    relay(*relays.pop(0))
            while relays:
                yield
                relay(*relays.pop(0))
            yield
            for q, us in sources:
                even = (q + us) % 2 == 0
                m.arrive(("Y" if even else "X", q, us), row(q, p.yn if even else p.xn, us))
                m.arrive(("Z", q, us), row(q, p.dg, us))

        def relay(q, us):
            if (q + us) % 2 == 0:
                tile = row(q, p.xn, us)
                m.arrive(("X", q, us), tile)
                m.send(("Z", q, us), tile, tile, p.at(ctx=p.yn))
            else:
                tile = row(q, p.yn, us)
                m.arrive(("Y", q, us), tile)
                m.send(("Z", q, us), tile, tile, p.at(ctx=p.xn))

        def out_proj():
            head_dp, head_u = lax.rem(p.ctx, 2), p.dp * 2 + lax.div(p.ctx, 2)
            source_dp, source_ctx = u // 2, 2 * (u % 2) + p.dp

            def column(part, c):
                return oall.at[part, :, pl.ds(pl.multiple_of(c * quarter, quarter), quarter)]

            own = [
                (head_dp == p.dp) & (p.ctx == j) & (head_u == u) for j in range(4)
            ]
            for j in range(4):
                there = oall.at[u, :, pl.ds(j * quarter, quarter)]
                here = pltpu.make_async_copy(
                    ow_ref.at[j], there, m.send_sems.at[m.number("O")]
                )

                @pl.when(own[j])
                def _(here=here):
                    here.start()
                    here.wait()

                other = pltpu.make_async_remote_copy(
                    src_ref=ow_ref.at[j],
                    dst_ref=there,
                    send_sem=m.send_sems.at[m.number(("S", j))],
                    recv_sem=m.recv_sems.at[m.number(("o", u))],
                    device_id=(head_dp, j, head_u),
                    device_id_type=MESH,
                )
                pl.when(jnp.logical_not(own[j]))(other.start)
            for _ in range(7):
                yield
            for us in range(4):
                mine = (source_dp == p.dp) & (source_ctx == p.ctx) & (us == u)

                @pl.when(jnp.logical_not(mine))
                def _(us=us):
                    m.arrive(("o", us), column(us, p.ctx))

            yield
            mine = column(pl.ds(0, 4), p.ctx)
            m.send("ox", mine, mine, p.at(ctx=p.xn))
            m.send("oy", mine, mine, p.at(ctx=p.yn))
            yield
            low, high = pl.ds(0, 2), pl.ds(2, 2)
            m.arrive("ox", column(pl.ds(0, 4), p.xn))
            m.send("o0", column(low, p.xn), column(low, p.xn), p.at(ctx=p.yn))
            m.arrive("oy", column(pl.ds(0, 4), p.yn))
            m.send("o1", column(high, p.yn), column(high, p.yn), p.at(ctx=p.xn))
            yield
            for j in range(4):
                other = pltpu.make_async_remote_copy(
                    src_ref=ow_ref.at[j],
                    dst_ref=ow_ref.at[j],
                    send_sem=m.send_sems.at[m.number(("S", j))],
                    recv_sem=m.recv_sems.at[m.number(("o", u))],
                    device_id=p.at(dp=p.other),
                    device_id_type=MESH,
                )
                pl.when(jnp.logical_not(own[j]))(other.wait_send)
            m.arrive("o0", column(low, p.dg))
            m.arrive("o1", column(high, p.dg))

        def feed():
            mine = gall.at[p.dp * 4 + p.ctx]
            copy = m.local("F", gu_ref.at[p.dp * 4 + p.ctx], mine)
            decays = m.local("D", dec_ref, dall.at[p.dp * 4 + p.ctx])
            spots = [(q, c, i) for i, c in enumerate((p.ctx, p.xn, p.yn, p.dg)) for q in range(2)][1:]
            for q, c, i in spots:
                dp = p.dp if q == 0 else p.other
                m.send(("d", q, i), dec_ref, dall.at[p.dp * 4 + p.ctx], p.at(dp=dp, ctx=c))
                m.send(("f", q, i), gu_ref.at[dp * 4 + c], mine, p.at(dp=dp, ctx=c))
            for _ in range(5):
                yield
            for q, c, i in spots:
                dp = p.dp if q == 0 else p.other
                m.arrive(("d", q, i), dall.at[dp * 4 + c])
                m.arrive(("f", q, i), gall.at[dp * 4 + c])
            copy.wait()
            decays.wait()

        return [
            attn(),
            later(line_gather(m, "h", hid_ref, hall, 6), 1),
            later(out_proj(), 1),
            later(feed(), 6),
        ]

    return run_kernel(
        "start",
        1,
        4,
        everyone,
        streams,
        [
            ((8, tokens, width), BF16, HBM),
            ((8, *decay.shape), F32, HBM),
            ((32, rows, cols), BF16, HBM),
            ((4, out_rows, 4 * quarter), BF16, HBM),
            ((8, rows, ff2), BF16, HBM),
        ],
        [(hidden, HBM), (decay, HBM), (packed, HBM), (outw, HBM), (gu, HBM)],
    )


def state_exchange(state, number):
    def streams(m, own, out):
        return [
            plane_gather(m, "s", own, out, state_slot, (pl.ds(0, 1), pl.ds(1, 1)), pair=False)
        ]

    [out] = run_kernel(
        "state",
        number,
        1,
        lambda p: [p.at(ctx=p.xn), p.at(ctx=p.yn)],
        streams,
        [((4, *state.shape), state.dtype, HBM)],
        [(state, HBM)],
    )
    return out


def reduce_line(part, cot, number):
    _, tokens, width = part.shape
    half = tokens // 2

    def streams(m, part_ref, cot_ref, out, cots, sib, right, left, sums):
        return [
            line_reduce(m, "s", part_ref, out, sib, right, left, sums),
            plane_gather(m, "C", cot_ref, cots, token_slot, (pl.ds(0, half), pl.ds(half, half))),
        ]

    return run_kernel(
        "reduce_line",
        number,
        4,
        lambda p: line_partners(p) + plane_partners(p)[1:],
        streams,
        [((tokens, width), F32, VMEM), ((8, tokens, width), BF16, HBM)],
        [(part, VMEM), (cot, HBM)],
        [((4, tokens, width), BF16)] * 4,
    )


def gather_plane(own, number):
    tokens, width = own.shape
    half = tokens // 2

    def streams(m, own_ref, out):
        return [
            plane_gather(
                m, "k", own_ref, out, token_slot, (pl.ds(0, half), pl.ds(half, half))
            )
        ]

    [out] = run_kernel(
        "gather_plane",
        number,
        1,
        plane_partners,
        streams,
        [((8, tokens, width), BF16, HBM)],
        [(own, VMEM)],
    )
    return out


def reduce_plane(part, number):
    _, tokens, width = part.shape

    def streams(m, part_ref, out, sib, sums, got, got2):
        return [plane_reduce(m, "s", part_ref, out, sib, sums, got, got2)]

    [out] = run_kernel(
        "reduce_plane",
        number,
        1,
        plane_partners,
        streams,
        [((tokens, width), F32, VMEM)],
        [(part, VMEM)],
        [
            ((4, tokens, width), BF16),
            ((4, tokens, width), BF16),
            ((2, tokens, width), BF16),
            ((tokens, width), BF16),
        ],
    )
    return out


def gather_line_reduce_plane(own, part, down, gates, number):
    _, tokens, width = part.shape
    shapes = [g.shape for g in (down, *gates)]

    def streams(m, own_ref, part_ref, d_ref, g_ref, h_ref, out, total, dout, gout, hout, *scratch):
        sib, sums, got, got2 = scratch[:4]
        more = scratch[4:]
        return [
            line_gather(m, "k", own_ref, out),
            plane_reduce(m, "s", part_ref, total, sib, sums, got, got2),
            *[
                line_reduce(m, i, ref, o, None, *more[3 * i : 3 * i + 3])
                for i, (ref, o) in enumerate(((d_ref, dout), (g_ref, gout), (h_ref, hout)))
            ],
        ]

    return run_kernel(
        "gather_line",
        number,
        4,
        lambda p: line_partners(p) + plane_partners(p)[1:],
        streams,
        [
            ((8, tokens, width), BF16, HBM),
            ((tokens, width), F32, VMEM),
            (shapes[0][1:], F32, VMEM),
            (shapes[1][1:], BF16, VMEM),
            (shapes[2][1:], BF16, VMEM),
        ],
        [(own, VMEM), (part, VMEM), (down, VMEM), (gates[0], VMEM), (gates[1], VMEM)],
        [
            ((4, tokens, width), BF16),
            ((4, tokens, width), BF16),
            ((2, tokens, width), BF16),
            ((tokens, width), BF16),
            *[(shape, BF16) for shape in shapes for _ in range(3)],
        ],
        vmem=56,
    )


def last_exchange(part, grads, gout, gffn, inputs, term):
    _, tokens, width = part.shape
    rows, cols = grads.shape[3:]
    out_rows = gout.shape[1]
    quarter = width // 4
    ff2 = gffn.shape[2]

    def streams(
        m, part_ref, g_ref, o_ref, f_ref, in_ref, t_ref, out, gall, oall, fall, gains,
        sib, right, left, sums, gotx, goty, gotx2, goty2, oxs, oys, ox2, oy2, away,
    ):
        p = m.place
        u = p.uly

        def attn():
            for i, (cx, cy) in ((1, (p.dg, p.dg)), (0, (p.xn, p.yn))):
                for t in range(4):
                    m.send(("gx", i, t), g_ref.at[0, cx, t], gotx.at[i, t], p.at(ctx=p.xn))
                    m.send(("gy", i, t), g_ref.at[1, cy, t], goty.at[i, t], p.at(ctx=p.yn))
            yield
            for t in range(4):
                m.arrive(("gx", 1, t), gotx.at[1, t])
                add_up(gotx.at[1, t], [g_ref.at[0, p.yn, t], gotx.at[1, t]])
                m.send(("gy2", t), gotx.at[1, t], goty2.at[t], p.at(ctx=p.yn))
                m.arrive(("gy", 1, t), goty.at[1, t])
                add_up(goty.at[1, t], [g_ref.at[1, p.xn, t], goty.at[1, t]])
                m.send(("gx2", t), goty.at[1, t], gotx2.at[t], p.at(ctx=p.xn))
            yield
            yield
            for t in range(4):
                for dp, got, got2, tags in (
                    (0, gotx, goty2, ("gx", "gy2")),
                    (1, goty, gotx2, ("gy", "gx2")),
                ):
                    m.arrive((tags[0], 0, t), got.at[0, t])
                    m.arrive((tags[1], t), got2.at[t])
                    add_up(got.at[0, t], [g_ref.at[dp, p.ctx, t], got.at[0, t], got2.at[t]])
                    there = gall.at[p.dp * 4 + u]
                    if t == u:

                        @pl.when(p.dp == dp)
                        def _(got=got, there=there):
                            here = pltpu.make_async_copy(
                                got.at[0, u], there, m.send_sems.at[m.number("G")]
                            )
                            here.start()
                            here.wait()

                        @pl.when(p.dp != dp)
                        def _(got=got, there=there, dp=dp):
                            m.remote(
                                ("gc", u), got.at[0, u], there, (dp, p.ctx, u)
                            ).start()
                    else:
                        k = m.number(("gs", dp, t))
                        copies = []
                        for q in range(2):
                            copies.append(
                                pltpu.make_async_remote_copy(
                                    src_ref=got.at[0, t],
                                    dst_ref=there,
                                    send_sem=m.send_sems.at[k],
                                    recv_sem=m.recv_sems.at[m.number(("g", q, u))],
                                    device_id=(dp, p.ctx, t),
                                    device_id_type=MESH,
                                )
                            )
                        pl.when(p.dp == dp)(copies[0].start)
                        pl.when(p.dp != dp)(copies[1].start)
                        m.sent.append(copies[0])
            for _ in range(6):
                yield
            m.remote(("gc", u), gotx.at[0, u], gotx.at[0, u], p.at(dp=p.other)).wait_send()
            m.arrive(("gc", u), gall.at[p.other * 4 + u])
            for us in range(4):
                if us != u:
                    m.arrive(("g", 0, us), gall.at[p.dp * 4 + us])
                    m.arrive(("g", 1, us), gall.at[p.other * 4 + us])

        def out_proj():
            def column(ref, part, c):
                return ref.at[part, :, pl.ds(pl.multiple_of(c * quarter, quarter), quarter)]

            low, high = pl.ds(0, 2), pl.ds(2, 2)
            for i, (cx, cy) in ((1, (p.dg, p.dg)), (0, (p.xn, p.yn))):
                m.send(("ox", i), column(o_ref, low, cx), oxs.at[i], p.at(ctx=p.xn))
                m.send(("oy", i), column(o_ref, high, cy), oys.at[i], p.at(ctx=p.yn))
            yield
            m.arrive(("ox", 1), oxs.at[1])
            for t in range(2):
                add_up(oxs.at[1, t], [column(o_ref, t, p.yn), oxs.at[1, t]])
            m.send("oy2", oxs.at[1], oy2, p.at(ctx=p.yn))
            m.arrive(("oy", 1), oys.at[1])
            for t in range(2):
                add_up(oys.at[1, t], [column(o_ref, 2 + t, p.xn), oys.at[1, t]])
            m.send("ox2", oys.at[1], ox2, p.at(ctx=p.xn))
            yield
            m.arrive(("ox", 0), oxs.at[0])
            m.arrive(("oy", 0), oys.at[0])
            m.arrive("oy2", oy2)
            m.arrive("ox2", ox2)
            home_dp, home_ctx = u // 2, 2 * (u % 2) + p.dp
            here_all = []
            for us in range(4):
                got, got2 = (oxs, oy2) if us < 2 else (oys, ox2)
                t = us % 2
                add_up(got.at[0, t], [column(o_ref, us, p.ctx), got.at[0, t], got2.at[t]])
                own = (home_dp == p.dp) & (home_ctx == p.ctx) & (us == u)
                there = oall.at[p.ctx]
                here = pltpu.make_async_copy(
                    got.at[0, t], there, m.send_sems.at[m.number("O")]
                )

                @pl.when(own)
                def _(here=here):
                    here.start()
                    here.wait()

                for j in range(4):
                    copy = pltpu.make_async_remote_copy(
                        src_ref=got.at[0, t],
                        dst_ref=there,
                        send_sem=m.send_sems.at[m.number(("os", us))],
                        recv_sem=m.recv_sems.at[m.number(("o", j))],
                        device_id=(home_dp, home_ctx, us),
                        device_id_type=MESH,
                    )
                    pl.when(jnp.logical_not(own) & (p.ctx == j))(copy.start)
                here_all.append((own, copy))
            yield
            head_dp, head_u = lax.rem(p.ctx, 2), p.dp * 2 + lax.div(p.ctx, 2)
            for j in range(4):
                mine = (head_dp == p.dp) & (p.ctx == j) & (head_u == u)

                @pl.when(jnp.logical_not(mine))
                def _(j=j):
                    m.arrive(("o", j), oall.at[j])

            for own, copy in here_all:
                pl.when(jnp.logical_not(own))(copy.wait_send)

        def feed():
            mine = fall.at[p.dp * 4 + p.ctx]
            copy = m.local("F", f_ref.at[p.dp * 4 + p.ctx], mine)
            spots = [(q, c, i) for i, c in enumerate((p.ctx, p.xn, p.yn, p.dg)) for q in range(2)][1:]
            for q, c, i in spots:
                dp = p.dp if q == 0 else p.other
                m.send(("f", q, i), f_ref.at[dp * 4 + c], mine, p.at(dp=dp, ctx=c))
            for _ in range(4):
                yield
            for q, c, i in spots:
                dp = p.dp if q == 0 else p.other
                m.arrive(("f", q, i), fall.at[dp * 4 + c])
            copy.wait()

        def tokens_stream():
            yield from line_reduce(m, "s", part_ref, out, sib, right, left, sums)

            def body(i, total):
                at = pl.ds(pl.multiple_of(i * 16, 16), 16)
                values = in_ref[at, :].astype(F32)
                normed, _ = normalize(values)
                return total + jnp.sum(out[at, :] * normed, axis=0, keepdims=True)

            total = lax.fori_loop(0, tokens // 16, body, jnp.zeros((1, width), F32))
            row = lax.broadcasted_iota(jnp.int32, (8, width), 0)
            gains[...] = jnp.where(
                row == 0,
                jnp.broadcast_to(total, (8, width)),
                jnp.where(row == 1, jnp.broadcast_to(t_ref[...], (8, width)), 0.0),
            )
            for i, device in enumerate((p.at(dp=p.other), p.at(ctx=p.xn), p.at(ctx=p.yn))):
                m.remote(("n", i), gains, away.at[i], device).start()
                yield
                m.remote(("n", i), gains, away.at[i], device).wait()
                gains[...] = gains[...] + away[i]
            copies = [
                m.remote(("N", u, other), gains, away.at[3 + u], p.at(uly=other))
                for other in range(4)
                if other != u
            ]
            for copy in copies:
                copy.start()
            yield
            mine = gains[...]
            for other in range(4):
                if other != u:
                    m.arrive(("N", other, u), away.at[3 + other])
                    mine = mine + away[3 + other]
            for copy in copies:
                copy.wait_send()
            gains[...] = mine

        return [
            tokens_stream(),
            attn(),
            later(out_proj(), 1),
            later(feed(), 5),
        ]

    return run_kernel(
        "last",
        2,
        4,
        everyone,
        streams,
        [
            ((tokens, width), F32, VMEM),
            ((8, rows, cols), BF16, HBM),
            ((4, out_rows, quarter), BF16, HBM),
            ((8, rows, ff2), BF16, HBM),
            ((8, width), F32, VMEM),
        ],
        [(part, VMEM), (grads, VMEM), (gout, VMEM), (gffn, HBM), (inputs, VMEM), (term, VMEM)],
        [
            *[((4, tokens, width), BF16)] * 4,
            *[((2, 4, rows, cols), BF16)] * 2,
            *[((4, rows, cols), BF16)] * 2,
            *[((2, 2, out_rows, quarter), BF16)] * 2,
            *[((2, out_rows, quarter), BF16)] * 2,
            ((7, 8, width), F32),
        ],
        vmem=56,
    )


def local(
    hidden_in,
    cotangent,
    log_decay,
    w_query,
    w_key,
    w_value,
    w_swish,
    w_output,
    w_gate,
    w_up,
    w_down,
    gain_attn,
    gain_ffn,
):
    bf16, f32 = BF16, F32
    dp, ctx = lax.axis_index(DP), lax.axis_index(CTX)
    tokens = hidden_in.shape[1]
    width = hidden_in.shape[2]
    rows = w_query.shape[0]
    out_rows = w_output.shape[0]
    key, val, ff = KEY_DIM, VALUE_DIM, w_gate.shape[1] // 8

    gains = jnp.pad(jnp.stack([gain_attn, gain_ffn], axis=1), ((0, 0), (0, 30)))
    packed, outw, gate_up = pack(w_query, w_key, w_value, w_swish, w_output, w_gate, w_up, gains)
    attn_cols = 2 * key + 2 * val
    hidden_all, decays, w_all, w_out, gate_up = start_exchange(
        hidden_in[0],
        log_decay[0],
        packed,
        outw,
        gate_up,
    )
    w_gu = lax.all_gather(gate_up, ULY, axis=0)
    w_gu = w_gu.transpose(1, 0, 2, 3).reshape(32 * rows, 2 * ff)
    w_down, gate_up = lax.optimization_barrier((w_down, gate_up))
    w_dn = lax.all_gather(w_down, ULY, axis=0, tiled=True)
    w_all = w_all.reshape(32 * rows, packed.shape[2])
    w_attn = w_all[:, :attn_cols]
    gain_one = w_all[:, attn_cols].astype(f32)
    gain_two = w_all[:, attn_cols + 1].astype(f32)
    w_out = w_out.reshape(4 * out_rows, width)

    normed_all, _ = normalize(hidden_all.reshape(8 * tokens, width).astype(f32))
    scaled_one = (normed_all * gain_one).astype(bf16)
    qkvs = matmul(scaled_one, w_attn)
    block = 4 * tokens
    q = qkvs[:, :key].astype(bf16).reshape(2, block, key)
    k = qkvs[:, key : 2 * key].astype(bf16).reshape(2, block, key)
    v = qkvs[:, 2 * key : 2 * key + val].astype(bf16).reshape(2, block, val)
    swish_pre = qkvs[:, 2 * key + val :]

    decays = lax.dynamic_index_in_dim(decays, dp, 1, keepdims=False).reshape(2, 4, block)
    decay = lax.dynamic_index_in_dim(decays, ctx, 1, keepdims=False)
    lasts = jnp.sum(decays, axis=2).T
    scale = 1.0 / math.sqrt(KEY_DIM)
    cumulative = running_sum(decay)
    later = lax.broadcasted_iota(jnp.int32, (block, block), 0) >= lax.broadcasted_iota(
        jnp.int32, (block, block), 1
    )
    gap = cumulative[:, :, None] - cumulative[:, None, :]
    mask = jnp.where(later[None], jnp.exp(jnp.minimum(gap, 0.0)), 0.0) * scale
    last = cumulative[:, -1:]
    tail = jnp.exp(last - cumulative)[:, :, None]
    reach = jnp.exp(cumulative)[:, :, None]

    weights = (pair_dot(2, 2, q, k) * mask).astype(bf16)
    k_tail = (k.astype(f32) * tail).astype(bf16)
    update = pair_dot(1, 1, k_tail, v)
    spots = jnp.arange(4)

    def between(j, near):
        inside = (spots > jnp.minimum(j, near)) & (spots < jnp.maximum(j, near))
        return jnp.exp(jnp.sum(jnp.where(inside[:, None], lasts, 0.0), 0))

    before = jnp.stack([jnp.where(j < ctx, between(j, ctx), 0.0) for j in range(4)])
    after = jnp.stack([jnp.where(j > ctx, between(j, ctx), 0.0) for j in range(4)])
    updates = state_exchange(update.astype(bf16), 3).astype(f32)
    state_in = jnp.sum(before[:, :, None, None] * updates, axis=0).astype(bf16)
    retained = pair_dot(2, 1, weights, v) + scale * reach * pair_dot(2, 1, q, state_in)
    head_normed, head_inverse = normalize(retained)
    head_out = head_normed.astype(bf16).reshape(2 * block, val).astype(f32)
    swish_act = jax.nn.silu(swish_pre)
    gated = (swish_act * head_out).astype(bf16)
    attn, top_all = reduce_line(
        matmul(gated, w_out).astype(bf16).reshape(8, tokens, width), cotangent[0], 4
    )
    top_all = top_all.reshape(8 * tokens, width)
    inputs = hidden_in[0].astype(f32)
    residual = inputs + attn

    normed_two, inverse_two = normalize(residual)
    scaled_two = gather_plane((normed_two * gain_two).astype(bf16), 5).reshape(8 * tokens, width)
    gu = matmul(scaled_two, w_gu)
    gate_pre, up_pre = gu[:, :ff], gu[:, ff:]
    gate_act = jax.nn.silu(gate_pre)
    product = (gate_act * up_pre).astype(bf16)
    grad_product = dot_nt(top_all, w_dn)
    grad_gu = jnp.concatenate(
        [
            (grad_product * up_pre * swish_slope(gate_pre)).astype(bf16),
            (grad_product * gate_act).astype(bf16),
        ],
        axis=1,
    )
    gs2 = reduce_plane(dot_nt(grad_gu, w_gu).astype(bf16).reshape(8, tokens, width), 6)
    grad_top = cotangent[0].astype(f32)
    gain_two_term = jnp.sum(gs2 * normed_two, axis=0, keepdims=True)
    grad_residual = grad_top + norm_back(gs2 * gain_two, normed_two, inverse_two)
    ggu = dot_t(scaled_two, grad_gu).astype(bf16).reshape(2, 4, 4, rows, 2 * ff)
    ggu = ggu.transpose(0, 2, 1, 3, 4).reshape(2, 4, 4 * rows, 2 * ff)
    grad_y, out_part, grad_down, ggu_0, ggu_1 = gather_line_reduce_plane(
        grad_residual.astype(bf16),
        matmul(product, w_dn).astype(bf16).reshape(8, tokens, width),
        dot_t(product, top_all).astype(bf16).reshape(4, out_rows, width),
        (ggu[0], ggu[1]),
        7,
    )
    ggu = jnp.concatenate([ggu_0, ggu_1]).reshape(8, rows, 2 * ff)
    layer_out = residual + out_part
    grad_y = grad_y.reshape(8 * tokens, width)

    grad_gated = dot_nt(grad_y, w_out)
    g_out = dot_t(gated, grad_y).astype(bf16)
    grad_swish_pre = (grad_gated * head_out * swish_slope(swish_pre)).astype(bf16)
    grad_head = (grad_gated * swish_act).astype(bf16).astype(f32).reshape(2, block, val)
    grad_retained = norm_back(grad_head, head_normed, head_inverse).astype(bf16)
    grad_scores = (pair_dot(2, 2, grad_retained, v) * mask).astype(bf16)
    q_reach = (q.astype(f32) * (reach * scale)).astype(bf16)
    grad_state = pair_dot(1, 1, q_reach, grad_retained)
    grad_states = state_exchange(grad_state.astype(bf16), 8).astype(f32)
    grad_update = jnp.sum(after[:, :, None, None] * grad_states, axis=0).astype(bf16)
    grad_q = pair_dot(2, 1, grad_scores, k) + scale * reach * pair_dot(2, 2, grad_retained, state_in
    )
    grad_k = pair_dot(1, 1, grad_scores, q) + tail * pair_dot(2, 2, v, grad_update)
    grad_v = pair_dot(1, 1, weights, grad_retained) + tail * pair_dot(2, 1, k, grad_update
    )
    grad_cat = jnp.concatenate(
        [
            grad_q.astype(bf16).reshape(2 * block, key),
            grad_k.astype(bf16).reshape(2 * block, key),
            grad_v.astype(bf16).reshape(2 * block, val),
            grad_swish_pre,
        ],
        axis=1,
    )
    gs1, gcat, g_out, ggu, gain_terms = last_exchange(
        dot_nt(grad_cat, w_attn).astype(bf16).reshape(8, tokens, width),
        dot_t(scaled_one, grad_cat).astype(bf16).reshape(2, 4, 4, rows, attn_cols),
        g_out.reshape(4, out_rows, width),
        ggu,
        hidden_in[0],
        gain_two_term,
    )
    normed_one, inverse_one = normalize(inputs)
    grad_input = grad_residual + norm_back(gs1 * gain_one, normed_one, inverse_one)

    grad_query, grad_key, grad_value, grad_swish, grad_output, grad_gate, grad_up = unpack(
        gcat, g_out, ggu
    )
    me = dp * 16 + ctx * 4 + lax.axis_index(ULY)
    gain_terms = lax.dynamic_slice_in_dim(gain_terms, me * rows, rows, axis=1)
    return (
        layer_out[None],
        grad_input[None],
        grad_query,
        grad_key,
        grad_value,
        grad_swish,
        grad_output,
        grad_gate,
        grad_up,
        grad_down,
        gain_terms[0],
        gain_terms[1],
    )


def solution(mesh):
    shape = mesh.shape
    planned = (shape[DP], shape[CTX], shape[ULY]) == (2, 4, 4)
    tokens = P(DP, (CTX, ULY), None)
    weight = P(EVERYWHERE, None)
    gain = P(EVERYWHERE)
    return jax.shard_map(
        local if planned else local_any,
        mesh=mesh,
        in_specs=(tokens, tokens, P(DP, ULY, CTX), *[weight] * 8, gain, gain),
        out_specs=(tokens, tokens, *[weight] * 8, gain, gain),
        check_vma=False,
    )
```

```python
import functools
import math

import jax
import jax.numpy as jnp
from jax import lax
from jax.experimental import pallas as pl
from jax.experimental.pallas import tpu as pltpu
from jax.sharding import PartitionSpec as P

RETENTION_HEADS = 8
KEY_DIM = 256
VALUE_DIM = 432


EPSILON = 1e-06
DP, CTX, ULY = "dp", "ctx", "ulysses"
EVERYWHERE = (DP, CTX, ULY)


def entering(value, axis, join, neutral, backward):
    count, mine = (lax.axis_size(axis), lax.axis_index(axis))
    pieces = jax.tree.map(lambda part: lax.all_gather(part, axis), value)
    if backward:
        pieces = jax.tree.map(lambda part: part[::-1], pieces)
        mine = count - 1 - mine
    subtotal = jax.tree.map(
        lambda part, zero: jnp.full_like(part, 0) + jnp.asarray(zero, part.dtype), value, neutral
    )

    def step(position, subtotal):
        longer = join(subtotal, jax.tree.map(lambda part: part[position], pieces))
        return jax.tree.map(lambda new, old: jnp.where(position < mine, new, old), longer, subtotal)

    return lax.fori_loop(0, count - 1, step, subtotal)


def normalize(values):
    inverse = lax.rsqrt(jnp.mean(values * values, axis=-1, keepdims=True) + EPSILON)
    return (values * inverse, inverse)


def norm_back(grad_normed, normed, inverse):
    return inverse * (grad_normed - normed * jnp.mean(grad_normed * normed, axis=-1, keepdims=True))


def swish_slope(values):
    sigma = jax.nn.sigmoid(values)
    return sigma * (1.0 + values * (1.0 - sigma))


def carry_forward(earlier, later):
    return (earlier[0] * later[0], later[0][:, None, None] * earlier[1] + later[1])


def carry_backward(earlier, later):
    return (earlier[0] * later[0], later[1] + later[0][:, None, None] * earlier[1])


def running_sum(values):
    size = values.shape[-1]
    upper = lax.broadcasted_iota(jnp.int32, (size, size), 0) <= lax.broadcasted_iota(
        jnp.int32, (size, size), 1
    )
    return jnp.dot(values, upper.astype(jnp.float32), precision=lax.Precision.HIGHEST)


def matmul(left, right):
    return jnp.dot(left, right, preferred_element_type=jnp.float32)


def local_any(
    hidden_in,
    cotangent,
    log_decay,
    w_query,
    w_key,
    w_value,
    w_swish,
    w_output,
    w_gate,
    w_up,
    w_down,
    gain_attn,
    gain_ffn,
):
    highest = lax.Precision.HIGHEST
    query_full, key_full, value_full, swish_full, output_full, gain_one = (
        lax.all_gather(w_query, EVERYWHERE, axis=0, tiled=True),
        lax.all_gather(w_key, EVERYWHERE, axis=0, tiled=True),
        lax.all_gather(w_value, EVERYWHERE, axis=0, tiled=True),
        lax.all_gather(w_swish, EVERYWHERE, axis=0, tiled=True),
        lax.all_gather(w_output, EVERYWHERE, axis=0, tiled=True),
        lax.all_gather(gain_attn, EVERYWHERE, axis=0, tiled=True),
    )
    inputs = hidden_in[0].astype(jnp.float32)
    tokens = inputs.shape[0]
    normed_one, inverse_one = normalize(inputs)
    scaled_one = (normed_one * gain_one.astype(jnp.float32)).astype(jnp.bfloat16)
    queries = (
        matmul(scaled_one, query_full)
        .astype(jnp.bfloat16)
        .reshape(tokens, RETENTION_HEADS, KEY_DIM)
    )
    keys_tok = (
        matmul(scaled_one, key_full).astype(jnp.bfloat16).reshape(tokens, RETENTION_HEADS, KEY_DIM)
    )
    values_tok = (
        matmul(scaled_one, value_full)
        .astype(jnp.bfloat16)
        .reshape(tokens, RETENTION_HEADS, VALUE_DIM)
    )
    swish_pre = matmul(scaled_one, swish_full)
    head_q, head_k, head_v = (
        lax.all_to_all(queries, ULY, split_axis=1, concat_axis=0, tiled=True),
        lax.all_to_all(keys_tok, ULY, split_axis=1, concat_axis=0, tiled=True),
        lax.all_to_all(values_tok, ULY, split_axis=1, concat_axis=0, tiled=True),
    )
    block = head_q.shape[0]
    scale = 1.0 / math.sqrt(KEY_DIM)
    cumulative = running_sum(log_decay[0])
    later = lax.broadcasted_iota(jnp.int32, (block, block), 0) >= lax.broadcasted_iota(
        jnp.int32, (block, block), 1
    )
    gap = cumulative[:, :, None] - cumulative[:, None, :]
    mask = jnp.where(later[None], jnp.exp(jnp.minimum(gap, 0.0)), 0.0) * scale
    scores = jnp.einsum("thd,shd->hts", head_q, head_k, preferred_element_type=jnp.float32)
    weights = (scores * mask).astype(jnp.bfloat16)
    intra = jnp.einsum("hts,she->the", weights, head_v, preferred_element_type=jnp.float32)
    query_f = head_q.astype(jnp.float32)
    key_f = head_k.astype(jnp.float32)
    value_f = head_v.astype(jnp.float32)
    tail = jnp.exp(cumulative[:, -1:] - cumulative).T[:, :, None]
    reach = jnp.exp(cumulative).T[:, :, None]
    update = jnp.einsum("shd,she->hde", key_f * tail, value_f, precision=highest)
    block_decay = jnp.exp(cumulative[:, -1])
    identity = (jnp.ones_like(block_decay), jnp.zeros_like(update))
    _, state_in = entering((block_decay, update), CTX, carry_forward, identity, False)
    retained = intra + scale * reach * jnp.einsum(
        "thd,hde->the", query_f, state_in, precision=highest
    )
    head_normed, head_inverse = normalize(retained)
    head_out = head_normed.astype(jnp.bfloat16)
    token_out = lax.all_to_all(
        head_out, ULY, split_axis=0, concat_axis=1, tiled=True
    ).reshape(tokens, RETENTION_HEADS * VALUE_DIM)
    token_out_f = token_out.astype(jnp.float32)
    swish_act = jax.nn.silu(swish_pre)
    gated = (swish_act * token_out_f).astype(jnp.bfloat16)
    residual = inputs + matmul(gated, output_full)
    gate_full, up_full, down_full, gain_two = (
        lax.all_gather(w_gate, EVERYWHERE, axis=0, tiled=True),
        lax.all_gather(w_up, EVERYWHERE, axis=0, tiled=True),
        lax.all_gather(w_down, EVERYWHERE, axis=0, tiled=True),
        lax.all_gather(gain_ffn, EVERYWHERE, axis=0, tiled=True),
    )
    normed_two, inverse_two = normalize(residual)
    scaled_two = (normed_two * gain_two.astype(jnp.float32)).astype(jnp.bfloat16)
    gate_pre = matmul(scaled_two, gate_full)
    up_pre = matmul(scaled_two, up_full)
    product = (jax.nn.silu(gate_pre) * up_pre).astype(jnp.bfloat16)
    layer_out = residual + matmul(product, down_full)
    grad_top = cotangent[0].astype(jnp.float32)
    grad_top_low = grad_top.astype(jnp.bfloat16)
    grad_product = matmul(grad_top_low, down_full.T)
    grad_down_term = matmul(product.T, grad_top_low)
    grad_gate_pre = (grad_product * up_pre * swish_slope(gate_pre)).astype(jnp.bfloat16)
    grad_up_pre = (grad_product * jax.nn.silu(gate_pre)).astype(jnp.bfloat16)
    grad_gate_term = matmul(scaled_two.T, grad_gate_pre)
    grad_up_term = matmul(scaled_two.T, grad_up_pre)
    grad_scaled_two = matmul(grad_gate_pre, gate_full.T) + matmul(grad_up_pre, up_full.T)
    grad_gain_two = jnp.sum(grad_scaled_two * normed_two, axis=0)
    grad_residual = grad_top + norm_back(
        grad_scaled_two * gain_two.astype(jnp.float32), normed_two, inverse_two
    )
    grad_gate, grad_up, grad_down, grad_gain_ffn = (
        lax.psum_scatter(grad_gate_term, EVERYWHERE, scatter_dimension=0, tiled=True),
        lax.psum_scatter(grad_up_term, EVERYWHERE, scatter_dimension=0, tiled=True),
        lax.psum_scatter(grad_down_term, EVERYWHERE, scatter_dimension=0, tiled=True),
        lax.psum_scatter(grad_gain_two, EVERYWHERE, scatter_dimension=0, tiled=True),
    )
    grad_y = grad_residual.astype(jnp.bfloat16)
    grad_output_term = matmul(gated.T, grad_y)
    grad_gated = matmul(grad_y, output_full.T)
    grad_swish_pre = (grad_gated * token_out_f * swish_slope(swish_pre)).astype(jnp.bfloat16)
    grad_token_out = (
        (grad_gated * swish_act).astype(jnp.bfloat16).reshape(tokens, RETENTION_HEADS, VALUE_DIM)
    )
    grad_swish_term = matmul(scaled_one.T, grad_swish_pre)
    grad_head_out = lax.all_to_all(
        grad_token_out, ULY, split_axis=1, concat_axis=0, tiled=True
    ).astype(jnp.float32)
    grad_retained = norm_back(grad_head_out, head_normed, head_inverse).astype(jnp.bfloat16)
    grad_retained_f = grad_retained.astype(jnp.float32)
    grad_weights = jnp.einsum(
        "the,she->hts", grad_retained, head_v, preferred_element_type=jnp.float32
    )
    grad_scores = (grad_weights * mask).astype(jnp.bfloat16)
    grad_state_in = scale * jnp.einsum(
        "thd,the->hde", query_f * reach, grad_retained_f, precision=highest
    )
    _, grad_update = entering((block_decay, grad_state_in), CTX, carry_backward, identity, True)
    grad_head_q = jnp.einsum(
        "hts,shd->thd", grad_scores, head_k, preferred_element_type=jnp.float32
    ) + scale * reach * jnp.einsum("the,hde->thd", grad_retained_f, state_in, precision=highest)
    grad_head_k = jnp.einsum(
        "hts,thd->shd", grad_scores, head_q, preferred_element_type=jnp.float32
    ) + tail * jnp.einsum("she,hde->shd", value_f, grad_update, precision=highest)
    grad_head_v = jnp.einsum(
        "hts,the->she", weights, grad_retained, preferred_element_type=jnp.float32
    ) + tail * jnp.einsum("shd,hde->she", key_f, grad_update, precision=highest)
    grad_queries, grad_keys, grad_values = (
        lax.all_to_all(
            grad_head_q.astype(jnp.bfloat16), ULY, split_axis=0, concat_axis=1, tiled=True
        ),
        lax.all_to_all(
            grad_head_k.astype(jnp.bfloat16), ULY, split_axis=0, concat_axis=1, tiled=True
        ),
        lax.all_to_all(
            grad_head_v.astype(jnp.bfloat16), ULY, split_axis=0, concat_axis=1, tiled=True
        ),
    )
    grad_queries = grad_queries.reshape(tokens, RETENTION_HEADS * KEY_DIM)
    grad_keys = grad_keys.reshape(tokens, RETENTION_HEADS * KEY_DIM)
    grad_values = grad_values.reshape(tokens, RETENTION_HEADS * VALUE_DIM)
    grad_query_term = matmul(scaled_one.T, grad_queries)
    grad_key_term = matmul(scaled_one.T, grad_keys)
    grad_value_term = matmul(scaled_one.T, grad_values)
    grad_scaled_one = (
        matmul(grad_queries, query_full.T)
        + matmul(grad_keys, key_full.T)
        + matmul(grad_values, value_full.T)
        + matmul(grad_swish_pre, swish_full.T)
    )
    grad_gain_one = jnp.sum(grad_scaled_one * normed_one, axis=0)
    grad_input = grad_residual + norm_back(
        grad_scaled_one * gain_one.astype(jnp.float32), normed_one, inverse_one
    )
    grad_query, grad_key, grad_value, grad_swish, grad_output, grad_gain_attn = (
        lax.psum_scatter(
            grad_query_term, EVERYWHERE, scatter_dimension=0, tiled=True
        ),
        lax.psum_scatter(grad_key_term, EVERYWHERE, scatter_dimension=0, tiled=True),
        lax.psum_scatter(
            grad_value_term, EVERYWHERE, scatter_dimension=0, tiled=True
        ),
        lax.psum_scatter(
            grad_swish_term, EVERYWHERE, scatter_dimension=0, tiled=True
        ),
        lax.psum_scatter(
            grad_output_term, EVERYWHERE, scatter_dimension=0, tiled=True
        ),
        lax.psum_scatter(grad_gain_one, EVERYWHERE, scatter_dimension=0, tiled=True),
    )
    return (
        layer_out[None],
        grad_input[None],
        grad_query,
        grad_key,
        grad_value,
        grad_swish,
        grad_output,
        grad_gate,
        grad_up,
        grad_down,
        grad_gain_attn,
        grad_gain_ffn,
    )


MESH = pl.DeviceIdType.MESH
BF16, F32 = jnp.bfloat16, jnp.float32
HBM, VMEM = pltpu.HBM, pltpu.VMEM
N_SEMS = 160


def dot_t(left, right):
    return lax.dot_general(left, right, (((0,), (0,)), ((), ())), preferred_element_type=F32)


def dot_nt(left, right):
    return lax.dot_general(left, right, (((1,), (1,)), ((), ())), preferred_element_type=F32)


def pair_dot(left_axis, right_axis, left, right):
    dims = (((left_axis,), (right_axis,)), ((0,), (0,)))
    return lax.dot_general(left, right, dims, preferred_element_type=F32)


class Place:
    def __init__(self, uly):
        self.dp, self.ctx, self.uly = lax.axis_index(DP), lax.axis_index(CTX), uly
        odd = lax.rem(self.ctx, 2)
        self.xn = self.ctx + 1 - 2 * odd
        self.yn = lax.rem(self.ctx + 2, 4)
        self.dg = self.yn + 1 - 2 * odd
        self.other = 1 - self.dp

    def at(self, dp=None, ctx=None, uly=None):
        return (
            self.dp if dp is None else dp,
            self.ctx if ctx is None else ctx,
            self.uly if uly is None else uly,
        )


class Mover:
    def __init__(self, place, names, send, recv, like=None):
        self.like = like
        self.place, self.names, self.send_sems, self.recv_sems = place, names, send, recv
        self.sent = []

    def number(self, name):
        return self.names.setdefault(name, len(self.names))

    def remote(self, name, src, dst, device):
        k = self.number(name)
        return pltpu.make_async_remote_copy(
            src_ref=src,
            dst_ref=dst,
            send_sem=self.send_sems.at[k],
            recv_sem=self.recv_sems.at[k],
            device_id=device,
            device_id_type=MESH,
        )

    def send(self, name, src, dst, device):
        copy = self.remote(name, src, dst, device)
        copy.start()
        self.sent.append(copy if self.like is None else name)

    def arrive(self, name, dst):
        self.remote(name, dst, dst, self.place.at(dp=self.place.other)).wait_recv()

    def local(self, name, src, dst):
        copy = pltpu.make_async_copy(src, dst, self.send_sems.at[self.number(name)])
        copy.start()
        return copy

    def finish(self):
        for copy in self.sent:
            if self.like is not None:
                ref = self.like()
                copy = self.remote(copy, ref, ref, self.place.at(dp=self.place.other))
            copy.wait_send()


def greet(devices):
    barrier = pltpu.get_barrier_semaphore()
    for device in devices:
        pl.semaphore_signal(barrier, inc=1, device_id=device, device_id_type=MESH)
    pl.semaphore_wait(barrier, len(devices))


def together(streams):
    streams = list(streams)
    while streams:
        left = []
        for stream in streams:
            if next(stream, 0) is None:
                left.append(stream)
        streams = left


def later(stream, stages):
    for _ in range(stages):
        yield
    yield from stream


def add_up(dst, sources, step=32):
    if len(dst.shape) > 2:
        for i in range(dst.shape[0]):
            add_up(dst.at[i], [source.at[i] for source in sources], step)
        return
    rows, columns = dst.shape
    by_rows = rows % step == 0
    step = step if by_rows else 256

    def body(i, carry):
        part = pl.ds(pl.multiple_of(i * step, step), step)
        at = (part, slice(None)) if by_rows else (slice(None), part)
        total = sources[0][at].astype(F32)
        for source in sources[1:]:
            total = total + source[at].astype(F32)
        dst[at] = total.astype(dst.dtype)
        return carry

    lax.fori_loop(0, (rows if by_rows else columns) // step, body, 0)


def line_gather(m, tag, own, out, pause=1):
    p = m.place
    u = p.uly
    copy = m.local(tag + "=", own, out.at[p.dp * 4 + u])
    if u < 3:
        m.send((tag, "r", u), own, out.at[p.dp * 4 + u], p.at(uly=u + 1))
    if u > 0:
        m.send((tag, "l", u), own, out.at[p.dp * 4 + u], p.at(uly=u - 1))
    m.send((tag, "c", u), own, out.at[p.dp * 4 + u], p.at(dp=p.other))
    for _ in range(pause):
        yield
    for d in range(1, 4):
        for way, b, onward in (("r", u - d, u + 1), ("l", u + d, u - 1)):
            if 0 <= b <= 3:
                block = out.at[p.dp * 4 + b]
                m.arrive((tag, way, b), block)
                if 0 <= onward <= 3:
                    m.send((tag, way, b), block, block, p.at(uly=onward))
                m.send((tag, "c", b), block, block, p.at(dp=p.other))
        yield
    for b in range(4):
        m.arrive((tag, "c", b), out.at[p.other * 4 + b])
    copy.wait()


def plane_gather(m, tag, own, out, slot, halves, pair=True):
    p = m.place

    def half(c, i):
        return slot(out, p.dp, c, halves[i])

    mine = slot(out, p.dp, p.ctx, None)
    copy = m.local(tag + "=", own, mine)
    m.send((tag, "x"), own, mine, p.at(ctx=p.xn))
    m.send((tag, "y"), own, mine, p.at(ctx=p.yn))
    if pair:
        m.send((tag, "c", 0), own, mine, p.at(dp=p.other))
    yield
    block = slot(out, p.dp, p.xn, None)
    m.arrive((tag, "x"), block)
    m.send((tag, "z", 0), half(p.xn, 0), half(p.xn, 0), p.at(ctx=p.yn))
    if pair:
        m.send((tag, "c", 1), block, block, p.at(dp=p.other))
    block = slot(out, p.dp, p.yn, None)
    m.arrive((tag, "y"), block)
    m.send((tag, "z", 1), half(p.yn, 1), half(p.yn, 1), p.at(ctx=p.xn))
    if pair:
        m.send((tag, "c", 2), block, block, p.at(dp=p.other))
    yield
    for i in range(2):
        block = half(p.dg, i)
        m.arrive((tag, "z", i), block)
        if pair:
            m.send((tag, "c", 3 + i), block, block, p.at(dp=p.other))
    yield
    if pair:
        for i, c in enumerate((p.ctx, p.xn, p.yn)):
            m.arrive((tag, "c", i), slot(out, p.other, c, None))
        for i in range(2):
            m.arrive((tag, "c", 3 + i), slot(out, p.other, p.dg, halves[i]))
    copy.wait()


def line_reduce(m, tag, part, out, sib, right, left):
    p = m.place
    u = p.uly
    order = (3, 0, 2, 1) if u < 2 else (0, 3, 1, 2)
    for b in order if sib is not None else ():
        m.send((tag, "c", b), part(p.other * 4 + b), sib.at[b], p.at(dp=p.other))
    met = set()

    def meet(b):
        if sib is None:
            return [part(b)]
        if b not in met:
            met.add(b)
            m.arrive((tag, "c", b), sib.at[b])
        return [part(p.dp * 4 + b), sib.at[b]]

    def onward(way, b, arrived, there):
        terms = meet(b)
        if arrived is not None:
            m.arrive((tag, way, b), arrived)
            terms.append(arrived)
        if len(terms) > 1:
            add_up(terms[-1], terms)
        m.send((tag, way, b), terms[-1], (right if way == "r" else left).at[b], p.at(uly=there))

    for slot in range(3):
        for b in range(4):
            if u < b and u + 3 - b == slot:
                onward("r", b, right.at[b] if u > 0 else None, u + 1)
            if u > b and 3 - u + b == slot:
                onward("l", b, left.at[b] if u < 3 else None, u - 1)
        yield
    terms = meet(u)
    if u > 0:
        m.arrive((tag, "r", u), right.at[u])
        terms.append(right.at[u])
    if u < 3:
        m.arrive((tag, "l", u), left.at[u])
        terms.append(left.at[u])
    add_up(out, terms)


def plane_reduce(m, tag, part, out, sib, sums, got, got2):
    p = m.place
    rows = out.shape[0]
    halves = (pl.ds(0, rows // 2), pl.ds(rows // 2, rows // 2))
    order = (p.dg, p.xn, p.yn, p.ctx)
    for i, c in enumerate(order):
        m.send((tag, "c", i), part.at[p.other * 4 + c], sib.at[c], p.at(dp=p.other))
    yield
    for i, c in enumerate(order):
        m.arrive((tag, "c", i), sib.at[c])
        add_up(sums.at[c], [part.at[p.dp * 4 + c], sib.at[c]])
        if i == 0:
            m.send((tag, "x", 1), sums.at[c, halves[0]], got.at[1, halves[0]], p.at(ctx=p.xn))
            m.send((tag, "y", 1), sums.at[c, halves[1]], got.at[1, halves[1]], p.at(ctx=p.yn))
        if i == 1:
            m.send((tag, "x", 0), sums.at[c, halves[0]], got.at[0, halves[0]], p.at(ctx=p.xn))
        if i == 2:
            m.send((tag, "y", 0), sums.at[c, halves[1]], got.at[0, halves[1]], p.at(ctx=p.yn))
    yield
    m.arrive((tag, "x", 1), got.at[1, halves[0]])
    add_up(got.at[1, halves[0]], [sums.at[p.yn, halves[0]], got.at[1, halves[0]]])
    m.send((tag, "y2"), got.at[1, halves[0]], got2.at[halves[0]], p.at(ctx=p.yn))
    m.arrive((tag, "y", 1), got.at[1, halves[1]])
    add_up(got.at[1, halves[1]], [sums.at[p.xn, halves[1]], got.at[1, halves[1]]])
    m.send((tag, "x2"), got.at[1, halves[1]], got2.at[halves[1]], p.at(ctx=p.xn))
    yield
    m.arrive((tag, "x", 0), got.at[0, halves[0]])
    m.arrive((tag, "y", 0), got.at[0, halves[1]])
    yield
    m.arrive((tag, "y2"), got2.at[halves[0]])
    m.arrive((tag, "x2"), got2.at[halves[1]])
    add_up(out, [sums.at[p.ctx], got.at[0], got2])


def run_kernel(name, number, branches, partners, streams, outs, ins, scratch=(), vmem=48, time=40):
    def kernel(*refs):
        send, recv = refs[-2:]
        refs = refs[:-2]
        uly = lax.axis_index(ULY)
        names = {}
        greet(partners(Place(uly)) if partners else [])

        def body(u):
            m = Mover(Place(u), names, send, recv)
            together(streams(m, *refs))
            m.finish()

        if branches == 1:
            body(uly)
        else:
            for u in range(4):
                pl.when(uly == u)(functools.partial(body, u))
        assert len(names) <= N_SEMS

    return pl.pallas_call(
        kernel,
        out_shape=[jax.ShapeDtypeStruct(*o[:2]) for o in outs],
        in_specs=[pl.BlockSpec(memory_space=s) for _, s in ins],
        out_specs=[pl.BlockSpec(memory_space=o[2]) for o in outs],
        scratch_shapes=[
            *[pltpu.VMEM(shape, dtype) for shape, dtype in scratch],
            pltpu.SemaphoreType.DMA((N_SEMS,)),
            pltpu.SemaphoreType.DMA((N_SEMS,)),
        ],
        name=name,
        cost_estimate=pl.CostEstimate(
            flops=0, bytes_accessed=time * 3_700_000, transcendentals=0
        ),
        compiler_params=pltpu.CompilerParams(
            collective_id=number, has_side_effects=True, vmem_limit_bytes=vmem << 20
        ),
    )(*[a for a, _ in ins])


def everyone(p):
    me = p.dp * 16 + p.ctx * 4 + p.uly
    found = []
    for k in range(1, 32):
        there = lax.rem(me + k, 32)
        found.append((lax.div(there, 16), lax.rem(lax.div(there, 4), 4), lax.rem(there, 4)))
    return found


def line_partners(p):
    found = [p.at(dp=p.other)]
    for d in range(1, 4):
        there = lax.rem(p.uly + d, 4)
        found += [p.at(uly=there), p.at(dp=p.other, uly=there)]
    return found


def plane_partners(p):
    return [p.at(dp=p.other), p.at(ctx=p.xn), p.at(ctx=p.yn)]


def token_slot(out, dp, c, part):
    view = out.at[dp * 4 + c]
    return view if part is None else view.at[part]


def state_slot(out, dp, c, part):
    view = out.at[c]
    return view if part is None else view.at[part]


def pack(w_query, w_key, w_value, w_swish, w_output, w_gate, w_up, gains):
    rows, (out_rows, width) = w_query.shape[0], w_output.shape
    key, val, ff, quarter = KEY_DIM, VALUE_DIM, w_gate.shape[1] // 8, width // 4
    cols = 2 * key + 2 * val + 32

    def kernel(q, k, v, s, o, g, u, n, packed, outw, gu):
        for d in range(2):
            for z in range(4):
                h, i = 2 * z + d, 4 * d + z
                at = 0
                for ref, w in ((q, key), (k, key), (v, val), (s, val)):
                    packed[i, :, at : at + w] = ref[:, h * w : (h + 1) * w]
                    at += w
                packed[i, :, at : at + 32] = n[...]
        for i in range(8):
            gu[i, :, :ff] = g[:, i * ff : (i + 1) * ff]
            gu[i, :, ff:] = u[:, i * ff : (i + 1) * ff]
        for j in range(4):
            outw[j] = o[:, j * quarter : (j + 1) * quarter]

    return pl.pallas_call(
        kernel,
        out_shape=[
            jax.ShapeDtypeStruct((8, rows, cols), BF16),
            jax.ShapeDtypeStruct((4, out_rows, quarter), BF16),
            jax.ShapeDtypeStruct((8, rows, 2 * ff), BF16),
        ],
        name="pack",
        compiler_params=pltpu.CompilerParams(vmem_limit_bytes=32 << 20),
    )(w_query, w_key, w_value, w_swish, w_output, w_gate, w_up, gains)


def unpack(heads, outg, slices):
    rows, (_, out_rows, quarter) = heads.shape[1], outg.shape
    key, val, ff = KEY_DIM, VALUE_DIM, slices.shape[2] // 2

    def kernel(hs, og, sl, q, k, v, s, o, g, u):
        for d in range(2):
            for z in range(4):
                h, i = 2 * z + d, 4 * d + z
                at = 0
                for ref, w in ((q, key), (k, key), (v, val), (s, val)):
                    ref[:, h * w : (h + 1) * w] = hs[i, :, at : at + w].astype(F32)
                    at += w
        for i in range(8):
            g[:, i * ff : (i + 1) * ff] = sl[i, :, :ff].astype(F32)
            u[:, i * ff : (i + 1) * ff] = sl[i, :, ff:].astype(F32)
        for j in range(4):
            o[:, j * quarter : (j + 1) * quarter] = og[j].astype(F32)

    wide = jax.ShapeDtypeStruct((rows, 8 * key), F32)
    wider = jax.ShapeDtypeStruct((rows, 8 * val), F32)
    ffs = jax.ShapeDtypeStruct((rows, 8 * ff), F32)
    return pl.pallas_call(
        kernel,
        out_shape=[
            wide, wide, wider, wider,
            jax.ShapeDtypeStruct((out_rows, 4 * quarter), F32),
            ffs, ffs,
        ],
        name="unpack",
        compiler_params=pltpu.CompilerParams(vmem_limit_bytes=32 << 20),
    )(heads, outg, slices)


def line_spread(m, tag, own, out):
    u = m.place.uly
    copy = m.local((tag, 8), own, out.at[u])
    if u < 3:
        m.send((tag, "r", u), own, out.at[u], m.place.at(uly=u + 1))
    if u > 0:
        m.send((tag, "l", u), own, out.at[u], m.place.at(uly=u - 1))
    copy.wait()
    yield
    for d in range(1, 4):
        for way, b, onward in (("r", u - d, u + 1), ("l", u + d, u - 1)):
            if 0 <= b <= 3:
                m.arrive((tag, way, b), out.at[b])
                if 0 <= onward <= 3:
                    m.send((tag, way, b), out.at[b], out.at[b], m.place.at(uly=onward))
        yield


def block_factors(cum, ctx, s, backward):
    count = cum.shape[1]
    lasts = [cum[4 * s + j : 4 * s + j + 1, count - 1 : count] for j in range(4)]
    found = []
    for j in range(4):
        total = jnp.zeros((1, 1), F32)
        for i in range(4):
            inside = ((i > ctx) & (i < j)) if backward else ((i > j) & (i < ctx))
            total = total + jnp.where(inside, lasts[i], 0.0)
        right = (j > ctx) if backward else (j < ctx)
        found.append(jnp.where(right, jnp.exp(total), 0.0))
    return found


def forward(hidden, cot, decay, packed, outw, gu, w_down):
    tokens, width = hidden.shape
    rows, cols = packed.shape[1:]
    out_rows, quarter = outw.shape[1:]
    ff2 = gu.shape[2]
    key, val = KEY_DIM, VALUE_DIM
    block, both = 4 * tokens, 8 * tokens
    half = block // 2
    scale = 1.0 / math.sqrt(key)
    at_s = 2 * key + val

    def start_streams(m, hid_ref, dec_ref, pk_ref, ow_ref, gu_ref, hall, dall, wall, oall, gall):
        p = m.place
        u = p.uly

        def row(q, c, us):
            dp = p.dp if q == 0 else p.other
            at = (dp * 16 + c * 4 + us) * rows
            return wall.at[pl.ds(pl.multiple_of(at, rows), rows)]

        def attn():
            sources = sorted(
                ((q, us) for q in range(2) for us in range(4)), key=lambda s: (abs(s[1] - u), s[0])
            )
            copy = None
            for q, to in sources:
                dp = p.dp if q == 0 else p.other
                mine = row(0, p.ctx, u)
                src = pk_ref.at[dp * 4 + to]
                if (q, to) == (0, u):
                    copy = m.local("T", src, mine)
                else:
                    m.send(("t", q, u), src, mine, p.at(dp=dp, uly=to))
            yield
            relays = []
            for n, (q, us) in enumerate(sources):
                tile = row(q, p.ctx, us)
                if (q, us) == (0, u):
                    copy.wait()
                else:
                    m.arrive(("t", q, us), tile)
                m.send(("X", q, us), tile, tile, p.at(ctx=p.xn))
                m.send(("Y", q, us), tile, tile, p.at(ctx=p.yn))
                relays.append((q, us))
                if n >= 2:
                    yield
                    relay(*relays.pop(0))
            while relays:
                yield
                relay(*relays.pop(0))
            yield
            for q, us in sources:
                even = (q + us) % 2 == 0
                m.arrive(("Y" if even else "X", q, us), row(q, p.yn if even else p.xn, us))
                m.arrive(("Z", q, us), row(q, p.dg, us))

        def relay(q, us):
            if (q + us) % 2 == 0:
                tile = row(q, p.xn, us)
                m.arrive(("X", q, us), tile)
                m.send(("Z", q, us), tile, tile, p.at(ctx=p.yn))
            else:
                tile = row(q, p.yn, us)
                m.arrive(("Y", q, us), tile)
                m.send(("Z", q, us), tile, tile, p.at(ctx=p.xn))

        def out_proj():
            head_dp, head_u = lax.rem(p.ctx, 2), p.dp * 2 + lax.div(p.ctx, 2)
            source_dp, source_ctx = u // 2, 2 * (u % 2) + p.dp

            def column(part, c):
                return oall.at[part, :, pl.ds(pl.multiple_of(c * quarter, quarter), quarter)]

            own = [
                (head_dp == p.dp) & (p.ctx == j) & (head_u == u) for j in range(4)
            ]
            for j in range(4):
                there = oall.at[u, :, pl.ds(j * quarter, quarter)]
                here = pltpu.make_async_copy(
                    ow_ref.at[j], there, m.send_sems.at[m.number("O")]
                )

                @pl.when(own[j])
                def _(here=here):
                    here.start()
                    here.wait()

                other = pltpu.make_async_remote_copy(
                    src_ref=ow_ref.at[j],
                    dst_ref=there,
                    send_sem=m.send_sems.at[m.number(("S", j))],
                    recv_sem=m.recv_sems.at[m.number(("o", u))],
                    device_id=(head_dp, j, head_u),
                    device_id_type=MESH,
                )
                pl.when(jnp.logical_not(own[j]))(other.start)
            for _ in range(7):
                yield
            for us in range(4):
                mine = (source_dp == p.dp) & (source_ctx == p.ctx) & (us == u)

                @pl.when(jnp.logical_not(mine))
                def _(us=us):
                    m.arrive(("o", us), column(us, p.ctx))

            yield
            mine = column(pl.ds(0, 4), p.ctx)
            m.send("ox", mine, mine, p.at(ctx=p.xn))
            m.send("oy", mine, mine, p.at(ctx=p.yn))
            yield
            low, high = pl.ds(0, 2), pl.ds(2, 2)
            m.arrive("ox", column(pl.ds(0, 4), p.xn))
            m.send("o0", column(low, p.xn), column(low, p.xn), p.at(ctx=p.yn))
            m.arrive("oy", column(pl.ds(0, 4), p.yn))
            m.send("o1", column(high, p.yn), column(high, p.yn), p.at(ctx=p.xn))
            yield
            for j in range(4):
                other = pltpu.make_async_remote_copy(
                    src_ref=ow_ref.at[j],
                    dst_ref=ow_ref.at[j],
                    send_sem=m.send_sems.at[m.number(("S", j))],
                    recv_sem=m.recv_sems.at[m.number(("o", u))],
                    device_id=p.at(dp=p.other),
                    device_id_type=MESH,
                )
                pl.when(jnp.logical_not(own[j]))(other.wait_send)
            m.arrive("o0", column(low, p.dg))
            m.arrive("o1", column(high, p.dg))

        def feed():
            mine = gall.at[p.dp * 4 + p.ctx]
            copy = m.local("F", gu_ref.at[p.dp * 4 + p.ctx], mine)
            decays = m.local("D", dec_ref, dall.at[p.dp * 4 + p.ctx])
            spots = [(q, c, i) for i, c in enumerate((p.ctx, p.xn, p.yn, p.dg)) for q in range(2)][1:]
            for q, c, i in spots:
                dp = p.dp if q == 0 else p.other
                m.send(("d", q, i), dec_ref, dall.at[p.dp * 4 + p.ctx], p.at(dp=dp, ctx=c))
                m.send(("f", q, i), gu_ref.at[dp * 4 + c], mine, p.at(dp=dp, ctx=c))
            for _ in range(5):
                yield
            for q, c, i in spots:
                dp = p.dp if q == 0 else p.other
                m.arrive(("d", q, i), dall.at[dp * 4 + c])
                m.arrive(("f", q, i), gall.at[dp * 4 + c])
            copy.wait()
            decays.wait()

        return [
            attn(),
            later(line_gather(m, "h", hid_ref, hall, 6), 1),
            later(out_proj(), 1),
            later(feed(), 6),
        ]

    def kernel(
        hid_ref, cot_ref, dec_ref, pk_ref, ow_ref, gu_ref, wd_ref,
        w_all, s1_all, w2d, q_ref, k_ref, v_ref, sw_ref, w_ref, mask_ref, st_ref, reach_ref, tail_ref, cum_ref,
        gain_ref, hn_ref, hi_ref, ga_ref, res_ref, s2_all, top_all, gu_all, wd_all,
        wall, s1, oall, dall, gall, dec8, cols8, upd, upds, ret, part, sib, right, left, s2, send, recv,
    ):
        uly = lax.axis_index(ULY)
        names = {}
        place = Place(uly)
        greet(everyone(place))
        common = Mover(place, names, send, recv)
        ctx = place.ctx

        def for_each(body):
            for u in range(4):
                pl.when(uly == u)(functools.partial(body, u))

        spread = []
        for u in range(4):
            for tag, own, out in (("g", gall, gu_all), ("e", wd_ref, wd_all)):
                m = Mover(Place(u), names, send, recv, lambda out=out: out.at[0])
                spread.append((u, m, line_spread(m, tag, own, out)))

        def spread_on(u):
            for v, _, stream in spread:
                if u == v:
                    next(stream, 0)

        def first(u):
            m = Mover(Place(u), names, send, recv)
            together(
                start_streams(m, hid_ref, dec_ref, pk_ref, ow_ref, gu_ref, s1, dall, wall, oall, gall)
            )
            m.finish()
            spread_on(u)

        for_each(first)
        keep = [common.local("w", wall, w_all)]

        table = wall[:, cols - 128 : cols].astype(F32).T
        first_gain = 128 - 32
        gain_ref[...] = table[first_gain : first_gain + 8]

        def norm_one(i, carry):
            b, at = lax.div(i, 4), pl.ds(pl.multiple_of(lax.rem(i, 4) * 32, 32), 32)
            normed, _ = normalize(s1[b, at, :].astype(F32))
            s1[b, at, :] = (normed * gain_ref[0:1, :]).astype(BF16)
            return carry

        lax.fori_loop(0, 32, norm_one, 0)
        keep.append(common.local("W", s1, s1_all))

        for i in range(8):
            dec8[i : i + 1, :] = dall[i, pl.ds(place.dp, 1), :]
        upper = lax.broadcasted_iota(jnp.int32, (block, block), 0) <= lax.broadcasted_iota(
            jnp.int32, (block, block), 1
        )
        cum_ref[...] = jnp.dot(
            dec8[...], upper.astype(F32), precision=lax.Precision.HIGHEST, preferred_element_type=F32
        )
        for s in range(2):
            dec8[s : s + 1, :] = cum_ref[pl.ds(4 * s + ctx, 1), :]
        cols8[...] = dec8[...].T
        for s in range(2):
            column = cols8[:, s : s + 1]
            reach_ref[s] = jnp.exp(column) * scale
            tail_ref[s] = jnp.exp(dec8[s : s + 1, block - 1 : block] - column)

        for s in range(2):
            lhs = s1[4 * s : 4 * s + 4].reshape(block, width)
            q_ref[s] = matmul(lhs, wall[:, :key]).astype(BF16)
            k_ref[s] = matmul(lhs, wall[:, key : 2 * key]).astype(BF16)
            rest = matmul(lhs, wall[:, 2 * key :])
            v_ref[s] = rest[:, :val].astype(BF16)
            sw_ref[pl.ds(s * block, block), :] = rest[:, val : 2 * val]
        for s in range(2):
            k_tail = (k_ref[s].astype(F32) * tail_ref[s]).astype(BF16)
            upd[s] = dot_t(k_tail, v_ref[s]).astype(BF16)
        states = plane_gather(
            common, "t", upd, upds, state_slot, (pl.ds(0, 1), pl.ds(1, 1)), pair=False
        )
        next(states)

        def intra(c, carry):
            s, h = lax.div(c, 2), lax.rem(c, 2)
            at = pl.ds(pl.multiple_of(h * half, half), half)
            here = pl.ds(pl.multiple_of(c * half, half), half)
            gap = cols8[at, :]
            column = jnp.where(s == 0, gap[:, 0:1], gap[:, 1:2])
            gap = column - dec8[pl.ds(s, 1), :]
            t = lax.broadcasted_iota(jnp.int32, (half, block), 0) + h * half
            later_on = t >= lax.broadcasted_iota(jnp.int32, (half, block), 1)
            mask = jnp.where(later_on, jnp.exp(jnp.minimum(gap, 0.0)), 0.0) * scale
            mask_ref[s, at, :] = mask
            weights = (dot_nt(q_ref[s, at, :], k_ref[s]) * mask).astype(BF16)
            w_ref[s, at, :] = weights
            ret[here, :] = matmul(weights, v_ref[s])
            return carry

        lax.fori_loop(0, 2, intra, 0)
        next(states)
        for_each(spread_on)
        lax.fori_loop(2, 4, intra, 0)
        for i in range(4):
            w2d[i * out_rows : (i + 1) * out_rows, :] = oall[i]
        for _ in states:
            pass
        for s in range(2):
            factors = block_factors(cum_ref, ctx, s, False)
            total = factors[0] * upds[0, s].astype(F32)
            for j in range(1, 4):
                total = total + factors[j] * upds[j, s].astype(F32)
            st_ref[s] = total.astype(BF16)

        def outer(c, carry):
            s, h = lax.div(c, 2), lax.rem(c, 2)
            at = pl.ds(pl.multiple_of(h * half, half), half)
            here = pl.ds(pl.multiple_of(c * half, half), half)
            retained = ret[here, :] + reach_ref[s, at, :] * matmul(q_ref[s, at, :], st_ref[s])
            normed, inverse = normalize(retained)
            hn_ref[here, :] = normed
            hi_ref[here, :] = inverse
            pre = sw_ref[here, :]
            gated = (pre * jax.nn.sigmoid(pre) * normed.astype(BF16).astype(F32)).astype(BF16)
            ga_ref[here, :] = gated
            for n in range(4):
                cut = pl.ds(n * quarter, quarter)
                value = matmul(gated, w2d[:, cut]).astype(BF16)
                part[pl.ds(2 * c, 2), :, cut] = value.reshape(2, tokens, quarter)
            return carry

        lax.fori_loop(0, 4, outer, 0)

        def reduce(u):
            m = Mover(Place(u), names, send, recv)
            low = tokens // 2
            together(
                [
                    line_reduce(m, "s", lambda i: part.at[i], res_ref, sib, right, left),
                    plane_gather(
                        m, "C", cot_ref, top_all, token_slot, (pl.ds(0, low), pl.ds(low, low))
                    ),
                ]
            )
            m.finish()
            spread_on(u)

        for_each(reduce)

        def norm_two(i, carry):
            at = pl.ds(pl.multiple_of(i * 16, 16), 16)
            residual = hid_ref[at, :].astype(F32) + res_ref[at, :]
            res_ref[at, :] = residual
            normed, _ = normalize(residual)
            s2[at, :] = (normed * gain_ref[1:2, :]).astype(BF16)
            return carry

        lax.fori_loop(0, tokens // 16, norm_two, 0)
        low = tokens // 2
        for _ in plane_gather(
            common, "k", s2, s2_all, token_slot, (pl.ds(0, low), pl.ds(low, low))
        ):
            pass

        def last(u):
            spread_on(u)
            for v, m, _ in spread:
                if u == v:
                    m.finish()

        for_each(last)
        for copy in keep:
            copy.wait()
        common.finish()
        assert len(names) <= N_SEMS

    vmem, hbm = pl.BlockSpec(memory_space=VMEM), pl.BlockSpec(memory_space=HBM)
    outs = [
        ((width, cols), BF16, hbm),
        ((8, tokens, width), BF16, hbm),
        ((4 * out_rows, width), BF16, vmem),
        ((2, block, key), BF16, vmem),
        ((2, block, key), BF16, vmem),
        ((2, block, val), BF16, vmem),
        ((both, val), F32, vmem),
        ((2, block, block), BF16, vmem),
        ((2, block, block), F32, vmem),
        ((2, key, val), BF16, vmem),
        ((2, block, 1), F32, vmem),
        ((2, block, 1), F32, vmem),
        ((8, block), F32, vmem),
        ((8, width), F32, vmem),
        ((both, val), F32, vmem),
        ((both, 1), F32, vmem),
        ((both, val), BF16, vmem),
        ((tokens, width), F32, vmem),
        ((8, tokens, width), BF16, hbm),
        ((8, tokens, width), BF16, hbm),
        ((4, 8, rows, ff2), BF16, hbm),
        ((4, out_rows, width), BF16, hbm),
    ]
    return pl.pallas_call(
        kernel,
        out_shape=[jax.ShapeDtypeStruct(shape, kind) for shape, kind, _ in outs],
        in_specs=[vmem, hbm, vmem, hbm, hbm, hbm, hbm],
        out_specs=[spec for _, _, spec in outs],
        scratch_shapes=[
            pltpu.VMEM((width, cols), BF16),
            pltpu.VMEM((8, tokens, width), BF16),
            pltpu.VMEM((4, out_rows, width), BF16),
            pltpu.VMEM((8, 2, block), F32),
            pltpu.VMEM((8, rows, ff2), BF16),
            pltpu.VMEM((8, block), F32),
            pltpu.VMEM((block, 8), F32),
            pltpu.VMEM((2, key, val), BF16),
            pltpu.VMEM((4, 2, key, val), BF16),
            pltpu.VMEM((both, val), F32),
            pltpu.VMEM((8, tokens, width), BF16),
            pltpu.VMEM((4, tokens, width), BF16),
            pltpu.VMEM((4, tokens, width), BF16),
            pltpu.VMEM((4, tokens, width), BF16),
            pltpu.VMEM((tokens, width), BF16),
            pltpu.SemaphoreType.DMA((N_SEMS,)),
            pltpu.SemaphoreType.DMA((N_SEMS,)),
        ],
        name="forward",
        compiler_params=pltpu.CompilerParams(
            collective_id=1, has_side_effects=True, vmem_limit_bytes=62 << 20
        ),
    )(hidden, cot, decay, packed, outw, gu, w_down)


def reduce_plane(part, down, number):
    _, tokens, width = part.shape

    def streams(m, part_ref, down_ref, out, dout, sib, sums, got, got2, right, left):
        return [
            plane_reduce(m, "s", part_ref, out, sib, sums, got, got2),
            line_reduce(m, "d", lambda b: down_ref.at[b], dout, None, right, left),
        ]

    return run_kernel(
        "reduce_plane",
        number,
        4,
        lambda p: line_partners(p) + plane_partners(p)[1:],
        streams,
        [((tokens, width), F32, VMEM), (down.shape[1:], F32, VMEM)],
        [(part, VMEM), (down, VMEM)],
        [
            ((4, tokens, width), BF16),
            ((4, tokens, width), BF16),
            ((2, tokens, width), BF16),
            ((tokens, width), BF16),
            (down.shape, BF16),
            (down.shape, BF16),
        ],
    )


def attention_back(
    own, lo, ggu, w_out, gated, normed, inverse, swish, q, k, v, weights, mask, state_in, reach, tail, cum
):
    tokens, width = own.shape
    both, val = gated.shape
    block, key = q.shape[1:]
    rows, cols = ggu.shape[3:]
    piece = w_out.shape[0] // 4
    half = block // 2
    at_v, at_s = 2 * key, 2 * key + val

    def kernel(
        own_ref, lo_ref, g_ref, wo_ref, ga_ref, hn_ref, hi_ref, sw_ref, q_ref, k_ref, v_ref, w_ref, mask_ref, st_ref,
        reach_ref, tail_ref, cum_ref, cat_ref, total, gout, gsum,
        gy, gr, gs, gq, gk, gv, gst, gsts, sib, sums, got, got2, right, left, send, recv,
    ):
        uly = lax.axis_index(ULY)
        names = {}
        place = Place(uly)
        greet(line_partners(place) + plane_partners(place)[1:])
        common = Mover(place, names, send, recv)
        movers = [Mover(Place(u), names, send, recv, lambda: right.at[0]) for u in range(4)]
        ways = [
            line_reduce(movers[u], "f", lambda b: g_ref.at[:, :, b], gsum, None, right, left)
            for u in range(4)
        ]

        def for_each(body):
            for u in range(4):
                pl.when(uly == u)(functools.partial(body, u))

        def first(u):
            def slot_zero():
                next(ways[u])
                yield

            m = Mover(Place(u), names, send, recv)
            together(
                [
                    plane_reduce(m, "s", lo_ref, total, sib, sums, got, got2),
                    line_gather(m, "k", own_ref, gy),
                    slot_zero(),
                ]
            )
            m.finish()

        for_each(first)

        def chunk(c):
            return pl.ds(pl.multiple_of(c * half, half), half)

        def gradients(c, carry):
            at = chunk(c)
            grad = gy[pl.ds(2 * c, 2)].reshape(half, width)
            gg = dot_nt(grad, wo_ref[...])
            pre = sw_ref[at, :]
            sigma = jax.nn.sigmoid(pre)
            head = hn_ref[at, :]
            low = head.astype(BF16).astype(F32)
            cat_ref[at, at_s : at_s + val] = (
                gg * low * (sigma * (1.0 + pre * (1.0 - sigma)))
            ).astype(BF16)
            gh = (gg * (pre * sigma)).astype(BF16).astype(F32)
            mean = jnp.mean(gh * head, axis=-1, keepdims=True)
            grad_retained = (hi_ref[at, :] * (gh - head * mean)).astype(BF16)
            gr[at, :] = grad_retained
            s = lax.div(c, 2)
            part = pl.ds(pl.multiple_of(lax.rem(c, 2) * half, half), half)
            gs[at, :] = (dot_nt(grad_retained, v_ref[s]) * mask_ref[s, part, :]).astype(BF16)
            return carry

        lax.fori_loop(0, both // half, gradients, 0)
        for s in range(2):
            at = pl.ds(s * block, block)
            reached = (q_ref[s].astype(F32) * reach_ref[s]).astype(BF16)
            gst[s] = dot_t(reached, gr[at, :]).astype(BF16)
        states = plane_gather(
            common, "t", gst, gsts, state_slot, (pl.ds(0, 1), pl.ds(1, 1)), pair=False
        )
        next(states)
        for_each(lambda u: next(ways[u]))

        for s in range(2):
            at = pl.ds(s * block, block)
            gq[at, :] = jnp.dot(gs[at, :], k_ref[s], preferred_element_type=F32)
            gk[at, :] = dot_t(gs[at, :], q_ref[s])
        next(states)
        for s in range(2):
            at = pl.ds(s * block, block)
            gv[at, :] = dot_t(w_ref[s], gr[at, :])

        def out_grad(n, carry):
            at = pl.ds(pl.multiple_of(n * 512, 512), 512)
            grad = gy[:, :, at].reshape(both, 512)
            value = dot_t(ga_ref[...], grad).astype(BF16)
            for i in range(4):
                gout[i, :, at] = value[i * piece : (i + 1) * piece]
            return carry

        lax.fori_loop(0, width // 512, out_grad, 0)
        for _ in states:
            pass
        for_each(lambda u: next(ways[u]))
        for s in range(2):
            at = pl.ds(s * block, block)
            factors = block_factors(cum_ref, place.ctx, s, True)
            update = factors[0] * gsts[0, s].astype(F32)
            for j in range(1, 4):
                update = update + factors[j] * gsts[j, s].astype(F32)
            update = update.astype(BF16)
            grad = gr[at, :]
            cat_ref[at, :key] = (gq[at, :] + reach_ref[s] * dot_nt(grad, st_ref[s])).astype(BF16)
            cat_ref[at, key:at_v] = (gk[at, :] + tail_ref[s] * dot_nt(v_ref[s], update)).astype(BF16)
            cat_ref[at, at_v:at_s] = (
                gv[at, :] + tail_ref[s] * jnp.dot(k_ref[s], update, preferred_element_type=F32)
            ).astype(BF16)

        def last(u):
            for _ in ways[u]:
                pass
            movers[u].finish()

        for_each(last)
        common.finish()
        assert len(names) <= N_SEMS

    vmem = pl.BlockSpec(memory_space=VMEM)
    return pl.pallas_call(
        kernel,
        out_shape=[
            jax.ShapeDtypeStruct((both, 2 * key + 2 * val), BF16),
            jax.ShapeDtypeStruct((tokens, width), F32),
            jax.ShapeDtypeStruct((4, piece, width), BF16),
            jax.ShapeDtypeStruct((2, 4, rows, cols), BF16),
        ],
        in_specs=[vmem] * 17,
        out_specs=[vmem] * 4,
        scratch_shapes=[
            pltpu.VMEM((8, tokens, width), BF16),
            pltpu.VMEM((both, val), BF16),
            pltpu.VMEM((both, block), BF16),
            pltpu.VMEM((both, key), F32),
            pltpu.VMEM((both, key), F32),
            pltpu.VMEM((both, val), F32),
            pltpu.VMEM((2, key, val), BF16),
            pltpu.VMEM((4, 2, key, val), BF16),
            pltpu.VMEM((4, tokens, width), BF16),
            pltpu.VMEM((4, tokens, width), BF16),
            pltpu.VMEM((2, tokens, width), BF16),
            pltpu.VMEM((tokens, width), BF16),
            pltpu.VMEM((4, 2, 4, rows, cols), BF16),
            pltpu.VMEM((4, 2, 4, rows, cols), BF16),
            pltpu.SemaphoreType.DMA((N_SEMS,)),
            pltpu.SemaphoreType.DMA((N_SEMS,)),
        ],
        name="attention_back",
        compiler_params=pltpu.CompilerParams(
            collective_id=7, has_side_effects=True, vmem_limit_bytes=62 << 20
        ),
    )(own, lo, ggu, w_out, gated, normed, inverse, swish, q, k, v, weights, mask, state_in, reach, tail, cum)


def last_exchange(part, grads, gout, gffn, inputs, term):
    _, tokens, width = part.shape
    rows, cols = grads.shape[3:]
    out_rows = gout.shape[1]
    quarter = width // 4
    ff2 = gffn.shape[2]

    def streams(
        m, part_ref, g_ref, o_ref, f_ref, in_ref, t_ref, out, gall, oall, fall, gains,
        sib, right, left, gotx, goty, gotx2, goty2, oxs, oys, ox2, oy2, away,
    ):
        p = m.place
        u = p.uly

        def attn():
            for i, (cx, cy) in ((1, (p.dg, p.dg)), (0, (p.xn, p.yn))):
                for t in range(4):
                    m.send(("gx", i, t), g_ref.at[0, cx, t], gotx.at[i, t], p.at(ctx=p.xn))
                    m.send(("gy", i, t), g_ref.at[1, cy, t], goty.at[i, t], p.at(ctx=p.yn))
            yield
            for t in range(4):
                m.arrive(("gx", 1, t), gotx.at[1, t])
                add_up(gotx.at[1, t], [g_ref.at[0, p.yn, t], gotx.at[1, t]])
                m.send(("gy2", t), gotx.at[1, t], goty2.at[t], p.at(ctx=p.yn))
                m.arrive(("gy", 1, t), goty.at[1, t])
                add_up(goty.at[1, t], [g_ref.at[1, p.xn, t], goty.at[1, t]])
                m.send(("gx2", t), goty.at[1, t], gotx2.at[t], p.at(ctx=p.xn))
            yield
            yield
            for t in range(4):
                for dp, got, got2, tags in (
                    (0, gotx, goty2, ("gx", "gy2")),
                    (1, goty, gotx2, ("gy", "gx2")),
                ):
                    m.arrive((tags[0], 0, t), got.at[0, t])
                    m.arrive((tags[1], t), got2.at[t])
                    add_up(got.at[0, t], [g_ref.at[dp, p.ctx, t], got.at[0, t], got2.at[t]])
                    there = gall.at[p.dp * 4 + u]
                    if t == u:

                        @pl.when(p.dp == dp)
                        def _(got=got, there=there):
                            here = pltpu.make_async_copy(
                                got.at[0, u], there, m.send_sems.at[m.number("G")]
                            )
                            here.start()
                            here.wait()

                        @pl.when(p.dp != dp)
                        def _(got=got, there=there, dp=dp):
                            m.remote(
                                ("gc", u), got.at[0, u], there, (dp, p.ctx, u)
                            ).start()
                    else:
                        k = m.number(("gs", dp, t))
                        copies = []
                        for q in range(2):
                            copies.append(
                                pltpu.make_async_remote_copy(
                                    src_ref=got.at[0, t],
                                    dst_ref=there,
                                    send_sem=m.send_sems.at[k],
                                    recv_sem=m.recv_sems.at[m.number(("g", q, u))],
                                    device_id=(dp, p.ctx, t),
                                    device_id_type=MESH,
                                )
                            )
                        pl.when(p.dp == dp)(copies[0].start)
                        pl.when(p.dp != dp)(copies[1].start)
                        m.sent.append(copies[0])
            for _ in range(6):
                yield
            m.remote(("gc", u), gotx.at[0, u], gotx.at[0, u], p.at(dp=p.other)).wait_send()
            m.arrive(("gc", u), gall.at[p.other * 4 + u])
            for us in range(4):
                if us != u:
                    m.arrive(("g", 0, us), gall.at[p.dp * 4 + us])
                    m.arrive(("g", 1, us), gall.at[p.other * 4 + us])

        def out_proj():
            def column(ref, part, c):
                return ref.at[part, :, pl.ds(pl.multiple_of(c * quarter, quarter), quarter)]

            low, high = pl.ds(0, 2), pl.ds(2, 2)
            for i, (cx, cy) in ((1, (p.dg, p.dg)), (0, (p.xn, p.yn))):
                m.send(("ox", i), column(o_ref, low, cx), oxs.at[i], p.at(ctx=p.xn))
                m.send(("oy", i), column(o_ref, high, cy), oys.at[i], p.at(ctx=p.yn))
            yield
            m.arrive(("ox", 1), oxs.at[1])
            for t in range(2):
                add_up(oxs.at[1, t], [column(o_ref, t, p.yn), oxs.at[1, t]])
            m.send("oy2", oxs.at[1], oy2, p.at(ctx=p.yn))
            m.arrive(("oy", 1), oys.at[1])
            for t in range(2):
                add_up(oys.at[1, t], [column(o_ref, 2 + t, p.xn), oys.at[1, t]])
            m.send("ox2", oys.at[1], ox2, p.at(ctx=p.xn))
            yield
            m.arrive(("ox", 0), oxs.at[0])
            m.arrive(("oy", 0), oys.at[0])
            m.arrive("oy2", oy2)
            m.arrive("ox2", ox2)
            home_dp, home_ctx = u // 2, 2 * (u % 2) + p.dp
            here_all = []
            for us in range(4):
                got, got2 = (oxs, oy2) if us < 2 else (oys, ox2)
                t = us % 2
                add_up(got.at[0, t], [column(o_ref, us, p.ctx), got.at[0, t], got2.at[t]])
                own = (home_dp == p.dp) & (home_ctx == p.ctx) & (us == u)
                there = oall.at[p.ctx]
                here = pltpu.make_async_copy(
                    got.at[0, t], there, m.send_sems.at[m.number("O")]
                )

                @pl.when(own)
                def _(here=here):
                    here.start()
                    here.wait()

                for j in range(4):
                    copy = pltpu.make_async_remote_copy(
                        src_ref=got.at[0, t],
                        dst_ref=there,
                        send_sem=m.send_sems.at[m.number(("os", us))],
                        recv_sem=m.recv_sems.at[m.number(("o", j))],
                        device_id=(home_dp, home_ctx, us),
                        device_id_type=MESH,
                    )
                    pl.when(jnp.logical_not(own) & (p.ctx == j))(copy.start)
                here_all.append((own, copy))
            yield
            head_dp, head_u = lax.rem(p.ctx, 2), p.dp * 2 + lax.div(p.ctx, 2)
            for j in range(4):
                mine = (head_dp == p.dp) & (p.ctx == j) & (head_u == u)

                @pl.when(jnp.logical_not(mine))
                def _(j=j):
                    m.arrive(("o", j), oall.at[j])

            for own, copy in here_all:
                pl.when(jnp.logical_not(own))(copy.wait_send)

        def feed():
            mine = fall.at[p.dp * 4 + p.ctx]
            copy = m.local("F", f_ref.at[p.dp * 4 + p.ctx], mine)
            spots = [(q, c, i) for i, c in enumerate((p.ctx, p.xn, p.yn, p.dg)) for q in range(2)][1:]
            for q, c, i in spots:
                dp = p.dp if q == 0 else p.other
                m.send(("f", q, i), f_ref.at[dp * 4 + c], mine, p.at(dp=dp, ctx=c))
            for _ in range(4):
                yield
            for q, c, i in spots:
                dp = p.dp if q == 0 else p.other
                m.arrive(("f", q, i), fall.at[dp * 4 + c])
            copy.wait()

        def tokens_stream():
            yield from line_reduce(m, "s", lambda i: part_ref.at[i], out, sib, right, left)

            def body(i, total):
                at = pl.ds(pl.multiple_of(i * 16, 16), 16)
                values = in_ref[at, :].astype(F32)
                normed, _ = normalize(values)
                return total + jnp.sum(out[at, :] * normed, axis=0, keepdims=True)

            total = lax.fori_loop(0, tokens // 16, body, jnp.zeros((1, width), F32))
            row = lax.broadcasted_iota(jnp.int32, (8, width), 0)
            gains[...] = jnp.where(
                row == 0,
                jnp.broadcast_to(total, (8, width)),
                jnp.where(row == 1, jnp.broadcast_to(t_ref[...], (8, width)), 0.0),
            )
            for i, device in enumerate((p.at(dp=p.other), p.at(ctx=p.xn), p.at(ctx=p.yn))):
                m.remote(("n", i), gains, away.at[i], device).start()
                yield
                m.remote(("n", i), gains, away.at[i], device).wait()
                gains[...] = gains[...] + away[i]
            copies = [
                m.remote(("N", u, other), gains, away.at[3 + u], p.at(uly=other))
                for other in range(4)
                if other != u
            ]
            for copy in copies:
                copy.start()
            yield
            mine = gains[...]
            for other in range(4):
                if other != u:
                    m.arrive(("N", other, u), away.at[3 + other])
                    mine = mine + away[3 + other]
            for copy in copies:
                copy.wait_send()
            gains[...] = mine

        return [
            tokens_stream(),
            attn(),
            later(out_proj(), 1),
            later(feed(), 5),
        ]

    return run_kernel(
        "last",
        2,
        4,
        everyone,
        streams,
        [
            ((tokens, width), F32, VMEM),
            ((8, rows, cols), BF16, HBM),
            ((4, out_rows, quarter), BF16, HBM),
            ((8, rows, ff2), BF16, HBM),
            ((8, width), F32, VMEM),
        ],
        [(part, VMEM), (grads, VMEM), (gout, VMEM), (gffn, HBM), (inputs, VMEM), (term, VMEM)],
        [
            *[((4, tokens, width), BF16)] * 3,
            *[((2, 4, rows, cols), BF16)] * 2,
            *[((4, rows, cols), BF16)] * 2,
            *[((2, 2, out_rows, quarter), BF16)] * 2,
            *[((2, out_rows, quarter), BF16)] * 2,
            ((7, 8, width), F32),
        ],
        vmem=56,
    )


def local(
    hidden_in,
    cotangent,
    log_decay,
    w_query,
    w_key,
    w_value,
    w_swish,
    w_output,
    w_gate,
    w_up,
    w_down,
    gain_attn,
    gain_ffn,
):
    bf16, f32 = BF16, F32
    dp, ctx = lax.axis_index(DP), lax.axis_index(CTX)
    tokens = hidden_in.shape[1]
    width = hidden_in.shape[2]
    rows = w_query.shape[0]
    out_rows = w_output.shape[0]
    key, val, ff = KEY_DIM, VALUE_DIM, w_gate.shape[1] // 8

    gains = jnp.pad(jnp.stack([gain_attn, gain_ffn], axis=1), ((0, 0), (0, 30)))
    packed, outw, gate_up = pack(w_query, w_key, w_value, w_swish, w_output, w_gate, w_up, gains)
    attn_cols = 2 * key + 2 * val
    block = 4 * tokens
    (
        w_all, scaled_one, w_out, q, k, v, swish_pre, weights, mask, state_in, reach, tail, cum,
        gains, head_normed, head_inverse, gated, residual, scaled_two, top_all, w_gu, w_dn,
    ) = forward(hidden_in[0], cotangent[0], log_decay[0], packed, outw, gate_up, w_down)
    w_attn = w_all[:, :attn_cols]
    gain_one, gain_two = gains[0], gains[1]
    scaled_one = scaled_one.reshape(8 * tokens, width)
    scaled_two = scaled_two.reshape(8 * tokens, width)
    top_all = top_all.reshape(8 * tokens, width)
    w_gu = w_gu.transpose(1, 0, 2, 3).reshape(32 * rows, 2 * ff)
    w_dn = w_dn.reshape(4 * out_rows, width)
    inputs = hidden_in[0].astype(f32)
    normed_two, inverse_two = normalize(residual)
    gu = matmul(scaled_two, w_gu)
    gate_pre, up_pre = gu[:, :ff], gu[:, ff:]
    gate_act = jax.nn.silu(gate_pre)
    product = (gate_act * up_pre).astype(bf16)
    grad_product = dot_nt(top_all, w_dn)
    grad_gu = jnp.concatenate(
        [
            (grad_product * up_pre * swish_slope(gate_pre)).astype(bf16),
            (grad_product * gate_act).astype(bf16),
        ],
        axis=1,
    )
    gs2, grad_down = reduce_plane(
        dot_nt(grad_gu, w_gu).astype(bf16).reshape(8, tokens, width),
        dot_t(product, top_all).astype(bf16).reshape(4, out_rows, width),
        6,
    )
    grad_top = cotangent[0].astype(f32)
    gain_two_term = jnp.sum(gs2 * normed_two, axis=0, keepdims=True)
    grad_residual = grad_top + norm_back(gs2 * gain_two, normed_two, inverse_two)
    grad_cat, out_part, g_out, ggu = attention_back(
        grad_residual.astype(bf16),
        matmul(product, w_dn).astype(bf16).reshape(8, tokens, width),
        dot_t(scaled_two, grad_gu).astype(bf16).reshape(2, 4, 4, rows, 2 * ff),
        w_out,
        gated,
        head_normed,
        head_inverse,
        swish_pre,
        q,
        k,
        v,
        weights,
        mask,
        state_in,
        reach,
        tail,
        cum,
    )
    layer_out = residual + out_part
    gs1, gcat, g_out, ggu, gain_terms = last_exchange(
        dot_nt(grad_cat, w_attn).astype(bf16).reshape(8, tokens, width),
        dot_t(scaled_one, grad_cat).astype(bf16).reshape(2, 4, 4, rows, attn_cols),
        g_out,
        ggu.reshape(8, rows, 2 * ff),
        hidden_in[0],
        gain_two_term,
    )
    normed_one, inverse_one = normalize(inputs)
    grad_input = grad_residual + norm_back(gs1 * gain_one, normed_one, inverse_one)

    grad_query, grad_key, grad_value, grad_swish, grad_output, grad_gate, grad_up = unpack(
        gcat, g_out, ggu
    )
    me = dp * 16 + ctx * 4 + lax.axis_index(ULY)
    gain_terms = lax.dynamic_slice_in_dim(gain_terms, me * rows, rows, axis=1)
    return (
        layer_out[None],
        grad_input[None],
        grad_query,
        grad_key,
        grad_value,
        grad_swish,
        grad_output,
        grad_gate,
        grad_up,
        grad_down,
        gain_terms[0],
        gain_terms[1],
    )


def solution(mesh):
    shape = mesh.shape
    planned = (shape[DP], shape[CTX], shape[ULY]) == (2, 4, 4)
    tokens = P(DP, (CTX, ULY), None)
    weight = P(EVERYWHERE, None)
    gain = P(EVERYWHERE)
    return jax.shard_map(
        local if planned else local_any,
        mesh=mesh,
        in_specs=(tokens, tokens, P(DP, ULY, CTX), *[weight] * 8, gain, gain),
        out_specs=(tokens, tokens, *[weight] * 8, gain, gain),
        check_vma=False,
    )
```

```python
import functools
import math

import jax
import jax.numpy as jnp
from jax import lax
from jax.experimental import pallas as pl
from jax.experimental.pallas import tpu as pltpu
from jax.sharding import PartitionSpec as P

RETENTION_HEADS = 8
KEY_DIM = 256
VALUE_DIM = 432


EPSILON = 1e-06
DP, CTX, ULY = "dp", "ctx", "ulysses"
EVERYWHERE = (DP, CTX, ULY)


def entering(value, axis, join, neutral, backward):
    count, mine = (lax.axis_size(axis), lax.axis_index(axis))
    pieces = jax.tree.map(lambda part: lax.all_gather(part, axis), value)
    if backward:
        pieces = jax.tree.map(lambda part: part[::-1], pieces)
        mine = count - 1 - mine
    subtotal = jax.tree.map(
        lambda part, zero: jnp.full_like(part, 0) + jnp.asarray(zero, part.dtype), value, neutral
    )

    def step(position, subtotal):
        longer = join(subtotal, jax.tree.map(lambda part: part[position], pieces))
        return jax.tree.map(lambda new, old: jnp.where(position < mine, new, old), longer, subtotal)

    return lax.fori_loop(0, count - 1, step, subtotal)


def normalize(values):
    inverse = lax.rsqrt(jnp.mean(values * values, axis=-1, keepdims=True) + EPSILON)
    return (values * inverse, inverse)


def norm_back(grad_normed, normed, inverse):
    return inverse * (grad_normed - normed * jnp.mean(grad_normed * normed, axis=-1, keepdims=True))


def swish_slope(values):
    sigma = jax.nn.sigmoid(values)
    return sigma * (1.0 + values * (1.0 - sigma))


def carry_forward(earlier, later):
    return (earlier[0] * later[0], later[0][:, None, None] * earlier[1] + later[1])


def carry_backward(earlier, later):
    return (earlier[0] * later[0], later[1] + later[0][:, None, None] * earlier[1])


def running_sum(values):
    size = values.shape[-1]
    upper = lax.broadcasted_iota(jnp.int32, (size, size), 0) <= lax.broadcasted_iota(
        jnp.int32, (size, size), 1
    )
    return jnp.dot(values, upper.astype(jnp.float32), precision=lax.Precision.HIGHEST)


def matmul(left, right):
    return jnp.dot(left, right, preferred_element_type=jnp.float32)


def local_any(
    hidden_in,
    cotangent,
    log_decay,
    w_query,
    w_key,
    w_value,
    w_swish,
    w_output,
    w_gate,
    w_up,
    w_down,
    gain_attn,
    gain_ffn,
):
    highest = lax.Precision.HIGHEST
    query_full, key_full, value_full, swish_full, output_full, gain_one = (
        lax.all_gather(w_query, EVERYWHERE, axis=0, tiled=True),
        lax.all_gather(w_key, EVERYWHERE, axis=0, tiled=True),
        lax.all_gather(w_value, EVERYWHERE, axis=0, tiled=True),
        lax.all_gather(w_swish, EVERYWHERE, axis=0, tiled=True),
        lax.all_gather(w_output, EVERYWHERE, axis=0, tiled=True),
        lax.all_gather(gain_attn, EVERYWHERE, axis=0, tiled=True),
    )
    inputs = hidden_in[0].astype(jnp.float32)
    tokens = inputs.shape[0]
    normed_one, inverse_one = normalize(inputs)
    scaled_one = (normed_one * gain_one.astype(jnp.float32)).astype(jnp.bfloat16)
    queries = (
        matmul(scaled_one, query_full)
        .astype(jnp.bfloat16)
        .reshape(tokens, RETENTION_HEADS, KEY_DIM)
    )
    keys_tok = (
        matmul(scaled_one, key_full).astype(jnp.bfloat16).reshape(tokens, RETENTION_HEADS, KEY_DIM)
    )
    values_tok = (
        matmul(scaled_one, value_full)
        .astype(jnp.bfloat16)
        .reshape(tokens, RETENTION_HEADS, VALUE_DIM)
    )
    swish_pre = matmul(scaled_one, swish_full)
    head_q, head_k, head_v = (
        lax.all_to_all(queries, ULY, split_axis=1, concat_axis=0, tiled=True),
        lax.all_to_all(keys_tok, ULY, split_axis=1, concat_axis=0, tiled=True),
        lax.all_to_all(values_tok, ULY, split_axis=1, concat_axis=0, tiled=True),
    )
    block = head_q.shape[0]
    scale = 1.0 / math.sqrt(KEY_DIM)
    cumulative = running_sum(log_decay[0])
    later = lax.broadcasted_iota(jnp.int32, (block, block), 0) >= lax.broadcasted_iota(
        jnp.int32, (block, block), 1
    )
    gap = cumulative[:, :, None] - cumulative[:, None, :]
    mask = jnp.where(later[None], jnp.exp(jnp.minimum(gap, 0.0)), 0.0) * scale
    scores = jnp.einsum("thd,shd->hts", head_q, head_k, preferred_element_type=jnp.float32)
    weights = (scores * mask).astype(jnp.bfloat16)
    intra = jnp.einsum("hts,she->the", weights, head_v, preferred_element_type=jnp.float32)
    query_f = head_q.astype(jnp.float32)
    key_f = head_k.astype(jnp.float32)
    value_f = head_v.astype(jnp.float32)
    tail = jnp.exp(cumulative[:, -1:] - cumulative).T[:, :, None]
    reach = jnp.exp(cumulative).T[:, :, None]
    update = jnp.einsum("shd,she->hde", key_f * tail, value_f, precision=highest)
    block_decay = jnp.exp(cumulative[:, -1])
    identity = (jnp.ones_like(block_decay), jnp.zeros_like(update))
    _, state_in = entering((block_decay, update), CTX, carry_forward, identity, False)
    retained = intra + scale * reach * jnp.einsum(
        "thd,hde->the", query_f, state_in, precision=highest
    )
    head_normed, head_inverse = normalize(retained)
    head_out = head_normed.astype(jnp.bfloat16)
    token_out = lax.all_to_all(
        head_out, ULY, split_axis=0, concat_axis=1, tiled=True
    ).reshape(tokens, RETENTION_HEADS * VALUE_DIM)
    token_out_f = token_out.astype(jnp.float32)
    swish_act = jax.nn.silu(swish_pre)
    gated = (swish_act * token_out_f).astype(jnp.bfloat16)
    residual = inputs + matmul(gated, output_full)
    gate_full, up_full, down_full, gain_two = (
        lax.all_gather(w_gate, EVERYWHERE, axis=0, tiled=True),
        lax.all_gather(w_up, EVERYWHERE, axis=0, tiled=True),
        lax.all_gather(w_down, EVERYWHERE, axis=0, tiled=True),
        lax.all_gather(gain_ffn, EVERYWHERE, axis=0, tiled=True),
    )
    normed_two, inverse_two = normalize(residual)
    scaled_two = (normed_two * gain_two.astype(jnp.float32)).astype(jnp.bfloat16)
    gate_pre = matmul(scaled_two, gate_full)
    up_pre = matmul(scaled_two, up_full)
    product = (jax.nn.silu(gate_pre) * up_pre).astype(jnp.bfloat16)
    layer_out = residual + matmul(product, down_full)
    grad_top = cotangent[0].astype(jnp.float32)
    grad_top_low = grad_top.astype(jnp.bfloat16)
    grad_product = matmul(grad_top_low, down_full.T)
    grad_down_term = matmul(product.T, grad_top_low)
    grad_gate_pre = (grad_product * up_pre * swish_slope(gate_pre)).astype(jnp.bfloat16)
    grad_up_pre = (grad_product * jax.nn.silu(gate_pre)).astype(jnp.bfloat16)
    grad_gate_term = matmul(scaled_two.T, grad_gate_pre)
    grad_up_term = matmul(scaled_two.T, grad_up_pre)
    grad_scaled_two = matmul(grad_gate_pre, gate_full.T) + matmul(grad_up_pre, up_full.T)
    grad_gain_two = jnp.sum(grad_scaled_two * normed_two, axis=0)
    grad_residual = grad_top + norm_back(
        grad_scaled_two * gain_two.astype(jnp.float32), normed_two, inverse_two
    )
    grad_gate, grad_up, grad_down, grad_gain_ffn = (
        lax.psum_scatter(grad_gate_term, EVERYWHERE, scatter_dimension=0, tiled=True),
        lax.psum_scatter(grad_up_term, EVERYWHERE, scatter_dimension=0, tiled=True),
        lax.psum_scatter(grad_down_term, EVERYWHERE, scatter_dimension=0, tiled=True),
        lax.psum_scatter(grad_gain_two, EVERYWHERE, scatter_dimension=0, tiled=True),
    )
    grad_y = grad_residual.astype(jnp.bfloat16)
    grad_output_term = matmul(gated.T, grad_y)
    grad_gated = matmul(grad_y, output_full.T)
    grad_swish_pre = (grad_gated * token_out_f * swish_slope(swish_pre)).astype(jnp.bfloat16)
    grad_token_out = (
        (grad_gated * swish_act).astype(jnp.bfloat16).reshape(tokens, RETENTION_HEADS, VALUE_DIM)
    )
    grad_swish_term = matmul(scaled_one.T, grad_swish_pre)
    grad_head_out = lax.all_to_all(
        grad_token_out, ULY, split_axis=1, concat_axis=0, tiled=True
    ).astype(jnp.float32)
    grad_retained = norm_back(grad_head_out, head_normed, head_inverse).astype(jnp.bfloat16)
    grad_retained_f = grad_retained.astype(jnp.float32)
    grad_weights = jnp.einsum(
        "the,she->hts", grad_retained, head_v, preferred_element_type=jnp.float32
    )
    grad_scores = (grad_weights * mask).astype(jnp.bfloat16)
    grad_state_in = scale * jnp.einsum(
        "thd,the->hde", query_f * reach, grad_retained_f, precision=highest
    )
    _, grad_update = entering((block_decay, grad_state_in), CTX, carry_backward, identity, True)
    grad_head_q = jnp.einsum(
        "hts,shd->thd", grad_scores, head_k, preferred_element_type=jnp.float32
    ) + scale * reach * jnp.einsum("the,hde->thd", grad_retained_f, state_in, precision=highest)
    grad_head_k = jnp.einsum(
        "hts,thd->shd", grad_scores, head_q, preferred_element_type=jnp.float32
    ) + tail * jnp.einsum("she,hde->shd", value_f, grad_update, precision=highest)
    grad_head_v = jnp.einsum(
        "hts,the->she", weights, grad_retained, preferred_element_type=jnp.float32
    ) + tail * jnp.einsum("shd,hde->she", key_f, grad_update, precision=highest)
    grad_queries, grad_keys, grad_values = (
        lax.all_to_all(
            grad_head_q.astype(jnp.bfloat16), ULY, split_axis=0, concat_axis=1, tiled=True
        ),
        lax.all_to_all(
            grad_head_k.astype(jnp.bfloat16), ULY, split_axis=0, concat_axis=1, tiled=True
        ),
        lax.all_to_all(
            grad_head_v.astype(jnp.bfloat16), ULY, split_axis=0, concat_axis=1, tiled=True
        ),
    )
    grad_queries = grad_queries.reshape(tokens, RETENTION_HEADS * KEY_DIM)
    grad_keys = grad_keys.reshape(tokens, RETENTION_HEADS * KEY_DIM)
    grad_values = grad_values.reshape(tokens, RETENTION_HEADS * VALUE_DIM)
    grad_query_term = matmul(scaled_one.T, grad_queries)
    grad_key_term = matmul(scaled_one.T, grad_keys)
    grad_value_term = matmul(scaled_one.T, grad_values)
    grad_scaled_one = (
        matmul(grad_queries, query_full.T)
        + matmul(grad_keys, key_full.T)
        + matmul(grad_values, value_full.T)
        + matmul(grad_swish_pre, swish_full.T)
    )
    grad_gain_one = jnp.sum(grad_scaled_one * normed_one, axis=0)
    grad_input = grad_residual + norm_back(
        grad_scaled_one * gain_one.astype(jnp.float32), normed_one, inverse_one
    )
    grad_query, grad_key, grad_value, grad_swish, grad_output, grad_gain_attn = (
        lax.psum_scatter(
            grad_query_term, EVERYWHERE, scatter_dimension=0, tiled=True
        ),
        lax.psum_scatter(grad_key_term, EVERYWHERE, scatter_dimension=0, tiled=True),
        lax.psum_scatter(
            grad_value_term, EVERYWHERE, scatter_dimension=0, tiled=True
        ),
        lax.psum_scatter(
            grad_swish_term, EVERYWHERE, scatter_dimension=0, tiled=True
        ),
        lax.psum_scatter(
            grad_output_term, EVERYWHERE, scatter_dimension=0, tiled=True
        ),
        lax.psum_scatter(grad_gain_one, EVERYWHERE, scatter_dimension=0, tiled=True),
    )
    return (
        layer_out[None],
        grad_input[None],
        grad_query,
        grad_key,
        grad_value,
        grad_swish,
        grad_output,
        grad_gate,
        grad_up,
        grad_down,
        grad_gain_attn,
        grad_gain_ffn,
    )


MESH = pl.DeviceIdType.MESH
BF16, F32 = jnp.bfloat16, jnp.float32
HBM, VMEM = pltpu.HBM, pltpu.VMEM
N_SEMS = 160


def dot_t(left, right):
    return lax.dot_general(left, right, (((0,), (0,)), ((), ())), preferred_element_type=F32)


def dot_nt(left, right):
    return lax.dot_general(left, right, (((1,), (1,)), ((), ())), preferred_element_type=F32)


def pair_dot(left_axis, right_axis, left, right):
    dims = (((left_axis,), (right_axis,)), ((0,), (0,)))
    return lax.dot_general(left, right, dims, preferred_element_type=F32)


class Place:
    def __init__(self, uly):
        self.dp, self.ctx, self.uly = lax.axis_index(DP), lax.axis_index(CTX), uly
        odd = lax.rem(self.ctx, 2)
        self.xn = self.ctx + 1 - 2 * odd
        self.yn = lax.rem(self.ctx + 2, 4)
        self.dg = self.yn + 1 - 2 * odd
        self.other = 1 - self.dp

    def at(self, dp=None, ctx=None, uly=None):
        return (
            self.dp if dp is None else dp,
            self.ctx if ctx is None else ctx,
            self.uly if uly is None else uly,
        )


class Mover:
    def __init__(self, place, names, send, recv, like=None, like_whole=None):
        self.like, self.like_whole = like, like_whole
        self.place, self.names, self.send_sems, self.recv_sems = place, names, send, recv
        self.sent, self.whole = [], []

    def number(self, name):
        return self.names.setdefault(name, len(self.names))

    def remote(self, name, src, dst, device):
        k = self.number(name)
        return pltpu.make_async_remote_copy(
            src_ref=src,
            dst_ref=dst,
            send_sem=self.send_sems.at[k],
            recv_sem=self.recv_sems.at[k],
            device_id=device,
            device_id_type=MESH,
        )

    def send(self, name, src, dst, device):
        copy = self.remote(name, src, dst, device)
        copy.start()
        self.sent.append(copy if self.like is None else name)

    def send_whole(self, name, src, dst, device):
        copy = self.remote(name, src, dst, device)
        copy.start()
        self.whole.append((copy if self.like is None else None, name, None))

    def arrive(self, name, dst):
        self.remote(name, dst, dst, self.place.at(dp=self.place.other)).wait_recv()

    def local(self, name, src, dst):
        copy = pltpu.make_async_copy(src, dst, self.send_sems.at[self.number(name)])
        copy.start()
        return copy

    def finish(self):
        for copy, name, _ in self.whole:
            if self.like is not None:
                ref = self.like_whole()
                copy = self.remote(name, ref, ref, self.place.at(dp=self.place.other))
            copy.wait_send()
        for copy in self.sent:
            if self.like is not None:
                ref = self.like()
                copy = self.remote(copy, ref, ref, self.place.at(dp=self.place.other))
            copy.wait_send()


def greet(devices):
    barrier = pltpu.get_barrier_semaphore()
    for device in devices:
        pl.semaphore_signal(barrier, inc=1, device_id=device, device_id_type=MESH)
    pl.semaphore_wait(barrier, len(devices))


def together(streams):
    streams = list(streams)
    while streams:
        left = []
        for stream in streams:
            if next(stream, 0) is None:
                left.append(stream)
        streams = left


def later(stream, stages):
    for _ in range(stages):
        yield
    yield from stream


def add_up(dst, sources, step=32):
    if len(dst.shape) > 2:
        for i in range(dst.shape[0]):
            add_up(dst.at[i], [source.at[i] for source in sources], step)
        return
    rows, columns = dst.shape
    by_rows = rows % step == 0
    step = step if by_rows else 256

    def body(i, carry):
        part = pl.ds(pl.multiple_of(i * step, step), step)
        at = (part, slice(None)) if by_rows else (slice(None), part)
        total = sources[0][at].astype(F32)
        for source in sources[1:]:
            total = total + source[at].astype(F32)
        dst[at] = total.astype(dst.dtype)
        return carry

    lax.fori_loop(0, (rows if by_rows else columns) // step, body, 0)


def line_gather(m, tag, own, out, pause=1):
    p = m.place
    u = p.uly
    copy = m.local(tag + "=", own, out.at[p.dp * 4 + u])
    if u < 3:
        m.send((tag, "r", u), own, out.at[p.dp * 4 + u], p.at(uly=u + 1))
    if u > 0:
        m.send((tag, "l", u), own, out.at[p.dp * 4 + u], p.at(uly=u - 1))
    m.send((tag, "c", u), own, out.at[p.dp * 4 + u], p.at(dp=p.other))
    for _ in range(pause):
        yield
    for d in range(1, 4):
        for way, b, onward in (("r", u - d, u + 1), ("l", u + d, u - 1)):
            if 0 <= b <= 3:
                block = out.at[p.dp * 4 + b]
                m.arrive((tag, way, b), block)
                if 0 <= onward <= 3:
                    m.send((tag, way, b), block, block, p.at(uly=onward))
                m.send((tag, "c", b), block, block, p.at(dp=p.other))
        yield
    for b in range(4):
        m.arrive((tag, "c", b), out.at[p.other * 4 + b])
    copy.wait()


def plane_gather(m, tag, own, out, slot, halves, pair=True):
    p = m.place

    def half(c, i):
        return slot(out, p.dp, c, halves[i])

    mine = slot(out, p.dp, p.ctx, None)
    copy = m.local(tag + "=", own, mine)
    m.send((tag, "x"), own, mine, p.at(ctx=p.xn))
    m.send((tag, "y"), own, mine, p.at(ctx=p.yn))
    if pair:
        m.send((tag, "c", 0), own, mine, p.at(dp=p.other))
    yield
    block = slot(out, p.dp, p.xn, None)
    m.arrive((tag, "x"), block)
    m.send((tag, "z", 0), half(p.xn, 0), half(p.xn, 0), p.at(ctx=p.yn))
    if pair:
        m.send((tag, "c", 1), block, block, p.at(dp=p.other))
    block = slot(out, p.dp, p.yn, None)
    m.arrive((tag, "y"), block)
    m.send((tag, "z", 1), half(p.yn, 1), half(p.yn, 1), p.at(ctx=p.xn))
    if pair:
        m.send((tag, "c", 2), block, block, p.at(dp=p.other))
    yield
    for i in range(2):
        block = half(p.dg, i)
        m.arrive((tag, "z", i), block)
        if pair:
            m.send((tag, "c", 3 + i), block, block, p.at(dp=p.other))
    yield
    if pair:
        for i, c in enumerate((p.ctx, p.xn, p.yn)):
            m.arrive((tag, "c", i), slot(out, p.other, c, None))
        for i in range(2):
            m.arrive((tag, "c", 3 + i), slot(out, p.other, p.dg, halves[i]))
    copy.wait()


def halves_of_rows(view, i):
    rows = view.shape[0] // 2
    return view.at[pl.ds(i * rows, rows)]


def halves_of_columns(view, i):
    columns = view.shape[1] // 2
    return view.at[:, pl.ds(i * columns, columns)]


def line_reduce(m, tag, part, out, sib, right, left, cut=halves_of_rows):
    p = m.place
    u = p.uly
    order = (3, 0, 2, 1) if u < 2 else (0, 3, 1, 2)
    for b in order if sib is not None else ():
        m.send_whole((tag, "c", b), part(p.other * 4 + b), sib.at[b], p.at(dp=p.other))
    met = set()

    def meet(b, i):
        if sib is None:
            return [cut(part(b), i)]
        if b not in met:
            met.add(b)
            m.arrive((tag, "c", b), sib.at[b])
        return [cut(part(p.dp * 4 + b), i), cut(sib.at[b], i)]

    def onward(way, b, i, arrived, there):
        terms = meet(b, i)
        if arrived is not None:
            arrived = cut(arrived.at[b], i)
            m.arrive((tag, way, b, i), arrived)
            terms.append(arrived)
        if len(terms) > 1:
            add_up(terms[-1], terms)
        away = cut((right if way == "r" else left).at[b], i)
        m.send((tag, way, b, i), terms[-1], away, p.at(uly=there))

    for slot in range(3):
        for b in range(4):
            for i in range(2):
                if u < b and u + 3 - b == slot:
                    onward("r", b, i, right if u > 0 else None, u + 1)
        for b in range(4):
            for i in range(2):
                if u > b and 3 - u + b == slot:
                    onward("l", b, i, left if u < 3 else None, u - 1)
        yield
    for i in range(2):
        terms = meet(u, i)
        if u > 0:
            m.arrive((tag, "r", u, i), cut(right.at[u], i))
            terms.append(cut(right.at[u], i))
        if u < 3:
            m.arrive((tag, "l", u, i), cut(left.at[u], i))
            terms.append(cut(left.at[u], i))
        add_up(cut(out, i), terms)


def plane_reduce(m, tag, part, out, sib, sums, got, got2):
    p = m.place
    rows = out.shape[0]
    halves = (pl.ds(0, rows // 2), pl.ds(rows // 2, rows // 2))
    order = (p.dg, p.xn, p.yn, p.ctx)
    for i, c in enumerate(order):
        m.send((tag, "c", i), part.at[p.other * 4 + c], sib.at[c], p.at(dp=p.other))
    yield
    for i, c in enumerate(order):
        m.arrive((tag, "c", i), sib.at[c])
        add_up(sums.at[c], [part.at[p.dp * 4 + c], sib.at[c]])
        if i == 0:
            m.send((tag, "x", 1), sums.at[c, halves[0]], got.at[1, halves[0]], p.at(ctx=p.xn))
            m.send((tag, "y", 1), sums.at[c, halves[1]], got.at[1, halves[1]], p.at(ctx=p.yn))
        if i == 1:
            m.send((tag, "x", 0), sums.at[c, halves[0]], got.at[0, halves[0]], p.at(ctx=p.xn))
        if i == 2:
            m.send((tag, "y", 0), sums.at[c, halves[1]], got.at[0, halves[1]], p.at(ctx=p.yn))
    yield
    m.arrive((tag, "x", 1), got.at[1, halves[0]])
    add_up(got.at[1, halves[0]], [sums.at[p.yn, halves[0]], got.at[1, halves[0]]])
    m.send((tag, "y2"), got.at[1, halves[0]], got2.at[halves[0]], p.at(ctx=p.yn))
    m.arrive((tag, "y", 1), got.at[1, halves[1]])
    add_up(got.at[1, halves[1]], [sums.at[p.xn, halves[1]], got.at[1, halves[1]]])
    m.send((tag, "x2"), got.at[1, halves[1]], got2.at[halves[1]], p.at(ctx=p.xn))
    yield
    m.arrive((tag, "x", 0), got.at[0, halves[0]])
    m.arrive((tag, "y", 0), got.at[0, halves[1]])
    yield
    m.arrive((tag, "y2"), got2.at[halves[0]])
    m.arrive((tag, "x2"), got2.at[halves[1]])
    add_up(out, [sums.at[p.ctx], got.at[0], got2])


def run_kernel(name, number, branches, partners, streams, outs, ins, scratch=(), vmem=48, time=40):
    def kernel(*refs):
        send, recv = refs[-2:]
        refs = refs[:-2]
        uly = lax.axis_index(ULY)
        names = {}
        greet(partners(Place(uly)) if partners else [])

        def body(u):
            m = Mover(Place(u), names, send, recv)
            together(streams(m, *refs))
            m.finish()

        if branches == 1:
            body(uly)
        else:
            for u in range(4):
                pl.when(uly == u)(functools.partial(body, u))
        assert len(names) <= N_SEMS

    return pl.pallas_call(
        kernel,
        out_shape=[jax.ShapeDtypeStruct(*o[:2]) for o in outs],
        in_specs=[pl.BlockSpec(memory_space=s) for _, s in ins],
        out_specs=[pl.BlockSpec(memory_space=o[2]) for o in outs],
        scratch_shapes=[
            *[pltpu.VMEM(shape, dtype) for shape, dtype in scratch],
            pltpu.SemaphoreType.DMA((N_SEMS,)),
            pltpu.SemaphoreType.DMA((N_SEMS,)),
        ],
        name=name,
        cost_estimate=pl.CostEstimate(
            flops=0, bytes_accessed=time * 3_700_000, transcendentals=0
        ),
        compiler_params=pltpu.CompilerParams(
            collective_id=number, has_side_effects=True, vmem_limit_bytes=vmem << 20
        ),
    )(*[a for a, _ in ins])


def everyone(p):
    me = p.dp * 16 + p.ctx * 4 + p.uly
    found = []
    for k in range(1, 32):
        there = lax.rem(me + k, 32)
        found.append((lax.div(there, 16), lax.rem(lax.div(there, 4), 4), lax.rem(there, 4)))
    return found


def line_partners(p):
    found = [p.at(dp=p.other)]
    for d in range(1, 4):
        there = lax.rem(p.uly + d, 4)
        found += [p.at(uly=there), p.at(dp=p.other, uly=there)]
    return found


def plane_partners(p):
    return [p.at(dp=p.other), p.at(ctx=p.xn), p.at(ctx=p.yn)]


def token_slot(out, dp, c, part):
    view = out.at[dp * 4 + c]
    return view if part is None else view.at[part]


def state_slot(out, dp, c, part):
    view = out.at[c]
    return view if part is None else view.at[part]


def pack(w_query, w_key, w_value, w_swish, w_output, w_gate, w_up, gains):
    rows, (out_rows, width) = w_query.shape[0], w_output.shape
    key, val, ff, quarter = KEY_DIM, VALUE_DIM, w_gate.shape[1] // 8, width // 4
    cols = 2 * key + 2 * val + 32

    def kernel(q, k, v, s, o, g, u, n, packed, outw, gu):
        for d in range(2):
            for z in range(4):
                h, i = 2 * z + d, 4 * d + z
                at = 0
                for ref, w in ((q, key), (k, key), (v, val), (s, val)):
                    packed[i, :, at : at + w] = ref[:, h * w : (h + 1) * w]
                    at += w
                packed[i, :, at : at + 32] = n[...]
        for i in range(8):
            gu[i, :, :ff] = g[:, i * ff : (i + 1) * ff]
            gu[i, :, ff:] = u[:, i * ff : (i + 1) * ff]
        for j in range(4):
            outw[j] = o[:, j * quarter : (j + 1) * quarter]

    return pl.pallas_call(
        kernel,
        out_shape=[
            jax.ShapeDtypeStruct((8, rows, cols), BF16),
            jax.ShapeDtypeStruct((4, out_rows, quarter), BF16),
            jax.ShapeDtypeStruct((8, rows, 2 * ff), BF16),
        ],
        name="pack",
        compiler_params=pltpu.CompilerParams(vmem_limit_bytes=32 << 20),
    )(w_query, w_key, w_value, w_swish, w_output, w_gate, w_up, gains)


def unpack(heads, outg, slices):
    rows, (_, out_rows, quarter) = heads.shape[1], outg.shape
    key, val, ff = KEY_DIM, VALUE_DIM, slices.shape[2] // 2

    def kernel(hs, og, sl, q, k, v, s, o, g, u):
        for d in range(2):
            for z in range(4):
                h, i = 2 * z + d, 4 * d + z
                at = 0
                for ref, w in ((q, key), (k, key), (v, val), (s, val)):
                    ref[:, h * w : (h + 1) * w] = hs[i, :, at : at + w].astype(F32)
                    at += w
        for i in range(8):
            g[:, i * ff : (i + 1) * ff] = sl[i, :, :ff].astype(F32)
            u[:, i * ff : (i + 1) * ff] = sl[i, :, ff:].astype(F32)
        for j in range(4):
            o[:, j * quarter : (j + 1) * quarter] = og[j].astype(F32)

    wide = jax.ShapeDtypeStruct((rows, 8 * key), F32)
    wider = jax.ShapeDtypeStruct((rows, 8 * val), F32)
    ffs = jax.ShapeDtypeStruct((rows, 8 * ff), F32)
    return pl.pallas_call(
        kernel,
        out_shape=[
            wide, wide, wider, wider,
            jax.ShapeDtypeStruct((out_rows, 4 * quarter), F32),
            ffs, ffs,
        ],
        name="unpack",
        compiler_params=pltpu.CompilerParams(vmem_limit_bytes=32 << 20),
    )(heads, outg, slices)


def line_spread(m, tag, own, slot):
    u = m.place.uly
    copy = m.local((tag, 8), own, slot(u))
    if u < 3:
        m.send((tag, "r", u), own, slot(u), m.place.at(uly=u + 1))
    if u > 0:
        m.send((tag, "l", u), own, slot(u), m.place.at(uly=u - 1))
    copy.wait()
    yield
    for d in range(1, 4):
        for way, b, onward in (("r", u - d, u + 1), ("l", u + d, u - 1)):
            if 0 <= b <= 3:
                m.arrive((tag, way, b), slot(b))
                if 0 <= onward <= 3:
                    m.send((tag, way, b), slot(b), slot(b), m.place.at(uly=onward))
        yield


def block_factors(cum, ctx, s, backward):
    count = cum.shape[1]
    lasts = [cum[4 * s + j : 4 * s + j + 1, count - 1 : count] for j in range(4)]
    found = []
    for j in range(4):
        total = jnp.zeros((1, 1), F32)
        for i in range(4):
            inside = ((i > ctx) & (i < j)) if backward else ((i > j) & (i < ctx))
            total = total + jnp.where(inside, lasts[i], 0.0)
        right = (j > ctx) if backward else (j < ctx)
        found.append(jnp.where(right, jnp.exp(total), 0.0))
    return found


def forward(hidden, cot, decay, packed, outw, gu, w_down):
    tokens, width = hidden.shape
    rows, cols = packed.shape[1:]
    out_rows, quarter = outw.shape[1:]
    ff2 = gu.shape[2]
    key, val = KEY_DIM, VALUE_DIM
    block, both = 4 * tokens, 8 * tokens
    half = block // 2
    scale = 1.0 / math.sqrt(key)
    at_s = 2 * key + val

    def start_streams(m, hid_ref, dec_ref, pk_ref, gu_ref, hall, dall, wall, gall):
        p = m.place
        u = p.uly

        def row(q, c, us):
            dp = p.dp if q == 0 else p.other
            at = (dp * 16 + c * 4 + us) * rows
            return wall.at[pl.ds(pl.multiple_of(at, rows), rows)]

        def attn():
            sources = sorted(
                ((q, us) for q in range(2) for us in range(4)), key=lambda s: (abs(s[1] - u), s[0])
            )
            copy = None
            for q, to in sources:
                dp = p.dp if q == 0 else p.other
                mine = row(0, p.ctx, u)
                src = pk_ref.at[dp * 4 + to]
                if (q, to) == (0, u):
                    copy = m.local("T", src, mine)
                else:
                    m.send(("t", q, u), src, mine, p.at(dp=dp, uly=to))
            yield
            relays = []
            for n, (q, us) in enumerate(sources):
                tile = row(q, p.ctx, us)
                if (q, us) == (0, u):
                    copy.wait()
                else:
                    m.arrive(("t", q, us), tile)
                m.send(("X", q, us), tile, tile, p.at(ctx=p.xn))
                m.send(("Y", q, us), tile, tile, p.at(ctx=p.yn))
                relays.append((q, us))
                if n >= 2:
                    yield
                    relay(*relays.pop(0))
            while relays:
                yield
                relay(*relays.pop(0))
            yield
            for q, us in sources:
                even = (q + us) % 2 == 0
                m.arrive(("Y" if even else "X", q, us), row(q, p.yn if even else p.xn, us))
                m.arrive(("Z", q, us), row(q, p.dg, us))

        def relay(q, us):
            if (q + us) % 2 == 0:
                tile = row(q, p.xn, us)
                m.arrive(("X", q, us), tile)
                m.send(("Z", q, us), tile, tile, p.at(ctx=p.yn))
            else:
                tile = row(q, p.yn, us)
                m.arrive(("Y", q, us), tile)
                m.send(("Z", q, us), tile, tile, p.at(ctx=p.xn))

        def feed():
            mine = gall.at[p.dp * 4 + p.ctx]
            copy = m.local("F", gu_ref.at[p.dp * 4 + p.ctx], mine)
            decays = m.local("D", dec_ref, dall.at[p.dp * 4 + p.ctx])
            spots = [(q, c, i) for i, c in enumerate((p.ctx, p.xn, p.yn, p.dg)) for q in range(2)][1:]
            for q, c, i in spots:
                dp = p.dp if q == 0 else p.other
                m.send(("d", q, i), dec_ref, dall.at[p.dp * 4 + p.ctx], p.at(dp=dp, ctx=c))
                m.send(("f", q, i), gu_ref.at[dp * 4 + c], mine, p.at(dp=dp, ctx=c))
            for _ in range(5):
                yield
            for q, c, i in spots:
                dp = p.dp if q == 0 else p.other
                m.arrive(("d", q, i), dall.at[dp * 4 + c])
                m.arrive(("f", q, i), gall.at[dp * 4 + c])
            copy.wait()
            decays.wait()

        return [
            attn(),
            later(line_gather(m, "h", hid_ref, hall, 6), 1),
            later(feed(), 6),
        ]

    def quarter_of(oall, part, c):
        return oall.at[part, :, pl.ds(pl.multiple_of(c * quarter, quarter), quarter)]

    def out_rows_go(m, ow_ref, oall):
        p = m.place
        u = p.uly
        head_dp, head_u = lax.rem(p.ctx, 2), p.dp * 2 + lax.div(p.ctx, 2)
        found = []
        for j in range(4):
            there = oall.at[u, :, pl.ds(j * quarter, quarter)]
            away = pltpu.make_async_remote_copy(
                src_ref=ow_ref.at[j],
                dst_ref=there,
                send_sem=m.send_sems.at[m.number(("S", j))],
                recv_sem=m.recv_sems.at[m.number(("o", u))],
                device_id=(head_dp, j, head_u),
                device_id_type=MESH,
            )
            here = (ow_ref.at[j], there, m.send_sems.at[m.number("O")])
            own = (head_dp == p.dp) & (p.ctx == j) & (head_u == u)
            found.append((own, away, here))
        return found

    def out_start(m, ow_ref, oall):
        for own, away, here in out_rows_go(m, ow_ref, oall):

            @pl.when(own)
            def _(here=here):
                copy = pltpu.make_async_copy(*here)
                copy.start()
                copy.wait()

            pl.when(jnp.logical_not(own))(away.start)

    def out_share(m, ow_ref, oall):
        p = m.place
        u = p.uly
        for us in range(4):
            mine = (u // 2 == p.dp) & (2 * (u % 2) + p.dp == p.ctx) & (us == u)

            @pl.when(jnp.logical_not(mine))
            def _(us=us):
                m.arrive(("o", us), quarter_of(oall, us, p.ctx))

        mine = quarter_of(oall, pl.ds(0, 4), p.ctx)
        m.send("ox", mine, mine, p.at(ctx=p.xn))
        m.send("oy", mine, mine, p.at(ctx=p.yn))
        for own, away, _ in out_rows_go(m, ow_ref, oall):
            pl.when(jnp.logical_not(own))(away.wait_send)

    def out_relay(m, oall):
        p = m.place
        low, high = pl.ds(0, 2), pl.ds(2, 2)
        m.arrive("ox", quarter_of(oall, pl.ds(0, 4), p.xn))
        m.send("o0", quarter_of(oall, low, p.xn), quarter_of(oall, low, p.xn), p.at(ctx=p.yn))
        m.arrive("oy", quarter_of(oall, pl.ds(0, 4), p.yn))
        m.send("o1", quarter_of(oall, high, p.yn), quarter_of(oall, high, p.yn), p.at(ctx=p.xn))

    def out_end(m, oall):
        p = m.place
        m.arrive("o0", quarter_of(oall, pl.ds(0, 2), p.dg))
        m.arrive("o1", quarter_of(oall, pl.ds(2, 2), p.dg))

    def kernel(
        hid_ref, cot_ref, dec_ref, pk_ref, ow_ref, gu_ref, wd_ref,
        w_all, s1_all, w2d, q_ref, k_ref, v_ref, sw_ref, w_ref, mask_ref, st_ref, reach_ref, tail_ref, cum_ref,
        gain_ref, hn_ref, hi_ref, ga_ref, res_ref, s2_all, top_all, gu_all, wd_all,
        wall, s1, oall, dall, gall, dec8, cols8, upd, upds, ret, part, sib, right, left, s2, send, recv,
    ):
        uly = lax.axis_index(ULY)
        names = {}
        place = Place(uly)
        greet(everyone(place))
        common = Mover(place, names, send, recv)
        ctx = place.ctx

        def for_each(body):
            for u in range(4):
                pl.when(uly == u)(functools.partial(body, u))

        spread = []
        for u in range(4):
            for tag, own, slot in (
                ("g", gall, lambda b: gu_all.at[:, b]),
                ("e", wd_ref, lambda b: wd_all.at[b]),
            ):
                m = Mover(Place(u), names, send, recv, lambda slot=slot: slot(0))
                spread.append((u, m, line_spread(m, tag, own, slot)))

        def spread_on(u):
            for v, _, stream in spread:
                if u == v:
                    next(stream, 0)

        def first(u):
            m = Mover(Place(u), names, send, recv)
            together(
                start_streams(m, hid_ref, dec_ref, pk_ref, gu_ref, s1, dall, wall, gall)
            )
            m.finish()
            out_start(Mover(Place(u), names, send, recv), ow_ref, oall)
            spread_on(u)

        for_each(first)
        keep = [common.local("w", wall, w_all)]

        table = wall[:, cols - 128 : cols].astype(F32).T
        first_gain = 128 - 32
        gain_ref[...] = table[first_gain : first_gain + 8]

        def norm_one(i, carry):
            b, at = lax.div(i, 4), pl.ds(pl.multiple_of(lax.rem(i, 4) * 32, 32), 32)
            normed, _ = normalize(s1[b, at, :].astype(F32))
            s1[b, at, :] = (normed * gain_ref[0:1, :]).astype(BF16)
            return carry

        lax.fori_loop(0, 32, norm_one, 0)
        keep.append(common.local("W", s1, s1_all))

        for i in range(8):
            dec8[i : i + 1, :] = dall[i, pl.ds(place.dp, 1), :]
        upper = lax.broadcasted_iota(jnp.int32, (block, block), 0) <= lax.broadcasted_iota(
            jnp.int32, (block, block), 1
        )
        cum_ref[...] = jnp.dot(
            dec8[...], upper.astype(F32), precision=lax.Precision.HIGHEST, preferred_element_type=F32
        )
        for s in range(2):
            dec8[s : s + 1, :] = cum_ref[pl.ds(4 * s + ctx, 1), :]
        cols8[...] = dec8[...].T
        for s in range(2):
            column = cols8[:, s : s + 1]
            reach_ref[s] = jnp.exp(column) * scale
            tail_ref[s] = jnp.exp(dec8[s : s + 1, block - 1 : block] - column)

        for s in range(2):
            lhs = s1[4 * s : 4 * s + 4].reshape(block, width)
            q_ref[s] = matmul(lhs, wall[:, :key]).astype(BF16)
            k_ref[s] = matmul(lhs, wall[:, key : 2 * key]).astype(BF16)
            rest = matmul(lhs, wall[:, 2 * key :])
            v_ref[s] = rest[:, :val].astype(BF16)
            sw_ref[pl.ds(s * block, block), :] = rest[:, val : 2 * val]
        for s in range(2):
            k_tail = (k_ref[s].astype(F32) * tail_ref[s]).astype(BF16)
            upd[s] = dot_t(k_tail, v_ref[s]).astype(BF16)
        states = plane_gather(
            common, "t", upd, upds, state_slot, (pl.ds(0, 1), pl.ds(1, 1)), pair=False
        )
        next(states)
        whole = [
            Mover(Place(u), names, send, recv, lambda: quarter_of(oall, pl.ds(0, 4), 0))
            for u in range(4)
        ]
        for_each(lambda u: out_share(whole[u], ow_ref, oall))

        def intra(c, carry):
            s, h = lax.div(c, 2), lax.rem(c, 2)
            at = pl.ds(pl.multiple_of(h * half, half), half)
            here = pl.ds(pl.multiple_of(c * half, half), half)
            gap = cols8[at, :]
            column = jnp.where(s == 0, gap[:, 0:1], gap[:, 1:2])
            gap = column - dec8[pl.ds(s, 1), :]
            t = lax.broadcasted_iota(jnp.int32, (half, block), 0) + h * half
            later_on = t >= lax.broadcasted_iota(jnp.int32, (half, block), 1)
            mask = jnp.where(later_on, jnp.exp(jnp.minimum(gap, 0.0)), 0.0) * scale
            mask_ref[s, at, :] = mask
            weights = (dot_nt(q_ref[s, at, :], k_ref[s]) * mask).astype(BF16)
            w_ref[s, at, :] = weights
            ret[here, :] = matmul(weights, v_ref[s])
            return carry

        lax.fori_loop(0, 2, intra, 0)
        next(states)
        out_relay(common, oall)
        for_each(spread_on)
        lax.fori_loop(2, 4, intra, 0)
        out_end(common, oall)
        for i in range(4):
            w2d[i * out_rows : (i + 1) * out_rows, :] = oall[i]
        for _ in states:
            pass
        for s in range(2):
            factors = block_factors(cum_ref, ctx, s, False)
            total = factors[0] * upds[0, s].astype(F32)
            for j in range(1, 4):
                total = total + factors[j] * upds[j, s].astype(F32)
            st_ref[s] = total.astype(BF16)

        def outer(c, carry):
            s, h = lax.div(c, 2), lax.rem(c, 2)
            at = pl.ds(pl.multiple_of(h * half, half), half)
            here = pl.ds(pl.multiple_of(c * half, half), half)
            retained = ret[here, :] + reach_ref[s, at, :] * matmul(q_ref[s, at, :], st_ref[s])
            normed, inverse = normalize(retained)
            hn_ref[here, :] = normed
            hi_ref[here, :] = inverse
            pre = sw_ref[here, :]
            gated = (pre * jax.nn.sigmoid(pre) * normed.astype(BF16).astype(F32)).astype(BF16)
            ga_ref[here, :] = gated
            for n in range(4):
                cut = pl.ds(n * quarter, quarter)
                value = matmul(gated, w2d[:, cut]).astype(BF16)
                part[pl.ds(2 * c, 2), :, cut] = value.reshape(2, tokens, quarter)
            return carry

        lax.fori_loop(0, 4, outer, 0)

        def reduce(u):
            m = Mover(Place(u), names, send, recv)
            low = tokens // 2
            together(
                [
                    line_reduce(m, "s", lambda i: part.at[i], res_ref, sib, right, left),
                    plane_gather(
                        m, "C", cot_ref, top_all, token_slot, (pl.ds(0, low), pl.ds(low, low))
                    ),
                ]
            )
            m.finish()
            spread_on(u)

        for_each(reduce)

        def norm_two(i, carry):
            at = pl.ds(pl.multiple_of(i * 16, 16), 16)
            residual = hid_ref[at, :].astype(F32) + res_ref[at, :]
            res_ref[at, :] = residual
            normed, _ = normalize(residual)
            s2[at, :] = (normed * gain_ref[1:2, :]).astype(BF16)
            return carry

        lax.fori_loop(0, tokens // 16, norm_two, 0)
        low = tokens // 2
        for _ in plane_gather(
            common, "k", s2, s2_all, token_slot, (pl.ds(0, low), pl.ds(low, low))
        ):
            pass

        def last(u):
            spread_on(u)
            whole[u].finish()
            for v, m, _ in spread:
                if u == v:
                    m.finish()

        for_each(last)
        for copy in keep:
            copy.wait()
        common.finish()
        assert len(names) <= N_SEMS

    vmem, hbm = pl.BlockSpec(memory_space=VMEM), pl.BlockSpec(memory_space=HBM)
    outs = [
        ((width, cols), BF16, hbm),
        ((8, tokens, width), BF16, hbm),
        ((4 * out_rows, width), BF16, vmem),
        ((2, block, key), BF16, vmem),
        ((2, block, key), BF16, vmem),
        ((2, block, val), BF16, vmem),
        ((both, val), F32, vmem),
        ((2, block, block), BF16, vmem),
        ((2, block, block), F32, vmem),
        ((2, key, val), BF16, vmem),
        ((2, block, 1), F32, vmem),
        ((2, block, 1), F32, vmem),
        ((8, block), F32, vmem),
        ((8, width), F32, vmem),
        ((both, val), F32, vmem),
        ((both, 1), F32, vmem),
        ((both, val), BF16, vmem),
        ((tokens, width), F32, vmem),
        ((8, tokens, width), BF16, vmem),
        ((8, tokens, width), BF16, vmem),
        ((8, 4, rows, ff2), BF16, vmem),
        ((4, out_rows, width), BF16, vmem),
    ]
    return pl.pallas_call(
        kernel,
        out_shape=[jax.ShapeDtypeStruct(shape, kind) for shape, kind, _ in outs],
        in_specs=[vmem, hbm, vmem, hbm, hbm, hbm, hbm],
        out_specs=[spec for _, _, spec in outs],
        scratch_shapes=[
            pltpu.VMEM((width, cols), BF16),
            pltpu.VMEM((8, tokens, width), BF16),
            pltpu.VMEM((4, out_rows, width), BF16),
            pltpu.VMEM((8, 2, block), F32),
            pltpu.VMEM((8, rows, ff2), BF16),
            pltpu.VMEM((8, block), F32),
            pltpu.VMEM((block, 8), F32),
            pltpu.VMEM((2, key, val), BF16),
            pltpu.VMEM((4, 2, key, val), BF16),
            pltpu.VMEM((both, val), F32),
            pltpu.VMEM((8, tokens, width), BF16),
            pltpu.VMEM((4, tokens, width), BF16),
            pltpu.VMEM((4, tokens, width), BF16),
            pltpu.VMEM((4, tokens, width), BF16),
            pltpu.VMEM((tokens, width), BF16),
            pltpu.SemaphoreType.DMA((N_SEMS,)),
            pltpu.SemaphoreType.DMA((N_SEMS,)),
        ],
        name="forward",
        compiler_params=pltpu.CompilerParams(
            collective_id=1, has_side_effects=True, vmem_limit_bytes=62 << 20
        ),
    )(hidden, cot, decay, packed, outw, gu, w_down)


def feed_forward(scaled, top, w_gu, w_dn, residual, cot, gains):
    _, tokens, width = scaled.shape
    out_rows = w_dn.shape[1]
    rows, ff2 = w_gu.shape[2:]
    ff = ff2 // 2
    block = 4 * tokens

    def kernel(
        s2_ref, top_ref, gu_ref, wd_ref, res_ref, cot_ref, gain_ref, grad, grad_low, term, dout, lo, ggu,
        w_d, prod, grad_gu, part, down, total, sib, sums, got, got2, right, left, send, recv,
    ):
        uly = lax.axis_index(ULY)
        names = {}
        p = Place(uly)
        greet(line_partners(p) + plane_partners(p)[1:])
        common = Mover(p, names, send, recv)
        movers = [
            Mover(Place(u), names, send, recv, lambda: halves_of_columns(right.at[0], 0))
            for u in range(4)
        ]
        lines = [
            line_reduce(m, "d", lambda b: down.at[b], dout, None, right, left, halves_of_columns)
            for m in movers
        ]

        def for_each(body):
            for u in range(4):
                pl.when(uly == u)(functools.partial(body, u))

        for i in range(4):
            w_d[i * out_rows : (i + 1) * out_rows, :] = wd_ref[i]

        def weights():
            return gu_ref[...].reshape(32 * rows, ff2)

        def tokens_of(s):
            here = pl.ds(pl.multiple_of(s * block, block), block)
            lhs = s2_ref[pl.ds(4 * s, 4)].reshape(block, width)
            pre = matmul(lhs, weights())
            gate_pre, up_pre = pre[:, :ff], pre[:, ff:]
            grad_product = dot_nt(top_ref[pl.ds(4 * s, 4)].reshape(block, width), w_d[...])
            sigma = jax.nn.sigmoid(gate_pre)
            act = gate_pre * sigma
            prod[here, :] = (act * up_pre).astype(BF16)
            slope = sigma * (1.0 + gate_pre * (1.0 - sigma))
            grad_gu[here, :ff] = (grad_product * up_pre * slope).astype(BF16)
            grad_gu[here, ff:] = (grad_product * act).astype(BF16)

        def tokens_back(s):
            here = pl.ds(pl.multiple_of(s * block, block), block)

            def back(n, carry):
                at = pl.ds(pl.multiple_of(n * 512, 512), 512)
                right_side = gu_ref[pl.ds(2 * n, 2)].reshape(512, ff2)
                value = dot_nt(grad_gu[here, :], right_side).astype(BF16)
                part[pl.ds(4 * s, 4), :, at] = value.reshape(4, tokens, 512)
                return carry

            lax.fori_loop(0, width // 512, back, 0)

        reduced = plane_reduce(common, "s", part, total, sib, sums, got, got2)
        tokens_of(p.other)
        tokens_of(p.dp)

        def down_grad(n, carry):
            at = pl.ds(pl.multiple_of(n * 512, 512), 512)
            value = dot_t(prod[...], top_ref[:, :, at].reshape(2 * block, 512)).astype(BF16)
            for i in range(4):
                down[i, :, at] = value[i * out_rows : (i + 1) * out_rows]
            return carry

        lax.fori_loop(0, width // 512, down_grad, 0)
        for_each(lambda u: next(lines[u]))
        tokens_back(p.other)
        next(reduced)
        tokens_back(p.dp)
        next(reduced)

        def up_grad(n, carry):
            at = pl.ds(pl.multiple_of(n * 4 * rows, 4 * rows), 4 * rows)
            value = dot_t(s2_ref[:, :, at].reshape(2 * block, 4 * rows), grad_gu[...])
            ggu[n] = value.astype(BF16).reshape(4, rows, ff2)
            return carry

        lax.fori_loop(0, 4, up_grad, 0)
        next(reduced)
        lax.fori_loop(4, 8, up_grad, 0)
        for_each(lambda u: next(lines[u]))

        def out_part(n, carry):
            at = pl.ds(pl.multiple_of(n * 512, 512), 512)
            value = matmul(prod[...], w_d[:, at]).astype(BF16)
            lo[:, :, at] = value.reshape(8, tokens, 512)
            return carry

        lax.fori_loop(0, width // 512, out_part, 0)
        for _ in reduced:
            pass

        def back(i, carry):
            at = pl.ds(pl.multiple_of(i * 16, 16), 16)
            normed, inverse = normalize(res_ref[at, :])
            scaled_grad = total[at, :]
            value = cot_ref[at, :].astype(F32) + norm_back(
                scaled_grad * gain_ref[1:2, :], normed, inverse
            )
            grad[at, :] = value
            grad_low[at, :] = value.astype(BF16)
            return carry + jnp.sum(scaled_grad * normed, axis=0, keepdims=True)

        term[...] = lax.fori_loop(0, tokens // 16, back, jnp.zeros((1, width), F32))

        def last(u):
            for _ in lines[u]:
                pass
            movers[u].finish()

        for_each(last)
        common.finish()
        assert len(names) <= N_SEMS

    vmem = pl.BlockSpec(memory_space=VMEM)
    return pl.pallas_call(
        kernel,
        out_shape=[
            jax.ShapeDtypeStruct((tokens, width), F32),
            jax.ShapeDtypeStruct((tokens, width), BF16),
            jax.ShapeDtypeStruct((1, width), F32),
            jax.ShapeDtypeStruct((out_rows, width), F32),
            jax.ShapeDtypeStruct((8, tokens, width), BF16),
            jax.ShapeDtypeStruct((8, 4, rows, ff2), BF16),
        ],
        in_specs=[vmem] * 7,
        out_specs=[vmem] * 6,
        scratch_shapes=[
            pltpu.VMEM((4 * out_rows, width), BF16),
            pltpu.VMEM((2 * block, ff), BF16),
            pltpu.VMEM((2 * block, ff2), BF16),
            pltpu.VMEM((8, tokens, width), BF16),
            pltpu.VMEM((4, out_rows, width), BF16),
            pltpu.VMEM((tokens, width), F32),
            pltpu.VMEM((4, tokens, width), BF16),
            pltpu.VMEM((4, tokens, width), BF16),
            pltpu.VMEM((2, tokens, width), BF16),
            pltpu.VMEM((tokens, width), BF16),
            pltpu.VMEM((4, out_rows, width), BF16),
            pltpu.VMEM((4, out_rows, width), BF16),
            pltpu.SemaphoreType.DMA((N_SEMS,)),
            pltpu.SemaphoreType.DMA((N_SEMS,)),
        ],
        name="feed_forward",
        compiler_params=pltpu.CompilerParams(
            collective_id=3, has_side_effects=True, vmem_limit_bytes=62 << 20
        ),
    )(scaled, top, w_gu, w_dn, residual, cot, gains)


def attention_back(
    own, lo, ggu, w_out, gated, normed, inverse, swish, q, k, v, weights, mask, state_in, reach, tail, cum
):
    tokens, width = own.shape
    both, val = gated.shape
    block, key = q.shape[1:]
    rows, cols = ggu.shape[3:]
    piece = w_out.shape[0] // 4
    half = block // 2
    at_v, at_s = 2 * key, 2 * key + val

    def kernel(
        own_ref, lo_ref, g_ref, wo_ref, ga_ref, hn_ref, hi_ref, sw_ref, q_ref, k_ref, v_ref, w_ref, mask_ref, st_ref,
        reach_ref, tail_ref, cum_ref, cat_ref, total, gout, gsum,
        gy, gr, gs, gq, gk, gv, gst, gsts, sib, sums, got, got2, right, left, send, recv,
    ):
        uly = lax.axis_index(ULY)
        names = {}
        place = Place(uly)
        greet(line_partners(place) + plane_partners(place)[1:])
        common = Mover(place, names, send, recv)
        movers = [Mover(Place(u), names, send, recv, lambda: right.at[0, 0]) for u in range(4)]
        ways = [
            line_reduce(
                movers[u],
                "f",
                lambda b: g_ref.at[:, :, b],
                gsum,
                None,
                right,
                left,
                lambda view, i: view.at[i],
            )
            for u in range(4)
        ]

        def for_each(body):
            for u in range(4):
                pl.when(uly == u)(functools.partial(body, u))

        def first(u):
            def slot_zero():
                next(ways[u])
                yield

            m = Mover(Place(u), names, send, recv)
            together(
                [
                    plane_reduce(m, "s", lo_ref, total, sib, sums, got, got2),
                    line_gather(m, "k", own_ref, gy),
                    slot_zero(),
                ]
            )
            m.finish()
            next(ways[u])

        for_each(first)

        def chunk(c):
            return pl.ds(pl.multiple_of(c * half, half), half)

        def gradients(c, carry):
            at = chunk(c)
            grad = gy[pl.ds(2 * c, 2)].reshape(half, width)
            gg = dot_nt(grad, wo_ref[...])
            pre = sw_ref[at, :]
            sigma = jax.nn.sigmoid(pre)
            head = hn_ref[at, :]
            low = head.astype(BF16).astype(F32)
            cat_ref[at, at_s : at_s + val] = (
                gg * low * (sigma * (1.0 + pre * (1.0 - sigma)))
            ).astype(BF16)
            gh = (gg * (pre * sigma)).astype(BF16).astype(F32)
            mean = jnp.mean(gh * head, axis=-1, keepdims=True)
            grad_retained = (hi_ref[at, :] * (gh - head * mean)).astype(BF16)
            gr[at, :] = grad_retained
            s = lax.div(c, 2)
            part = pl.ds(pl.multiple_of(lax.rem(c, 2) * half, half), half)
            gs[at, :] = (dot_nt(grad_retained, v_ref[s]) * mask_ref[s, part, :]).astype(BF16)
            return carry

        lax.fori_loop(0, both // half, gradients, 0)
        for s in range(2):
            at = pl.ds(s * block, block)
            reached = (q_ref[s].astype(F32) * reach_ref[s]).astype(BF16)
            gst[s] = dot_t(reached, gr[at, :]).astype(BF16)
        states = plane_gather(
            common, "t", gst, gsts, state_slot, (pl.ds(0, 1), pl.ds(1, 1)), pair=False
        )
        next(states)

        for s in range(2):
            at = pl.ds(s * block, block)
            gq[at, :] = jnp.dot(gs[at, :], k_ref[s], preferred_element_type=F32)
            gk[at, :] = dot_t(gs[at, :], q_ref[s])
        next(states)
        for s in range(2):
            at = pl.ds(s * block, block)
            gv[at, :] = dot_t(w_ref[s], gr[at, :])

        def out_grad(n, carry):
            at = pl.ds(pl.multiple_of(n * 512, 512), 512)
            grad = gy[:, :, at].reshape(both, 512)
            value = dot_t(ga_ref[...], grad).astype(BF16)
            for i in range(4):
                gout[i, :, at] = value[i * piece : (i + 1) * piece]
            return carry

        lax.fori_loop(0, width // 512, out_grad, 0)
        for _ in states:
            pass
        for_each(lambda u: next(ways[u]))
        for s in range(2):
            at = pl.ds(s * block, block)
            factors = block_factors(cum_ref, place.ctx, s, True)
            update = factors[0] * gsts[0, s].astype(F32)
            for j in range(1, 4):
                update = update + factors[j] * gsts[j, s].astype(F32)
            update = update.astype(BF16)
            grad = gr[at, :]
            cat_ref[at, :key] = (gq[at, :] + reach_ref[s] * dot_nt(grad, st_ref[s])).astype(BF16)
            cat_ref[at, key:at_v] = (gk[at, :] + tail_ref[s] * dot_nt(v_ref[s], update)).astype(BF16)
            cat_ref[at, at_v:at_s] = (
                gv[at, :] + tail_ref[s] * jnp.dot(k_ref[s], update, preferred_element_type=F32)
            ).astype(BF16)

        def last(u):
            for _ in ways[u]:
                pass
            movers[u].finish()

        for_each(last)
        common.finish()
        assert len(names) <= N_SEMS

    vmem = pl.BlockSpec(memory_space=VMEM)
    return pl.pallas_call(
        kernel,
        out_shape=[
            jax.ShapeDtypeStruct((both, 2 * key + 2 * val), BF16),
            jax.ShapeDtypeStruct((tokens, width), F32),
            jax.ShapeDtypeStruct((4, piece, width), BF16),
            jax.ShapeDtypeStruct((2, 4, rows, cols), BF16),
        ],
        in_specs=[vmem] * 17,
        out_specs=[vmem] * 4,
        scratch_shapes=[
            pltpu.VMEM((8, tokens, width), BF16),
            pltpu.VMEM((both, val), BF16),
            pltpu.VMEM((both, block), BF16),
            pltpu.VMEM((both, key), F32),
            pltpu.VMEM((both, key), F32),
            pltpu.VMEM((both, val), F32),
            pltpu.VMEM((2, key, val), BF16),
            pltpu.VMEM((4, 2, key, val), BF16),
            pltpu.VMEM((4, tokens, width), BF16),
            pltpu.VMEM((4, tokens, width), BF16),
            pltpu.VMEM((2, tokens, width), BF16),
            pltpu.VMEM((tokens, width), BF16),
            pltpu.VMEM((4, 2, 4, rows, cols), BF16),
            pltpu.VMEM((4, 2, 4, rows, cols), BF16),
            pltpu.SemaphoreType.DMA((N_SEMS,)),
            pltpu.SemaphoreType.DMA((N_SEMS,)),
        ],
        name="attention_back",
        compiler_params=pltpu.CompilerParams(
            collective_id=7, has_side_effects=True, vmem_limit_bytes=62 << 20
        ),
    )(own, lo, ggu, w_out, gated, normed, inverse, swish, q, k, v, weights, mask, state_in, reach, tail, cum)


def last_exchange(grad_cat, w_all, scaled, gout, gffn, inputs, term):
    tokens, width = inputs.shape
    both, cols = grad_cat.shape
    block = both // 2
    out_rows = gout.shape[1]
    quarter = width // 4
    rows, ff2 = gffn.shape[1:]

    def streams(
        m, line, tile, o_ref, f_ref, in_ref, t_ref, out, gall, oall, fall, gains,
        gotx, goty, gotx2, goty2, oxs, oys, ox2, oy2, away,
    ):
        p = m.place
        u = p.uly

        def attn():
            for t in range(4):
                m.arrive(("gx", 1, t), gotx.at[1, t])
                add_up(gotx.at[1, t], [tile(0, p.yn, t), gotx.at[1, t]])
                m.send(("gy2", t), gotx.at[1, t], goty2.at[t], p.at(ctx=p.yn))
                m.arrive(("gy", 1, t), goty.at[1, t])
                add_up(goty.at[1, t], [tile(1, p.xn, t), goty.at[1, t]])
                m.send(("gx2", t), goty.at[1, t], gotx2.at[t], p.at(ctx=p.xn))
            yield
            yield
            for t in range(4):
                for dp, got, got2, tags in (
                    (0, gotx, goty2, ("gx", "gy2")),
                    (1, goty, gotx2, ("gy", "gx2")),
                ):
                    m.arrive((tags[0], 0, t), got.at[0, t])
                    m.arrive((tags[1], t), got2.at[t])
                    add_up(got.at[0, t], [tile(dp, p.ctx, t), got.at[0, t], got2.at[t]])
                    there = gall.at[p.dp * 4 + u]
                    if t == u:

                        @pl.when(p.dp == dp)
                        def _(got=got, there=there):
                            here = pltpu.make_async_copy(
                                got.at[0, u], there, m.send_sems.at[m.number("G")]
                            )
                            here.start()
                            here.wait()

                        @pl.when(p.dp != dp)
                        def _(got=got, there=there, dp=dp):
                            m.remote(
                                ("gc", u), got.at[0, u], there, (dp, p.ctx, u)
                            ).start()
                    else:
                        k = m.number(("gs", dp, t))
                        copies = []
                        for q in range(2):
                            copies.append(
                                pltpu.make_async_remote_copy(
                                    src_ref=got.at[0, t],
                                    dst_ref=there,
                                    send_sem=m.send_sems.at[k],
                                    recv_sem=m.recv_sems.at[m.number(("g", q, u))],
                                    device_id=(dp, p.ctx, t),
                                    device_id_type=MESH,
                                )
                            )
                        pl.when(p.dp == dp)(copies[0].start)
                        pl.when(p.dp != dp)(copies[1].start)
                        m.sent.append(copies[0])
            for _ in range(6):
                yield
            m.remote(("gc", u), gotx.at[0, u], gotx.at[0, u], p.at(dp=p.other)).wait_send()
            m.arrive(("gc", u), gall.at[p.other * 4 + u])
            for us in range(4):
                if us != u:
                    m.arrive(("g", 0, us), gall.at[p.dp * 4 + us])
                    m.arrive(("g", 1, us), gall.at[p.other * 4 + us])

        def out_proj():
            def column(ref, part, c):
                return ref.at[part, :, pl.ds(pl.multiple_of(c * quarter, quarter), quarter)]

            low, high = pl.ds(0, 2), pl.ds(2, 2)
            for i, (cx, cy) in ((1, (p.dg, p.dg)), (0, (p.xn, p.yn))):
                m.send(("ox", i), column(o_ref, low, cx), oxs.at[i], p.at(ctx=p.xn))
                m.send(("oy", i), column(o_ref, high, cy), oys.at[i], p.at(ctx=p.yn))
            yield
            m.arrive(("ox", 1), oxs.at[1])
            for t in range(2):
                add_up(oxs.at[1, t], [column(o_ref, t, p.yn), oxs.at[1, t]])
            m.send("oy2", oxs.at[1], oy2, p.at(ctx=p.yn))
            m.arrive(("oy", 1), oys.at[1])
            for t in range(2):
                add_up(oys.at[1, t], [column(o_ref, 2 + t, p.xn), oys.at[1, t]])
            m.send("ox2", oys.at[1], ox2, p.at(ctx=p.xn))
            yield
            m.arrive(("ox", 0), oxs.at[0])
            m.arrive(("oy", 0), oys.at[0])
            m.arrive("oy2", oy2)
            m.arrive("ox2", ox2)
            home_dp, home_ctx = u // 2, 2 * (u % 2) + p.dp
            here_all = []
            for us in range(4):
                got, got2 = (oxs, oy2) if us < 2 else (oys, ox2)
                t = us % 2
                add_up(got.at[0, t], [column(o_ref, us, p.ctx), got.at[0, t], got2.at[t]])
                own = (home_dp == p.dp) & (home_ctx == p.ctx) & (us == u)
                there = oall.at[p.ctx]
                here = pltpu.make_async_copy(
                    got.at[0, t], there, m.send_sems.at[m.number("O")]
                )

                @pl.when(own)
                def _(here=here):
                    here.start()
                    here.wait()

                for j in range(4):
                    copy = pltpu.make_async_remote_copy(
                        src_ref=got.at[0, t],
                        dst_ref=there,
                        send_sem=m.send_sems.at[m.number(("os", us))],
                        recv_sem=m.recv_sems.at[m.number(("o", j))],
                        device_id=(home_dp, home_ctx, us),
                        device_id_type=MESH,
                    )
                    pl.when(jnp.logical_not(own) & (p.ctx == j))(copy.start)
                here_all.append((own, copy))
            yield
            head_dp, head_u = lax.rem(p.ctx, 2), p.dp * 2 + lax.div(p.ctx, 2)
            for j in range(4):
                mine = (head_dp == p.dp) & (p.ctx == j) & (head_u == u)

                @pl.when(jnp.logical_not(mine))
                def _(j=j):
                    m.arrive(("o", j), oall.at[j])

            for own, copy in here_all:
                pl.when(jnp.logical_not(own))(copy.wait_send)

        def feed():
            mine = fall.at[p.dp * 4 + p.ctx]
            copy = m.local("F", f_ref.at[p.dp * 4 + p.ctx], mine)
            spots = [(q, c, i) for i, c in enumerate((p.ctx, p.xn, p.yn, p.dg)) for q in range(2)][1:]
            for q, c, i in spots:
                dp = p.dp if q == 0 else p.other
                m.send(("f", q, i), f_ref.at[dp * 4 + c], mine, p.at(dp=dp, ctx=c))
            for _ in range(4):
                yield
            for q, c, i in spots:
                dp = p.dp if q == 0 else p.other
                m.arrive(("f", q, i), fall.at[dp * 4 + c])
            copy.wait()

        def tokens_stream():
            yield from line

            def body(i, total):
                at = pl.ds(pl.multiple_of(i * 16, 16), 16)
                values = in_ref[at, :].astype(F32)
                normed, _ = normalize(values)
                return total + jnp.sum(out[at, :] * normed, axis=0, keepdims=True)

            total = lax.fori_loop(0, tokens // 16, body, jnp.zeros((1, width), F32))
            row = lax.broadcasted_iota(jnp.int32, (8, width), 0)
            gains[...] = jnp.where(
                row == 0,
                jnp.broadcast_to(total, (8, width)),
                jnp.where(row == 1, jnp.broadcast_to(t_ref[...], (8, width)), 0.0),
            )
            for i, device in enumerate((p.at(dp=p.other), p.at(ctx=p.xn), p.at(ctx=p.yn))):
                m.remote(("n", i), gains, away.at[i], device).start()
                yield
                m.remote(("n", i), gains, away.at[i], device).wait()
                gains[...] = gains[...] + away[i]
            copies = [
                m.remote(("N", u, other), gains, away.at[3 + u], p.at(uly=other))
                for other in range(4)
                if other != u
            ]
            for copy in copies:
                copy.start()
            yield
            mine = gains[...]
            for other in range(4):
                if other != u:
                    m.arrive(("N", other, u), away.at[3 + other])
                    mine = mine + away[3 + other]
            for copy in copies:
                copy.wait_send()
            gains[...] = mine

        return [
            attn(),
            tokens_stream(),
            later(out_proj(), 1),
            later(feed(), 5),
        ]

    def kernel(
        cat_ref, wa_ref, s1_ref, o_ref, f_ref, in_ref, t_ref, out, gall, oall, fall, gains,
        grads, part, sib, right, left, gotx, goty, gotx2, goty2, oxs, oys, ox2, oy2, away, send, recv,
    ):
        uly = lax.axis_index(ULY)
        names = {}
        p = Place(uly)
        greet(everyone(p))
        common = Mover(p, names, send, recv)

        def for_each(body):
            for u in range(4):
                pl.when(uly == u)(functools.partial(body, u))

        def tile(dp, c, t):
            return grads.at[dp, c, pl.ds(t * rows, rows)]

        def weight_grad(dp, c):
            at = pl.ds(pl.multiple_of((dp * 4 + c) * 4 * rows, 4 * rows), 4 * rows)
            grads[dp, c] = dot_t(s1_ref[:, :, at].reshape(both, 4 * rows), cat_ref[...]).astype(BF16)

        def token_grad(i, carry):
            s = jnp.where(i < 4, p.other, p.dp)
            n = pl.ds(pl.multiple_of(lax.rem(i, 4) * quarter, quarter), quarter)
            rows_s = pl.ds(pl.multiple_of(s * block, block), block)
            value = dot_nt(cat_ref[rows_s, :], wa_ref[n, :cols]).astype(BF16)
            part[pl.ds(4 * s, 4), :, n] = value.reshape(4, tokens, quarter)
            return carry

        def to_x(i, c):
            weight_grad(0, c)
            for t in range(4):
                common.send(("gx", i, t), tile(0, c, t), gotx.at[i, t], p.at(ctx=p.xn))

        def to_y(i, c):
            weight_grad(1, c)
            for t in range(4):
                common.send(("gy", i, t), tile(1, c, t), goty.at[i, t], p.at(ctx=p.yn))

        to_x(1, p.dg)
        to_y(1, p.dg)
        lax.fori_loop(0, 8, token_grad, 0)
        movers = [
            Mover(
                Place(u), names, send, recv, lambda: halves_of_rows(sib.at[0], 0), lambda: sib.at[0]
            )
            for u in range(4)
        ]
        lines = [
            line_reduce(m, "s", lambda i: part.at[i], out, sib, right, left) for m in movers
        ]
        for_each(lambda u: next(lines[u]))
        to_x(0, p.xn)
        to_y(0, p.yn)
        weight_grad(0, p.yn)
        weight_grad(1, p.xn)
        weight_grad(0, p.ctx)
        weight_grad(1, p.ctx)

        def rest(u):
            m = Mover(Place(u), names, send, recv)
            together(
                streams(
                    m, lines[u], tile, o_ref, f_ref, in_ref, t_ref, out, gall, oall, fall, gains,
                    gotx, goty, gotx2, goty2, oxs, oys, ox2, oy2, away,
                )
            )
            m.finish()
            movers[u].finish()

        for_each(rest)
        common.finish()
        assert len(names) <= N_SEMS

    vmem, hbm = pl.BlockSpec(memory_space=VMEM), pl.BlockSpec(memory_space=HBM)
    return pl.pallas_call(
        kernel,
        out_shape=[
            jax.ShapeDtypeStruct((tokens, width), F32),
            jax.ShapeDtypeStruct((8, rows, cols), BF16),
            jax.ShapeDtypeStruct((4, out_rows, quarter), BF16),
            jax.ShapeDtypeStruct((8, rows, ff2), BF16),
            jax.ShapeDtypeStruct((8, width), F32),
        ],
        in_specs=[vmem, vmem, vmem, vmem, hbm, vmem, vmem],
        out_specs=[vmem, hbm, hbm, hbm, vmem],
        scratch_shapes=[
            pltpu.VMEM((2, 4, 4 * rows, cols), BF16),
            pltpu.VMEM((8, tokens, width), BF16),
            *[pltpu.VMEM((4, tokens, width), BF16)] * 3,
            *[pltpu.VMEM((2, 4, rows, cols), BF16)] * 2,
            *[pltpu.VMEM((4, rows, cols), BF16)] * 2,
            *[pltpu.VMEM((2, 2, out_rows, quarter), BF16)] * 2,
            *[pltpu.VMEM((2, out_rows, quarter), BF16)] * 2,
            pltpu.VMEM((7, 8, width), F32),
            pltpu.SemaphoreType.DMA((N_SEMS,)),
            pltpu.SemaphoreType.DMA((N_SEMS,)),
        ],
        name="last",
        compiler_params=pltpu.CompilerParams(
            collective_id=2, has_side_effects=True, vmem_limit_bytes=62 << 20
        ),
    )(grad_cat, w_all, scaled, gout, gffn, inputs, term)


def local(
    hidden_in,
    cotangent,
    log_decay,
    w_query,
    w_key,
    w_value,
    w_swish,
    w_output,
    w_gate,
    w_up,
    w_down,
    gain_attn,
    gain_ffn,
):
    bf16, f32 = BF16, F32
    dp, ctx = lax.axis_index(DP), lax.axis_index(CTX)
    tokens = hidden_in.shape[1]
    width = hidden_in.shape[2]
    rows = w_query.shape[0]
    out_rows = w_output.shape[0]
    key, val, ff = KEY_DIM, VALUE_DIM, w_gate.shape[1] // 8

    gains = jnp.pad(jnp.stack([gain_attn, gain_ffn], axis=1), ((0, 0), (0, 30)))
    packed, outw, gate_up = pack(w_query, w_key, w_value, w_swish, w_output, w_gate, w_up, gains)
    block = 4 * tokens
    (
        w_all, scaled_one, w_out, q, k, v, swish_pre, weights, mask, state_in, reach, tail, cum,
        gains, head_normed, head_inverse, gated, residual, scaled_two, top_all, w_gu, w_dn,
    ) = forward(hidden_in[0], cotangent[0], log_decay[0], packed, outw, gate_up, w_down)
    gain_one = gains[0]
    grad_residual, grad_y, gain_two_term, grad_down, layer_part, ggu = feed_forward(
        scaled_two, top_all, w_gu, w_dn, residual, cotangent[0], gains
    )
    inputs = hidden_in[0].astype(f32)
    grad_cat, out_part, g_out, ggu = attention_back(
        grad_y,
        layer_part,
        ggu.reshape(2, 4, 4, rows, 2 * ff),
        w_out,
        gated,
        head_normed,
        head_inverse,
        swish_pre,
        q,
        k,
        v,
        weights,
        mask,
        state_in,
        reach,
        tail,
        cum,
    )
    layer_out = residual + out_part
    gs1, gcat, g_out, ggu, gain_terms = last_exchange(
        grad_cat,
        w_all,
        scaled_one,
        g_out,
        ggu.reshape(8, rows, 2 * ff),
        hidden_in[0],
        gain_two_term,
    )
    normed_one, inverse_one = normalize(inputs)
    grad_input = grad_residual + norm_back(gs1 * gain_one, normed_one, inverse_one)

    grad_query, grad_key, grad_value, grad_swish, grad_output, grad_gate, grad_up = unpack(
        gcat, g_out, ggu
    )
    me = dp * 16 + ctx * 4 + lax.axis_index(ULY)
    gain_terms = lax.dynamic_slice_in_dim(gain_terms, me * rows, rows, axis=1)
    return (
        layer_out[None],
        grad_input[None],
        grad_query,
        grad_key,
        grad_value,
        grad_swish,
        grad_output,
        grad_gate,
        grad_up,
        grad_down,
        gain_terms[0],
        gain_terms[1],
    )


def solution(mesh):
    shape = mesh.shape
    planned = (shape[DP], shape[CTX], shape[ULY]) == (2, 4, 4)
    tokens = P(DP, (CTX, ULY), None)
    weight = P(EVERYWHERE, None)
    gain = P(EVERYWHERE)
    return jax.shard_map(
        local if planned else local_any,
        mesh=mesh,
        in_specs=(tokens, tokens, P(DP, ULY, CTX), *[weight] * 8, gain, gain),
        out_specs=(tokens, tokens, *[weight] * 8, gain, gain),
        check_vma=False,
    )
```

```python
import functools
import math

import jax
import jax.numpy as jnp
from jax import lax
from jax.experimental import pallas as pl
from jax.experimental.pallas import tpu as pltpu
from jax.sharding import PartitionSpec as P

RETENTION_HEADS = 8
KEY_DIM = 256
VALUE_DIM = 432


EPSILON = 1e-06
DP, CTX, ULY = "dp", "ctx", "ulysses"
EVERYWHERE = (DP, CTX, ULY)


def entering(value, axis, join, neutral, backward):
    count, mine = (lax.axis_size(axis), lax.axis_index(axis))
    pieces = jax.tree.map(lambda part: lax.all_gather(part, axis), value)
    if backward:
        pieces = jax.tree.map(lambda part: part[::-1], pieces)
        mine = count - 1 - mine
    subtotal = jax.tree.map(
        lambda part, zero: jnp.full_like(part, 0) + jnp.asarray(zero, part.dtype), value, neutral
    )

    def step(position, subtotal):
        longer = join(subtotal, jax.tree.map(lambda part: part[position], pieces))
        return jax.tree.map(lambda new, old: jnp.where(position < mine, new, old), longer, subtotal)

    return lax.fori_loop(0, count - 1, step, subtotal)


def normalize(values):
    inverse = lax.rsqrt(jnp.mean(values * values, axis=-1, keepdims=True) + EPSILON)
    return (values * inverse, inverse)


def norm_back(grad_normed, normed, inverse):
    return inverse * (grad_normed - normed * jnp.mean(grad_normed * normed, axis=-1, keepdims=True))


def swish_slope(values):
    sigma = jax.nn.sigmoid(values)
    return sigma * (1.0 + values * (1.0 - sigma))


def carry_forward(earlier, later):
    return (earlier[0] * later[0], later[0][:, None, None] * earlier[1] + later[1])


def carry_backward(earlier, later):
    return (earlier[0] * later[0], later[1] + later[0][:, None, None] * earlier[1])


def running_sum(values):
    size = values.shape[-1]
    upper = lax.broadcasted_iota(jnp.int32, (size, size), 0) <= lax.broadcasted_iota(
        jnp.int32, (size, size), 1
    )
    return jnp.dot(values, upper.astype(jnp.float32), precision=lax.Precision.HIGHEST)


def matmul(left, right):
    return jnp.dot(left, right, preferred_element_type=jnp.float32)


def local_any(
    hidden_in,
    cotangent,
    log_decay,
    w_query,
    w_key,
    w_value,
    w_swish,
    w_output,
    w_gate,
    w_up,
    w_down,
    gain_attn,
    gain_ffn,
):
    highest = lax.Precision.HIGHEST
    query_full, key_full, value_full, swish_full, output_full, gain_one = (
        lax.all_gather(w_query, EVERYWHERE, axis=0, tiled=True),
        lax.all_gather(w_key, EVERYWHERE, axis=0, tiled=True),
        lax.all_gather(w_value, EVERYWHERE, axis=0, tiled=True),
        lax.all_gather(w_swish, EVERYWHERE, axis=0, tiled=True),
        lax.all_gather(w_output, EVERYWHERE, axis=0, tiled=True),
        lax.all_gather(gain_attn, EVERYWHERE, axis=0, tiled=True),
    )
    inputs = hidden_in[0].astype(jnp.float32)
    tokens = inputs.shape[0]
    normed_one, inverse_one = normalize(inputs)
    scaled_one = (normed_one * gain_one.astype(jnp.float32)).astype(jnp.bfloat16)
    queries = (
        matmul(scaled_one, query_full)
        .astype(jnp.bfloat16)
        .reshape(tokens, RETENTION_HEADS, KEY_DIM)
    )
    keys_tok = (
        matmul(scaled_one, key_full).astype(jnp.bfloat16).reshape(tokens, RETENTION_HEADS, KEY_DIM)
    )
    values_tok = (
        matmul(scaled_one, value_full)
        .astype(jnp.bfloat16)
        .reshape(tokens, RETENTION_HEADS, VALUE_DIM)
    )
    swish_pre = matmul(scaled_one, swish_full)
    head_q, head_k, head_v = (
        lax.all_to_all(queries, ULY, split_axis=1, concat_axis=0, tiled=True),
        lax.all_to_all(keys_tok, ULY, split_axis=1, concat_axis=0, tiled=True),
        lax.all_to_all(values_tok, ULY, split_axis=1, concat_axis=0, tiled=True),
    )
    block = head_q.shape[0]
    scale = 1.0 / math.sqrt(KEY_DIM)
    cumulative = running_sum(log_decay[0])
    later = lax.broadcasted_iota(jnp.int32, (block, block), 0) >= lax.broadcasted_iota(
        jnp.int32, (block, block), 1
    )
    gap = cumulative[:, :, None] - cumulative[:, None, :]
    mask = jnp.where(later[None], jnp.exp(jnp.minimum(gap, 0.0)), 0.0) * scale
    scores = jnp.einsum("thd,shd->hts", head_q, head_k, preferred_element_type=jnp.float32)
    weights = (scores * mask).astype(jnp.bfloat16)
    intra = jnp.einsum("hts,she->the", weights, head_v, preferred_element_type=jnp.float32)
    query_f = head_q.astype(jnp.float32)
    key_f = head_k.astype(jnp.float32)
    value_f = head_v.astype(jnp.float32)
    tail = jnp.exp(cumulative[:, -1:] - cumulative).T[:, :, None]
    reach = jnp.exp(cumulative).T[:, :, None]
    update = jnp.einsum("shd,she->hde", key_f * tail, value_f, precision=highest)
    block_decay = jnp.exp(cumulative[:, -1])
    identity = (jnp.ones_like(block_decay), jnp.zeros_like(update))
    _, state_in = entering((block_decay, update), CTX, carry_forward, identity, False)
    retained = intra + scale * reach * jnp.einsum(
        "thd,hde->the", query_f, state_in, precision=highest
    )
    head_normed, head_inverse = normalize(retained)
    head_out = head_normed.astype(jnp.bfloat16)
    token_out = lax.all_to_all(
        head_out, ULY, split_axis=0, concat_axis=1, tiled=True
    ).reshape(tokens, RETENTION_HEADS * VALUE_DIM)
    token_out_f = token_out.astype(jnp.float32)
    swish_act = jax.nn.silu(swish_pre)
    gated = (swish_act * token_out_f).astype(jnp.bfloat16)
    residual = inputs + matmul(gated, output_full)
    gate_full, up_full, down_full, gain_two = (
        lax.all_gather(w_gate, EVERYWHERE, axis=0, tiled=True),
        lax.all_gather(w_up, EVERYWHERE, axis=0, tiled=True),
        lax.all_gather(w_down, EVERYWHERE, axis=0, tiled=True),
        lax.all_gather(gain_ffn, EVERYWHERE, axis=0, tiled=True),
    )
    normed_two, inverse_two = normalize(residual)
    scaled_two = (normed_two * gain_two.astype(jnp.float32)).astype(jnp.bfloat16)
    gate_pre = matmul(scaled_two, gate_full)
    up_pre = matmul(scaled_two, up_full)
    product = (jax.nn.silu(gate_pre) * up_pre).astype(jnp.bfloat16)
    layer_out = residual + matmul(product, down_full)
    grad_top = cotangent[0].astype(jnp.float32)
    grad_top_low = grad_top.astype(jnp.bfloat16)
    grad_product = matmul(grad_top_low, down_full.T)
    grad_down_term = matmul(product.T, grad_top_low)
    grad_gate_pre = (grad_product * up_pre * swish_slope(gate_pre)).astype(jnp.bfloat16)
    grad_up_pre = (grad_product * jax.nn.silu(gate_pre)).astype(jnp.bfloat16)
    grad_gate_term = matmul(scaled_two.T, grad_gate_pre)
    grad_up_term = matmul(scaled_two.T, grad_up_pre)
    grad_scaled_two = matmul(grad_gate_pre, gate_full.T) + matmul(grad_up_pre, up_full.T)
    grad_gain_two = jnp.sum(grad_scaled_two * normed_two, axis=0)
    grad_residual = grad_top + norm_back(
        grad_scaled_two * gain_two.astype(jnp.float32), normed_two, inverse_two
    )
    grad_gate, grad_up, grad_down, grad_gain_ffn = (
        lax.psum_scatter(grad_gate_term, EVERYWHERE, scatter_dimension=0, tiled=True),
        lax.psum_scatter(grad_up_term, EVERYWHERE, scatter_dimension=0, tiled=True),
        lax.psum_scatter(grad_down_term, EVERYWHERE, scatter_dimension=0, tiled=True),
        lax.psum_scatter(grad_gain_two, EVERYWHERE, scatter_dimension=0, tiled=True),
    )
    grad_y = grad_residual.astype(jnp.bfloat16)
    grad_output_term = matmul(gated.T, grad_y)
    grad_gated = matmul(grad_y, output_full.T)
    grad_swish_pre = (grad_gated * token_out_f * swish_slope(swish_pre)).astype(jnp.bfloat16)
    grad_token_out = (
        (grad_gated * swish_act).astype(jnp.bfloat16).reshape(tokens, RETENTION_HEADS, VALUE_DIM)
    )
    grad_swish_term = matmul(scaled_one.T, grad_swish_pre)
    grad_head_out = lax.all_to_all(
        grad_token_out, ULY, split_axis=1, concat_axis=0, tiled=True
    ).astype(jnp.float32)
    grad_retained = norm_back(grad_head_out, head_normed, head_inverse).astype(jnp.bfloat16)
    grad_retained_f = grad_retained.astype(jnp.float32)
    grad_weights = jnp.einsum(
        "the,she->hts", grad_retained, head_v, preferred_element_type=jnp.float32
    )
    grad_scores = (grad_weights * mask).astype(jnp.bfloat16)
    grad_state_in = scale * jnp.einsum(
        "thd,the->hde", query_f * reach, grad_retained_f, precision=highest
    )
    _, grad_update = entering((block_decay, grad_state_in), CTX, carry_backward, identity, True)
    grad_head_q = jnp.einsum(
        "hts,shd->thd", grad_scores, head_k, preferred_element_type=jnp.float32
    ) + scale * reach * jnp.einsum("the,hde->thd", grad_retained_f, state_in, precision=highest)
    grad_head_k = jnp.einsum(
        "hts,thd->shd", grad_scores, head_q, preferred_element_type=jnp.float32
    ) + tail * jnp.einsum("she,hde->shd", value_f, grad_update, precision=highest)
    grad_head_v = jnp.einsum(
        "hts,the->she", weights, grad_retained, preferred_element_type=jnp.float32
    ) + tail * jnp.einsum("shd,hde->she", key_f, grad_update, precision=highest)
    grad_queries, grad_keys, grad_values = (
        lax.all_to_all(
            grad_head_q.astype(jnp.bfloat16), ULY, split_axis=0, concat_axis=1, tiled=True
        ),
        lax.all_to_all(
            grad_head_k.astype(jnp.bfloat16), ULY, split_axis=0, concat_axis=1, tiled=True
        ),
        lax.all_to_all(
            grad_head_v.astype(jnp.bfloat16), ULY, split_axis=0, concat_axis=1, tiled=True
        ),
    )
    grad_queries = grad_queries.reshape(tokens, RETENTION_HEADS * KEY_DIM)
    grad_keys = grad_keys.reshape(tokens, RETENTION_HEADS * KEY_DIM)
    grad_values = grad_values.reshape(tokens, RETENTION_HEADS * VALUE_DIM)
    grad_query_term = matmul(scaled_one.T, grad_queries)
    grad_key_term = matmul(scaled_one.T, grad_keys)
    grad_value_term = matmul(scaled_one.T, grad_values)
    grad_scaled_one = (
        matmul(grad_queries, query_full.T)
        + matmul(grad_keys, key_full.T)
        + matmul(grad_values, value_full.T)
        + matmul(grad_swish_pre, swish_full.T)
    )
    grad_gain_one = jnp.sum(grad_scaled_one * normed_one, axis=0)
    grad_input = grad_residual + norm_back(
        grad_scaled_one * gain_one.astype(jnp.float32), normed_one, inverse_one
    )
    grad_query, grad_key, grad_value, grad_swish, grad_output, grad_gain_attn = (
        lax.psum_scatter(
            grad_query_term, EVERYWHERE, scatter_dimension=0, tiled=True
        ),
        lax.psum_scatter(grad_key_term, EVERYWHERE, scatter_dimension=0, tiled=True),
        lax.psum_scatter(
            grad_value_term, EVERYWHERE, scatter_dimension=0, tiled=True
        ),
        lax.psum_scatter(
            grad_swish_term, EVERYWHERE, scatter_dimension=0, tiled=True
        ),
        lax.psum_scatter(
            grad_output_term, EVERYWHERE, scatter_dimension=0, tiled=True
        ),
        lax.psum_scatter(grad_gain_one, EVERYWHERE, scatter_dimension=0, tiled=True),
    )
    return (
        layer_out[None],
        grad_input[None],
        grad_query,
        grad_key,
        grad_value,
        grad_swish,
        grad_output,
        grad_gate,
        grad_up,
        grad_down,
        grad_gain_attn,
        grad_gain_ffn,
    )


MESH = pl.DeviceIdType.MESH
BF16, F32 = jnp.bfloat16, jnp.float32
HBM, VMEM = pltpu.HBM, pltpu.VMEM
N_SEMS = 160


def dot_t(left, right):
    return lax.dot_general(left, right, (((0,), (0,)), ((), ())), preferred_element_type=F32)


def dot_nt(left, right):
    return lax.dot_general(left, right, (((1,), (1,)), ((), ())), preferred_element_type=F32)


def pair_dot(left_axis, right_axis, left, right):
    dims = (((left_axis,), (right_axis,)), ((0,), (0,)))
    return lax.dot_general(left, right, dims, preferred_element_type=F32)


class Place:
    def __init__(self, uly):
        self.dp, self.ctx, self.uly = lax.axis_index(DP), lax.axis_index(CTX), uly
        odd = lax.rem(self.ctx, 2)
        self.xn = self.ctx + 1 - 2 * odd
        self.yn = lax.rem(self.ctx + 2, 4)
        self.dg = self.yn + 1 - 2 * odd
        self.other = 1 - self.dp

    def at(self, dp=None, ctx=None, uly=None):
        return (
            self.dp if dp is None else dp,
            self.ctx if ctx is None else ctx,
            self.uly if uly is None else uly,
        )


class Mover:
    def __init__(self, place, names, send, recv, like=None, like_whole=None):
        self.like, self.like_whole = like, like_whole
        self.place, self.names, self.send_sems, self.recv_sems = place, names, send, recv
        self.sent, self.whole = [], []

    def number(self, name):
        return self.names.setdefault(name, len(self.names))

    def remote(self, name, src, dst, device):
        k = self.number(name)
        return pltpu.make_async_remote_copy(
            src_ref=src,
            dst_ref=dst,
            send_sem=self.send_sems.at[k],
            recv_sem=self.recv_sems.at[k],
            device_id=device,
            device_id_type=MESH,
        )

    def send(self, name, src, dst, device):
        copy = self.remote(name, src, dst, device)
        copy.start()
        self.sent.append(copy if self.like is None else name)

    def send_whole(self, name, src, dst, device):
        copy = self.remote(name, src, dst, device)
        copy.start()
        self.whole.append((copy if self.like is None else None, name, None))

    def arrive(self, name, dst):
        self.remote(name, dst, dst, self.place.at(dp=self.place.other)).wait_recv()

    def local(self, name, src, dst):
        copy = pltpu.make_async_copy(src, dst, self.send_sems.at[self.number(name)])
        copy.start()
        return copy

    def finish(self):
        for copy, name, _ in self.whole:
            if self.like is not None:
                ref = self.like_whole()
                copy = self.remote(name, ref, ref, self.place.at(dp=self.place.other))
            copy.wait_send()
        for copy in self.sent:
            if self.like is not None:
                ref = self.like()
                copy = self.remote(copy, ref, ref, self.place.at(dp=self.place.other))
            copy.wait_send()


def greet(devices):
    barrier = pltpu.get_barrier_semaphore()
    for device in devices:
        pl.semaphore_signal(barrier, inc=1, device_id=device, device_id_type=MESH)
    pl.semaphore_wait(barrier, len(devices))


def together(streams):
    streams = list(streams)
    while streams:
        left = []
        for stream in streams:
            if next(stream, 0) is None:
                left.append(stream)
        streams = left


def later(stream, stages):
    for _ in range(stages):
        yield
    yield from stream


def add_up(dst, sources, step=32):
    if len(dst.shape) > 2:
        for i in range(dst.shape[0]):
            add_up(dst.at[i], [source.at[i] for source in sources], step)
        return
    rows, columns = dst.shape
    by_rows = rows % step == 0
    step = step if by_rows else 256

    def body(i, carry):
        part = pl.ds(pl.multiple_of(i * step, step), step)
        at = (part, slice(None)) if by_rows else (slice(None), part)
        total = sources[0][at].astype(F32)
        for source in sources[1:]:
            total = total + source[at].astype(F32)
        dst[at] = total.astype(dst.dtype)
        return carry

    lax.fori_loop(0, (rows if by_rows else columns) // step, body, 0)


def halves_of_rows(view, i):
    rows = view.shape[0] // 2
    return view.at[pl.ds(i * rows, rows)]


def halves_of_columns(view, i):
    columns = view.shape[1] // 2
    return view.at[:, pl.ds(i * columns, columns)]


def line_gather(m, tag, own, out, pause=1):
    p = m.place
    u = p.uly
    mine = out.at[p.dp * 4 + u]
    copy = m.local((tag, "="), own, mine)
    for i in range(2):
        src, dst = halves_of_rows(own, i), halves_of_rows(mine, i)
        if u < 3:
            m.send((tag, "r", u, i), src, dst, p.at(uly=u + 1))
        if u > 0:
            m.send((tag, "l", u, i), src, dst, p.at(uly=u - 1))
    m.send((tag, "c", u), own, mine, p.at(dp=p.other))
    for _ in range(pause):
        yield
    for d in range(1, 4):
        for i in range(2):
            for way, b, onward in (("r", u - d, u + 1), ("l", u + d, u - 1)):
                if 0 <= b <= 3:
                    half = halves_of_rows(out.at[p.dp * 4 + b], i)
                    m.arrive((tag, way, b, i), half)
                    if 0 <= onward <= 3:
                        m.send((tag, way, b, i), half, half, p.at(uly=onward))
        for b in (u - d, u + d):
            if 0 <= b <= 3:
                block = out.at[p.dp * 4 + b]
                m.send((tag, "c", b), block, block, p.at(dp=p.other))
        yield
    for b in range(4):
        m.arrive((tag, "c", b), out.at[p.other * 4 + b])
    copy.wait()


def plane_gather(m, tag, own, out, slot, halves, pair=True):
    p = m.place

    def half(c, i):
        return slot(out, p.dp, c, halves[i])

    mine = slot(out, p.dp, p.ctx, None)
    copy = m.local((tag, "="), own, mine)
    m.send((tag, "x"), own, mine, p.at(ctx=p.xn))
    m.send((tag, "y"), own, mine, p.at(ctx=p.yn))
    if pair:
        m.send((tag, "c", 0), own, mine, p.at(dp=p.other))
    yield
    block = slot(out, p.dp, p.xn, None)
    m.arrive((tag, "x"), block)
    m.send((tag, "z", 0), half(p.xn, 0), half(p.xn, 0), p.at(ctx=p.yn))
    if pair:
        m.send((tag, "c", 1), block, block, p.at(dp=p.other))
    block = slot(out, p.dp, p.yn, None)
    m.arrive((tag, "y"), block)
    m.send((tag, "z", 1), half(p.yn, 1), half(p.yn, 1), p.at(ctx=p.xn))
    if pair:
        m.send((tag, "c", 2), block, block, p.at(dp=p.other))
    yield
    for i in range(2):
        block = half(p.dg, i)
        m.arrive((tag, "z", i), block)
        if pair:
            m.send((tag, "c", 3 + i), block, block, p.at(dp=p.other))
    yield
    if pair:
        for i, c in enumerate((p.ctx, p.xn, p.yn)):
            m.arrive((tag, "c", i), slot(out, p.other, c, None))
        for i in range(2):
            m.arrive((tag, "c", 3 + i), slot(out, p.other, p.dg, halves[i]))
    copy.wait()


def line_reduce(m, tag, part, out, sib, right, left, cut=halves_of_rows):
    p = m.place
    u = p.uly
    order = (3, 0, 2, 1) if u < 2 else (0, 3, 1, 2)
    for b in order if sib is not None else ():
        m.send_whole((tag, "c", b), part(p.other * 4 + b), sib.at[b], p.at(dp=p.other))
    met = set()

    def meet(b, i):
        if sib is None:
            return [cut(part(b), i)]
        if b not in met:
            met.add(b)
            m.arrive((tag, "c", b), sib.at[b])
        return [cut(part(p.dp * 4 + b), i), cut(sib.at[b], i)]

    def onward(way, b, i, arrived, there):
        terms = meet(b, i)
        if arrived is not None:
            arrived = cut(arrived.at[b], i)
            m.arrive((tag, way, b, i), arrived)
            terms.append(arrived)
        if len(terms) > 1:
            add_up(terms[-1], terms)
        away = cut((right if way == "r" else left).at[b], i)
        m.send((tag, way, b, i), terms[-1], away, p.at(uly=there))

    for slot in range(3):
        for b in range(4):
            for i in range(2):
                if u < b and u + 3 - b == slot:
                    onward("r", b, i, right if u > 0 else None, u + 1)
        for b in range(4):
            for i in range(2):
                if u > b and 3 - u + b == slot:
                    onward("l", b, i, left if u < 3 else None, u - 1)
        yield
    for i in range(2):
        terms = meet(u, i)
        if u > 0:
            m.arrive((tag, "r", u, i), cut(right.at[u], i))
            terms.append(cut(right.at[u], i))
        if u < 3:
            m.arrive((tag, "l", u, i), cut(left.at[u], i))
            terms.append(cut(left.at[u], i))
        add_up(cut(out, i), terms)


def plane_reduce(m, tag, part, out, sib, sums, got, got2):
    p = m.place
    rows = out.shape[0]
    halves = (pl.ds(0, rows // 2), pl.ds(rows // 2, rows // 2))
    order = (p.dg, p.xn, p.yn, p.ctx)
    for i, c in enumerate(order):
        m.send((tag, "c", i), part.at[p.other * 4 + c], sib.at[c], p.at(dp=p.other))
    yield
    for i, c in enumerate(order):
        m.arrive((tag, "c", i), sib.at[c])
        add_up(sums.at[c], [part.at[p.dp * 4 + c], sib.at[c]])
        if i == 0:
            m.send((tag, "x", 1), sums.at[c, halves[0]], got.at[1, halves[0]], p.at(ctx=p.xn))
            m.send((tag, "y", 1), sums.at[c, halves[1]], got.at[1, halves[1]], p.at(ctx=p.yn))
        if i == 1:
            m.send((tag, "x", 0), sums.at[c, halves[0]], got.at[0, halves[0]], p.at(ctx=p.xn))
        if i == 2:
            m.send((tag, "y", 0), sums.at[c, halves[1]], got.at[0, halves[1]], p.at(ctx=p.yn))
    yield
    m.arrive((tag, "x", 1), got.at[1, halves[0]])
    add_up(got.at[1, halves[0]], [sums.at[p.yn, halves[0]], got.at[1, halves[0]]])
    m.send((tag, "y2"), got.at[1, halves[0]], got2.at[halves[0]], p.at(ctx=p.yn))
    m.arrive((tag, "y", 1), got.at[1, halves[1]])
    add_up(got.at[1, halves[1]], [sums.at[p.xn, halves[1]], got.at[1, halves[1]]])
    m.send((tag, "x2"), got.at[1, halves[1]], got2.at[halves[1]], p.at(ctx=p.xn))
    yield
    m.arrive((tag, "x", 0), got.at[0, halves[0]])
    m.arrive((tag, "y", 0), got.at[0, halves[1]])
    yield
    m.arrive((tag, "y2"), got2.at[halves[0]])
    m.arrive((tag, "x2"), got2.at[halves[1]])
    add_up(out, [sums.at[p.ctx], got.at[0], got2])


class Stage:
    def __init__(self, loads, stores):
        self.loads, self.stores, self.started = loads, stores, []
        for copy in loads.values():
            copy.start()

    def need(self, *which):
        for i in which:
            self.loads.pop(i).wait()

    def put(self, *which):
        for i in which:
            copy = self.stores.pop(i)
            copy.start()
            self.started.append(copy)

    def end(self):
        self.need(*list(self.loads))
        self.put(*list(self.stores))
        for copy in self.started:
            copy.wait()


def staged_call(kernel, name, ins, outs, scratch, remote=None):
    in_held = [i for i, (_, held) in enumerate(ins) if held]
    out_held = [i for i, (_, _, held) in enumerate(outs) if held]

    def body(*refs):
        given, results = list(refs[: len(ins)]), list(refs[len(ins) : len(ins) + len(outs)])
        rest = refs[len(ins) + len(outs) :]
        held, own, sems = rest[: len(in_held) + len(out_held)], rest[len(in_held) + len(out_held) : -1], rest[-1]
        loads, stores = {}, {}
        for j, i in enumerate(in_held):
            loads[i] = pltpu.make_async_copy(given[i], held[j], sems.at[j])
            given[i] = held[j]
        for j, i in enumerate(out_held, len(in_held)):
            stores[i] = pltpu.make_async_copy(held[j], results[i], sems.at[j])
            results[i] = held[j]
        stage = Stage(loads, stores)
        kernel(stage, *given, *results, *own)
        stage.end()

    params = {} if remote is None else {"collective_id": remote, "has_side_effects": True}
    return pl.pallas_call(
        body,
        out_shape=[jax.ShapeDtypeStruct(shape, kind) for shape, kind, _ in outs],
        in_specs=[pl.BlockSpec(memory_space=HBM)] * len(ins),
        out_specs=[pl.BlockSpec(memory_space=HBM)] * len(outs),
        scratch_shapes=[
            *[pltpu.VMEM(ins[i][0].shape, ins[i][0].dtype) for i in in_held],
            *[pltpu.VMEM(*outs[i][:2]) for i in out_held],
            *[pltpu.VMEM(shape, kind) for shape, kind in scratch],
            *([pltpu.SemaphoreType.DMA((N_SEMS,))] * 2 if remote is not None else []),
            pltpu.SemaphoreType.DMA((len(in_held) + len(out_held),)),
        ],
        name=name,
        compiler_params=pltpu.CompilerParams(vmem_limit_bytes=62 << 20, **params),
    )(*[array for array, _ in ins])


def everyone(p):
    me = p.dp * 16 + p.ctx * 4 + p.uly
    found = []
    for k in range(1, 32):
        there = lax.rem(me + k, 32)
        found.append((lax.div(there, 16), lax.rem(lax.div(there, 4), 4), lax.rem(there, 4)))
    return found


def line_partners(p):
    found = [p.at(dp=p.other)]
    for d in range(1, 4):
        there = lax.rem(p.uly + d, 4)
        found += [p.at(uly=there), p.at(dp=p.other, uly=there)]
    return found


def plane_partners(p):
    return [p.at(dp=p.other), p.at(ctx=p.xn), p.at(ctx=p.yn)]


def token_slot(out, dp, c, part):
    view = out.at[dp * 4 + c]
    return view if part is None else view.at[part]


def state_slot(out, dp, c, part):
    view = out.at[c]
    return view if part is None else view.at[part]


def pack(w_query, w_key, w_value, w_swish, w_output, w_gate, w_up, gains):
    rows, (out_rows, width) = w_query.shape[0], w_output.shape
    key, val, ff, quarter = KEY_DIM, VALUE_DIM, w_gate.shape[1] // 8, width // 4
    cols = 2 * key + 2 * val + 32

    def kernel(stage, q, k, v, s, o, g, u, n, packed, outw, gu):
        stage.need(*range(8))
        for d in range(2):
            for z in range(4):
                h, i = 2 * z + d, 4 * d + z
                at = 0
                for ref, w in ((q, key), (k, key), (v, val), (s, val)):
                    packed[i, :, at : at + w] = ref[:, h * w : (h + 1) * w]
                    at += w
                packed[i, :, at : at + 32] = n[...]
        for i in range(8):
            gu[i, :, :ff] = g[:, i * ff : (i + 1) * ff]
            gu[i, :, ff:] = u[:, i * ff : (i + 1) * ff]
        for j in range(4):
            outw[j] = o[:, j * quarter : (j + 1) * quarter]

    weights = (w_query, w_key, w_value, w_swish, w_output, w_gate, w_up, gains)
    return staged_call(
        kernel,
        "pack",
        [(w, True) for w in weights],
        [
            ((8, rows, cols), BF16, True),
            ((4, out_rows, quarter), BF16, True),
            ((8, rows, 2 * ff), BF16, True),
        ],
        [],
    )


def unpack(heads, outg, slices):
    rows, (_, out_rows, quarter) = heads.shape[1], outg.shape
    key, val, ff = KEY_DIM, VALUE_DIM, slices.shape[2] // 2

    def kernel(stage, hs, og, sl, q, k, v, s, o, g, u):
        stage.need(0, 1, 2)
        for d in range(2):
            for z in range(4):
                h, i = 2 * z + d, 4 * d + z
                at = 0
                for ref, w in ((q, key), (k, key), (v, val), (s, val)):
                    ref[:, h * w : (h + 1) * w] = hs[i, :, at : at + w].astype(F32)
                    at += w
        for i in range(8):
            g[:, i * ff : (i + 1) * ff] = sl[i, :, :ff].astype(F32)
            u[:, i * ff : (i + 1) * ff] = sl[i, :, ff:].astype(F32)
        for j in range(4):
            o[:, j * quarter : (j + 1) * quarter] = og[j].astype(F32)

    widths = (8 * key, 8 * key, 8 * val, 8 * val, 4 * quarter, 8 * ff, 8 * ff)
    heights = (rows, rows, rows, rows, out_rows, rows, rows)
    return staged_call(
        kernel,
        "unpack",
        [(heads, True), (outg, True), (slices, True)],
        [(shape, F32, True) for shape in zip(heights, widths)],
        [],
    )


def line_spread(m, tag, own, slot):
    u = m.place.uly
    copy = m.local((tag, 8), own, slot(u))
    if u < 3:
        m.send((tag, "r", u), own, slot(u), m.place.at(uly=u + 1))
    if u > 0:
        m.send((tag, "l", u), own, slot(u), m.place.at(uly=u - 1))
    copy.wait()
    yield
    for d in range(1, 4):
        for way, b, onward in (("r", u - d, u + 1), ("l", u + d, u - 1)):
            if 0 <= b <= 3:
                m.arrive((tag, way, b), slot(b))
                if 0 <= onward <= 3:
                    m.send((tag, way, b), slot(b), slot(b), m.place.at(uly=onward))
        yield


def block_factors(cum, ctx, s, backward):
    count = cum.shape[1]
    lasts = [cum[4 * s + j : 4 * s + j + 1, count - 1 : count] for j in range(4)]
    found = []
    for j in range(4):
        total = jnp.zeros((1, 1), F32)
        for i in range(4):
            inside = ((i > ctx) & (i < j)) if backward else ((i > j) & (i < ctx))
            total = total + jnp.where(inside, lasts[i], 0.0)
        right = (j > ctx) if backward else (j < ctx)
        found.append(jnp.where(right, jnp.exp(total), 0.0))
    return found


def forward(hidden, cot, decay, packed, outw, gu, w_down):
    tokens, width = hidden.shape
    rows, cols = packed.shape[1:]
    out_rows, quarter = outw.shape[1:]
    ff2 = gu.shape[2]
    key, val = KEY_DIM, VALUE_DIM
    block, both = 4 * tokens, 8 * tokens
    half = block // 2
    scale = 1.0 / math.sqrt(key)
    at_s = 2 * key + val

    def start_streams(m, hid_ref, dec_ref, pk_ref, gu_ref, hall, dall, wall, gall):
        p = m.place
        u = p.uly

        def row(q, c, us):
            dp = p.dp if q == 0 else p.other
            at = (dp * 16 + c * 4 + us) * rows
            return wall.at[pl.ds(pl.multiple_of(at, rows), rows)]

        def attn():
            sources = sorted(
                ((q, us) for q in range(2) for us in range(4)), key=lambda s: (abs(s[1] - u), s[0])
            )
            copy = None
            for q, to in sources:
                dp = p.dp if q == 0 else p.other
                mine = row(0, p.ctx, u)
                src = pk_ref.at[dp * 4 + to]
                if (q, to) == (0, u):
                    copy = m.local("T", src, mine)
                else:
                    m.send(("t", q, u), src, mine, p.at(dp=dp, uly=to))
            yield
            relays = []
            for n, (q, us) in enumerate(sources):
                tile = row(q, p.ctx, us)
                if (q, us) == (0, u):
                    copy.wait()
                else:
                    m.arrive(("t", q, us), tile)
                m.send(("X", q, us), tile, tile, p.at(ctx=p.xn))
                m.send(("Y", q, us), tile, tile, p.at(ctx=p.yn))
                relays.append((q, us))
                if n >= 2:
                    yield
                    relay(*relays.pop(0))
            while relays:
                yield
                relay(*relays.pop(0))
            yield
            for q, us in sources:
                even = (q + us) % 2 == 0
                m.arrive(("Y" if even else "X", q, us), row(q, p.yn if even else p.xn, us))
                m.arrive(("Z", q, us), row(q, p.dg, us))

        def relay(q, us):
            if (q + us) % 2 == 0:
                tile = row(q, p.xn, us)
                m.arrive(("X", q, us), tile)
                m.send(("Z", q, us), tile, tile, p.at(ctx=p.yn))
            else:
                tile = row(q, p.yn, us)
                m.arrive(("Y", q, us), tile)
                m.send(("Z", q, us), tile, tile, p.at(ctx=p.xn))

        def feed():
            mine = gall.at[p.dp * 4 + p.ctx]
            copy = m.local("F", gu_ref.at[p.dp * 4 + p.ctx], mine)
            decays = m.local("D", dec_ref, dall.at[p.dp * 4 + p.ctx])
            spots = [(q, c, i) for i, c in enumerate((p.ctx, p.xn, p.yn, p.dg)) for q in range(2)][1:]
            for q, c, i in spots:
                dp = p.dp if q == 0 else p.other
                m.send(("d", q, i), dec_ref, dall.at[p.dp * 4 + p.ctx], p.at(dp=dp, ctx=c))
                m.send(("f", q, i), gu_ref.at[dp * 4 + c], mine, p.at(dp=dp, ctx=c))
            for _ in range(5):
                yield
            for q, c, i in spots:
                dp = p.dp if q == 0 else p.other
                m.arrive(("d", q, i), dall.at[dp * 4 + c])
                m.arrive(("f", q, i), gall.at[dp * 4 + c])
            copy.wait()
            decays.wait()

        return [
            attn(),
            later(line_gather(m, "h", hid_ref, hall, 6), 1),
            later(feed(), 2),
        ]

    def quarter_of(oall, part, c):
        return oall.at[part, :, pl.ds(pl.multiple_of(c * quarter, quarter), quarter)]

    def out_rows_go(m, ow_ref, oall):
        p = m.place
        u = p.uly
        head_dp, head_u = lax.rem(p.ctx, 2), p.dp * 2 + lax.div(p.ctx, 2)
        found = []
        for j in range(4):
            there = oall.at[u, :, pl.ds(j * quarter, quarter)]
            away = pltpu.make_async_remote_copy(
                src_ref=ow_ref.at[j],
                dst_ref=there,
                send_sem=m.send_sems.at[m.number(("S", j))],
                recv_sem=m.recv_sems.at[m.number(("o", u))],
                device_id=(head_dp, j, head_u),
                device_id_type=MESH,
            )
            here = (ow_ref.at[j], there, m.send_sems.at[m.number("O")])
            own = (head_dp == p.dp) & (p.ctx == j) & (head_u == u)
            found.append((own, away, here))
        return found

    def out_start(m, ow_ref, oall):
        for own, away, here in out_rows_go(m, ow_ref, oall):

            @pl.when(own)
            def _(here=here):
                copy = pltpu.make_async_copy(*here)
                copy.start()
                copy.wait()

            pl.when(jnp.logical_not(own))(away.start)

    def out_share(m, ow_ref, oall):
        p = m.place
        u = p.uly
        for us in range(4):
            mine = (u // 2 == p.dp) & (2 * (u % 2) + p.dp == p.ctx) & (us == u)

            @pl.when(jnp.logical_not(mine))
            def _(us=us):
                m.arrive(("o", us), quarter_of(oall, us, p.ctx))

        mine = quarter_of(oall, pl.ds(0, 4), p.ctx)
        m.send("ox", mine, mine, p.at(ctx=p.xn))
        m.send("oy", mine, mine, p.at(ctx=p.yn))
        for own, away, _ in out_rows_go(m, ow_ref, oall):
            pl.when(jnp.logical_not(own))(away.wait_send)

    def out_relay(m, oall):
        p = m.place
        low, high = pl.ds(0, 2), pl.ds(2, 2)
        m.arrive("ox", quarter_of(oall, pl.ds(0, 4), p.xn))
        m.send("o0", quarter_of(oall, low, p.xn), quarter_of(oall, low, p.xn), p.at(ctx=p.yn))
        m.arrive("oy", quarter_of(oall, pl.ds(0, 4), p.yn))
        m.send("o1", quarter_of(oall, high, p.yn), quarter_of(oall, high, p.yn), p.at(ctx=p.xn))

    def out_end(m, oall):
        p = m.place
        m.arrive("o0", quarter_of(oall, pl.ds(0, 2), p.dg))
        m.arrive("o1", quarter_of(oall, pl.ds(2, 2), p.dg))

    def kernel(
        stage, hid_ref, cot_ref, dec_ref, pk_ref, ow_ref, gu_ref, wd_ref,
        w_all, s1_all, w2d, q_ref, k_ref, v_ref, sw_ref, w_ref, mask_ref, st_ref, reach_ref, tail_ref, cum_ref,
        gain_ref, hn_ref, hi_ref, ga_ref, res_ref, s2_all, top_all, gu_all, wd_all,
        wall, s1, oall, dall, gall, dec8, cols8, upd, upds, ret, part, sib, right, left, s2, send, recv,
    ):
        uly = lax.axis_index(ULY)
        names = {}
        place = Place(uly)
        greet(everyone(place))
        stage.need(0)
        common = Mover(place, names, send, recv)
        ctx = place.ctx

        def for_each(body):
            for u in range(4):
                pl.when(uly == u)(functools.partial(body, u))

        spread = []
        for u in range(4):
            for tag, own, slot in (
                ("g", gall, lambda b: gu_all.at[:, b]),
                ("e", wd_ref, lambda b: wd_all.at[b]),
            ):
                m = Mover(Place(u), names, send, recv, lambda slot=slot: slot(0))
                spread.append((u, m, line_spread(m, tag, own, slot)))

        def spread_on(u):
            for v, _, stream in spread:
                if u == v:
                    next(stream, 0)

        def first(u):
            m = Mover(Place(u), names, send, recv)

            def spread_stage():
                out_start(Mover(Place(u), names, send, recv), ow_ref, oall)
                spread_on(u)
                yield

            together(
                [
                    *start_streams(m, hid_ref, dec_ref, pk_ref, gu_ref, s1, dall, wall, gall),
                    later(spread_stage(), 8),
                ]
            )
            m.finish()

        for_each(first)
        keep = [common.local("w", wall, w_all)]

        table = wall[:, cols - 128 : cols].astype(F32).T
        first_gain = 128 - 32
        gain_ref[...] = table[first_gain : first_gain + 8]

        def norm_one(i, carry):
            b, at = lax.div(i, 4), pl.ds(pl.multiple_of(lax.rem(i, 4) * 32, 32), 32)
            normed, _ = normalize(s1[b, at, :].astype(F32))
            s1[b, at, :] = (normed * gain_ref[0:1, :]).astype(BF16)
            return carry

        lax.fori_loop(0, 32, norm_one, 0)
        keep.append(common.local("W", s1, s1_all))

        for i in range(8):
            dec8[i : i + 1, :] = dall[i, pl.ds(place.dp, 1), :]
        upper = lax.broadcasted_iota(jnp.int32, (block, block), 0) <= lax.broadcasted_iota(
            jnp.int32, (block, block), 1
        )
        cum_ref[...] = jnp.dot(
            dec8[...], upper.astype(F32), precision=lax.Precision.HIGHEST, preferred_element_type=F32
        )
        for s in range(2):
            dec8[s : s + 1, :] = cum_ref[pl.ds(4 * s + ctx, 1), :]
        cols8[...] = dec8[...].T
        for s in range(2):
            column = cols8[:, s : s + 1]
            reach_ref[s] = jnp.exp(column) * scale
            tail_ref[s] = jnp.exp(dec8[s : s + 1, block - 1 : block] - column)

        whole = [
            Mover(Place(u), names, send, recv, lambda: quarter_of(oall, pl.ds(0, 4), 0))
            for u in range(4)
        ]
        for_each(lambda u: out_share(whole[u], ow_ref, oall))

        for s in range(2):
            lhs = s1[4 * s : 4 * s + 4].reshape(block, width)
            q_ref[s] = matmul(lhs, wall[:, :key]).astype(BF16)
            k_ref[s] = matmul(lhs, wall[:, key : 2 * key]).astype(BF16)
            rest = matmul(lhs, wall[:, 2 * key :])
            v_ref[s] = rest[:, :val].astype(BF16)
            sw_ref[pl.ds(s * block, block), :] = rest[:, val : 2 * val]
        out_relay(common, oall)
        for_each(spread_on)
        for s in range(2):
            k_tail = (k_ref[s].astype(F32) * tail_ref[s]).astype(BF16)
            upd[s] = dot_t(k_tail, v_ref[s]).astype(BF16)
        states = plane_gather(
            common, "t", upd, upds, state_slot, (pl.ds(0, 1), pl.ds(1, 1)), pair=False
        )
        next(states)

        def intra(c, carry):
            s, h = lax.div(c, 2), lax.rem(c, 2)
            at = pl.ds(pl.multiple_of(h * half, half), half)
            here = pl.ds(pl.multiple_of(c * half, half), half)
            gap = cols8[at, :]
            column = jnp.where(s == 0, gap[:, 0:1], gap[:, 1:2])
            gap = column - dec8[pl.ds(s, 1), :]
            t = lax.broadcasted_iota(jnp.int32, (half, block), 0) + h * half
            later_on = t >= lax.broadcasted_iota(jnp.int32, (half, block), 1)
            mask = jnp.where(later_on, jnp.exp(jnp.minimum(gap, 0.0)), 0.0) * scale
            mask_ref[s, at, :] = mask
            weights = (dot_nt(q_ref[s, at, :], k_ref[s]) * mask).astype(BF16)
            w_ref[s, at, :] = weights
            ret[here, :] = matmul(weights, v_ref[s])
            return carry

        lax.fori_loop(0, 2, intra, 0)
        next(states)
        lax.fori_loop(2, 4, intra, 0)
        out_end(common, oall)
        for i in range(4):
            w2d[i * out_rows : (i + 1) * out_rows, :] = oall[i]
        for _ in states:
            pass
        for s in range(2):
            factors = block_factors(cum_ref, ctx, s, False)
            total = factors[0] * upds[0, s].astype(F32)
            for j in range(1, 4):
                total = total + factors[j] * upds[j, s].astype(F32)
            st_ref[s] = total.astype(BF16)

        def outer(c, carry):
            s, h = lax.div(c, 2), lax.rem(c, 2)
            at = pl.ds(pl.multiple_of(h * half, half), half)
            here = pl.ds(pl.multiple_of(c * half, half), half)
            retained = ret[here, :] + reach_ref[s, at, :] * matmul(q_ref[s, at, :], st_ref[s])
            normed, inverse = normalize(retained)
            hn_ref[here, :] = normed
            hi_ref[here, :] = inverse
            pre = sw_ref[here, :]
            gated = (pre * jax.nn.sigmoid(pre) * normed.astype(BF16).astype(F32)).astype(BF16)
            ga_ref[here, :] = gated
            for n in range(4):
                cut = pl.ds(n * quarter, quarter)
                value = matmul(gated, w2d[:, cut]).astype(BF16)
                part[pl.ds(2 * c, 2), :, cut] = value.reshape(2, tokens, quarter)
            return carry

        lax.fori_loop(0, 4, outer, 0)
        stage.put(*range(2, 17))

        def reduce(u):
            m = Mover(Place(u), names, send, recv)
            low = tokens // 2

            def spread_stage():
                spread_on(u)
                yield

            together(
                [
                    line_reduce(m, "s", lambda i: part.at[i], res_ref, sib, right, left),
                    plane_gather(
                        m, "C", cot_ref, top_all, token_slot, (pl.ds(0, low), pl.ds(low, low))
                    ),
                    later(spread_stage(), 2),
                ]
            )
            m.finish()

        for_each(reduce)

        def norm_two(i, carry):
            at = pl.ds(pl.multiple_of(i * 16, 16), 16)
            residual = hid_ref[at, :].astype(F32) + res_ref[at, :]
            res_ref[at, :] = residual
            normed, _ = normalize(residual)
            s2[at, :] = (normed * gain_ref[1:2, :]).astype(BF16)
            return carry

        lax.fori_loop(0, tokens // 16, norm_two, 0)
        low = tokens // 2
        for _ in plane_gather(
            common, "k", s2, s2_all, token_slot, (pl.ds(0, low), pl.ds(low, low))
        ):
            pass

        def last(u):
            spread_on(u)
            whole[u].finish()
            for v, m, _ in spread:
                if u == v:
                    m.finish()

        for_each(last)
        for copy in keep:
            copy.wait()
        common.finish()
        assert len(names) <= N_SEMS

    return staged_call(
        kernel,
        "forward",
        [
            (hidden, True), (cot, False), (decay, False), (packed, False), (outw, False), (gu, False), (w_down, False)
        ],
        [
            ((width, cols), BF16, False),
            ((8, tokens, width), BF16, False),
            ((4 * out_rows, width), BF16, True),
            ((2, block, key), BF16, True),
            ((2, block, key), BF16, True),
            ((2, block, val), BF16, True),
            ((both, val), F32, True),
            ((2, block, block), BF16, True),
            ((2, block, block), F32, True),
            ((2, key, val), BF16, True),
            ((2, block, 1), F32, True),
            ((2, block, 1), F32, True),
            ((8, block), F32, True),
            ((8, width), F32, True),
            ((both, val), F32, True),
            ((both, 1), F32, True),
            ((both, val), BF16, True),
            ((tokens, width), F32, True),
            ((8, tokens, width), BF16, False),
            ((8, tokens, width), BF16, False),
            ((8, 4, rows, ff2), BF16, False),
            ((4, out_rows, width), BF16, False),
        ],
        [
            ((width, cols), BF16),
            ((8, tokens, width), BF16),
            ((4, out_rows, width), BF16),
            ((8, 2, block), F32),
            ((8, rows, ff2), BF16),
            ((8, block), F32),
            ((block, 8), F32),
            ((2, key, val), BF16),
            ((4, 2, key, val), BF16),
            ((both, val), F32),
            ((8, tokens, width), BF16),
            ((4, tokens, width), BF16),
            ((4, tokens, width), BF16),
            ((4, tokens, width), BF16),
            ((tokens, width), BF16),
        ],
        1,
    )


def feed_forward(scaled, top, w_gu, w_dn, residual, cot, gains):
    _, tokens, width = scaled.shape
    out_rows = w_dn.shape[1]
    rows, ff2 = w_gu.shape[2:]
    ff = ff2 // 2
    block = 4 * tokens

    def kernel(
        stage, s2_ref, top_ref, gu_ref, wd_ref, res_ref, cot_ref, gain_ref, grad, grad_low, term, dout, lo, ggu,
        w_d, prod, grad_gu, part, down, total, sib, sums, got, got2, right, left, send, recv,
    ):
        uly = lax.axis_index(ULY)
        names = {}
        p = Place(uly)
        greet(line_partners(p) + plane_partners(p)[1:])
        common = Mover(p, names, send, recv)
        movers = [
            Mover(Place(u), names, send, recv, lambda: halves_of_columns(right.at[0], 0))
            for u in range(4)
        ]
        lines = [
            line_reduce(m, "d", lambda b: down.at[b], dout, None, right, left, halves_of_columns)
            for m in movers
        ]

        def for_each(body):
            for u in range(4):
                pl.when(uly == u)(functools.partial(body, u))

        stage.need(0, 1, 2, 3)
        for i in range(4):
            w_d[i * out_rows : (i + 1) * out_rows, :] = wd_ref[i]

        def weights():
            return gu_ref[...].reshape(32 * rows, ff2)

        def tokens_of(s):
            here = pl.ds(pl.multiple_of(s * block, block), block)
            lhs = s2_ref[pl.ds(4 * s, 4)].reshape(block, width)
            pre = matmul(lhs, weights())
            gate_pre, up_pre = pre[:, :ff], pre[:, ff:]
            grad_product = dot_nt(top_ref[pl.ds(4 * s, 4)].reshape(block, width), w_d[...])
            sigma = jax.nn.sigmoid(gate_pre)
            act = gate_pre * sigma
            prod[here, :] = (act * up_pre).astype(BF16)
            slope = sigma * (1.0 + gate_pre * (1.0 - sigma))
            grad_gu[here, :ff] = (grad_product * up_pre * slope).astype(BF16)
            grad_gu[here, ff:] = (grad_product * act).astype(BF16)

        def tokens_back(s):
            here = pl.ds(pl.multiple_of(s * block, block), block)

            def back(n, carry):
                at = pl.ds(pl.multiple_of(n * 512, 512), 512)
                right_side = gu_ref[pl.ds(2 * n, 2)].reshape(512, ff2)
                value = dot_nt(grad_gu[here, :], right_side).astype(BF16)
                part[pl.ds(4 * s, 4), :, at] = value.reshape(4, tokens, 512)
                return carry

            lax.fori_loop(0, width // 512, back, 0)

        reduced = plane_reduce(common, "s", part, total, sib, sums, got, got2)
        tokens_of(p.other)
        tokens_of(p.dp)

        def down_grad(n, carry):
            at = pl.ds(pl.multiple_of(n * 512, 512), 512)
            value = dot_t(prod[...], top_ref[:, :, at].reshape(2 * block, 512)).astype(BF16)
            for i in range(4):
                down[i, :, at] = value[i * out_rows : (i + 1) * out_rows]
            return carry

        lax.fori_loop(0, width // 512, down_grad, 0)
        for_each(lambda u: next(lines[u]))
        tokens_back(p.other)
        next(reduced)
        tokens_back(p.dp)
        next(reduced)
        for_each(lambda u: next(lines[u]))

        def up_grad(n, carry):
            at = pl.ds(pl.multiple_of(n * 4 * rows, 4 * rows), 4 * rows)
            value = dot_t(s2_ref[:, :, at].reshape(2 * block, 4 * rows), grad_gu[...])
            ggu[n] = value.astype(BF16).reshape(4, rows, ff2)
            return carry

        lax.fori_loop(0, 8, up_grad, 0)
        stage.put(5)
        for_each(lambda u: next(lines[u]))
        next(reduced)

        def out_part(n, carry):
            at = pl.ds(pl.multiple_of(n * 512, 512), 512)
            value = matmul(prod[...], w_d[:, at]).astype(BF16)
            lo[:, :, at] = value.reshape(8, tokens, 512)
            return carry

        lax.fori_loop(0, width // 512, out_part, 0)
        stage.put(4)
        for _ in reduced:
            pass
        stage.need(4, 5, 6)

        def back(i, carry):
            at = pl.ds(pl.multiple_of(i * 16, 16), 16)
            normed, inverse = normalize(res_ref[at, :])
            scaled_grad = total[at, :]
            value = cot_ref[at, :].astype(F32) + norm_back(
                scaled_grad * gain_ref[1:2, :], normed, inverse
            )
            grad[at, :] = value
            grad_low[at, :] = value.astype(BF16)
            return carry + jnp.sum(scaled_grad * normed, axis=0, keepdims=True)

        term[...] = lax.fori_loop(0, tokens // 16, back, jnp.zeros((1, width), F32))

        def last(u):
            for _ in lines[u]:
                pass
            movers[u].finish()

        for_each(last)
        common.finish()
        assert len(names) <= N_SEMS

    return staged_call(
        kernel,
        "feed_forward",
        [(array, True) for array in (scaled, top, w_gu, w_dn, residual, cot, gains)],
        [
            ((tokens, width), F32, True),
            ((tokens, width), BF16, True),
            ((1, width), F32, True),
            ((out_rows, width), F32, True),
            ((8, tokens, width), BF16, True),
            ((8, 4, rows, ff2), BF16, True),
        ],
        [
            ((4 * out_rows, width), BF16),
            ((2 * block, ff), BF16),
            ((2 * block, ff2), BF16),
            ((8, tokens, width), BF16),
            ((4, out_rows, width), BF16),
            ((tokens, width), F32),
            ((4, tokens, width), BF16),
            ((4, tokens, width), BF16),
            ((2, tokens, width), BF16),
            ((tokens, width), BF16),
            ((4, out_rows, width), BF16),
            ((4, out_rows, width), BF16),
        ],
        3,
    )


def attention_back(
    own, lo, ggu, w_out, gated, normed, inverse, swish, q, k, v, weights, mask, state_in, reach, tail, cum
):
    tokens, width = own.shape
    both, val = gated.shape
    block, key = q.shape[1:]
    rows, cols = ggu.shape[3:]
    piece = w_out.shape[0] // 4
    half = block // 2
    at_v, at_s = 2 * key, 2 * key + val

    def kernel(
        stage, own_ref, lo_ref, g_ref, wo_ref, ga_ref, hn_ref, hi_ref, sw_ref, q_ref, k_ref, v_ref, w_ref, mask_ref, st_ref,
        reach_ref, tail_ref, cum_ref, cat_ref, total, gout, gsum,
        gy, gr, gs, gq, gk, gv, gst, gsts, sib, chip, got, got2, right, left, send, recv,
    ):
        uly = lax.axis_index(ULY)
        names = {}
        place = Place(uly)
        greet(line_partners(place) + plane_partners(place)[1:])
        stage.need(0, 1, 2)
        common = Mover(place, names, send, recv)
        movers = [Mover(Place(u), names, send, recv, lambda: right.at[0, 0]) for u in range(4)]
        ways = [
            line_reduce(
                movers[u],
                "f",
                lambda b: g_ref.at[:, :, b],
                gsum,
                None,
                right,
                left,
                lambda view, i: view.at[i],
            )
            for u in range(4)
        ]

        def for_each(body):
            for u in range(4):
                pl.when(uly == u)(functools.partial(body, u))

        def first(u):
            def sums():
                yield
                next(ways[u])
                yield
                yield
                next(ways[u])

            m = Mover(Place(u), names, send, recv)
            together(
                [
                    plane_reduce(m, "s", lo_ref, total, sib, chip, got, got2),
                    sums(),
                    line_gather(m, "k", own_ref, gy),
                ]
            )
            m.finish()

        for_each(first)

        stage.put(1)
        stage.need(*range(3, 17))

        def chunk(c):
            return pl.ds(pl.multiple_of(c * half, half), half)

        def gradients(c, carry):
            at = chunk(c)
            grad = gy[pl.ds(2 * c, 2)].reshape(half, width)
            gg = dot_nt(grad, wo_ref[...])
            pre = sw_ref[at, :]
            sigma = jax.nn.sigmoid(pre)
            head = hn_ref[at, :]
            low = head.astype(BF16).astype(F32)
            cat_ref[at, at_s : at_s + val] = (
                gg * low * (sigma * (1.0 + pre * (1.0 - sigma)))
            ).astype(BF16)
            gh = (gg * (pre * sigma)).astype(BF16).astype(F32)
            mean = jnp.mean(gh * head, axis=-1, keepdims=True)
            grad_retained = (hi_ref[at, :] * (gh - head * mean)).astype(BF16)
            gr[at, :] = grad_retained
            s = lax.div(c, 2)
            part = pl.ds(pl.multiple_of(lax.rem(c, 2) * half, half), half)
            gs[at, :] = (dot_nt(grad_retained, v_ref[s]) * mask_ref[s, part, :]).astype(BF16)
            return carry

        lax.fori_loop(0, both // half, gradients, 0)
        for s in range(2):
            at = pl.ds(s * block, block)
            reached = (q_ref[s].astype(F32) * reach_ref[s]).astype(BF16)
            gst[s] = dot_t(reached, gr[at, :]).astype(BF16)
        states = plane_gather(
            common, "t", gst, gsts, state_slot, (pl.ds(0, 1), pl.ds(1, 1)), pair=False
        )
        next(states)
        for_each(lambda u: next(ways[u]))

        for s in range(2):
            at = pl.ds(s * block, block)
            gq[at, :] = jnp.dot(gs[at, :], k_ref[s], preferred_element_type=F32)
            gk[at, :] = dot_t(gs[at, :], q_ref[s])
        next(states)
        for s in range(2):
            at = pl.ds(s * block, block)
            gv[at, :] = dot_t(w_ref[s], gr[at, :])

        def out_grad(n, carry):
            at = pl.ds(pl.multiple_of(n * 512, 512), 512)
            grad = gy[:, :, at].reshape(both, 512)
            value = dot_t(ga_ref[...], grad).astype(BF16)
            for i in range(4):
                gout[i, :, at] = value[i * piece : (i + 1) * piece]
            return carry

        lax.fori_loop(0, width // 512, out_grad, 0)
        stage.put(2)
        for _ in states:
            pass
        for s in range(2):
            at = pl.ds(s * block, block)
            factors = block_factors(cum_ref, place.ctx, s, True)
            update = factors[0] * gsts[0, s].astype(F32)
            for j in range(1, 4):
                update = update + factors[j] * gsts[j, s].astype(F32)
            update = update.astype(BF16)
            grad = gr[at, :]
            cat_ref[at, :key] = (gq[at, :] + reach_ref[s] * dot_nt(grad, st_ref[s])).astype(BF16)
            cat_ref[at, key:at_v] = (gk[at, :] + tail_ref[s] * dot_nt(v_ref[s], update)).astype(BF16)
            cat_ref[at, at_v:at_s] = (
                gv[at, :] + tail_ref[s] * jnp.dot(k_ref[s], update, preferred_element_type=F32)
            ).astype(BF16)

        def last(u):
            for _ in ways[u]:
                pass
            movers[u].finish()

        for_each(last)
        common.finish()
        assert len(names) <= N_SEMS

    arrays = (own, lo, ggu, w_out, gated, normed, inverse, swish, q, k, v, weights, mask, state_in, reach, tail, cum)
    return staged_call(
        kernel,
        "attention_back",
        [(array, True) for array in arrays],
        [
            ((both, 2 * key + 2 * val), BF16, True),
            ((tokens, width), F32, True),
            ((4, piece, width), BF16, True),
            ((2, 4, rows, cols), BF16, True),
        ],
        [
            ((8, tokens, width), BF16),
            ((both, val), BF16),
            ((both, block), BF16),
            ((both, key), F32),
            ((both, key), F32),
            ((both, val), F32),
            ((2, key, val), BF16),
            ((4, 2, key, val), BF16),
            ((4, tokens, width), BF16),
            ((4, tokens, width), BF16),
            ((2, tokens, width), BF16),
            ((tokens, width), BF16),
            ((4, 2, 4, rows, cols), BF16),
            ((4, 2, 4, rows, cols), BF16),
        ],
        7,
    )


def last_exchange(grad_cat, w_all, scaled, gout, gffn, inputs, term):
    tokens, width = inputs.shape
    both, cols = grad_cat.shape
    block = both // 2
    out_rows = gout.shape[1]
    quarter = width // 4
    rows, ff2 = gffn.shape[1:]

    def streams(
        m, line, tile, o_ref, f_ref, in_ref, t_ref, out, gall, oall, fall, gains,
        gotx, goty, gotx2, goty2, oxs, oys, ox2, oy2, away,
    ):
        p = m.place
        u = p.uly

        def attn():
            for t in range(4):
                m.arrive(("gx", 1, t), gotx.at[1, t])
                add_up(gotx.at[1, t], [tile(0, p.yn, t), gotx.at[1, t]])
                m.send(("gy2", t), gotx.at[1, t], goty2.at[t], p.at(ctx=p.yn))
                m.arrive(("gy", 1, t), goty.at[1, t])
                add_up(goty.at[1, t], [tile(1, p.xn, t), goty.at[1, t]])
                m.send(("gx2", t), goty.at[1, t], gotx2.at[t], p.at(ctx=p.xn))
            yield
            yield
            for t in range(4):
                for dp, got, got2, tags in (
                    (0, gotx, goty2, ("gx", "gy2")),
                    (1, goty, gotx2, ("gy", "gx2")),
                ):
                    m.arrive((tags[0], 0, t), got.at[0, t])
                    m.arrive((tags[1], t), got2.at[t])
                    add_up(got.at[0, t], [tile(dp, p.ctx, t), got.at[0, t], got2.at[t]])
                    there = gall.at[p.dp * 4 + u]
                    if t == u:

                        @pl.when(p.dp == dp)
                        def _(got=got, there=there):
                            here = pltpu.make_async_copy(
                                got.at[0, u], there, m.send_sems.at[m.number("G")]
                            )
                            here.start()
                            here.wait()

                        @pl.when(p.dp != dp)
                        def _(got=got, there=there, dp=dp):
                            m.remote(
                                ("gc", u), got.at[0, u], there, (dp, p.ctx, u)
                            ).start()
                    else:
                        k = m.number(("gs", dp, t))
                        copies = []
                        for q in range(2):
                            copies.append(
                                pltpu.make_async_remote_copy(
                                    src_ref=got.at[0, t],
                                    dst_ref=there,
                                    send_sem=m.send_sems.at[k],
                                    recv_sem=m.recv_sems.at[m.number(("g", q, u))],
                                    device_id=(dp, p.ctx, t),
                                    device_id_type=MESH,
                                )
                            )
                        pl.when(p.dp == dp)(copies[0].start)
                        pl.when(p.dp != dp)(copies[1].start)
                        m.sent.append(copies[0])
            for _ in range(6):
                yield
            m.remote(("gc", u), gotx.at[0, u], gotx.at[0, u], p.at(dp=p.other)).wait_send()
            m.arrive(("gc", u), gall.at[p.other * 4 + u])
            for us in range(4):
                if us != u:
                    m.arrive(("g", 0, us), gall.at[p.dp * 4 + us])
                    m.arrive(("g", 1, us), gall.at[p.other * 4 + us])

        def out_proj():
            def column(ref, part, c):
                return ref.at[part, :, pl.ds(pl.multiple_of(c * quarter, quarter), quarter)]

            low, high = pl.ds(0, 2), pl.ds(2, 2)
            for i, (cx, cy) in ((1, (p.dg, p.dg)), (0, (p.xn, p.yn))):
                m.send(("ox", i), column(o_ref, low, cx), oxs.at[i], p.at(ctx=p.xn))
                m.send(("oy", i), column(o_ref, high, cy), oys.at[i], p.at(ctx=p.yn))
            yield
            m.arrive(("ox", 1), oxs.at[1])
            for t in range(2):
                add_up(oxs.at[1, t], [column(o_ref, t, p.yn), oxs.at[1, t]])
            m.send("oy2", oxs.at[1], oy2, p.at(ctx=p.yn))
            m.arrive(("oy", 1), oys.at[1])
            for t in range(2):
                add_up(oys.at[1, t], [column(o_ref, 2 + t, p.xn), oys.at[1, t]])
            m.send("ox2", oys.at[1], ox2, p.at(ctx=p.xn))
            yield
            m.arrive(("ox", 0), oxs.at[0])
            m.arrive(("oy", 0), oys.at[0])
            m.arrive("oy2", oy2)
            m.arrive("ox2", ox2)
            home_dp, home_ctx = u // 2, 2 * (u % 2) + p.dp
            here_all = []
            for us in range(4):
                got, got2 = (oxs, oy2) if us < 2 else (oys, ox2)
                t = us % 2
                add_up(got.at[0, t], [column(o_ref, us, p.ctx), got.at[0, t], got2.at[t]])
                own = (home_dp == p.dp) & (home_ctx == p.ctx) & (us == u)
                there = oall.at[p.ctx]
                here = pltpu.make_async_copy(
                    got.at[0, t], there, m.send_sems.at[m.number("O")]
                )

                @pl.when(own)
                def _(here=here):
                    here.start()
                    here.wait()

                for j in range(4):
                    copy = pltpu.make_async_remote_copy(
                        src_ref=got.at[0, t],
                        dst_ref=there,
                        send_sem=m.send_sems.at[m.number(("os", us))],
                        recv_sem=m.recv_sems.at[m.number(("o", j))],
                        device_id=(home_dp, home_ctx, us),
                        device_id_type=MESH,
                    )
                    pl.when(jnp.logical_not(own) & (p.ctx == j))(copy.start)
                here_all.append((own, copy))
            yield
            head_dp, head_u = lax.rem(p.ctx, 2), p.dp * 2 + lax.div(p.ctx, 2)
            for j in range(4):
                mine = (head_dp == p.dp) & (p.ctx == j) & (head_u == u)

                @pl.when(jnp.logical_not(mine))
                def _(j=j):
                    m.arrive(("o", j), oall.at[j])

            for own, copy in here_all:
                pl.when(jnp.logical_not(own))(copy.wait_send)

        def feed():
            mine = fall.at[p.dp * 4 + p.ctx]
            copy = m.local("F", f_ref.at[p.dp * 4 + p.ctx], mine)
            spots = [(q, c, i) for i, c in enumerate((p.ctx, p.xn, p.yn, p.dg)) for q in range(2)][1:]
            for q, c, i in spots:
                dp = p.dp if q == 0 else p.other
                m.send(("f", q, i), f_ref.at[dp * 4 + c], mine, p.at(dp=dp, ctx=c))
            for _ in range(4):
                yield
            for q, c, i in spots:
                dp = p.dp if q == 0 else p.other
                m.arrive(("f", q, i), fall.at[dp * 4 + c])
            copy.wait()

        def tokens_stream():
            yield from line

            def body(i, total):
                at = pl.ds(pl.multiple_of(i * 16, 16), 16)
                values = in_ref[at, :].astype(F32)
                normed, _ = normalize(values)
                return total + jnp.sum(out[at, :] * normed, axis=0, keepdims=True)

            total = lax.fori_loop(0, tokens // 16, body, jnp.zeros((1, width), F32))
            row = lax.broadcasted_iota(jnp.int32, (8, width), 0)
            gains[...] = jnp.where(
                row == 0,
                jnp.broadcast_to(total, (8, width)),
                jnp.where(row == 1, jnp.broadcast_to(t_ref[...], (8, width)), 0.0),
            )
            for i, device in enumerate((p.at(dp=p.other), p.at(ctx=p.xn), p.at(ctx=p.yn))):
                m.remote(("n", i), gains, away.at[i], device).start()
                yield
                m.remote(("n", i), gains, away.at[i], device).wait()
                gains[...] = gains[...] + away[i]
            copies = [
                m.remote(("N", u, other), gains, away.at[3 + u], p.at(uly=other))
                for other in range(4)
                if other != u
            ]
            for copy in copies:
                copy.start()
            yield
            mine = gains[...]
            for other in range(4):
                if other != u:
                    m.arrive(("N", other, u), away.at[3 + other])
                    mine = mine + away[3 + other]
            for copy in copies:
                copy.wait_send()
            gains[...] = mine

        return [
            attn(),
            tokens_stream(),
            later(out_proj(), 1),
            later(feed(), 5),
        ]

    def kernel(
        stage, cat_ref, wa_ref, s1_ref, o_ref, f_ref, in_ref, t_ref, out, gall, oall, fall, gains,
        grads, part, sib, right, left, gotx, goty, gotx2, goty2, oxs, oys, ox2, oy2, away, send, recv,
    ):
        uly = lax.axis_index(ULY)
        names = {}
        p = Place(uly)
        greet(everyone(p))
        stage.need(0, 2)
        common = Mover(p, names, send, recv)

        def for_each(body):
            for u in range(4):
                pl.when(uly == u)(functools.partial(body, u))

        def tile(dp, c, t):
            return grads.at[dp, c, pl.ds(t * rows, rows)]

        def weight_grad(dp, c):
            at = pl.ds(pl.multiple_of((dp * 4 + c) * 4 * rows, 4 * rows), 4 * rows)
            grads[dp, c] = dot_t(s1_ref[:, :, at].reshape(both, 4 * rows), cat_ref[...]).astype(BF16)

        def token_grad(i, carry):
            s = jnp.where(i < 4, p.other, p.dp)
            n = pl.ds(pl.multiple_of(lax.rem(i, 4) * quarter, quarter), quarter)
            rows_s = pl.ds(pl.multiple_of(s * block, block), block)
            value = dot_nt(cat_ref[rows_s, :], wa_ref[n, :cols]).astype(BF16)
            part[pl.ds(4 * s, 4), :, n] = value.reshape(4, tokens, quarter)
            return carry

        def to_x(i, c):
            weight_grad(0, c)
            for t in range(4):
                common.send(("gx", i, t), tile(0, c, t), gotx.at[i, t], p.at(ctx=p.xn))

        def to_y(i, c):
            weight_grad(1, c)
            for t in range(4):
                common.send(("gy", i, t), tile(1, c, t), goty.at[i, t], p.at(ctx=p.yn))

        to_x(1, p.dg)
        to_y(1, p.dg)
        stage.need(1)
        lax.fori_loop(0, 8, token_grad, 0)
        movers = [
            Mover(
                Place(u), names, send, recv, lambda: halves_of_rows(sib.at[0], 0), lambda: sib.at[0]
            )
            for u in range(4)
        ]
        lines = [
            line_reduce(m, "s", lambda i: part.at[i], out, sib, right, left) for m in movers
        ]
        for_each(lambda u: next(lines[u]))
        to_x(0, p.xn)
        to_y(0, p.yn)
        weight_grad(0, p.yn)
        weight_grad(1, p.xn)
        weight_grad(0, p.ctx)
        weight_grad(1, p.ctx)
        stage.need(3, 5, 6)

        def rest(u):
            m = Mover(Place(u), names, send, recv)
            together(
                streams(
                    m, lines[u], tile, o_ref, f_ref, in_ref, t_ref, out, gall, oall, fall, gains,
                    gotx, goty, gotx2, goty2, oxs, oys, ox2, oy2, away,
                )
            )
            m.finish()
            movers[u].finish()

        for_each(rest)
        common.finish()
        assert len(names) <= N_SEMS

    arrays = (grad_cat, w_all, scaled, gout, gffn, inputs, term)
    return staged_call(
        kernel,
        "last",
        [(array, i != 4) for i, array in enumerate(arrays)],
        [
            ((tokens, width), F32, True),
            ((8, rows, cols), BF16, False),
            ((4, out_rows, quarter), BF16, False),
            ((8, rows, ff2), BF16, False),
            ((8, width), F32, True),
        ],
        [
            ((2, 4, 4 * rows, cols), BF16),
            ((8, tokens, width), BF16),
            *[((4, tokens, width), BF16)] * 3,
            *[((2, 4, rows, cols), BF16)] * 2,
            *[((4, rows, cols), BF16)] * 2,
            *[((2, 2, out_rows, quarter), BF16)] * 2,
            *[((2, out_rows, quarter), BF16)] * 2,
            ((7, 8, width), F32),
        ],
        2,
    )


def local(
    hidden_in,
    cotangent,
    log_decay,
    w_query,
    w_key,
    w_value,
    w_swish,
    w_output,
    w_gate,
    w_up,
    w_down,
    gain_attn,
    gain_ffn,
):
    bf16, f32 = BF16, F32
    dp, ctx = lax.axis_index(DP), lax.axis_index(CTX)
    tokens = hidden_in.shape[1]
    width = hidden_in.shape[2]
    rows = w_query.shape[0]
    out_rows = w_output.shape[0]
    key, val, ff = KEY_DIM, VALUE_DIM, w_gate.shape[1] // 8

    gains = jnp.pad(jnp.stack([gain_attn, gain_ffn], axis=1), ((0, 0), (0, 30)))
    packed, outw, gate_up = pack(w_query, w_key, w_value, w_swish, w_output, w_gate, w_up, gains)
    block = 4 * tokens
    (
        w_all, scaled_one, w_out, q, k, v, swish_pre, weights, mask, state_in, reach, tail, cum,
        gains, head_normed, head_inverse, gated, residual, scaled_two, top_all, w_gu, w_dn,
    ) = forward(hidden_in[0], cotangent[0], log_decay[0], packed, outw, gate_up, w_down)
    gain_one = gains[0]
    grad_residual, grad_y, gain_two_term, grad_down, layer_part, ggu = feed_forward(
        scaled_two, top_all, w_gu, w_dn, residual, cotangent[0], gains
    )
    inputs = hidden_in[0].astype(f32)
    grad_cat, out_part, g_out, ggu = attention_back(
        grad_y,
        layer_part,
        ggu.reshape(2, 4, 4, rows, 2 * ff),
        w_out,
        gated,
        head_normed,
        head_inverse,
        swish_pre,
        q,
        k,
        v,
        weights,
        mask,
        state_in,
        reach,
        tail,
        cum,
    )
    layer_out = residual + out_part
    gs1, gcat, g_out, ggu, gain_terms = last_exchange(
        grad_cat,
        w_all,
        scaled_one,
        g_out,
        ggu.reshape(8, rows, 2 * ff),
        hidden_in[0],
        gain_two_term,
    )
    normed_one, inverse_one = normalize(inputs)
    grad_input = grad_residual + norm_back(gs1 * gain_one, normed_one, inverse_one)

    grad_query, grad_key, grad_value, grad_swish, grad_output, grad_gate, grad_up = unpack(
        gcat, g_out, ggu
    )
    me = dp * 16 + ctx * 4 + lax.axis_index(ULY)
    gain_terms = lax.dynamic_slice_in_dim(gain_terms, me * rows, rows, axis=1)
    return (
        layer_out[None],
        grad_input[None],
        grad_query,
        grad_key,
        grad_value,
        grad_swish,
        grad_output,
        grad_gate,
        grad_up,
        grad_down,
        gain_terms[0],
        gain_terms[1],
    )


def solution(mesh):
    shape = mesh.shape
    planned = (shape[DP], shape[CTX], shape[ULY]) == (2, 4, 4)
    tokens = P(DP, (CTX, ULY), None)
    weight = P(EVERYWHERE, None)
    gain = P(EVERYWHERE)
    return jax.shard_map(
        local if planned else local_any,
        mesh=mesh,
        in_specs=(tokens, tokens, P(DP, ULY, CTX), *[weight] * 8, gain, gain),
        out_specs=(tokens, tokens, *[weight] * 8, gain, gain),
        check_vma=False,
    )
```

```python
import functools
import math

import jax
import jax.numpy as jnp
from jax import lax
from jax.experimental import pallas as pl
from jax.experimental.pallas import tpu as pltpu
from jax.sharding import PartitionSpec as P

RETENTION_HEADS = 8
KEY_DIM = 256
VALUE_DIM = 432


EPSILON = 1e-06
DP, CTX, ULY = "dp", "ctx", "ulysses"
EVERYWHERE = (DP, CTX, ULY)


def entering(value, axis, join, neutral, backward):
    count, mine = (lax.axis_size(axis), lax.axis_index(axis))
    pieces = jax.tree.map(lambda part: lax.all_gather(part, axis), value)
    if backward:
        pieces = jax.tree.map(lambda part: part[::-1], pieces)
        mine = count - 1 - mine
    subtotal = jax.tree.map(
        lambda part, zero: jnp.full_like(part, 0) + jnp.asarray(zero, part.dtype), value, neutral
    )

    def step(position, subtotal):
        longer = join(subtotal, jax.tree.map(lambda part: part[position], pieces))
        return jax.tree.map(lambda new, old: jnp.where(position < mine, new, old), longer, subtotal)

    return lax.fori_loop(0, count - 1, step, subtotal)


def normalize(values):
    inverse = lax.rsqrt(jnp.mean(values * values, axis=-1, keepdims=True) + EPSILON)
    return (values * inverse, inverse)


def norm_back(grad_normed, normed, inverse):
    return inverse * (grad_normed - normed * jnp.mean(grad_normed * normed, axis=-1, keepdims=True))


def swish_slope(values):
    sigma = jax.nn.sigmoid(values)
    return sigma * (1.0 + values * (1.0 - sigma))


def carry_forward(earlier, later):
    return (earlier[0] * later[0], later[0][:, None, None] * earlier[1] + later[1])


def carry_backward(earlier, later):
    return (earlier[0] * later[0], later[1] + later[0][:, None, None] * earlier[1])


def running_sum(values):
    size = values.shape[-1]
    upper = lax.broadcasted_iota(jnp.int32, (size, size), 0) <= lax.broadcasted_iota(
        jnp.int32, (size, size), 1
    )
    return jnp.dot(values, upper.astype(jnp.float32), precision=lax.Precision.HIGHEST)


def matmul(left, right):
    return jnp.dot(left, right, preferred_element_type=jnp.float32)


def local_any(
    hidden_in,
    cotangent,
    log_decay,
    w_query,
    w_key,
    w_value,
    w_swish,
    w_output,
    w_gate,
    w_up,
    w_down,
    gain_attn,
    gain_ffn,
):
    highest = lax.Precision.HIGHEST
    query_full, key_full, value_full, swish_full, output_full, gain_one = (
        lax.all_gather(w_query, EVERYWHERE, axis=0, tiled=True),
        lax.all_gather(w_key, EVERYWHERE, axis=0, tiled=True),
        lax.all_gather(w_value, EVERYWHERE, axis=0, tiled=True),
        lax.all_gather(w_swish, EVERYWHERE, axis=0, tiled=True),
        lax.all_gather(w_output, EVERYWHERE, axis=0, tiled=True),
        lax.all_gather(gain_attn, EVERYWHERE, axis=0, tiled=True),
    )
    inputs = hidden_in[0].astype(jnp.float32)
    tokens = inputs.shape[0]
    normed_one, inverse_one = normalize(inputs)
    scaled_one = (normed_one * gain_one.astype(jnp.float32)).astype(jnp.bfloat16)
    queries = (
        matmul(scaled_one, query_full)
        .astype(jnp.bfloat16)
        .reshape(tokens, RETENTION_HEADS, KEY_DIM)
    )
    keys_tok = (
        matmul(scaled_one, key_full).astype(jnp.bfloat16).reshape(tokens, RETENTION_HEADS, KEY_DIM)
    )
    values_tok = (
        matmul(scaled_one, value_full)
        .astype(jnp.bfloat16)
        .reshape(tokens, RETENTION_HEADS, VALUE_DIM)
    )
    swish_pre = matmul(scaled_one, swish_full)
    head_q, head_k, head_v = (
        lax.all_to_all(queries, ULY, split_axis=1, concat_axis=0, tiled=True),
        lax.all_to_all(keys_tok, ULY, split_axis=1, concat_axis=0, tiled=True),
        lax.all_to_all(values_tok, ULY, split_axis=1, concat_axis=0, tiled=True),
    )
    block = head_q.shape[0]
    scale = 1.0 / math.sqrt(KEY_DIM)
    cumulative = running_sum(log_decay[0])
    later = lax.broadcasted_iota(jnp.int32, (block, block), 0) >= lax.broadcasted_iota(
        jnp.int32, (block, block), 1
    )
    gap = cumulative[:, :, None] - cumulative[:, None, :]
    mask = jnp.where(later[None], jnp.exp(jnp.minimum(gap, 0.0)), 0.0) * scale
    scores = jnp.einsum("thd,shd->hts", head_q, head_k, preferred_element_type=jnp.float32)
    weights = (scores * mask).astype(jnp.bfloat16)
    intra = jnp.einsum("hts,she->the", weights, head_v, preferred_element_type=jnp.float32)
    query_f = head_q.astype(jnp.float32)
    key_f = head_k.astype(jnp.float32)
    value_f = head_v.astype(jnp.float32)
    tail = jnp.exp(cumulative[:, -1:] - cumulative).T[:, :, None]
    reach = jnp.exp(cumulative).T[:, :, None]
    update = jnp.einsum("shd,she->hde", key_f * tail, value_f, precision=highest)
    block_decay = jnp.exp(cumulative[:, -1])
    identity = (jnp.ones_like(block_decay), jnp.zeros_like(update))
    _, state_in = entering((block_decay, update), CTX, carry_forward, identity, False)
    retained = intra + scale * reach * jnp.einsum(
        "thd,hde->the", query_f, state_in, precision=highest
    )
    head_normed, head_inverse = normalize(retained)
    head_out = head_normed.astype(jnp.bfloat16)
    token_out = lax.all_to_all(
        head_out, ULY, split_axis=0, concat_axis=1, tiled=True
    ).reshape(tokens, RETENTION_HEADS * VALUE_DIM)
    token_out_f = token_out.astype(jnp.float32)
    swish_act = jax.nn.silu(swish_pre)
    gated = (swish_act * token_out_f).astype(jnp.bfloat16)
    residual = inputs + matmul(gated, output_full)
    gate_full, up_full, down_full, gain_two = (
        lax.all_gather(w_gate, EVERYWHERE, axis=0, tiled=True),
        lax.all_gather(w_up, EVERYWHERE, axis=0, tiled=True),
        lax.all_gather(w_down, EVERYWHERE, axis=0, tiled=True),
        lax.all_gather(gain_ffn, EVERYWHERE, axis=0, tiled=True),
    )
    normed_two, inverse_two = normalize(residual)
    scaled_two = (normed_two * gain_two.astype(jnp.float32)).astype(jnp.bfloat16)
    gate_pre = matmul(scaled_two, gate_full)
    up_pre = matmul(scaled_two, up_full)
    product = (jax.nn.silu(gate_pre) * up_pre).astype(jnp.bfloat16)
    layer_out = residual + matmul(product, down_full)
    grad_top = cotangent[0].astype(jnp.float32)
    grad_top_low = grad_top.astype(jnp.bfloat16)
    grad_product = matmul(grad_top_low, down_full.T)
    grad_down_term = matmul(product.T, grad_top_low)
    grad_gate_pre = (grad_product * up_pre * swish_slope(gate_pre)).astype(jnp.bfloat16)
    grad_up_pre = (grad_product * jax.nn.silu(gate_pre)).astype(jnp.bfloat16)
    grad_gate_term = matmul(scaled_two.T, grad_gate_pre)
    grad_up_term = matmul(scaled_two.T, grad_up_pre)
    grad_scaled_two = matmul(grad_gate_pre, gate_full.T) + matmul(grad_up_pre, up_full.T)
    grad_gain_two = jnp.sum(grad_scaled_two * normed_two, axis=0)
    grad_residual = grad_top + norm_back(
        grad_scaled_two * gain_two.astype(jnp.float32), normed_two, inverse_two
    )
    grad_gate, grad_up, grad_down, grad_gain_ffn = (
        lax.psum_scatter(grad_gate_term, EVERYWHERE, scatter_dimension=0, tiled=True),
        lax.psum_scatter(grad_up_term, EVERYWHERE, scatter_dimension=0, tiled=True),
        lax.psum_scatter(grad_down_term, EVERYWHERE, scatter_dimension=0, tiled=True),
        lax.psum_scatter(grad_gain_two, EVERYWHERE, scatter_dimension=0, tiled=True),
    )
    grad_y = grad_residual.astype(jnp.bfloat16)
    grad_output_term = matmul(gated.T, grad_y)
    grad_gated = matmul(grad_y, output_full.T)
    grad_swish_pre = (grad_gated * token_out_f * swish_slope(swish_pre)).astype(jnp.bfloat16)
    grad_token_out = (
        (grad_gated * swish_act).astype(jnp.bfloat16).reshape(tokens, RETENTION_HEADS, VALUE_DIM)
    )
    grad_swish_term = matmul(scaled_one.T, grad_swish_pre)
    grad_head_out = lax.all_to_all(
        grad_token_out, ULY, split_axis=1, concat_axis=0, tiled=True
    ).astype(jnp.float32)
    grad_retained = norm_back(grad_head_out, head_normed, head_inverse).astype(jnp.bfloat16)
    grad_retained_f = grad_retained.astype(jnp.float32)
    grad_weights = jnp.einsum(
        "the,she->hts", grad_retained, head_v, preferred_element_type=jnp.float32
    )
    grad_scores = (grad_weights * mask).astype(jnp.bfloat16)
    grad_state_in = scale * jnp.einsum(
        "thd,the->hde", query_f * reach, grad_retained_f, precision=highest
    )
    _, grad_update = entering((block_decay, grad_state_in), CTX, carry_backward, identity, True)
    grad_head_q = jnp.einsum(
        "hts,shd->thd", grad_scores, head_k, preferred_element_type=jnp.float32
    ) + scale * reach * jnp.einsum("the,hde->thd", grad_retained_f, state_in, precision=highest)
    grad_head_k = jnp.einsum(
        "hts,thd->shd", grad_scores, head_q, preferred_element_type=jnp.float32
    ) + tail * jnp.einsum("she,hde->shd", value_f, grad_update, precision=highest)
    grad_head_v = jnp.einsum(
        "hts,the->she", weights, grad_retained, preferred_element_type=jnp.float32
    ) + tail * jnp.einsum("shd,hde->she", key_f, grad_update, precision=highest)
    grad_queries, grad_keys, grad_values = (
        lax.all_to_all(
            grad_head_q.astype(jnp.bfloat16), ULY, split_axis=0, concat_axis=1, tiled=True
        ),
        lax.all_to_all(
            grad_head_k.astype(jnp.bfloat16), ULY, split_axis=0, concat_axis=1, tiled=True
        ),
        lax.all_to_all(
            grad_head_v.astype(jnp.bfloat16), ULY, split_axis=0, concat_axis=1, tiled=True
        ),
    )
    grad_queries = grad_queries.reshape(tokens, RETENTION_HEADS * KEY_DIM)
    grad_keys = grad_keys.reshape(tokens, RETENTION_HEADS * KEY_DIM)
    grad_values = grad_values.reshape(tokens, RETENTION_HEADS * VALUE_DIM)
    grad_query_term = matmul(scaled_one.T, grad_queries)
    grad_key_term = matmul(scaled_one.T, grad_keys)
    grad_value_term = matmul(scaled_one.T, grad_values)
    grad_scaled_one = (
        matmul(grad_queries, query_full.T)
        + matmul(grad_keys, key_full.T)
        + matmul(grad_values, value_full.T)
        + matmul(grad_swish_pre, swish_full.T)
    )
    grad_gain_one = jnp.sum(grad_scaled_one * normed_one, axis=0)
    grad_input = grad_residual + norm_back(
        grad_scaled_one * gain_one.astype(jnp.float32), normed_one, inverse_one
    )
    grad_query, grad_key, grad_value, grad_swish, grad_output, grad_gain_attn = (
        lax.psum_scatter(
            grad_query_term, EVERYWHERE, scatter_dimension=0, tiled=True
        ),
        lax.psum_scatter(grad_key_term, EVERYWHERE, scatter_dimension=0, tiled=True),
        lax.psum_scatter(
            grad_value_term, EVERYWHERE, scatter_dimension=0, tiled=True
        ),
        lax.psum_scatter(
            grad_swish_term, EVERYWHERE, scatter_dimension=0, tiled=True
        ),
        lax.psum_scatter(
            grad_output_term, EVERYWHERE, scatter_dimension=0, tiled=True
        ),
        lax.psum_scatter(grad_gain_one, EVERYWHERE, scatter_dimension=0, tiled=True),
    )
    return (
        layer_out[None],
        grad_input[None],
        grad_query,
        grad_key,
        grad_value,
        grad_swish,
        grad_output,
        grad_gate,
        grad_up,
        grad_down,
        grad_gain_attn,
        grad_gain_ffn,
    )


MESH = pl.DeviceIdType.MESH
BF16, F32 = jnp.bfloat16, jnp.float32
HBM, VMEM = pltpu.HBM, pltpu.VMEM
N_SEMS = 160


def dot_t(left, right):
    return lax.dot_general(left, right, (((0,), (0,)), ((), ())), preferred_element_type=F32)


def dot_nt(left, right):
    return lax.dot_general(left, right, (((1,), (1,)), ((), ())), preferred_element_type=F32)


def pair_dot(left_axis, right_axis, left, right):
    dims = (((left_axis,), (right_axis,)), ((0,), (0,)))
    return lax.dot_general(left, right, dims, preferred_element_type=F32)


class Place:
    def __init__(self, uly):
        self.dp, self.ctx, self.uly = lax.axis_index(DP), lax.axis_index(CTX), uly
        odd = lax.rem(self.ctx, 2)
        self.xn = self.ctx + 1 - 2 * odd
        self.yn = lax.rem(self.ctx + 2, 4)
        self.dg = self.yn + 1 - 2 * odd
        self.other = 1 - self.dp

    def at(self, dp=None, ctx=None, uly=None):
        return (
            self.dp if dp is None else dp,
            self.ctx if ctx is None else ctx,
            self.uly if uly is None else uly,
        )


class Mover:
    def __init__(self, place, names, send, recv, like=None, like_whole=None):
        self.like, self.like_whole = like, like_whole
        self.place, self.names, self.send_sems, self.recv_sems = place, names, send, recv
        self.sent, self.whole = [], []

    def number(self, name):
        return self.names.setdefault(name, len(self.names))

    def remote(self, name, src, dst, device):
        k = self.number(name)
        return pltpu.make_async_remote_copy(
            src_ref=src,
            dst_ref=dst,
            send_sem=self.send_sems.at[k],
            recv_sem=self.recv_sems.at[k],
            device_id=device,
            device_id_type=MESH,
        )

    def send(self, name, src, dst, device):
        copy = self.remote(name, src, dst, device)
        copy.start()
        self.sent.append(copy if self.like is None else name)

    def send_whole(self, name, src, dst, device):
        copy = self.remote(name, src, dst, device)
        copy.start()
        self.whole.append((copy if self.like is None else None, name, None))

    def arrive(self, name, dst):
        self.remote(name, dst, dst, self.place.at(dp=self.place.other)).wait_recv()

    def local(self, name, src, dst):
        copy = pltpu.make_async_copy(src, dst, self.send_sems.at[self.number(name)])
        copy.start()
        return copy

    def finish(self):
        for copy, name, _ in self.whole:
            if self.like is not None:
                ref = self.like_whole()
                copy = self.remote(name, ref, ref, self.place.at(dp=self.place.other))
            copy.wait_send()
        for copy in self.sent:
            if self.like is not None:
                ref = self.like()
                copy = self.remote(copy, ref, ref, self.place.at(dp=self.place.other))
            copy.wait_send()


def greet(devices, meanwhile=None):
    barrier = pltpu.get_barrier_semaphore()
    for device in devices:
        pl.semaphore_signal(barrier, inc=1, device_id=device, device_id_type=MESH)
    if meanwhile is not None:
        meanwhile()
    pl.semaphore_wait(barrier, len(devices))


def together(streams):
    streams = list(streams)
    while streams:
        left = []
        for stream in streams:
            if next(stream, 0) is None:
                left.append(stream)
        streams = left


def later(stream, stages):
    for _ in range(stages):
        yield
    yield from stream


def add_up(dst, sources, step=32):
    if len(dst.shape) > 2:
        for i in range(dst.shape[0]):
            add_up(dst.at[i], [source.at[i] for source in sources], step)
        return
    rows, columns = dst.shape
    by_rows = rows % step == 0
    step = step if by_rows else 256

    def body(i, carry):
        part = pl.ds(pl.multiple_of(i * step, step), step)
        at = (part, slice(None)) if by_rows else (slice(None), part)
        total = sources[0][at].astype(F32)
        for source in sources[1:]:
            total = total + source[at].astype(F32)
        dst[at] = total.astype(dst.dtype)
        return carry

    lax.fori_loop(0, (rows if by_rows else columns) // step, body, 0)


def halves_of_rows(view, i):
    rows = view.shape[0] // 2
    return view.at[pl.ds(i * rows, rows)]


def halves_of_columns(view, i):
    columns = view.shape[1] // 2
    return view.at[:, pl.ds(i * columns, columns)]


def line_gather(m, tag, own, out, pause=1):
    p = m.place
    u = p.uly
    mine = out.at[p.dp * 4 + u]
    copy = m.local((tag, "="), own, mine)
    for i in range(2):
        src, dst = halves_of_rows(own, i), halves_of_rows(mine, i)
        if u < 3:
            m.send((tag, "r", u, i), src, dst, p.at(uly=u + 1))
        if u > 0:
            m.send((tag, "l", u, i), src, dst, p.at(uly=u - 1))
    m.send((tag, "c", u), own, mine, p.at(dp=p.other))
    for _ in range(pause):
        yield
    for d in range(1, 4):
        for i in range(2):
            for way, b, onward in (("r", u - d, u + 1), ("l", u + d, u - 1)):
                if 0 <= b <= 3:
                    half = halves_of_rows(out.at[p.dp * 4 + b], i)
                    m.arrive((tag, way, b, i), half)
                    if 0 <= onward <= 3:
                        m.send((tag, way, b, i), half, half, p.at(uly=onward))
        for b in (u - d, u + d):
            if 0 <= b <= 3:
                block = out.at[p.dp * 4 + b]
                m.send((tag, "c", b), block, block, p.at(dp=p.other))
        yield
    for b in range(4):
        m.arrive((tag, "c", b), out.at[p.other * 4 + b])
    copy.wait()


def plane_gather(m, tag, own, out, slot, halves, pair=True):
    p = m.place

    def half(c, i):
        return slot(out, p.dp, c, halves[i])

    mine = slot(out, p.dp, p.ctx, None)
    copy = m.local((tag, "="), own, mine)
    m.send((tag, "x"), own, mine, p.at(ctx=p.xn))
    m.send((tag, "y"), own, mine, p.at(ctx=p.yn))
    if pair:
        m.send((tag, "c", 0), own, mine, p.at(dp=p.other))
    yield
    block = slot(out, p.dp, p.xn, None)
    m.arrive((tag, "x"), block)
    m.send((tag, "z", 0), half(p.xn, 0), half(p.xn, 0), p.at(ctx=p.yn))
    if pair:
        m.send((tag, "c", 1), block, block, p.at(dp=p.other))
    block = slot(out, p.dp, p.yn, None)
    m.arrive((tag, "y"), block)
    m.send((tag, "z", 1), half(p.yn, 1), half(p.yn, 1), p.at(ctx=p.xn))
    if pair:
        m.send((tag, "c", 2), block, block, p.at(dp=p.other))
    yield
    for i in range(2):
        block = half(p.dg, i)
        m.arrive((tag, "z", i), block)
        if pair:
            m.send((tag, "c", 3 + i), block, block, p.at(dp=p.other))
    yield
    if pair:
        for i, c in enumerate((p.ctx, p.xn, p.yn)):
            m.arrive((tag, "c", i), slot(out, p.other, c, None))
        for i in range(2):
            m.arrive((tag, "c", 3 + i), slot(out, p.other, p.dg, halves[i]))
    copy.wait()


def line_reduce(m, tag, part, out, sib, right, left, cut=halves_of_rows):
    p = m.place
    u = p.uly
    order = (3, 0, 2, 1) if u < 2 else (0, 3, 1, 2)
    for b in order if sib is not None else ():
        m.send_whole((tag, "c", b), part(p.other * 4 + b), sib.at[b], p.at(dp=p.other))
    met = set()

    def meet(b, i):
        if sib is None:
            return [cut(part(b), i)]
        if b not in met:
            met.add(b)
            m.arrive((tag, "c", b), sib.at[b])
        return [cut(part(p.dp * 4 + b), i), cut(sib.at[b], i)]

    def onward(way, b, i, arrived, there):
        terms = meet(b, i)
        if arrived is not None:
            arrived = cut(arrived.at[b], i)
            m.arrive((tag, way, b, i), arrived)
            terms.append(arrived)
        if len(terms) > 1:
            add_up(terms[-1], terms)
        away = cut((right if way == "r" else left).at[b], i)
        m.send((tag, way, b, i), terms[-1], away, p.at(uly=there))

    for slot in range(3):
        for b in range(4):
            for i in range(2):
                if u < b and u + 3 - b == slot:
                    onward("r", b, i, right if u > 0 else None, u + 1)
        for b in range(4):
            for i in range(2):
                if u > b and 3 - u + b == slot:
                    onward("l", b, i, left if u < 3 else None, u - 1)
        yield
    for i in range(2):
        terms = meet(u, i)
        if u > 0:
            m.arrive((tag, "r", u, i), cut(right.at[u], i))
            terms.append(cut(right.at[u], i))
        if u < 3:
            m.arrive((tag, "l", u, i), cut(left.at[u], i))
            terms.append(cut(left.at[u], i))
        add_up(cut(out, i), terms)


def plane_reduce(m, tag, part, out, sib, sums, got, got2):
    p = m.place
    rows = out.shape[0]
    halves = (pl.ds(0, rows // 2), pl.ds(rows // 2, rows // 2))
    order = (p.dg, p.xn, p.yn, p.ctx)
    for i, c in enumerate(order):
        m.send((tag, "c", i), part.at[p.other * 4 + c], sib.at[c], p.at(dp=p.other))
    yield
    for i, c in enumerate(order):
        m.arrive((tag, "c", i), sib.at[c])
        add_up(sums.at[c], [part.at[p.dp * 4 + c], sib.at[c]])
        if i == 0:
            m.send((tag, "x", 1), sums.at[c, halves[0]], got.at[1, halves[0]], p.at(ctx=p.xn))
            m.send((tag, "y", 1), sums.at[c, halves[1]], got.at[1, halves[1]], p.at(ctx=p.yn))
        if i == 1:
            m.send((tag, "x", 0), sums.at[c, halves[0]], got.at[0, halves[0]], p.at(ctx=p.xn))
        if i == 2:
            m.send((tag, "y", 0), sums.at[c, halves[1]], got.at[0, halves[1]], p.at(ctx=p.yn))
    yield
    m.arrive((tag, "x", 1), got.at[1, halves[0]])
    add_up(got.at[1, halves[0]], [sums.at[p.yn, halves[0]], got.at[1, halves[0]]])
    m.send((tag, "y2"), got.at[1, halves[0]], got2.at[halves[0]], p.at(ctx=p.yn))
    m.arrive((tag, "y", 1), got.at[1, halves[1]])
    add_up(got.at[1, halves[1]], [sums.at[p.xn, halves[1]], got.at[1, halves[1]]])
    m.send((tag, "x2"), got.at[1, halves[1]], got2.at[halves[1]], p.at(ctx=p.xn))
    yield
    m.arrive((tag, "x", 0), got.at[0, halves[0]])
    m.arrive((tag, "y", 0), got.at[0, halves[1]])
    yield
    m.arrive((tag, "y2"), got2.at[halves[0]])
    m.arrive((tag, "x2"), got2.at[halves[1]])
    add_up(out, [sums.at[p.ctx], got.at[0], got2])


class Stage:
    def __init__(self, loads, stores, first):
        self.loads, self.stores, self.started = loads, stores, []
        for i in (*first, *(i for i in loads if i not in first)):
            loads[i].start()

    def need(self, *which):
        for i in which:
            self.loads.pop(i).wait()

    def put(self, *which):
        for i in which:
            copy = self.stores.pop(i)
            copy.start()
            self.started.append(copy)

    def end(self):
        self.need(*list(self.loads))
        self.put(*list(self.stores))
        for copy in self.started:
            copy.wait()


def staged_call(kernel, name, ins, outs, scratch, remote=None, first=()):
    in_held = [i for i, (_, held) in enumerate(ins) if held]
    out_held = [i for i, (_, _, held) in enumerate(outs) if held]

    def body(*refs):
        given, results = list(refs[: len(ins)]), list(refs[len(ins) : len(ins) + len(outs)])
        rest = refs[len(ins) + len(outs) :]
        held, own, sems = rest[: len(in_held) + len(out_held)], rest[len(in_held) + len(out_held) : -1], rest[-1]
        loads, stores = {}, {}
        for j, i in enumerate(in_held):
            loads[i] = pltpu.make_async_copy(given[i], held[j], sems.at[j])
            given[i] = held[j]
        for j, i in enumerate(out_held, len(in_held)):
            stores[i] = pltpu.make_async_copy(held[j], results[i], sems.at[j])
            results[i] = held[j]
        stage = Stage(loads, stores, first)
        kernel(stage, *given, *results, *own)
        stage.end()

    params = {} if remote is None else {"collective_id": remote, "has_side_effects": True}
    return pl.pallas_call(
        body,
        out_shape=[jax.ShapeDtypeStruct(shape, kind) for shape, kind, _ in outs],
        in_specs=[pl.BlockSpec(memory_space=HBM)] * len(ins),
        out_specs=[pl.BlockSpec(memory_space=HBM)] * len(outs),
        scratch_shapes=[
            *[pltpu.VMEM(ins[i][0].shape, ins[i][0].dtype) for i in in_held],
            *[pltpu.VMEM(*outs[i][:2]) for i in out_held],
            *[pltpu.VMEM(shape, kind) for shape, kind in scratch],
            *([pltpu.SemaphoreType.DMA((N_SEMS,))] * 2 if remote is not None else []),
            pltpu.SemaphoreType.DMA((len(in_held) + len(out_held),)),
        ],
        name=name,
        compiler_params=pltpu.CompilerParams(vmem_limit_bytes=62 << 20, **params),
    )(*[array for array, _ in ins])


def everyone(p):
    me = p.dp * 16 + p.ctx * 4 + p.uly
    found = []
    for k in range(1, 32):
        there = lax.rem(me + k, 32)
        found.append((lax.div(there, 16), lax.rem(lax.div(there, 4), 4), lax.rem(there, 4)))
    return found


def line_partners(p):
    found = [p.at(dp=p.other)]
    for d in range(1, 4):
        there = lax.rem(p.uly + d, 4)
        found += [p.at(uly=there), p.at(dp=p.other, uly=there)]
    return found


def plane_partners(p):
    return [p.at(dp=p.other), p.at(ctx=p.xn), p.at(ctx=p.yn)]


def token_slot(out, dp, c, part):
    view = out.at[dp * 4 + c]
    return view if part is None else view.at[part]


def state_slot(out, dp, c, part):
    view = out.at[c]
    return view if part is None else view.at[part]


def finish(heads, outg, slices, residual, layer_part, grad, grad_scaled, hidden, gains, terms, down):
    rows, (_, out_rows, quarter) = heads.shape[1], outg.shape
    tokens, width = hidden.shape
    key, val, ff = KEY_DIM, VALUE_DIM, slices.shape[2] // 2

    def kernel(
        stage, hs, og, sl, res, part, gr, gs, hid, gain, term, down_in, q, k, v, s, o, g, u, y, x, down_out, n1, n2
    ):
        stage.need(3, 4, 5, 6, 7, 8, 9)
        me = lax.axis_index(DP) * 16 + lax.axis_index(CTX) * 4 + lax.axis_index(ULY)
        pair = pl.ds(pl.multiple_of(lax.div(me, 2) * 2 * rows, 2 * rows), 2 * rows)
        own = jnp.where(lax.rem(me, 2) == 0, term[:, pair][:, :rows], term[:, pair][:, rows:])
        n1[...] = own[0:1]
        n2[...] = own[1:2]

        def body(i, carry):
            at = pl.ds(pl.multiple_of(i * 16, 16), 16)
            y[at, :] = res[at, :] + part[at, :]
            normed, inverse = normalize(hid[at, :].astype(F32))
            x[at, :] = gr[at, :] + norm_back(gs[at, :] * gain[0:1, :], normed, inverse)
            return carry

        lax.fori_loop(0, tokens // 16, body, 0)
        stage.put(7, 8)
        stage.need(10)
        down_out[...] = down_in[...]
        stage.put(9)
        stage.need(0, 1, 2)
        for d in range(2):
            for z in range(4):
                h, i = 2 * z + d, 4 * d + z
                at = 0
                for ref, w in ((q, key), (k, key), (v, val), (s, val)):
                    ref[:, h * w : (h + 1) * w] = hs[i, :, at : at + w].astype(F32)
                    at += w
        stage.put(0, 1, 2, 3)
        for i in range(8):
            g[:, i * ff : (i + 1) * ff] = sl[i, :, :ff].astype(F32)
            u[:, i * ff : (i + 1) * ff] = sl[i, :, ff:].astype(F32)
        stage.put(5, 6)
        for j in range(4):
            o[:, j * quarter : (j + 1) * quarter] = og[j].astype(F32)

    widths = (8 * key, 8 * key, 8 * val, 8 * val, 4 * quarter, 8 * ff, 8 * ff)
    heights = (rows, rows, rows, rows, out_rows, rows, rows)
    arrays = (heads, outg, slices, residual, layer_part, grad, grad_scaled, hidden, gains, terms, down)
    shapes = [*zip(heights, widths), (tokens, width), (tokens, width), down.shape, (1, rows), (1, rows)]
    return staged_call(
        kernel,
        "finish",
        [(array, True) for array in arrays],
        [(shape, F32, True) for shape in shapes],
        [],
    )


def line_spread(m, tag, own, slot):
    u = m.place.uly
    copy = m.local((tag, 8), own, slot(u))
    if u < 3:
        m.send((tag, "r", u), own, slot(u), m.place.at(uly=u + 1))
    if u > 0:
        m.send((tag, "l", u), own, slot(u), m.place.at(uly=u - 1))
    copy.wait()
    yield
    for d in range(1, 4):
        for way, b, onward in (("r", u - d, u + 1), ("l", u + d, u - 1)):
            if 0 <= b <= 3:
                m.arrive((tag, way, b), slot(b))
                if 0 <= onward <= 3:
                    m.send((tag, way, b), slot(b), slot(b), m.place.at(uly=onward))
        yield


def block_factors(cum, ctx, s, backward):
    count = cum.shape[1]
    lasts = [cum[4 * s + j : 4 * s + j + 1, count - 1 : count] for j in range(4)]
    found = []
    for j in range(4):
        total = jnp.zeros((1, 1), F32)
        for i in range(4):
            inside = ((i > ctx) & (i < j)) if backward else ((i > j) & (i < ctx))
            total = total + jnp.where(inside, lasts[i], 0.0)
        right = (j > ctx) if backward else (j < ctx)
        found.append(jnp.where(right, jnp.exp(total), 0.0))
    return found


def forward(hidden, cot, decay, w_down, w_query, w_key, w_value, w_swish, w_output, w_gate, w_up, gains):
    tokens, width = hidden.shape
    key, val = KEY_DIM, VALUE_DIM
    rows, cols = w_query.shape[0], 2 * key + 2 * val + gains.shape[1]
    out_rows, quarter = w_output.shape[0], width // 4
    ff = w_gate.shape[1] // 8
    ff2 = 2 * ff
    block, both = 4 * tokens, 8 * tokens
    half = block // 2
    scale = 1.0 / math.sqrt(key)
    at_s = 2 * key + val

    def start_streams(m, hid_ref, dec_ref, pk_ref, gu_ref, hall, dall, wall, gall):
        p = m.place
        u = p.uly

        def row(q, c, us):
            dp = p.dp if q == 0 else p.other
            at = (dp * 16 + c * 4 + us) * rows
            return wall.at[pl.ds(pl.multiple_of(at, rows), rows)]

        def attn():
            sources = sorted(
                ((q, us) for q in range(2) for us in range(4)), key=lambda s: (abs(s[1] - u), s[0])
            )
            copy = None
            for q, to in sources:
                dp = p.dp if q == 0 else p.other
                mine = row(0, p.ctx, u)
                src = pk_ref.at[dp * 4 + to]
                if (q, to) == (0, u):
                    copy = m.local("T", src, mine)
                else:
                    m.send(("t", q, u), src, mine, p.at(dp=dp, uly=to))
            yield
            relays = []
            for n, (q, us) in enumerate(sources):
                tile = row(q, p.ctx, us)
                if (q, us) == (0, u):
                    copy.wait()
                else:
                    m.arrive(("t", q, us), tile)
                m.send(("X", q, us), tile, tile, p.at(ctx=p.xn))
                m.send(("Y", q, us), tile, tile, p.at(ctx=p.yn))
                relays.append((q, us))
                if n >= 2:
                    yield
                    relay(*relays.pop(0))
            while relays:
                yield
                relay(*relays.pop(0))
            yield
            for q, us in sources:
                even = (q + us) % 2 == 0
                m.arrive(("Y" if even else "X", q, us), row(q, p.yn if even else p.xn, us))
                m.arrive(("Z", q, us), row(q, p.dg, us))

        def relay(q, us):
            if (q + us) % 2 == 0:
                tile = row(q, p.xn, us)
                m.arrive(("X", q, us), tile)
                m.send(("Z", q, us), tile, tile, p.at(ctx=p.yn))
            else:
                tile = row(q, p.yn, us)
                m.arrive(("Y", q, us), tile)
                m.send(("Z", q, us), tile, tile, p.at(ctx=p.xn))

        def feed():
            mine = gall.at[p.dp * 4 + p.ctx]
            copy = m.local("F", gu_ref.at[p.dp * 4 + p.ctx], mine)
            decays = m.local("D", dec_ref, dall.at[p.dp * 4 + p.ctx])
            spots = [(q, c, i) for i, c in enumerate((p.ctx, p.xn, p.yn, p.dg)) for q in range(2)][1:]
            for q, c, i in spots:
                dp = p.dp if q == 0 else p.other
                m.send(("d", q, i), dec_ref, dall.at[p.dp * 4 + p.ctx], p.at(dp=dp, ctx=c))
                m.send(("f", q, i), gu_ref.at[dp * 4 + c], mine, p.at(dp=dp, ctx=c))
            for _ in range(5):
                yield
            for q, c, i in spots:
                dp = p.dp if q == 0 else p.other
                m.arrive(("d", q, i), dall.at[dp * 4 + c])
                m.arrive(("f", q, i), gall.at[dp * 4 + c])
            copy.wait()
            decays.wait()

        return [
            attn(),
            later(line_gather(m, "h", hid_ref, hall, 6), 1),
            later(feed(), 2),
        ]

    def quarter_of(oall, part, c):
        return oall.at[part, :, pl.ds(pl.multiple_of(c * quarter, quarter), quarter)]

    def out_rows_go(m, ow_ref, oall):
        p = m.place
        u = p.uly
        head_dp, head_u = lax.rem(p.ctx, 2), p.dp * 2 + lax.div(p.ctx, 2)
        found = []
        for j in range(4):
            there = oall.at[u, :, pl.ds(j * quarter, quarter)]
            away = pltpu.make_async_remote_copy(
                src_ref=ow_ref.at[j],
                dst_ref=there,
                send_sem=m.send_sems.at[m.number(("S", j))],
                recv_sem=m.recv_sems.at[m.number(("o", u))],
                device_id=(head_dp, j, head_u),
                device_id_type=MESH,
            )
            here = (ow_ref.at[j], there, m.send_sems.at[m.number("O")])
            own = (head_dp == p.dp) & (p.ctx == j) & (head_u == u)
            found.append((own, away, here))
        return found

    def out_start(m, ow_ref, oall):
        for own, away, here in out_rows_go(m, ow_ref, oall):

            @pl.when(own)
            def _(here=here):
                copy = pltpu.make_async_copy(*here)
                copy.start()
                copy.wait()

            pl.when(jnp.logical_not(own))(away.start)

    def out_share(m, ow_ref, oall):
        p = m.place
        u = p.uly
        for us in range(4):
            mine = (u // 2 == p.dp) & (2 * (u % 2) + p.dp == p.ctx) & (us == u)

            @pl.when(jnp.logical_not(mine))
            def _(us=us):
                m.arrive(("o", us), quarter_of(oall, us, p.ctx))

        mine = quarter_of(oall, pl.ds(0, 4), p.ctx)
        m.send("ox", mine, mine, p.at(ctx=p.xn))
        m.send("oy", mine, mine, p.at(ctx=p.yn))
        for own, away, _ in out_rows_go(m, ow_ref, oall):
            pl.when(jnp.logical_not(own))(away.wait_send)

    def out_relay(m, oall):
        p = m.place
        low, high = pl.ds(0, 2), pl.ds(2, 2)
        m.arrive("ox", quarter_of(oall, pl.ds(0, 4), p.xn))
        m.send("o0", quarter_of(oall, low, p.xn), quarter_of(oall, low, p.xn), p.at(ctx=p.yn))
        m.arrive("oy", quarter_of(oall, pl.ds(0, 4), p.yn))
        m.send("o1", quarter_of(oall, high, p.yn), quarter_of(oall, high, p.yn), p.at(ctx=p.xn))

    def out_end(m, oall):
        p = m.place
        m.arrive("o0", quarter_of(oall, pl.ds(0, 2), p.dg))
        m.arrive("o1", quarter_of(oall, pl.ds(2, 2), p.dg))

    def kernel(
        stage, hid_ref, cot_ref, dec_ref, wd_ref, wq_ref, wk_ref, wv_ref, ws_ref, wo_ref, wg_ref, wu_ref, n_ref,
        w_all, s1_all, w2d, q_ref, k_ref, v_ref, sw_ref, w_ref, mask_ref, st_ref, reach_ref, tail_ref, cum_ref,
        gain_ref, hn_ref, hi_ref, ga_ref, res_ref, s2_all, top_all, gu_all, wd_all,
        pk_ref, ow_ref, gu_ref, wall, s1, oall, dall, gall, dec8, cols8, upd, upds, ret, part, sib, right, left, s2, send, recv,
    ):
        uly = lax.axis_index(ULY)
        names = {}
        place = Place(uly)

        def pack():
            stage.need(*range(4, 12))
            for d in range(2):
                for z in range(4):
                    h, i = 2 * z + d, 4 * d + z
                    at = 0
                    for ref, w in ((wq_ref, key), (wk_ref, key), (wv_ref, val), (ws_ref, val)):
                        pk_ref[i, :, at : at + w] = ref[:, h * w : (h + 1) * w]
                        at += w
                    pk_ref[i, :, at:] = n_ref[...]
            for i in range(8):
                gu_ref[i, :, :ff] = wg_ref[:, i * ff : (i + 1) * ff]
                gu_ref[i, :, ff:] = wu_ref[:, i * ff : (i + 1) * ff]
            for j in range(4):
                ow_ref[j] = wo_ref[:, j * quarter : (j + 1) * quarter]

        greet(everyone(place), pack)
        stage.need(0)
        common = Mover(place, names, send, recv)
        ctx = place.ctx

        def for_each(body):
            for u in range(4):
                pl.when(uly == u)(functools.partial(body, u))

        spread = []
        for u in range(4):
            for tag, own, slot in (
                ("g", gall, lambda b: gu_all.at[:, b]),
                ("e", wd_ref, lambda b: wd_all.at[b]),
            ):
                m = Mover(Place(u), names, send, recv, lambda slot=slot: slot(0))
                spread.append((u, m, line_spread(m, tag, own, slot)))

        def spread_on(u):
            for v, _, stream in spread:
                if u == v:
                    next(stream, 0)

        def first(u):
            m = Mover(Place(u), names, send, recv)

            def spread_stage():
                out_start(Mover(Place(u), names, send, recv), ow_ref, oall)
                spread_on(u)
                yield

            together(
                [
                    *start_streams(m, hid_ref, dec_ref, pk_ref, gu_ref, s1, dall, wall, gall),
                    later(spread_stage(), 8),
                ]
            )
            m.finish()

        for_each(first)
        keep = [common.local("w", wall, w_all)]

        table = wall[:, cols - 128 : cols].astype(F32).T
        first_gain = 128 - 32
        gain_ref[...] = table[first_gain : first_gain + 8]

        def norm_one(i, carry):
            b, at = lax.div(i, 4), pl.ds(pl.multiple_of(lax.rem(i, 4) * 32, 32), 32)
            normed, _ = normalize(s1[b, at, :].astype(F32))
            s1[b, at, :] = (normed * gain_ref[0:1, :]).astype(BF16)
            return carry

        lax.fori_loop(0, 32, norm_one, 0)
        keep.append(common.local("W", s1, s1_all))

        for i in range(8):
            dec8[i : i + 1, :] = dall[i, pl.ds(place.dp, 1), :]
        upper = lax.broadcasted_iota(jnp.int32, (block, block), 0) <= lax.broadcasted_iota(
            jnp.int32, (block, block), 1
        )
        cum_ref[...] = jnp.dot(
            dec8[...], upper.astype(F32), precision=lax.Precision.HIGHEST, preferred_element_type=F32
        )
        for s in range(2):
            dec8[s : s + 1, :] = cum_ref[pl.ds(4 * s + ctx, 1), :]
        cols8[...] = dec8[...].T
        for s in range(2):
            column = cols8[:, s : s + 1]
            reach_ref[s] = jnp.exp(column) * scale
            tail_ref[s] = jnp.exp(dec8[s : s + 1, block - 1 : block] - column)

        whole = [
            Mover(Place(u), names, send, recv, lambda: quarter_of(oall, pl.ds(0, 4), 0))
            for u in range(4)
        ]
        for_each(lambda u: out_share(whole[u], ow_ref, oall))

        for s in range(2):
            lhs = s1[4 * s : 4 * s + 4].reshape(block, width)
            q_ref[s] = matmul(lhs, wall[:, :key]).astype(BF16)
            k_ref[s] = matmul(lhs, wall[:, key : 2 * key]).astype(BF16)
            rest = matmul(lhs, wall[:, 2 * key :])
            v_ref[s] = rest[:, :val].astype(BF16)
            sw_ref[pl.ds(s * block, block), :] = rest[:, val : 2 * val]
        out_relay(common, oall)
        for s in range(2):
            k_tail = (k_ref[s].astype(F32) * tail_ref[s]).astype(BF16)
            upd[s] = dot_t(k_tail, v_ref[s]).astype(BF16)
        states = plane_gather(
            common, "t", upd, upds, state_slot, (pl.ds(0, 1), pl.ds(1, 1)), pair=False
        )
        next(states)

        def intra(c, carry):
            s, h = lax.div(c, 2), lax.rem(c, 2)
            at = pl.ds(pl.multiple_of(h * half, half), half)
            here = pl.ds(pl.multiple_of(c * half, half), half)
            gap = cols8[at, :]
            column = jnp.where(s == 0, gap[:, 0:1], gap[:, 1:2])
            gap = column - dec8[pl.ds(s, 1), :]
            t = lax.broadcasted_iota(jnp.int32, (half, block), 0) + h * half
            later_on = t >= lax.broadcasted_iota(jnp.int32, (half, block), 1)
            mask = jnp.where(later_on, jnp.exp(jnp.minimum(gap, 0.0)), 0.0) * scale
            mask_ref[s, at, :] = mask
            weights = (dot_nt(q_ref[s, at, :], k_ref[s]) * mask).astype(BF16)
            w_ref[s, at, :] = weights
            ret[here, :] = matmul(weights, v_ref[s])
            return carry

        lax.fori_loop(0, 2, intra, 0)
        for_each(spread_on)
        next(states)
        lax.fori_loop(2, 4, intra, 0)
        out_end(common, oall)
        for i in range(4):
            w2d[i * out_rows : (i + 1) * out_rows, :] = oall[i]
        for _ in states:
            pass
        for s in range(2):
            factors = block_factors(cum_ref, ctx, s, False)
            total = factors[0] * upds[0, s].astype(F32)
            for j in range(1, 4):
                total = total + factors[j] * upds[j, s].astype(F32)
            st_ref[s] = total.astype(BF16)

        def outer(c, carry):
            s, h = lax.div(c, 2), lax.rem(c, 2)
            at = pl.ds(pl.multiple_of(h * half, half), half)
            here = pl.ds(pl.multiple_of(c * half, half), half)
            retained = ret[here, :] + reach_ref[s, at, :] * matmul(q_ref[s, at, :], st_ref[s])
            normed, inverse = normalize(retained)
            hn_ref[here, :] = normed
            hi_ref[here, :] = inverse
            pre = sw_ref[here, :]
            gated = (pre * jax.nn.sigmoid(pre) * normed.astype(BF16).astype(F32)).astype(BF16)
            ga_ref[here, :] = gated
            for n in range(4):
                cut = pl.ds(n * quarter, quarter)
                value = matmul(gated, w2d[:, cut]).astype(BF16)
                part[pl.ds(2 * c, 2), :, cut] = value.reshape(2, tokens, quarter)
            return carry

        lax.fori_loop(0, 4, outer, 0)
        stage.put(*range(2, 17))

        def reduce(u):
            m = Mover(Place(u), names, send, recv)
            low = tokens // 2

            def spread_stage():
                spread_on(u)
                yield

            together(
                [
                    line_reduce(m, "s", lambda i: part.at[i], res_ref, sib, right, left),
                    plane_gather(
                        m, "C", cot_ref, top_all, token_slot, (pl.ds(0, low), pl.ds(low, low))
                    ),
                    later(spread_stage(), 2),
                ]
            )
            m.finish()

        for_each(reduce)

        def norm_two(i, carry):
            at = pl.ds(pl.multiple_of(i * 16, 16), 16)
            residual = hid_ref[at, :].astype(F32) + res_ref[at, :]
            res_ref[at, :] = residual
            normed, _ = normalize(residual)
            s2[at, :] = (normed * gain_ref[1:2, :]).astype(BF16)
            return carry

        lax.fori_loop(0, tokens // 16, norm_two, 0)
        low = tokens // 2
        for _ in plane_gather(
            common, "k", s2, s2_all, token_slot, (pl.ds(0, low), pl.ds(low, low))
        ):
            pass

        def last(u):
            spread_on(u)
            whole[u].finish()
            for v, m, _ in spread:
                if u == v:
                    m.finish()

        for_each(last)
        for copy in keep:
            copy.wait()
        common.finish()
        assert len(names) <= N_SEMS

    return staged_call(
        kernel,
        "forward",
        [
            (hidden, True), (cot, False), (decay, False), (w_down, False), (w_query, True), (w_key, True),
            (w_value, True), (w_swish, True), (w_output, True), (w_gate, True), (w_up, True), (gains, True),
        ],
        [
            ((width, cols), BF16, False),
            ((8, tokens, width), BF16, False),
            ((4 * out_rows, width), BF16, True),
            ((2, block, key), BF16, True),
            ((2, block, key), BF16, True),
            ((2, block, val), BF16, True),
            ((both, val), F32, True),
            ((2, block, block), BF16, True),
            ((2, block, block), F32, True),
            ((2, key, val), BF16, True),
            ((2, block, 1), F32, True),
            ((2, block, 1), F32, True),
            ((8, block), F32, True),
            ((8, width), F32, True),
            ((both, val), F32, True),
            ((both, 1), F32, True),
            ((both, val), BF16, True),
            ((tokens, width), F32, True),
            ((8, tokens, width), BF16, False),
            ((8, tokens, width), BF16, False),
            ((8, 4, rows, ff2), BF16, False),
            ((4, out_rows, width), BF16, False),
        ],
        [
            ((8, rows, cols), BF16),
            ((4, out_rows, quarter), BF16),
            ((8, rows, ff2), BF16),
            ((width, cols), BF16),
            ((8, tokens, width), BF16),
            ((4, out_rows, width), BF16),
            ((8, 2, block), F32),
            ((8, rows, ff2), BF16),
            ((8, block), F32),
            ((block, 8), F32),
            ((2, key, val), BF16),
            ((4, 2, key, val), BF16),
            ((both, val), F32),
            ((8, tokens, width), BF16),
            ((4, tokens, width), BF16),
            ((4, tokens, width), BF16),
            ((4, tokens, width), BF16),
            ((tokens, width), BF16),
        ],
        1,
    )


def feed_forward(scaled, top, w_gu, w_dn, residual, cot, gains):
    _, tokens, width = scaled.shape
    out_rows = w_dn.shape[1]
    rows, ff2 = w_gu.shape[2:]
    ff = ff2 // 2
    block = 4 * tokens

    def kernel(
        stage, s2_ref, top_ref, gu_ref, wd_ref, res_ref, cot_ref, gain_ref, grad, grad_low, term, dout, lo, ggu,
        w_d, prod, grad_gu, part, down, total, sib, sums, got, got2, right, left, send, recv,
    ):
        uly = lax.axis_index(ULY)
        names = {}
        p = Place(uly)
        greet(line_partners(p) + plane_partners(p)[1:])
        common = Mover(p, names, send, recv)
        movers = [
            Mover(Place(u), names, send, recv, lambda: halves_of_columns(right.at[0], 0))
            for u in range(4)
        ]
        lines = [
            line_reduce(m, "d", lambda b: down.at[b], dout, None, right, left, halves_of_columns)
            for m in movers
        ]

        def for_each(body):
            for u in range(4):
                pl.when(uly == u)(functools.partial(body, u))

        stage.need(0, 2)

        def weights():
            return gu_ref[...].reshape(32 * rows, ff2)

        def tokens_of(s):
            here = pl.ds(pl.multiple_of(s * block, block), block)
            lhs = s2_ref[pl.ds(4 * s, 4)].reshape(block, width)
            pre = matmul(lhs, weights())
            gate_pre, up_pre = pre[:, :ff], pre[:, ff:]
            if 1 in stage.loads:
                stage.need(1, 3)
                for i in range(4):
                    w_d[i * out_rows : (i + 1) * out_rows, :] = wd_ref[i]
            grad_product = dot_nt(top_ref[pl.ds(4 * s, 4)].reshape(block, width), w_d[...])
            sigma = jax.nn.sigmoid(gate_pre)
            act = gate_pre * sigma
            prod[here, :] = (act * up_pre).astype(BF16)
            slope = sigma * (1.0 + gate_pre * (1.0 - sigma))
            grad_gu[here, :ff] = (grad_product * up_pre * slope).astype(BF16)
            grad_gu[here, ff:] = (grad_product * act).astype(BF16)

        def tokens_back(s):
            here = pl.ds(pl.multiple_of(s * block, block), block)

            value = dot_nt(grad_gu[here, :], weights()).astype(BF16)
            part[pl.ds(4 * s, 4)] = value.reshape(4, tokens, width)

        reduced = plane_reduce(common, "s", part, total, sib, sums, got, got2)
        tokens_of(p.other)
        tokens_of(p.dp)

        def down_grad(n, carry):
            at = pl.ds(pl.multiple_of(n * 512, 512), 512)
            value = dot_t(prod[...], top_ref[:, :, at].reshape(2 * block, 512)).astype(BF16)
            for i in range(4):
                down[i, :, at] = value[i * out_rows : (i + 1) * out_rows]
            return carry

        lax.fori_loop(0, width // 512, down_grad, 0)
        for_each(lambda u: next(lines[u]))
        tokens_back(p.other)
        next(reduced)
        tokens_back(p.dp)
        next(reduced)
        for_each(lambda u: next(lines[u]))

        def up_grad(n, carry):
            at = pl.ds(pl.multiple_of(n * 4 * rows, 4 * rows), 4 * rows)
            value = dot_t(s2_ref[:, :, at].reshape(2 * block, 4 * rows), grad_gu[...])
            ggu[n] = value.astype(BF16).reshape(4, rows, ff2)
            return carry

        lax.fori_loop(0, 8, up_grad, 0)
        stage.put(5)
        for_each(lambda u: next(lines[u]))
        next(reduced)

        def out_part(n, carry):
            at = pl.ds(pl.multiple_of(n * 512, 512), 512)
            value = matmul(prod[...], w_d[:, at]).astype(BF16)
            lo[:, :, at] = value.reshape(8, tokens, 512)
            return carry

        lax.fori_loop(0, width // 512, out_part, 0)
        stage.put(4)
        for _ in reduced:
            pass
        stage.need(4, 5, 6)

        def back(i, carry):
            at = pl.ds(pl.multiple_of(i * 16, 16), 16)
            normed, inverse = normalize(res_ref[at, :])
            scaled_grad = total[at, :]
            value = cot_ref[at, :].astype(F32) + norm_back(
                scaled_grad * gain_ref[1:2, :], normed, inverse
            )
            grad[at, :] = value
            grad_low[at, :] = value.astype(BF16)
            return carry + jnp.sum(scaled_grad * normed, axis=0, keepdims=True)

        term[...] = lax.fori_loop(0, tokens // 16, back, jnp.zeros((1, width), F32))

        def last(u):
            for _ in lines[u]:
                pass
            movers[u].finish()

        for_each(last)
        common.finish()
        assert len(names) <= N_SEMS

    return staged_call(
        kernel,
        "feed_forward",
        [(array, True) for array in (scaled, top, w_gu, w_dn, residual, cot, gains)],
        [
            ((tokens, width), F32, True),
            ((tokens, width), BF16, True),
            ((1, width), F32, True),
            ((out_rows, width), F32, True),
            ((8, tokens, width), BF16, True),
            ((8, 4, rows, ff2), BF16, True),
        ],
        [
            ((4 * out_rows, width), BF16),
            ((2 * block, ff), BF16),
            ((2 * block, ff2), BF16),
            ((8, tokens, width), BF16),
            ((4, out_rows, width), BF16),
            ((tokens, width), F32),
            ((4, tokens, width), BF16),
            ((4, tokens, width), BF16),
            ((2, tokens, width), BF16),
            ((tokens, width), BF16),
            ((4, out_rows, width), BF16),
            ((4, out_rows, width), BF16),
        ],
        3,
        (0, 2),
    )


def attention_back(
    own, lo, ggu, w_out, gated, normed, inverse, swish, q, k, v, weights, mask, state_in, reach, tail, cum
):
    tokens, width = own.shape
    both, val = gated.shape
    block, key = q.shape[1:]
    rows, cols = ggu.shape[3:]
    piece = w_out.shape[0] // 4
    half = block // 2
    at_v, at_s = 2 * key, 2 * key + val

    def kernel(
        stage, own_ref, lo_ref, g_ref, wo_ref, ga_ref, hn_ref, hi_ref, sw_ref, q_ref, k_ref, v_ref, w_ref, mask_ref, st_ref,
        reach_ref, tail_ref, cum_ref, cat_ref, total, gout, gsum,
        gy, gr, gs, gq, gk, gv, gst, gsts, sib, chip, got, got2, right, left, send, recv,
    ):
        uly = lax.axis_index(ULY)
        names = {}
        place = Place(uly)
        greet(line_partners(place) + plane_partners(place)[1:])
        stage.need(0, 1, 2)
        common = Mover(place, names, send, recv)
        movers = [Mover(Place(u), names, send, recv, lambda: right.at[0, 0]) for u in range(4)]
        ways = [
            line_reduce(
                movers[u],
                "f",
                lambda b: g_ref.at[:, :, b],
                gsum,
                None,
                right,
                left,
                lambda view, i: view.at[i],
            )
            for u in range(4)
        ]

        def for_each(body):
            for u in range(4):
                pl.when(uly == u)(functools.partial(body, u))

        def first(u):
            def sums():
                yield
                next(ways[u])
                yield
                yield
                next(ways[u])

            m = Mover(Place(u), names, send, recv)
            together(
                [
                    plane_reduce(m, "s", lo_ref, total, sib, chip, got, got2),
                    sums(),
                    line_gather(m, "k", own_ref, gy),
                ]
            )
            m.finish()

        for_each(first)

        stage.put(1)
        stage.need(*range(3, 17))

        def chunk(c):
            return pl.ds(pl.multiple_of(c * half, half), half)

        def gradients(c, carry):
            at = chunk(c)
            grad = gy[pl.ds(2 * c, 2)].reshape(half, width)
            gg = dot_nt(grad, wo_ref[...])
            pre = sw_ref[at, :]
            sigma = jax.nn.sigmoid(pre)
            head = hn_ref[at, :]
            low = head.astype(BF16).astype(F32)
            cat_ref[at, at_s : at_s + val] = (
                gg * low * (sigma * (1.0 + pre * (1.0 - sigma)))
            ).astype(BF16)
            gh = (gg * (pre * sigma)).astype(BF16).astype(F32)
            mean = jnp.mean(gh * head, axis=-1, keepdims=True)
            grad_retained = (hi_ref[at, :] * (gh - head * mean)).astype(BF16)
            gr[at, :] = grad_retained
            s = lax.div(c, 2)
            part = pl.ds(pl.multiple_of(lax.rem(c, 2) * half, half), half)
            gs[at, :] = (dot_nt(grad_retained, v_ref[s]) * mask_ref[s, part, :]).astype(BF16)
            return carry

        lax.fori_loop(0, both // half, gradients, 0)
        for s in range(2):
            at = pl.ds(s * block, block)
            reached = (q_ref[s].astype(F32) * reach_ref[s]).astype(BF16)
            gst[s] = dot_t(reached, gr[at, :]).astype(BF16)
        states = plane_gather(
            common, "t", gst, gsts, state_slot, (pl.ds(0, 1), pl.ds(1, 1)), pair=False
        )
        next(states)
        for_each(lambda u: next(ways[u]))

        for s in range(2):
            at = pl.ds(s * block, block)
            gq[at, :] = jnp.dot(gs[at, :], k_ref[s], preferred_element_type=F32)
            gk[at, :] = dot_t(gs[at, :], q_ref[s])
        next(states)
        for s in range(2):
            at = pl.ds(s * block, block)
            gv[at, :] = dot_t(w_ref[s], gr[at, :])

        def out_grad(n, carry):
            at = pl.ds(pl.multiple_of(n * 512, 512), 512)
            grad = gy[:, :, at].reshape(both, 512)
            value = dot_t(ga_ref[...], grad).astype(BF16)
            for i in range(4):
                gout[i, :, at] = value[i * piece : (i + 1) * piece]
            return carry

        lax.fori_loop(0, width // 512, out_grad, 0)
        stage.put(2)
        for _ in states:
            pass
        for s in range(2):
            at = pl.ds(s * block, block)
            factors = block_factors(cum_ref, place.ctx, s, True)
            update = factors[0] * gsts[0, s].astype(F32)
            for j in range(1, 4):
                update = update + factors[j] * gsts[j, s].astype(F32)
            update = update.astype(BF16)
            grad = gr[at, :]
            cat_ref[at, :key] = (gq[at, :] + reach_ref[s] * dot_nt(grad, st_ref[s])).astype(BF16)
            cat_ref[at, key:at_v] = (gk[at, :] + tail_ref[s] * dot_nt(v_ref[s], update)).astype(BF16)
            cat_ref[at, at_v:at_s] = (
                gv[at, :] + tail_ref[s] * jnp.dot(k_ref[s], update, preferred_element_type=F32)
            ).astype(BF16)

        def last(u):
            for _ in ways[u]:
                pass
            movers[u].finish()

        for_each(last)
        common.finish()
        assert len(names) <= N_SEMS

    arrays = (own, lo, ggu, w_out, gated, normed, inverse, swish, q, k, v, weights, mask, state_in, reach, tail, cum)
    return staged_call(
        kernel,
        "attention_back",
        [(array, True) for array in arrays],
        [
            ((both, 2 * key + 2 * val), BF16, True),
            ((tokens, width), F32, True),
            ((4, piece, width), BF16, True),
            ((2, 4, rows, cols), BF16, True),
        ],
        [
            ((8, tokens, width), BF16),
            ((both, val), BF16),
            ((both, block), BF16),
            ((both, key), F32),
            ((both, key), F32),
            ((both, val), F32),
            ((2, key, val), BF16),
            ((4, 2, key, val), BF16),
            ((4, tokens, width), BF16),
            ((4, tokens, width), BF16),
            ((2, tokens, width), BF16),
            ((tokens, width), BF16),
            ((4, 2, 4, rows, cols), BF16),
            ((4, 2, 4, rows, cols), BF16),
        ],
        7,
    )


def last_exchange(grad_cat, w_all, scaled, gout, gffn, inputs, term):
    tokens, width = inputs.shape
    both, cols = grad_cat.shape
    block = both // 2
    out_rows = gout.shape[1]
    quarter = width // 4
    rows, ff2 = gffn.shape[1:]

    def streams(
        m, line, tile, o_ref, f_ref, in_ref, t_ref, out, gall, oall, fall, gains,
        gotx, goty, gotx2, goty2, oxs, oys, ox2, oy2, away,
    ):
        p = m.place
        u = p.uly

        def attn():
            for t in range(4):
                m.arrive(("gx", 1, t), gotx.at[1, t])
                add_up(gotx.at[1, t], [tile(0, p.yn, t), gotx.at[1, t]])
                m.send(("gy2", t), gotx.at[1, t], goty2.at[t], p.at(ctx=p.yn))
                m.arrive(("gy", 1, t), goty.at[1, t])
                add_up(goty.at[1, t], [tile(1, p.xn, t), goty.at[1, t]])
                m.send(("gx2", t), goty.at[1, t], gotx2.at[t], p.at(ctx=p.xn))
            yield
            yield
            for t in range(4):
                for dp, got, got2, tags in (
                    (0, gotx, goty2, ("gx", "gy2")),
                    (1, goty, gotx2, ("gy", "gx2")),
                ):
                    m.arrive((tags[0], 0, t), got.at[0, t])
                    m.arrive((tags[1], t), got2.at[t])
                    add_up(got.at[0, t], [tile(dp, p.ctx, t), got.at[0, t], got2.at[t]])
                    there = gall.at[p.dp * 4 + u]
                    if t == u:

                        @pl.when(p.dp == dp)
                        def _(got=got, there=there):
                            here = pltpu.make_async_copy(
                                got.at[0, u], there, m.send_sems.at[m.number("G")]
                            )
                            here.start()
                            here.wait()

                        @pl.when(p.dp != dp)
                        def _(got=got, there=there, dp=dp):
                            m.remote(
                                ("gc", u), got.at[0, u], there, (dp, p.ctx, u)
                            ).start()
                    else:
                        k = m.number(("gs", dp, t))
                        copies = []
                        for q in range(2):
                            copies.append(
                                pltpu.make_async_remote_copy(
                                    src_ref=got.at[0, t],
                                    dst_ref=there,
                                    send_sem=m.send_sems.at[k],
                                    recv_sem=m.recv_sems.at[m.number(("g", q, u))],
                                    device_id=(dp, p.ctx, t),
                                    device_id_type=MESH,
                                )
                            )
                        pl.when(p.dp == dp)(copies[0].start)
                        pl.when(p.dp != dp)(copies[1].start)
                        m.sent.append(copies[0])
            for _ in range(6):
                yield
            m.remote(("gc", u), gotx.at[0, u], gotx.at[0, u], p.at(dp=p.other)).wait_send()
            m.arrive(("gc", u), gall.at[p.other * 4 + u])
            for us in range(4):
                if us != u:
                    m.arrive(("g", 0, us), gall.at[p.dp * 4 + us])
                    m.arrive(("g", 1, us), gall.at[p.other * 4 + us])

        def out_proj():
            def column(ref, part, c):
                return ref.at[part, :, pl.ds(pl.multiple_of(c * quarter, quarter), quarter)]

            low, high = pl.ds(0, 2), pl.ds(2, 2)
            for i, (cx, cy) in ((1, (p.dg, p.dg)), (0, (p.xn, p.yn))):
                m.send(("ox", i), column(o_ref, low, cx), oxs.at[i], p.at(ctx=p.xn))
                m.send(("oy", i), column(o_ref, high, cy), oys.at[i], p.at(ctx=p.yn))
            yield
            m.arrive(("ox", 1), oxs.at[1])
            for t in range(2):
                add_up(oxs.at[1, t], [column(o_ref, t, p.yn), oxs.at[1, t]])
            m.send("oy2", oxs.at[1], oy2, p.at(ctx=p.yn))
            m.arrive(("oy", 1), oys.at[1])
            for t in range(2):
                add_up(oys.at[1, t], [column(o_ref, 2 + t, p.xn), oys.at[1, t]])
            m.send("ox2", oys.at[1], ox2, p.at(ctx=p.xn))
            yield
            m.arrive(("ox", 0), oxs.at[0])
            m.arrive(("oy", 0), oys.at[0])
            m.arrive("oy2", oy2)
            m.arrive("ox2", ox2)
            home_dp, home_ctx = u // 2, 2 * (u % 2) + p.dp
            here_all = []
            for us in range(4):
                got, got2 = (oxs, oy2) if us < 2 else (oys, ox2)
                t = us % 2
                add_up(got.at[0, t], [column(o_ref, us, p.ctx), got.at[0, t], got2.at[t]])
                own = (home_dp == p.dp) & (home_ctx == p.ctx) & (us == u)
                there = oall.at[p.ctx]
                here = pltpu.make_async_copy(
                    got.at[0, t], there, m.send_sems.at[m.number("O")]
                )

                @pl.when(own)
                def _(here=here):
                    here.start()
                    here.wait()

                for j in range(4):
                    copy = pltpu.make_async_remote_copy(
                        src_ref=got.at[0, t],
                        dst_ref=there,
                        send_sem=m.send_sems.at[m.number(("os", us))],
                        recv_sem=m.recv_sems.at[m.number(("o", j))],
                        device_id=(home_dp, home_ctx, us),
                        device_id_type=MESH,
                    )
                    pl.when(jnp.logical_not(own) & (p.ctx == j))(copy.start)
                here_all.append((own, copy))
            yield
            head_dp, head_u = lax.rem(p.ctx, 2), p.dp * 2 + lax.div(p.ctx, 2)
            for j in range(4):
                mine = (head_dp == p.dp) & (p.ctx == j) & (head_u == u)

                @pl.when(jnp.logical_not(mine))
                def _(j=j):
                    m.arrive(("o", j), oall.at[j])

            for own, copy in here_all:
                pl.when(jnp.logical_not(own))(copy.wait_send)

        def feed():
            mine = fall.at[p.dp * 4 + p.ctx]
            copy = m.local("F", f_ref.at[p.dp * 4 + p.ctx], mine)
            spots = [(q, c, i) for i, c in enumerate((p.ctx, p.xn, p.yn, p.dg)) for q in range(2)][1:]
            for q, c, i in spots:
                dp = p.dp if q == 0 else p.other
                m.send(("f", q, i), f_ref.at[dp * 4 + c], mine, p.at(dp=dp, ctx=c))
            for _ in range(4):
                yield
            for q, c, i in spots:
                dp = p.dp if q == 0 else p.other
                m.arrive(("f", q, i), fall.at[dp * 4 + c])
            copy.wait()

        def tokens_stream():
            yield from line

            def body(i, total):
                at = pl.ds(pl.multiple_of(i * 16, 16), 16)
                values = in_ref[at, :].astype(F32)
                normed, _ = normalize(values)
                return total + jnp.sum(out[at, :] * normed, axis=0, keepdims=True)

            total = lax.fori_loop(0, tokens // 16, body, jnp.zeros((1, width), F32))
            row = lax.broadcasted_iota(jnp.int32, (8, width), 0)
            gains[...] = jnp.where(
                row == 0,
                jnp.broadcast_to(total, (8, width)),
                jnp.where(row == 1, jnp.broadcast_to(t_ref[...], (8, width)), 0.0),
            )
            for i, device in enumerate((p.at(dp=p.other), p.at(ctx=p.xn), p.at(ctx=p.yn))):
                m.remote(("n", i), gains, away.at[i], device).start()
                yield
                m.remote(("n", i), gains, away.at[i], device).wait()
                gains[...] = gains[...] + away[i]
            copies = [
                m.remote(("N", u, other), gains, away.at[3 + u], p.at(uly=other))
                for other in range(4)
                if other != u
            ]
            for copy in copies:
                copy.start()
            yield
            mine = gains[...]
            for other in range(4):
                if other != u:
                    m.arrive(("N", other, u), away.at[3 + other])
                    mine = mine + away[3 + other]
            for copy in copies:
                copy.wait_send()
            gains[...] = mine

        return [
            attn(),
            tokens_stream(),
            later(out_proj(), 1),
            later(feed(), 5),
        ]

    def kernel(
        stage, cat_ref, wa_ref, s1_ref, o_ref, f_ref, in_ref, t_ref, out, gall, oall, fall, gains,
        grads, part, sib, right, left, gotx, goty, gotx2, goty2, oxs, oys, ox2, oy2, away, send, recv,
    ):
        uly = lax.axis_index(ULY)
        names = {}
        p = Place(uly)
        greet(everyone(p))
        stage.need(0, 2)
        common = Mover(p, names, send, recv)

        def for_each(body):
            for u in range(4):
                pl.when(uly == u)(functools.partial(body, u))

        def tile(dp, c, t):
            return grads.at[dp, c, pl.ds(t * rows, rows)]

        def weight_grad(dp, c):
            at = pl.ds(pl.multiple_of((dp * 4 + c) * 4 * rows, 4 * rows), 4 * rows)
            grads[dp, c] = dot_t(s1_ref[:, :, at].reshape(both, 4 * rows), cat_ref[...]).astype(BF16)

        def token_grad(s):
            rows_s = pl.ds(pl.multiple_of(s * block, block), block)
            value = dot_nt(cat_ref[rows_s, :], wa_ref[:, :cols]).astype(BF16)
            part[pl.ds(4 * s, 4)] = value.reshape(4, tokens, width)

        def to_x(i, c):
            weight_grad(0, c)
            for t in range(4):
                common.send(("gx", i, t), tile(0, c, t), gotx.at[i, t], p.at(ctx=p.xn))

        def to_y(i, c):
            weight_grad(1, c)
            for t in range(4):
                common.send(("gy", i, t), tile(1, c, t), goty.at[i, t], p.at(ctx=p.yn))

        to_x(1, p.dg)
        to_y(1, p.dg)
        stage.need(1)
        token_grad(p.other)
        token_grad(p.dp)
        movers = [
            Mover(
                Place(u), names, send, recv, lambda: halves_of_rows(sib.at[0], 0), lambda: sib.at[0]
            )
            for u in range(4)
        ]
        lines = [
            line_reduce(m, "s", lambda i: part.at[i], out, sib, right, left) for m in movers
        ]
        for_each(lambda u: next(lines[u]))
        to_x(0, p.xn)
        to_y(0, p.yn)
        weight_grad(0, p.yn)
        weight_grad(1, p.xn)
        weight_grad(0, p.ctx)
        weight_grad(1, p.ctx)
        stage.need(3, 5, 6)

        def rest(u):
            m = Mover(Place(u), names, send, recv)
            together(
                streams(
                    m, lines[u], tile, o_ref, f_ref, in_ref, t_ref, out, gall, oall, fall, gains,
                    gotx, goty, gotx2, goty2, oxs, oys, ox2, oy2, away,
                )
            )
            m.finish()
            movers[u].finish()

        for_each(rest)
        common.finish()
        assert len(names) <= N_SEMS

    arrays = (grad_cat, w_all, scaled, gout, gffn, inputs, term)
    return staged_call(
        kernel,
        "last",
        [(array, i != 4) for i, array in enumerate(arrays)],
        [
            ((tokens, width), F32, True),
            ((8, rows, cols), BF16, False),
            ((4, out_rows, quarter), BF16, False),
            ((8, rows, ff2), BF16, False),
            ((8, width), F32, True),
        ],
        [
            ((2, 4, 4 * rows, cols), BF16),
            ((8, tokens, width), BF16),
            *[((4, tokens, width), BF16)] * 3,
            *[((2, 4, rows, cols), BF16)] * 2,
            *[((4, rows, cols), BF16)] * 2,
            *[((2, 2, out_rows, quarter), BF16)] * 2,
            *[((2, out_rows, quarter), BF16)] * 2,
            ((7, 8, width), F32),
        ],
        2,
        (0, 2),
    )


def local(
    hidden_in,
    cotangent,
    log_decay,
    w_query,
    w_key,
    w_value,
    w_swish,
    w_output,
    w_gate,
    w_up,
    w_down,
    gain_attn,
    gain_ffn,
):
    bf16, f32 = BF16, F32
    dp, ctx = lax.axis_index(DP), lax.axis_index(CTX)
    tokens = hidden_in.shape[1]
    width = hidden_in.shape[2]
    rows = w_query.shape[0]
    out_rows = w_output.shape[0]
    key, val, ff = KEY_DIM, VALUE_DIM, w_gate.shape[1] // 8

    gains = jnp.pad(jnp.stack([gain_attn, gain_ffn], axis=1), ((0, 0), (0, 30)))
    block = 4 * tokens
    (
        w_all, scaled_one, w_out, q, k, v, swish_pre, weights, mask, state_in, reach, tail, cum,
        gains, head_normed, head_inverse, gated, residual, scaled_two, top_all, w_gu, w_dn,
    ) = forward(
        hidden_in[0], cotangent[0], log_decay[0], w_down,
        w_query, w_key, w_value, w_swish, w_output, w_gate, w_up, gains,
    )
    grad_residual, grad_y, gain_two_term, grad_down, layer_part, ggu = feed_forward(
        scaled_two, top_all, w_gu, w_dn, residual, cotangent[0], gains
    )
    grad_cat, out_part, g_out, ggu = attention_back(
        grad_y,
        layer_part,
        ggu.reshape(2, 4, 4, rows, 2 * ff),
        w_out,
        gated,
        head_normed,
        head_inverse,
        swish_pre,
        q,
        k,
        v,
        weights,
        mask,
        state_in,
        reach,
        tail,
        cum,
    )
    gs1, gcat, g_out, ggu, gain_terms = last_exchange(
        grad_cat,
        w_all,
        scaled_one,
        g_out,
        ggu.reshape(8, rows, 2 * ff),
        hidden_in[0],
        gain_two_term,
    )
    (
        grad_query, grad_key, grad_value, grad_swish, grad_output, grad_gate, grad_up,
        layer_out, grad_input, grad_down, gain_one_term, gain_two_term,
    ) = finish(
        gcat, g_out, ggu, residual, out_part, grad_residual, gs1, hidden_in[0], gains, gain_terms, grad_down
    )
    return (
        layer_out[None],
        grad_input[None],
        grad_query,
        grad_key,
        grad_value,
        grad_swish,
        grad_output,
        grad_gate,
        grad_up,
        grad_down,
        gain_one_term[0],
        gain_two_term[0],
    )


def solution(mesh):
    shape = mesh.shape
    planned = (shape[DP], shape[CTX], shape[ULY]) == (2, 4, 4)
    tokens = P(DP, (CTX, ULY), None)
    weight = P(EVERYWHERE, None)
    gain = P(EVERYWHERE)
    return jax.shard_map(
        local if planned else local_any,
        mesh=mesh,
        in_specs=(tokens, tokens, P(DP, ULY, CTX), *[weight] * 8, gain, gain),
        out_specs=(tokens, tokens, *[weight] * 8, gain, gain),
        check_vma=False,
    )
```

```python
import functools
import math

import jax
import jax.numpy as jnp
from jax import lax
from jax.experimental import pallas as pl
from jax.experimental.pallas import tpu as pltpu
from jax.sharding import PartitionSpec as P

RETENTION_HEADS = 8
KEY_DIM = 256
VALUE_DIM = 432


EPSILON = 1e-06
DP, CTX, ULY = "dp", "ctx", "ulysses"
EVERYWHERE = (DP, CTX, ULY)


def entering(value, axis, join, neutral, backward):
    count, mine = (lax.axis_size(axis), lax.axis_index(axis))
    pieces = jax.tree.map(lambda part: lax.all_gather(part, axis), value)
    if backward:
        pieces = jax.tree.map(lambda part: part[::-1], pieces)
        mine = count - 1 - mine
    subtotal = jax.tree.map(
        lambda part, zero: jnp.full_like(part, 0) + jnp.asarray(zero, part.dtype), value, neutral
    )

    def step(position, subtotal):
        longer = join(subtotal, jax.tree.map(lambda part: part[position], pieces))
        return jax.tree.map(lambda new, old: jnp.where(position < mine, new, old), longer, subtotal)

    return lax.fori_loop(0, count - 1, step, subtotal)


def normalize(values):
    inverse = lax.rsqrt(jnp.mean(values * values, axis=-1, keepdims=True) + EPSILON)
    return (values * inverse, inverse)


def norm_back(grad_normed, normed, inverse):
    return inverse * (grad_normed - normed * jnp.mean(grad_normed * normed, axis=-1, keepdims=True))


def swish_slope(values):
    sigma = jax.nn.sigmoid(values)
    return sigma * (1.0 + values * (1.0 - sigma))


def carry_forward(earlier, later):
    return (earlier[0] * later[0], later[0][:, None, None] * earlier[1] + later[1])


def carry_backward(earlier, later):
    return (earlier[0] * later[0], later[1] + later[0][:, None, None] * earlier[1])


def running_sum(values):
    size = values.shape[-1]
    upper = lax.broadcasted_iota(jnp.int32, (size, size), 0) <= lax.broadcasted_iota(
        jnp.int32, (size, size), 1
    )
    return jnp.dot(values, upper.astype(jnp.float32), precision=lax.Precision.HIGHEST)


def matmul(left, right):
    return jnp.dot(left, right, preferred_element_type=jnp.float32)


def local_any(
    hidden_in,
    cotangent,
    log_decay,
    w_query,
    w_key,
    w_value,
    w_swish,
    w_output,
    w_gate,
    w_up,
    w_down,
    gain_attn,
    gain_ffn,
):
    highest = lax.Precision.HIGHEST
    query_full, key_full, value_full, swish_full, output_full, gain_one = (
        lax.all_gather(w_query, EVERYWHERE, axis=0, tiled=True),
        lax.all_gather(w_key, EVERYWHERE, axis=0, tiled=True),
        lax.all_gather(w_value, EVERYWHERE, axis=0, tiled=True),
        lax.all_gather(w_swish, EVERYWHERE, axis=0, tiled=True),
        lax.all_gather(w_output, EVERYWHERE, axis=0, tiled=True),
        lax.all_gather(gain_attn, EVERYWHERE, axis=0, tiled=True),
    )
    inputs = hidden_in[0].astype(jnp.float32)
    tokens = inputs.shape[0]
    normed_one, inverse_one = normalize(inputs)
    scaled_one = (normed_one * gain_one.astype(jnp.float32)).astype(jnp.bfloat16)
    queries = (
        matmul(scaled_one, query_full)
        .astype(jnp.bfloat16)
        .reshape(tokens, RETENTION_HEADS, KEY_DIM)
    )
    keys_tok = (
        matmul(scaled_one, key_full).astype(jnp.bfloat16).reshape(tokens, RETENTION_HEADS, KEY_DIM)
    )
    values_tok = (
        matmul(scaled_one, value_full)
        .astype(jnp.bfloat16)
        .reshape(tokens, RETENTION_HEADS, VALUE_DIM)
    )
    swish_pre = matmul(scaled_one, swish_full)
    head_q, head_k, head_v = (
        lax.all_to_all(queries, ULY, split_axis=1, concat_axis=0, tiled=True),
        lax.all_to_all(keys_tok, ULY, split_axis=1, concat_axis=0, tiled=True),
        lax.all_to_all(values_tok, ULY, split_axis=1, concat_axis=0, tiled=True),
    )
    block = head_q.shape[0]
    scale = 1.0 / math.sqrt(KEY_DIM)
    cumulative = running_sum(log_decay[0])
    later = lax.broadcasted_iota(jnp.int32, (block, block), 0) >= lax.broadcasted_iota(
        jnp.int32, (block, block), 1
    )
    gap = cumulative[:, :, None] - cumulative[:, None, :]
    mask = jnp.where(later[None], jnp.exp(jnp.minimum(gap, 0.0)), 0.0) * scale
    scores = jnp.einsum("thd,shd->hts", head_q, head_k, preferred_element_type=jnp.float32)
    weights = (scores * mask).astype(jnp.bfloat16)
    intra = jnp.einsum("hts,she->the", weights, head_v, preferred_element_type=jnp.float32)
    query_f = head_q.astype(jnp.float32)
    key_f = head_k.astype(jnp.float32)
    value_f = head_v.astype(jnp.float32)
    tail = jnp.exp(cumulative[:, -1:] - cumulative).T[:, :, None]
    reach = jnp.exp(cumulative).T[:, :, None]
    update = jnp.einsum("shd,she->hde", key_f * tail, value_f, precision=highest)
    block_decay = jnp.exp(cumulative[:, -1])
    identity = (jnp.ones_like(block_decay), jnp.zeros_like(update))
    _, state_in = entering((block_decay, update), CTX, carry_forward, identity, False)
    retained = intra + scale * reach * jnp.einsum(
        "thd,hde->the", query_f, state_in, precision=highest
    )
    head_normed, head_inverse = normalize(retained)
    head_out = head_normed.astype(jnp.bfloat16)
    token_out = lax.all_to_all(
        head_out, ULY, split_axis=0, concat_axis=1, tiled=True
    ).reshape(tokens, RETENTION_HEADS * VALUE_DIM)
    token_out_f = token_out.astype(jnp.float32)
    swish_act = jax.nn.silu(swish_pre)
    gated = (swish_act * token_out_f).astype(jnp.bfloat16)
    residual = inputs + matmul(gated, output_full)
    gate_full, up_full, down_full, gain_two = (
        lax.all_gather(w_gate, EVERYWHERE, axis=0, tiled=True),
        lax.all_gather(w_up, EVERYWHERE, axis=0, tiled=True),
        lax.all_gather(w_down, EVERYWHERE, axis=0, tiled=True),
        lax.all_gather(gain_ffn, EVERYWHERE, axis=0, tiled=True),
    )
    normed_two, inverse_two = normalize(residual)
    scaled_two = (normed_two * gain_two.astype(jnp.float32)).astype(jnp.bfloat16)
    gate_pre = matmul(scaled_two, gate_full)
    up_pre = matmul(scaled_two, up_full)
    product = (jax.nn.silu(gate_pre) * up_pre).astype(jnp.bfloat16)
    layer_out = residual + matmul(product, down_full)
    grad_top = cotangent[0].astype(jnp.float32)
    grad_top_low = grad_top.astype(jnp.bfloat16)
    grad_product = matmul(grad_top_low, down_full.T)
    grad_down_term = matmul(product.T, grad_top_low)
    grad_gate_pre = (grad_product * up_pre * swish_slope(gate_pre)).astype(jnp.bfloat16)
    grad_up_pre = (grad_product * jax.nn.silu(gate_pre)).astype(jnp.bfloat16)
    grad_gate_term = matmul(scaled_two.T, grad_gate_pre)
    grad_up_term = matmul(scaled_two.T, grad_up_pre)
    grad_scaled_two = matmul(grad_gate_pre, gate_full.T) + matmul(grad_up_pre, up_full.T)
    grad_gain_two = jnp.sum(grad_scaled_two * normed_two, axis=0)
    grad_residual = grad_top + norm_back(
        grad_scaled_two * gain_two.astype(jnp.float32), normed_two, inverse_two
    )
    grad_gate, grad_up, grad_down, grad_gain_ffn = (
        lax.psum_scatter(grad_gate_term, EVERYWHERE, scatter_dimension=0, tiled=True),
        lax.psum_scatter(grad_up_term, EVERYWHERE, scatter_dimension=0, tiled=True),
        lax.psum_scatter(grad_down_term, EVERYWHERE, scatter_dimension=0, tiled=True),
        lax.psum_scatter(grad_gain_two, EVERYWHERE, scatter_dimension=0, tiled=True),
    )
    grad_y = grad_residual.astype(jnp.bfloat16)
    grad_output_term = matmul(gated.T, grad_y)
    grad_gated = matmul(grad_y, output_full.T)
    grad_swish_pre = (grad_gated * token_out_f * swish_slope(swish_pre)).astype(jnp.bfloat16)
    grad_token_out = (
        (grad_gated * swish_act).astype(jnp.bfloat16).reshape(tokens, RETENTION_HEADS, VALUE_DIM)
    )
    grad_swish_term = matmul(scaled_one.T, grad_swish_pre)
    grad_head_out = lax.all_to_all(
        grad_token_out, ULY, split_axis=1, concat_axis=0, tiled=True
    ).astype(jnp.float32)
    grad_retained = norm_back(grad_head_out, head_normed, head_inverse).astype(jnp.bfloat16)
    grad_retained_f = grad_retained.astype(jnp.float32)
    grad_weights = jnp.einsum(
        "the,she->hts", grad_retained, head_v, preferred_element_type=jnp.float32
    )
    grad_scores = (grad_weights * mask).astype(jnp.bfloat16)
    grad_state_in = scale * jnp.einsum(
        "thd,the->hde", query_f * reach, grad_retained_f, precision=highest
    )
    _, grad_update = entering((block_decay, grad_state_in), CTX, carry_backward, identity, True)
    grad_head_q = jnp.einsum(
        "hts,shd->thd", grad_scores, head_k, preferred_element_type=jnp.float32
    ) + scale * reach * jnp.einsum("the,hde->thd", grad_retained_f, state_in, precision=highest)
    grad_head_k = jnp.einsum(
        "hts,thd->shd", grad_scores, head_q, preferred_element_type=jnp.float32
    ) + tail * jnp.einsum("she,hde->shd", value_f, grad_update, precision=highest)
    grad_head_v = jnp.einsum(
        "hts,the->she", weights, grad_retained, preferred_element_type=jnp.float32
    ) + tail * jnp.einsum("shd,hde->she", key_f, grad_update, precision=highest)
    grad_queries, grad_keys, grad_values = (
        lax.all_to_all(
            grad_head_q.astype(jnp.bfloat16), ULY, split_axis=0, concat_axis=1, tiled=True
        ),
        lax.all_to_all(
            grad_head_k.astype(jnp.bfloat16), ULY, split_axis=0, concat_axis=1, tiled=True
        ),
        lax.all_to_all(
            grad_head_v.astype(jnp.bfloat16), ULY, split_axis=0, concat_axis=1, tiled=True
        ),
    )
    grad_queries = grad_queries.reshape(tokens, RETENTION_HEADS * KEY_DIM)
    grad_keys = grad_keys.reshape(tokens, RETENTION_HEADS * KEY_DIM)
    grad_values = grad_values.reshape(tokens, RETENTION_HEADS * VALUE_DIM)
    grad_query_term = matmul(scaled_one.T, grad_queries)
    grad_key_term = matmul(scaled_one.T, grad_keys)
    grad_value_term = matmul(scaled_one.T, grad_values)
    grad_scaled_one = (
        matmul(grad_queries, query_full.T)
        + matmul(grad_keys, key_full.T)
        + matmul(grad_values, value_full.T)
        + matmul(grad_swish_pre, swish_full.T)
    )
    grad_gain_one = jnp.sum(grad_scaled_one * normed_one, axis=0)
    grad_input = grad_residual + norm_back(
        grad_scaled_one * gain_one.astype(jnp.float32), normed_one, inverse_one
    )
    grad_query, grad_key, grad_value, grad_swish, grad_output, grad_gain_attn = (
        lax.psum_scatter(
            grad_query_term, EVERYWHERE, scatter_dimension=0, tiled=True
        ),
        lax.psum_scatter(grad_key_term, EVERYWHERE, scatter_dimension=0, tiled=True),
        lax.psum_scatter(
            grad_value_term, EVERYWHERE, scatter_dimension=0, tiled=True
        ),
        lax.psum_scatter(
            grad_swish_term, EVERYWHERE, scatter_dimension=0, tiled=True
        ),
        lax.psum_scatter(
            grad_output_term, EVERYWHERE, scatter_dimension=0, tiled=True
        ),
        lax.psum_scatter(grad_gain_one, EVERYWHERE, scatter_dimension=0, tiled=True),
    )
    return (
        layer_out[None],
        grad_input[None],
        grad_query,
        grad_key,
        grad_value,
        grad_swish,
        grad_output,
        grad_gate,
        grad_up,
        grad_down,
        grad_gain_attn,
        grad_gain_ffn,
    )


MESH = pl.DeviceIdType.MESH
BF16, F32 = jnp.bfloat16, jnp.float32
HBM, VMEM = pltpu.HBM, pltpu.VMEM
N_SEMS = 160


def dot_t(left, right):
    return lax.dot_general(left, right, (((0,), (0,)), ((), ())), preferred_element_type=F32)


def dot_nt(left, right):
    return lax.dot_general(left, right, (((1,), (1,)), ((), ())), preferred_element_type=F32)


def pair_dot(left_axis, right_axis, left, right):
    dims = (((left_axis,), (right_axis,)), ((0,), (0,)))
    return lax.dot_general(left, right, dims, preferred_element_type=F32)


class Place:
    def __init__(self, uly):
        self.dp, self.ctx, self.uly = lax.axis_index(DP), lax.axis_index(CTX), uly
        odd = lax.rem(self.ctx, 2)
        self.xn = self.ctx + 1 - 2 * odd
        self.yn = lax.rem(self.ctx + 2, 4)
        self.dg = self.yn + 1 - 2 * odd
        self.other = 1 - self.dp

    def at(self, dp=None, ctx=None, uly=None):
        return (
            self.dp if dp is None else dp,
            self.ctx if ctx is None else ctx,
            self.uly if uly is None else uly,
        )


class Mover:
    def __init__(self, place, names, send, recv, like=None, like_whole=None):
        self.like, self.like_whole = like, like_whole
        self.place, self.names, self.send_sems, self.recv_sems = place, names, send, recv
        self.sent, self.whole = [], []

    def number(self, name):
        return self.names.setdefault(name, len(self.names))

    def remote(self, name, src, dst, device):
        k = self.number(name)
        return pltpu.make_async_remote_copy(
            src_ref=src,
            dst_ref=dst,
            send_sem=self.send_sems.at[k],
            recv_sem=self.recv_sems.at[k],
            device_id=device,
            device_id_type=MESH,
        )

    def send(self, name, src, dst, device):
        copy = self.remote(name, src, dst, device)
        copy.start()
        self.sent.append(copy if self.like is None else name)

    def send_whole(self, name, src, dst, device):
        copy = self.remote(name, src, dst, device)
        copy.start()
        self.whole.append((copy if self.like is None else None, name, None))

    def arrive(self, name, dst):
        self.remote(name, dst, dst, self.place.at(dp=self.place.other)).wait_recv()

    def local(self, name, src, dst):
        copy = pltpu.make_async_copy(src, dst, self.send_sems.at[self.number(name)])
        copy.start()
        return copy

    def finish(self):
        for copy, name, _ in self.whole:
            if self.like is not None:
                ref = self.like_whole()
                copy = self.remote(name, ref, ref, self.place.at(dp=self.place.other))
            copy.wait_send()
        for copy in self.sent:
            if self.like is not None:
                ref = self.like()
                copy = self.remote(copy, ref, ref, self.place.at(dp=self.place.other))
            copy.wait_send()


def greet(devices, meanwhile=None):
    barrier = pltpu.get_barrier_semaphore()
    for device in devices:
        pl.semaphore_signal(barrier, inc=1, device_id=device, device_id_type=MESH)
    if meanwhile is not None:
        meanwhile()
    pl.semaphore_wait(barrier, len(devices))


def together(streams):
    streams = list(streams)
    while streams:
        left = []
        for stream in streams:
            if next(stream, 0) is None:
                left.append(stream)
        streams = left


def later(stream, stages):
    for _ in range(stages):
        yield
    yield from stream


def add_up(dst, sources, step=32):
    if len(dst.shape) > 2:
        for i in range(dst.shape[0]):
            add_up(dst.at[i], [source.at[i] for source in sources], step)
        return
    rows, columns = dst.shape
    by_rows = rows % step == 0
    step = step if by_rows else 256

    def body(i, carry):
        part = pl.ds(pl.multiple_of(i * step, step), step)
        at = (part, slice(None)) if by_rows else (slice(None), part)
        total = sources[0][at].astype(F32)
        for source in sources[1:]:
            total = total + source[at].astype(F32)
        dst[at] = total.astype(dst.dtype)
        return carry

    lax.fori_loop(0, (rows if by_rows else columns) // step, body, 0)


def halves_of_rows(view, i):
    rows = view.shape[0] // 2
    return view.at[pl.ds(i * rows, rows)]


def halves_of_columns(view, i):
    columns = view.shape[1] // 2
    return view.at[:, pl.ds(i * columns, columns)]


def line_gather(m, tag, own, out, pause=1):
    p = m.place
    u = p.uly
    mine = out.at[p.dp * 4 + u]
    copy = m.local((tag, "="), own, mine)
    for i in range(2):
        src, dst = halves_of_rows(own, i), halves_of_rows(mine, i)
        if u < 3:
            m.send((tag, "r", u, i), src, dst, p.at(uly=u + 1))
        if u > 0:
            m.send((tag, "l", u, i), src, dst, p.at(uly=u - 1))
    m.send((tag, "c", u), own, mine, p.at(dp=p.other))
    for _ in range(pause):
        yield
    for d in range(1, 4):
        for i in range(2):
            for way, b, onward in (("r", u - d, u + 1), ("l", u + d, u - 1)):
                if 0 <= b <= 3:
                    half = halves_of_rows(out.at[p.dp * 4 + b], i)
                    m.arrive((tag, way, b, i), half)
                    if 0 <= onward <= 3:
                        m.send((tag, way, b, i), half, half, p.at(uly=onward))
        for b in (u - d, u + d):
            if 0 <= b <= 3:
                block = out.at[p.dp * 4 + b]
                m.send((tag, "c", b), block, block, p.at(dp=p.other))
        yield
    for b in range(4):
        m.arrive((tag, "c", b), out.at[p.other * 4 + b])
    copy.wait()


def plane_gather(m, tag, own, out, slot, halves, pair=True):
    p = m.place

    def half(c, i):
        return slot(out, p.dp, c, halves[i])

    mine = slot(out, p.dp, p.ctx, None)
    copy = m.local((tag, "="), own, mine)
    m.send((tag, "x"), own, mine, p.at(ctx=p.xn))
    m.send((tag, "y"), own, mine, p.at(ctx=p.yn))
    if pair:
        m.send((tag, "c", 0), own, mine, p.at(dp=p.other))
    yield
    block = slot(out, p.dp, p.xn, None)
    m.arrive((tag, "x"), block)
    m.send((tag, "z", 0), half(p.xn, 0), half(p.xn, 0), p.at(ctx=p.yn))
    if pair:
        m.send((tag, "c", 1), block, block, p.at(dp=p.other))
    block = slot(out, p.dp, p.yn, None)
    m.arrive((tag, "y"), block)
    m.send((tag, "z", 1), half(p.yn, 1), half(p.yn, 1), p.at(ctx=p.xn))
    if pair:
        m.send((tag, "c", 2), block, block, p.at(dp=p.other))
    yield
    for i in range(2):
        block = half(p.dg, i)
        m.arrive((tag, "z", i), block)
        if pair:
            m.send((tag, "c", 3 + i), block, block, p.at(dp=p.other))
    yield
    if pair:
        for i, c in enumerate((p.ctx, p.xn, p.yn)):
            m.arrive((tag, "c", i), slot(out, p.other, c, None))
        for i in range(2):
            m.arrive((tag, "c", 3 + i), slot(out, p.other, p.dg, halves[i]))
    copy.wait()


def line_reduce(m, tag, part, out, sib, right, left, cut=halves_of_rows):
    p = m.place
    u = p.uly
    order = (3, 0, 2, 1) if u < 2 else (0, 3, 1, 2)
    for b in order if sib is not None else ():
        m.send_whole((tag, "c", b), part(p.other * 4 + b), sib.at[b], p.at(dp=p.other))
    met = set()

    def meet(b, i):
        if sib is None:
            return [cut(part(b), i)]
        if b not in met:
            met.add(b)
            m.arrive((tag, "c", b), sib.at[b])
        return [cut(part(p.dp * 4 + b), i), cut(sib.at[b], i)]

    def onward(way, b, i, arrived, there):
        terms = meet(b, i)
        if arrived is not None:
            arrived = cut(arrived.at[b], i)
            m.arrive((tag, way, b, i), arrived)
            terms.append(arrived)
        if len(terms) > 1:
            add_up(terms[-1], terms)
        away = cut((right if way == "r" else left).at[b], i)
        m.send((tag, way, b, i), terms[-1], away, p.at(uly=there))

    for slot in range(3):
        for b in range(4):
            for i in range(2):
                if u < b and u + 3 - b == slot:
                    onward("r", b, i, right if u > 0 else None, u + 1)
        for b in range(4):
            for i in range(2):
                if u > b and 3 - u + b == slot:
                    onward("l", b, i, left if u < 3 else None, u - 1)
        yield
    for i in range(2):
        terms = meet(u, i)
        if u > 0:
            m.arrive((tag, "r", u, i), cut(right.at[u], i))
            terms.append(cut(right.at[u], i))
        if u < 3:
            m.arrive((tag, "l", u, i), cut(left.at[u], i))
            terms.append(cut(left.at[u], i))
        add_up(cut(out, i), terms)


def plane_reduce(m, tag, part, out, sib, sums, got, got2):
    p = m.place
    rows = out.shape[0]
    halves = (pl.ds(0, rows // 2), pl.ds(rows // 2, rows // 2))
    order = (p.dg, p.xn, p.yn, p.ctx)
    for i, c in enumerate(order):
        m.send((tag, "c", i), part.at[p.other * 4 + c], sib.at[c], p.at(dp=p.other))
    yield
    for i, c in enumerate(order):
        m.arrive((tag, "c", i), sib.at[c])
        add_up(sums.at[c], [part.at[p.dp * 4 + c], sib.at[c]])
        if i == 0:
            m.send((tag, "x", 1), sums.at[c, halves[0]], got.at[1, halves[0]], p.at(ctx=p.xn))
            m.send((tag, "y", 1), sums.at[c, halves[1]], got.at[1, halves[1]], p.at(ctx=p.yn))
        if i == 1:
            m.send((tag, "x", 0), sums.at[c, halves[0]], got.at[0, halves[0]], p.at(ctx=p.xn))
        if i == 2:
            m.send((tag, "y", 0), sums.at[c, halves[1]], got.at[0, halves[1]], p.at(ctx=p.yn))
    yield
    m.arrive((tag, "x", 1), got.at[1, halves[0]])
    add_up(got.at[1, halves[0]], [sums.at[p.yn, halves[0]], got.at[1, halves[0]]])
    m.send((tag, "y2"), got.at[1, halves[0]], got2.at[halves[0]], p.at(ctx=p.yn))
    m.arrive((tag, "y", 1), got.at[1, halves[1]])
    add_up(got.at[1, halves[1]], [sums.at[p.xn, halves[1]], got.at[1, halves[1]]])
    m.send((tag, "x2"), got.at[1, halves[1]], got2.at[halves[1]], p.at(ctx=p.xn))
    yield
    m.arrive((tag, "x", 0), got.at[0, halves[0]])
    m.arrive((tag, "y", 0), got.at[0, halves[1]])
    yield
    m.arrive((tag, "y2"), got2.at[halves[0]])
    m.arrive((tag, "x2"), got2.at[halves[1]])
    add_up(out, [sums.at[p.ctx], got.at[0], got2])


class Stage:
    def __init__(self, loads, stores, first):
        self.loads, self.stores, self.started = loads, stores, []
        for i in (*first, *(i for i in loads if i not in first)):
            loads[i].start()

    def need(self, *which):
        for i in which:
            self.loads.pop(i).wait()

    def put(self, *which):
        for i in which:
            copy = self.stores.pop(i)
            copy.start()
            self.started.append(copy)

    def end(self):
        self.need(*list(self.loads))
        self.put(*list(self.stores))
        for copy in self.started:
            copy.wait()


def staged_call(kernel, name, ins, outs, scratch, remote=None, first=()):
    in_held = [i for i, (_, held) in enumerate(ins) if held]
    out_held = [i for i, (_, _, held) in enumerate(outs) if held]

    def body(*refs):
        given, results = list(refs[: len(ins)]), list(refs[len(ins) : len(ins) + len(outs)])
        rest = refs[len(ins) + len(outs) :]
        held, own, sems = rest[: len(in_held) + len(out_held)], rest[len(in_held) + len(out_held) : -1], rest[-1]
        loads, stores = {}, {}
        for j, i in enumerate(in_held):
            loads[i] = pltpu.make_async_copy(given[i], held[j], sems.at[j])
            given[i] = held[j]
        for j, i in enumerate(out_held, len(in_held)):
            stores[i] = pltpu.make_async_copy(held[j], results[i], sems.at[j])
            results[i] = held[j]
        stage = Stage(loads, stores, first)
        kernel(stage, *given, *results, *own)
        stage.end()

    params = {} if remote is None else {"collective_id": remote, "has_side_effects": True}
    return pl.pallas_call(
        body,
        out_shape=[jax.ShapeDtypeStruct(shape, kind) for shape, kind, _ in outs],
        in_specs=[pl.BlockSpec(memory_space=HBM)] * len(ins),
        out_specs=[pl.BlockSpec(memory_space=HBM)] * len(outs),
        scratch_shapes=[
            *[pltpu.VMEM(ins[i][0].shape, ins[i][0].dtype) for i in in_held],
            *[pltpu.VMEM(*outs[i][:2]) for i in out_held],
            *[pltpu.VMEM(shape, kind) for shape, kind in scratch],
            *([pltpu.SemaphoreType.DMA((N_SEMS,))] * 2 if remote is not None else []),
            pltpu.SemaphoreType.DMA((len(in_held) + len(out_held),)),
        ],
        name=name,
        compiler_params=pltpu.CompilerParams(vmem_limit_bytes=62 << 20, **params),
    )(*[array for array, _ in ins])


def everyone(p):
    me = p.dp * 16 + p.ctx * 4 + p.uly
    found = []
    for k in range(1, 32):
        there = lax.rem(me + k, 32)
        found.append((lax.div(there, 16), lax.rem(lax.div(there, 4), 4), lax.rem(there, 4)))
    return found


def line_partners(p):
    found = [p.at(dp=p.other)]
    for d in range(1, 4):
        there = lax.rem(p.uly + d, 4)
        found += [p.at(uly=there), p.at(dp=p.other, uly=there)]
    return found


def plane_partners(p):
    return [p.at(dp=p.other), p.at(ctx=p.xn), p.at(ctx=p.yn)]


def token_slot(out, dp, c, part):
    view = out.at[dp * 4 + c]
    return view if part is None else view.at[part]


def state_slot(out, dp, c, part):
    view = out.at[c]
    return view if part is None else view.at[part]


def finish(heads, outg, slices, residual, layer_part, grad, grad_scaled, hidden, gains, terms, down):
    rows, (_, out_rows, quarter) = heads.shape[1], outg.shape
    tokens, width = hidden.shape
    key, val, ff = KEY_DIM, VALUE_DIM, slices.shape[2] // 2

    def kernel(
        stage, hs, og, sl, res, part, gr, gs, hid, gain, term, down_in, q, k, v, s, o, g, u, y, x, down_out, n1, n2
    ):
        stage.need(3, 4, 5, 6, 7, 8, 9)
        me = lax.axis_index(DP) * 16 + lax.axis_index(CTX) * 4 + lax.axis_index(ULY)
        pair = pl.ds(pl.multiple_of(lax.div(me, 2) * 2 * rows, 2 * rows), 2 * rows)
        own = jnp.where(lax.rem(me, 2) == 0, term[:, pair][:, :rows], term[:, pair][:, rows:])
        n1[...] = own[0:1]
        n2[...] = own[1:2]

        def body(i, carry):
            at = pl.ds(pl.multiple_of(i * 16, 16), 16)
            y[at, :] = res[at, :] + part[at, :]
            normed, inverse = normalize(hid[at, :].astype(F32))
            x[at, :] = gr[at, :] + norm_back(gs[at, :] * gain[0:1, :], normed, inverse)
            return carry

        lax.fori_loop(0, tokens // 16, body, 0)
        stage.put(7, 8)
        stage.need(10)
        down_out[...] = down_in[...]
        stage.put(9)
        stage.need(0, 1, 2)
        for d in range(2):
            for z in range(4):
                h, i = 2 * z + d, 4 * d + z
                at = 0
                for ref, w in ((q, key), (k, key), (v, val), (s, val)):
                    ref[:, h * w : (h + 1) * w] = hs[i, :, at : at + w].astype(F32)
                    at += w
        stage.put(0, 1, 2, 3)
        for i in range(8):
            g[:, i * ff : (i + 1) * ff] = sl[i, :, :ff].astype(F32)
            u[:, i * ff : (i + 1) * ff] = sl[i, :, ff:].astype(F32)
        stage.put(5, 6)
        for j in range(4):
            o[:, j * quarter : (j + 1) * quarter] = og[j].astype(F32)

    widths = (8 * key, 8 * key, 8 * val, 8 * val, 4 * quarter, 8 * ff, 8 * ff)
    heights = (rows, rows, rows, rows, out_rows, rows, rows)
    arrays = (heads, outg, slices, residual, layer_part, grad, grad_scaled, hidden, gains, terms, down)
    shapes = [*zip(heights, widths), (tokens, width), (tokens, width), down.shape, (1, rows), (1, rows)]
    return staged_call(
        kernel,
        "finish",
        [(array, True) for array in arrays],
        [(shape, F32, True) for shape in shapes],
        [],
    )


def line_spread(m, tag, own, slot):
    u = m.place.uly
    copy = m.local((tag, 8), own, slot(u))
    if u < 3:
        m.send((tag, "r", u), own, slot(u), m.place.at(uly=u + 1))
    if u > 0:
        m.send((tag, "l", u), own, slot(u), m.place.at(uly=u - 1))
    copy.wait()
    yield
    for d in range(1, 4):
        for way, b, onward in (("r", u - d, u + 1), ("l", u + d, u - 1)):
            if 0 <= b <= 3:
                m.arrive((tag, way, b), slot(b))
                if 0 <= onward <= 3:
                    m.send((tag, way, b), slot(b), slot(b), m.place.at(uly=onward))
        yield


def block_factors(cum, ctx, s, backward):
    count = cum.shape[1]
    lasts = [cum[4 * s + j : 4 * s + j + 1, count - 1 : count] for j in range(4)]
    found = []
    for j in range(4):
        total = jnp.zeros((1, 1), F32)
        for i in range(4):
            inside = ((i > ctx) & (i < j)) if backward else ((i > j) & (i < ctx))
            total = total + jnp.where(inside, lasts[i], 0.0)
        right = (j > ctx) if backward else (j < ctx)
        found.append(jnp.where(right, jnp.exp(total), 0.0))
    return found


def forward(hidden, cot, decay, w_down, w_query, w_key, w_value, w_swish, w_output, w_gate, w_up, gains):
    tokens, width = hidden.shape
    key, val = KEY_DIM, VALUE_DIM
    rows, cols = w_query.shape[0], 2 * key + 2 * val + gains.shape[1]
    out_rows, quarter = w_output.shape[0], width // 4
    ff = w_gate.shape[1] // 8
    ff2 = 2 * ff
    block, both = 4 * tokens, 8 * tokens
    half = block // 2
    scale = 1.0 / math.sqrt(key)
    at_s = 2 * key + val

    def start_streams(m, hid_ref, dec_ref, pk_ref, gu_ref, hall, dall, wall, gall):
        p = m.place
        u = p.uly

        def row(q, c, us):
            dp = p.dp if q == 0 else p.other
            at = (dp * 16 + c * 4 + us) * rows
            return wall.at[pl.ds(pl.multiple_of(at, rows), rows)]

        def attn():
            sources = sorted(
                ((q, us) for q in range(2) for us in range(4)), key=lambda s: (abs(s[1] - u), s[0])
            )
            copy = None
            for q, to in sources:
                dp = p.dp if q == 0 else p.other
                mine = row(0, p.ctx, u)
                src = pk_ref.at[dp * 4 + to]
                if (q, to) == (0, u):
                    copy = m.local("T", src, mine)
                else:
                    m.send(("t", q, u), src, mine, p.at(dp=dp, uly=to))
            yield
            relays = []
            for n, (q, us) in enumerate(sources):
                tile = row(q, p.ctx, us)
                if (q, us) == (0, u):
                    copy.wait()
                else:
                    m.arrive(("t", q, us), tile)
                m.send(("X", q, us), tile, tile, p.at(ctx=p.xn))
                m.send(("Y", q, us), tile, tile, p.at(ctx=p.yn))
                relays.append((q, us))
                if n >= 2:
                    yield
                    relay(*relays.pop(0))
            while relays:
                yield
                relay(*relays.pop(0))
            yield
            for q, us in sources:
                even = (q + us) % 2 == 0
                m.arrive(("Y" if even else "X", q, us), row(q, p.yn if even else p.xn, us))
                m.arrive(("Z", q, us), row(q, p.dg, us))

        def relay(q, us):
            if (q + us) % 2 == 0:
                tile = row(q, p.xn, us)
                m.arrive(("X", q, us), tile)
                m.send(("Z", q, us), tile, tile, p.at(ctx=p.yn))
            else:
                tile = row(q, p.yn, us)
                m.arrive(("Y", q, us), tile)
                m.send(("Z", q, us), tile, tile, p.at(ctx=p.xn))

        def feed():
            mine = gall.at[p.dp * 4 + p.ctx]
            copy = m.local("F", gu_ref.at[p.dp * 4 + p.ctx], mine)
            decays = m.local("D", dec_ref, dall.at[p.dp * 4 + p.ctx])
            spots = [(q, c, i) for i, c in enumerate((p.ctx, p.xn, p.yn, p.dg)) for q in range(2)][1:]
            for q, c, i in spots:
                dp = p.dp if q == 0 else p.other
                m.send(("d", q, i), dec_ref, dall.at[p.dp * 4 + p.ctx], p.at(dp=dp, ctx=c))
                m.send(("f", q, i), gu_ref.at[dp * 4 + c], mine, p.at(dp=dp, ctx=c))
            for _ in range(5):
                yield
            for q, c, i in spots:
                dp = p.dp if q == 0 else p.other
                m.arrive(("d", q, i), dall.at[dp * 4 + c])
                m.arrive(("f", q, i), gall.at[dp * 4 + c])
            copy.wait()
            decays.wait()

        return [
            attn(),
            later(line_gather(m, "h", hid_ref, hall, 6), 1),
            later(feed(), 2),
        ]

    def quarter_of(oall, part, c):
        return oall.at[part, :, pl.ds(pl.multiple_of(c * quarter, quarter), quarter)]

    def out_rows_go(m, ow_ref, oall):
        p = m.place
        u = p.uly
        head_dp, head_u = lax.rem(p.ctx, 2), p.dp * 2 + lax.div(p.ctx, 2)
        found = []
        for j in range(4):
            there = oall.at[u, :, pl.ds(j * quarter, quarter)]
            away = pltpu.make_async_remote_copy(
                src_ref=ow_ref.at[j],
                dst_ref=there,
                send_sem=m.send_sems.at[m.number(("S", j))],
                recv_sem=m.recv_sems.at[m.number(("o", u))],
                device_id=(head_dp, j, head_u),
                device_id_type=MESH,
            )
            here = (ow_ref.at[j], there, m.send_sems.at[m.number("O")])
            own = (head_dp == p.dp) & (p.ctx == j) & (head_u == u)
            found.append((own, away, here))
        return found

    def out_start(m, ow_ref, oall):
        for own, away, here in out_rows_go(m, ow_ref, oall):

            @pl.when(own)
            def _(here=here):
                copy = pltpu.make_async_copy(*here)
                copy.start()
                copy.wait()

            pl.when(jnp.logical_not(own))(away.start)

    def out_share(m, ow_ref, oall):
        p = m.place
        u = p.uly
        for us in range(4):
            mine = (u // 2 == p.dp) & (2 * (u % 2) + p.dp == p.ctx) & (us == u)

            @pl.when(jnp.logical_not(mine))
            def _(us=us):
                m.arrive(("o", us), quarter_of(oall, us, p.ctx))

        mine = quarter_of(oall, pl.ds(0, 4), p.ctx)
        m.send("ox", mine, mine, p.at(ctx=p.xn))
        m.send("oy", mine, mine, p.at(ctx=p.yn))
        for own, away, _ in out_rows_go(m, ow_ref, oall):
            pl.when(jnp.logical_not(own))(away.wait_send)

    def out_relay(m, oall):
        p = m.place
        low, high = pl.ds(0, 2), pl.ds(2, 2)
        m.arrive("ox", quarter_of(oall, pl.ds(0, 4), p.xn))
        m.send("o0", quarter_of(oall, low, p.xn), quarter_of(oall, low, p.xn), p.at(ctx=p.yn))
        m.arrive("oy", quarter_of(oall, pl.ds(0, 4), p.yn))
        m.send("o1", quarter_of(oall, high, p.yn), quarter_of(oall, high, p.yn), p.at(ctx=p.xn))

    def out_end(m, oall):
        p = m.place
        m.arrive("o0", quarter_of(oall, pl.ds(0, 2), p.dg))
        m.arrive("o1", quarter_of(oall, pl.ds(2, 2), p.dg))

    def kernel(
        stage, hid_ref, cot_ref, dec_ref, wd_ref, wq_ref, wk_ref, wv_ref, ws_ref, wo_ref, wg_ref, wu_ref, n_ref,
        w_all, s1_all, w2d, q_ref, k_ref, v_ref, sw_ref, w_ref, mask_ref, st_ref, reach_ref, tail_ref, cum_ref,
        gain_ref, hn_ref, hi_ref, ga_ref, res_ref, s2_all, top_all, gu_all, wd_all,
        pk_ref, ow_ref, gu_ref, wall, s1, oall, dall, gall, dec8, cols8, upd, upds, ret, part, sib, right, left, s2, send, recv,
    ):
        uly = lax.axis_index(ULY)
        names = {}
        place = Place(uly)

        def pack():
            stage.need(*range(4, 12))
            for d in range(2):
                for z in range(4):
                    h, i = 2 * z + d, 4 * d + z
                    at = 0
                    for ref, w in ((wq_ref, key), (wk_ref, key), (wv_ref, val), (ws_ref, val)):
                        pk_ref[i, :, at : at + w] = ref[:, h * w : (h + 1) * w]
                        at += w
                    pk_ref[i, :, at:] = n_ref[...]
            for i in range(8):
                gu_ref[i, :, :ff] = wg_ref[:, i * ff : (i + 1) * ff]
                gu_ref[i, :, ff:] = wu_ref[:, i * ff : (i + 1) * ff]
            for j in range(4):
                ow_ref[j] = wo_ref[:, j * quarter : (j + 1) * quarter]

        greet(everyone(place), pack)
        stage.need(0)
        common = Mover(place, names, send, recv)
        ctx = place.ctx

        def for_each(body):
            for u in range(4):
                pl.when(uly == u)(functools.partial(body, u))

        spread = []
        for u in range(4):
            for tag, own, slot in (
                ("g", gall, lambda b: gu_all.at[:, b]),
                ("e", wd_ref, lambda b: wd_all.at[b]),
            ):
                m = Mover(Place(u), names, send, recv, lambda slot=slot: slot(0))
                spread.append((u, m, line_spread(m, tag, own, slot)))

        def spread_on(u):
            for v, _, stream in spread:
                if u == v:
                    next(stream, 0)

        def first(u):
            m = Mover(Place(u), names, send, recv)

            def spread_stage():
                out_start(Mover(Place(u), names, send, recv), ow_ref, oall)
                spread_on(u)
                yield

            together(
                [
                    *start_streams(m, hid_ref, dec_ref, pk_ref, gu_ref, s1, dall, wall, gall),
                    later(spread_stage(), 8),
                ]
            )
            m.finish()

        for_each(first)
        keep = [common.local("w", wall, w_all)]

        table = wall[:, cols - 128 : cols].astype(F32).T
        first_gain = 128 - 32
        gain_ref[...] = table[first_gain : first_gain + 8]

        def norm_one(i, carry):
            b, at = lax.div(i, 4), pl.ds(pl.multiple_of(lax.rem(i, 4) * 32, 32), 32)
            normed, _ = normalize(s1[b, at, :].astype(F32))
            s1[b, at, :] = (normed * gain_ref[0:1, :]).astype(BF16)
            return carry

        lax.fori_loop(0, 32, norm_one, 0)
        keep.append(common.local("W", s1, s1_all))

        for i in range(8):
            dec8[i : i + 1, :] = dall[i, pl.ds(place.dp, 1), :]
        upper = lax.broadcasted_iota(jnp.int32, (block, block), 0) <= lax.broadcasted_iota(
            jnp.int32, (block, block), 1
        )
        cum_ref[...] = jnp.dot(
            dec8[...], upper.astype(F32), precision=lax.Precision.HIGHEST, preferred_element_type=F32
        )
        for s in range(2):
            dec8[s : s + 1, :] = cum_ref[pl.ds(4 * s + ctx, 1), :]
        cols8[...] = dec8[...].T
        for s in range(2):
            column = cols8[:, s : s + 1]
            reach_ref[s] = jnp.exp(column) * scale
            tail_ref[s] = jnp.exp(dec8[s : s + 1, block - 1 : block] - column)

        whole = [
            Mover(Place(u), names, send, recv, lambda: quarter_of(oall, pl.ds(0, 4), 0))
            for u in range(4)
        ]
        for_each(lambda u: out_share(whole[u], ow_ref, oall))

        for s in range(2):
            lhs = s1[4 * s : 4 * s + 4].reshape(block, width)
            q_ref[s] = matmul(lhs, wall[:, :key]).astype(BF16)
            k_ref[s] = matmul(lhs, wall[:, key : 2 * key]).astype(BF16)
            rest = matmul(lhs, wall[:, 2 * key :])
            v_ref[s] = rest[:, :val].astype(BF16)
            sw_ref[pl.ds(s * block, block), :] = rest[:, val : 2 * val]
        out_relay(common, oall)
        for s in range(2):
            k_tail = (k_ref[s].astype(F32) * tail_ref[s]).astype(BF16)
            upd[s] = dot_t(k_tail, v_ref[s]).astype(BF16)
        states = plane_gather(
            common, "t", upd, upds, state_slot, (pl.ds(0, 1), pl.ds(1, 1)), pair=False
        )
        next(states)

        def intra(c, carry):
            s, h = lax.div(c, 2), lax.rem(c, 2)
            at = pl.ds(pl.multiple_of(h * half, half), half)
            here = pl.ds(pl.multiple_of(c * half, half), half)
            gap = cols8[at, :]
            column = jnp.where(s == 0, gap[:, 0:1], gap[:, 1:2])
            gap = column - dec8[pl.ds(s, 1), :]
            t = lax.broadcasted_iota(jnp.int32, (half, block), 0) + h * half
            later_on = t >= lax.broadcasted_iota(jnp.int32, (half, block), 1)
            mask = jnp.where(later_on, jnp.exp(jnp.minimum(gap, 0.0)), 0.0) * scale
            mask_ref[s, at, :] = mask
            weights = (dot_nt(q_ref[s, at, :], k_ref[s]) * mask).astype(BF16)
            w_ref[s, at, :] = weights
            ret[here, :] = matmul(weights, v_ref[s])
            return carry

        lax.fori_loop(0, 2, intra, 0)
        for_each(spread_on)
        next(states)
        lax.fori_loop(2, 4, intra, 0)
        out_end(common, oall)
        for i in range(4):
            w2d[i * out_rows : (i + 1) * out_rows, :] = oall[i]
        for _ in states:
            pass
        for s in range(2):
            factors = block_factors(cum_ref, ctx, s, False)
            total = factors[0] * upds[0, s].astype(F32)
            for j in range(1, 4):
                total = total + factors[j] * upds[j, s].astype(F32)
            st_ref[s] = total.astype(BF16)

        def outer(c, carry):
            s, h = lax.div(c, 2), lax.rem(c, 2)
            at = pl.ds(pl.multiple_of(h * half, half), half)
            here = pl.ds(pl.multiple_of(c * half, half), half)
            retained = ret[here, :] + reach_ref[s, at, :] * matmul(q_ref[s, at, :], st_ref[s])
            normed, inverse = normalize(retained)
            hn_ref[here, :] = normed
            hi_ref[here, :] = inverse
            pre = sw_ref[here, :]
            gated = (pre * jax.nn.sigmoid(pre) * normed.astype(BF16).astype(F32)).astype(BF16)
            ga_ref[here, :] = gated
            for n in range(4):
                cut = pl.ds(n * quarter, quarter)
                value = matmul(gated, w2d[:, cut]).astype(BF16)
                part[pl.ds(2 * c, 2), :, cut] = value.reshape(2, tokens, quarter)
            return carry

        lax.fori_loop(0, 4, outer, 0)
        stage.put(*range(2, 17))

        def reduce(u):
            m = Mover(Place(u), names, send, recv)
            low = tokens // 2

            def spread_stage():
                spread_on(u)
                yield

            together(
                [
                    line_reduce(m, "s", lambda i: part.at[i], res_ref, sib, right, left),
                    plane_gather(
                        m, "C", cot_ref, top_all, token_slot, (pl.ds(0, low), pl.ds(low, low))
                    ),
                    later(spread_stage(), 2),
                ]
            )
            m.finish()

        for_each(reduce)

        def norm_two(i, carry):
            at = pl.ds(pl.multiple_of(i * 16, 16), 16)
            residual = hid_ref[at, :].astype(F32) + res_ref[at, :]
            res_ref[at, :] = residual
            normed, _ = normalize(residual)
            s2[at, :] = (normed * gain_ref[1:2, :]).astype(BF16)
            return carry

        lax.fori_loop(0, tokens // 16, norm_two, 0)
        low = tokens // 2
        for _ in plane_gather(
            common, "k", s2, s2_all, token_slot, (pl.ds(0, low), pl.ds(low, low))
        ):
            pass

        def last(u):
            spread_on(u)
            whole[u].finish()
            for v, m, _ in spread:
                if u == v:
                    m.finish()

        for_each(last)
        for copy in keep:
            copy.wait()
        common.finish()
        assert len(names) <= N_SEMS

    return staged_call(
        kernel,
        "forward",
        [
            (hidden, True), (cot, False), (decay, False), (w_down, False), (w_query, True), (w_key, True),
            (w_value, True), (w_swish, True), (w_output, True), (w_gate, True), (w_up, True), (gains, True),
        ],
        [
            ((width, cols), BF16, False),
            ((8, tokens, width), BF16, False),
            ((4 * out_rows, width), BF16, True),
            ((2, block, key), BF16, True),
            ((2, block, key), BF16, True),
            ((2, block, val), BF16, True),
            ((both, val), F32, True),
            ((2, block, block), BF16, True),
            ((2, block, block), F32, True),
            ((2, key, val), BF16, True),
            ((2, block, 1), F32, True),
            ((2, block, 1), F32, True),
            ((8, block), F32, True),
            ((8, width), F32, True),
            ((both, val), F32, True),
            ((both, 1), F32, True),
            ((both, val), BF16, True),
            ((tokens, width), F32, True),
            ((8, tokens, width), BF16, False),
            ((8, tokens, width), BF16, False),
            ((8, 4, rows, ff2), BF16, False),
            ((4, out_rows, width), BF16, False),
        ],
        [
            ((8, rows, cols), BF16),
            ((4, out_rows, quarter), BF16),
            ((8, rows, ff2), BF16),
            ((width, cols), BF16),
            ((8, tokens, width), BF16),
            ((4, out_rows, width), BF16),
            ((8, 2, block), F32),
            ((8, rows, ff2), BF16),
            ((8, block), F32),
            ((block, 8), F32),
            ((2, key, val), BF16),
            ((4, 2, key, val), BF16),
            ((both, val), F32),
            ((8, tokens, width), BF16),
            ((4, tokens, width), BF16),
            ((4, tokens, width), BF16),
            ((4, tokens, width), BF16),
            ((tokens, width), BF16),
        ],
        1,
    )


def feed_forward(scaled, top, w_gu, w_dn, residual, cot, gains):
    _, tokens, width = scaled.shape
    out_rows = w_dn.shape[1]
    rows, ff2 = w_gu.shape[2:]
    ff = ff2 // 2
    block = 4 * tokens

    def kernel(
        stage, s2_ref, top_ref, gu_ref, wd_ref, res_ref, cot_ref, gain_ref, grad, grad_low, term, dout, lo, ggu,
        w_d, prod, grad_gu, part, down, total, sib, sums, got, got2, right, left, send, recv,
    ):
        uly = lax.axis_index(ULY)
        names = {}
        p = Place(uly)
        greet(line_partners(p) + plane_partners(p)[1:])
        common = Mover(p, names, send, recv)
        movers = [
            Mover(Place(u), names, send, recv, lambda: halves_of_columns(right.at[0], 0))
            for u in range(4)
        ]
        lines = [
            line_reduce(m, "d", lambda b: down.at[b], dout, None, right, left, halves_of_columns)
            for m in movers
        ]

        def for_each(body):
            for u in range(4):
                pl.when(uly == u)(functools.partial(body, u))

        stage.need(0, 2)

        def weights():
            return gu_ref[...].reshape(32 * rows, ff2)

        def tokens_of(s):
            here = pl.ds(pl.multiple_of(s * block, block), block)
            lhs = s2_ref[pl.ds(4 * s, 4)].reshape(block, width)
            pre = matmul(lhs, weights())
            gate_pre, up_pre = pre[:, :ff], pre[:, ff:]
            if 1 in stage.loads:
                stage.need(1, 3)
                for i in range(4):
                    w_d[i * out_rows : (i + 1) * out_rows, :] = wd_ref[i]
            grad_product = dot_nt(top_ref[pl.ds(4 * s, 4)].reshape(block, width), w_d[...])
            sigma = jax.nn.sigmoid(gate_pre)
            act = gate_pre * sigma
            prod[here, :] = (act * up_pre).astype(BF16)
            slope = sigma * (1.0 + gate_pre * (1.0 - sigma))
            grad_gu[here, :ff] = (grad_product * up_pre * slope).astype(BF16)
            grad_gu[here, ff:] = (grad_product * act).astype(BF16)

        def tokens_back(s):
            here = pl.ds(pl.multiple_of(s * block, block), block)

            value = dot_nt(grad_gu[here, :], weights()).astype(BF16)
            part[pl.ds(4 * s, 4)] = value.reshape(4, tokens, width)

        reduced = plane_reduce(common, "s", part, total, sib, sums, got, got2)
        tokens_of(p.other)
        tokens_of(p.dp)

        def down_grad(n, carry):
            at = pl.ds(pl.multiple_of(n * 512, 512), 512)
            value = dot_t(prod[...], top_ref[:, :, at].reshape(2 * block, 512)).astype(BF16)
            for i in range(4):
                down[i, :, at] = value[i * out_rows : (i + 1) * out_rows]
            return carry

        lax.fori_loop(0, width // 512, down_grad, 0)
        for_each(lambda u: next(lines[u]))
        tokens_back(p.other)
        next(reduced)
        tokens_back(p.dp)
        next(reduced)
        for_each(lambda u: next(lines[u]))

        def up_grad(n, carry):
            at = pl.ds(pl.multiple_of(n * 4 * rows, 4 * rows), 4 * rows)
            value = dot_t(s2_ref[:, :, at].reshape(2 * block, 4 * rows), grad_gu[...])
            ggu[n] = value.astype(BF16).reshape(4, rows, ff2)
            return carry

        lax.fori_loop(0, 8, up_grad, 0)
        stage.put(5)
        for_each(lambda u: next(lines[u]))
        next(reduced)

        def out_part(n, carry):
            at = pl.ds(pl.multiple_of(n * 512, 512), 512)
            value = matmul(prod[...], w_d[:, at]).astype(BF16)
            lo[:, :, at] = value.reshape(8, tokens, 512)
            return carry

        lax.fori_loop(0, width // 512, out_part, 0)
        stage.put(4)
        for _ in reduced:
            pass
        stage.need(4, 5, 6)

        def back(i, carry):
            at = pl.ds(pl.multiple_of(i * 16, 16), 16)
            normed, inverse = normalize(res_ref[at, :])
            scaled_grad = total[at, :]
            value = cot_ref[at, :].astype(F32) + norm_back(
                scaled_grad * gain_ref[1:2, :], normed, inverse
            )
            grad[at, :] = value
            grad_low[at, :] = value.astype(BF16)
            return carry + jnp.sum(scaled_grad * normed, axis=0, keepdims=True)

        term[...] = lax.fori_loop(0, tokens // 16, back, jnp.zeros((1, width), F32))

        def last(u):
            for _ in lines[u]:
                pass
            movers[u].finish()

        for_each(last)
        common.finish()
        assert len(names) <= N_SEMS

    return staged_call(
        kernel,
        "feed_forward",
        [(array, True) for array in (scaled, top, w_gu, w_dn, residual, cot, gains)],
        [
            ((tokens, width), F32, True),
            ((tokens, width), BF16, True),
            ((1, width), F32, True),
            ((out_rows, width), F32, True),
            ((8, tokens, width), BF16, True),
            ((8, 4, rows, ff2), BF16, True),
        ],
        [
            ((4 * out_rows, width), BF16),
            ((2 * block, ff), BF16),
            ((2 * block, ff2), BF16),
            ((8, tokens, width), BF16),
            ((4, out_rows, width), BF16),
            ((tokens, width), F32),
            ((4, tokens, width), BF16),
            ((4, tokens, width), BF16),
            ((2, tokens, width), BF16),
            ((tokens, width), BF16),
            ((4, out_rows, width), BF16),
            ((4, out_rows, width), BF16),
        ],
        3,
        (0, 2),
    )


def attention_back(
    own, lo, ggu, w_out, gated, normed, inverse, swish, q, k, v, weights, mask, state_in, reach, tail, cum
):
    tokens, width = own.shape
    both, val = gated.shape
    block, key = q.shape[1:]
    rows, cols = ggu.shape[3:]
    piece = w_out.shape[0] // 4
    half = block // 2
    at_v, at_s = 2 * key, 2 * key + val

    def kernel(
        stage, own_ref, lo_ref, g_ref, wo_ref, ga_ref, hn_ref, hi_ref, sw_ref, q_ref, k_ref, v_ref, w_ref, mask_ref, st_ref,
        reach_ref, tail_ref, cum_ref, cat_ref, total, osum, gsum,
        gout, oxs, oys, ox2, oy2, gy, gr, gs, gq, gk, gv, gst, gsts, sib, chip, got, got2, right, left, send, recv,
    ):
        uly = lax.axis_index(ULY)
        names = {}
        place = Place(uly)
        greet(line_partners(place) + plane_partners(place)[1:])
        stage.need(0, 1, 2)
        common = Mover(place, names, send, recv)
        movers = [Mover(Place(u), names, send, recv, lambda: right.at[0, 0]) for u in range(4)]
        ways = [
            line_reduce(
                movers[u],
                "f",
                lambda b: g_ref.at[:, :, b],
                gsum,
                None,
                right,
                left,
                lambda view, i: view.at[i],
            )
            for u in range(4)
        ]

        def for_each(body):
            for u in range(4):
                pl.when(uly == u)(functools.partial(body, u))

        def first(u):
            def sums():
                yield
                next(ways[u])
                yield
                yield
                next(ways[u])

            m = Mover(Place(u), names, send, recv)
            together(
                [
                    plane_reduce(m, "s", lo_ref, total, sib, chip, got, got2),
                    sums(),
                    line_gather(m, "k", own_ref, gy),
                ]
            )
            m.finish()

        for_each(first)

        stage.put(1)
        stage.need(*range(3, 17))

        def chunk(c):
            return pl.ds(pl.multiple_of(c * half, half), half)

        def gradients(c, carry):
            at = chunk(c)
            grad = gy[pl.ds(2 * c, 2)].reshape(half, width)
            gg = dot_nt(grad, wo_ref[...])
            pre = sw_ref[at, :]
            sigma = jax.nn.sigmoid(pre)
            head = hn_ref[at, :]
            low = head.astype(BF16).astype(F32)
            cat_ref[at, at_s : at_s + val] = (
                gg * low * (sigma * (1.0 + pre * (1.0 - sigma)))
            ).astype(BF16)
            gh = (gg * (pre * sigma)).astype(BF16).astype(F32)
            mean = jnp.mean(gh * head, axis=-1, keepdims=True)
            grad_retained = (hi_ref[at, :] * (gh - head * mean)).astype(BF16)
            gr[at, :] = grad_retained
            s = lax.div(c, 2)
            part = pl.ds(pl.multiple_of(lax.rem(c, 2) * half, half), half)
            gs[at, :] = (dot_nt(grad_retained, v_ref[s]) * mask_ref[s, part, :]).astype(BF16)
            return carry

        lax.fori_loop(0, both // half, gradients, 0)
        for s in range(2):
            at = pl.ds(s * block, block)
            reached = (q_ref[s].astype(F32) * reach_ref[s]).astype(BF16)
            gst[s] = dot_t(reached, gr[at, :]).astype(BF16)
        states = plane_gather(
            common, "t", gst, gsts, state_slot, (pl.ds(0, 1), pl.ds(1, 1)), pair=False
        )
        next(states)
        for_each(lambda u: next(ways[u]))

        for s in range(2):
            at = pl.ds(s * block, block)
            gq[at, :] = jnp.dot(gs[at, :], k_ref[s], preferred_element_type=F32)
            gk[at, :] = dot_t(gs[at, :], q_ref[s])
        def out_grad(n, carry):
            at = pl.ds(pl.multiple_of(n * 512, 512), 512)
            grad = gy[:, :, at].reshape(both, 512)
            value = dot_t(ga_ref[...], grad).astype(BF16)
            for i in range(4):
                gout[i, :, at] = value[i * piece : (i + 1) * piece]
            return carry

        lax.fori_loop(0, width // 512, out_grad, 0)
        next(states)

        quarter = width // 4

        def column(part, c):
            return gout.at[part, :, pl.ds(pl.multiple_of(c * quarter, quarter), quarter)]

        for i, (cx, cy) in ((1, (place.dg, place.dg)), (0, (place.xn, place.yn))):
            common.send(("ox", i), column(pl.ds(0, 2), cx), oxs.at[i], place.at(ctx=place.xn))
            common.send(("oy", i), column(pl.ds(2, 2), cy), oys.at[i], place.at(ctx=place.yn))
        for s in range(2):
            at = pl.ds(s * block, block)
            gv[at, :] = dot_t(w_ref[s], gr[at, :])
        for _ in states:
            pass
        for s in range(2):
            at = pl.ds(s * block, block)
            factors = block_factors(cum_ref, place.ctx, s, True)
            update = factors[0] * gsts[0, s].astype(F32)
            for j in range(1, 4):
                update = update + factors[j] * gsts[j, s].astype(F32)
            update = update.astype(BF16)
            grad = gr[at, :]
            cat_ref[at, :key] = (gq[at, :] + reach_ref[s] * dot_nt(grad, st_ref[s])).astype(BF16)
            cat_ref[at, key:at_v] = (gk[at, :] + tail_ref[s] * dot_nt(v_ref[s], update)).astype(BF16)
            cat_ref[at, at_v:at_s] = (
                gv[at, :] + tail_ref[s] * jnp.dot(k_ref[s], update, preferred_element_type=F32)
            ).astype(BF16)
        stage.put(0)
        common.arrive(("ox", 1), oxs.at[1])
        common.arrive(("oy", 1), oys.at[1])
        for t in range(2):
            add_up(oxs.at[1, t], [column(t, place.yn), oxs.at[1, t]])
            add_up(oys.at[1, t], [column(2 + t, place.xn), oys.at[1, t]])
        common.send("oy2", oxs.at[1], oy2, place.at(ctx=place.yn))
        common.send("ox2", oys.at[1], ox2, place.at(ctx=place.xn))

        def last(u):
            for _ in ways[u]:
                pass
            movers[u].finish()

        for_each(last)
        for name, ref in ((("ox", 0), oxs.at[0]), (("oy", 0), oys.at[0]), ("oy2", oy2), ("ox2", ox2)):
            common.arrive(name, ref)
        for us in range(4):
            got, got2 = (oxs, oy2) if us < 2 else (oys, ox2)
            add_up(osum.at[us], [column(us, place.ctx), got.at[0, us % 2], got2.at[us % 2]])
        common.finish()
        assert len(names) <= N_SEMS

    arrays = (own, lo, ggu, w_out, gated, normed, inverse, swish, q, k, v, weights, mask, state_in, reach, tail, cum)
    return staged_call(
        kernel,
        "attention_back",
        [(array, True) for array in arrays],
        [
            ((both, 2 * key + 2 * val), BF16, True),
            ((tokens, width), F32, True),
            ((4, piece, width // 4), BF16, True),
            ((2, 4, rows, cols), BF16, True),
        ],
        [
            ((4, piece, width), BF16),
            *[((2, 2, piece, width // 4), BF16)] * 2,
            *[((2, piece, width // 4), BF16)] * 2,
            ((8, tokens, width), BF16),
            ((both, val), BF16),
            ((both, block), BF16),
            ((both, key), F32),
            ((both, key), F32),
            ((both, val), F32),
            ((2, key, val), BF16),
            ((4, 2, key, val), BF16),
            ((4, tokens, width), BF16),
            ((4, tokens, width), BF16),
            ((2, tokens, width), BF16),
            ((tokens, width), BF16),
            ((4, 2, 4, rows, cols), BF16),
            ((4, 2, 4, rows, cols), BF16),
        ],
        7,
    )


def last_exchange(grad_cat, w_all, scaled, gout, gffn, inputs, term):
    tokens, width = inputs.shape
    both, cols = grad_cat.shape
    block = both // 2
    out_rows, quarter = gout.shape[1:]
    rows, ff2 = gffn.shape[1:]

    def streams(
        m, line, tile, f_ref, in_ref, t_ref, out, gall, fall, gains, gotx, goty, gotx2, goty2, away,
    ):
        p = m.place
        u = p.uly

        def attn():
            for t in range(4):
                m.arrive(("gx", 1, t), gotx.at[1, t])
                add_up(gotx.at[1, t], [tile(0, p.yn, t), gotx.at[1, t]])
                m.send(("gy2", t), gotx.at[1, t], goty2.at[t], p.at(ctx=p.yn))
                m.arrive(("gy", 1, t), goty.at[1, t])
                add_up(goty.at[1, t], [tile(1, p.xn, t), goty.at[1, t]])
                m.send(("gx2", t), goty.at[1, t], gotx2.at[t], p.at(ctx=p.xn))
            yield
            yield
            for t in range(4):
                for dp, got, got2, tags in (
                    (0, gotx, goty2, ("gx", "gy2")),
                    (1, goty, gotx2, ("gy", "gx2")),
                ):
                    m.arrive((tags[0], 0, t), got.at[0, t])
                    m.arrive((tags[1], t), got2.at[t])
                    add_up(got.at[0, t], [tile(dp, p.ctx, t), got.at[0, t], got2.at[t]])
                    there = gall.at[p.dp * 4 + u]
                    if t == u:

                        @pl.when(p.dp == dp)
                        def _(got=got, there=there):
                            here = pltpu.make_async_copy(
                                got.at[0, u], there, m.send_sems.at[m.number("G")]
                            )
                            here.start()
                            here.wait()

                        @pl.when(p.dp != dp)
                        def _(got=got, there=there, dp=dp):
                            m.remote(
                                ("gc", u), got.at[0, u], there, (dp, p.ctx, u)
                            ).start()
                    else:
                        k = m.number(("gs", dp, t))
                        copies = []
                        for q in range(2):
                            copies.append(
                                pltpu.make_async_remote_copy(
                                    src_ref=got.at[0, t],
                                    dst_ref=there,
                                    send_sem=m.send_sems.at[k],
                                    recv_sem=m.recv_sems.at[m.number(("g", q, u))],
                                    device_id=(dp, p.ctx, t),
                                    device_id_type=MESH,
                                )
                            )
                        pl.when(p.dp == dp)(copies[0].start)
                        pl.when(p.dp != dp)(copies[1].start)
                        m.sent.append(copies[0])
            for _ in range(6):
                yield
            m.remote(("gc", u), gotx.at[0, u], gotx.at[0, u], p.at(dp=p.other)).wait_send()
            m.arrive(("gc", u), gall.at[p.other * 4 + u])
            for us in range(4):
                if us != u:
                    m.arrive(("g", 0, us), gall.at[p.dp * 4 + us])
                    m.arrive(("g", 1, us), gall.at[p.other * 4 + us])

        def feed():
            mine = fall.at[p.dp * 4 + p.ctx]
            copy = m.local("F", f_ref.at[p.dp * 4 + p.ctx], mine)
            spots = [(q, c, i) for i, c in enumerate((p.ctx, p.xn, p.yn, p.dg)) for q in range(2)][1:]
            for q, c, i in spots:
                dp = p.dp if q == 0 else p.other
                m.send(("f", q, i), f_ref.at[dp * 4 + c], mine, p.at(dp=dp, ctx=c))
            for _ in range(4):
                yield
            for q, c, i in spots:
                dp = p.dp if q == 0 else p.other
                m.arrive(("f", q, i), fall.at[dp * 4 + c])
            copy.wait()

        def tokens_stream():
            yield from line

            def body(i, total):
                at = pl.ds(pl.multiple_of(i * 16, 16), 16)
                values = in_ref[at, :].astype(F32)
                normed, _ = normalize(values)
                return total + jnp.sum(out[at, :] * normed, axis=0, keepdims=True)

            total = lax.fori_loop(0, tokens // 16, body, jnp.zeros((1, width), F32))
            row = lax.broadcasted_iota(jnp.int32, (8, width), 0)
            gains[...] = jnp.where(
                row == 0,
                jnp.broadcast_to(total, (8, width)),
                jnp.where(row == 1, jnp.broadcast_to(t_ref[...], (8, width)), 0.0),
            )
            for i, device in enumerate((p.at(dp=p.other), p.at(ctx=p.xn), p.at(ctx=p.yn))):
                m.remote(("n", i), gains, away.at[i], device).start()
                yield
                m.remote(("n", i), gains, away.at[i], device).wait()
                gains[...] = gains[...] + away[i]
            copies = [
                m.remote(("N", u, other), gains, away.at[3 + u], p.at(uly=other))
                for other in range(4)
                if other != u
            ]
            for copy in copies:
                copy.start()
            yield
            mine = gains[...]
            for other in range(4):
                if other != u:
                    m.arrive(("N", other, u), away.at[3 + other])
                    mine = mine + away[3 + other]
            for copy in copies:
                copy.wait_send()
            gains[...] = mine

        return [
            attn(),
            tokens_stream(),
            later(feed(), 3),
        ]

    def kernel(
        stage, cat_ref, wa_ref, s1_ref, o_ref, f_ref, in_ref, t_ref, out, gall, oall, fall, gains,
        grads, part, sib, right, left, gotx, goty, gotx2, goty2, away, send, recv,
    ):
        uly = lax.axis_index(ULY)
        names = {}
        p = Place(uly)
        greet(everyone(p))
        stage.need(0, 2)
        common = Mover(p, names, send, recv)

        def for_each(body):
            for u in range(4):
                pl.when(uly == u)(functools.partial(body, u))

        def tile(dp, c, t):
            return grads.at[dp, c, pl.ds(t * rows, rows)]

        def weight_grad(dp, c):
            at = pl.ds(pl.multiple_of((dp * 4 + c) * 4 * rows, 4 * rows), 4 * rows)
            grads[dp, c] = dot_t(s1_ref[:, :, at].reshape(both, 4 * rows), cat_ref[...]).astype(BF16)

        def token_grad(s):
            rows_s = pl.ds(pl.multiple_of(s * block, block), block)
            value = dot_nt(cat_ref[rows_s, :], wa_ref[:, :cols]).astype(BF16)
            part[pl.ds(4 * s, 4)] = value.reshape(4, tokens, width)

        def to_x(i, c):
            weight_grad(0, c)
            for t in range(4):
                common.send(("gx", i, t), tile(0, c, t), gotx.at[i, t], p.at(ctx=p.xn))

        def to_y(i, c):
            weight_grad(1, c)
            for t in range(4):
                common.send(("gy", i, t), tile(1, c, t), goty.at[i, t], p.at(ctx=p.yn))

        def out_copies(m, senders):
            at = m.place
            home_dp, home_ctx = at.uly // 2, 2 * (at.uly % 2) + at.dp
            found = []
            for us in range(4):
                own = (home_dp == at.dp) & (home_ctx == at.ctx) & (us == at.uly)
                copies = [
                    pltpu.make_async_remote_copy(
                        src_ref=o_ref.at[us],
                        dst_ref=oall.at[at.ctx],
                        send_sem=m.send_sems.at[m.number(("os", us))],
                        recv_sem=m.recv_sems.at[m.number(("o", j))],
                        device_id=(home_dp, home_ctx, us),
                        device_id_type=MESH,
                    )
                    for j in senders
                ]
                found.append((us, own, copies))
            return found

        def out_start(u):
            m = Mover(Place(u), names, send, recv)
            for us, own, copies in out_copies(m, range(4)):

                @pl.when(own)
                def _(us=us):
                    here = pltpu.make_async_copy(
                        o_ref.at[us], oall.at[p.ctx], send.at[m.number("O")]
                    )
                    here.start()
                    here.wait()

                for j, copy in enumerate(copies):
                    pl.when(jnp.logical_not(own) & (p.ctx == j))(copy.start)

        def out_end(u):
            m = Mover(Place(u), names, send, recv)
            head_dp, head_u = lax.rem(p.ctx, 2), p.dp * 2 + lax.div(p.ctx, 2)
            for j in range(4):
                mine = (head_dp == p.dp) & (p.ctx == j) & (head_u == u)

                @pl.when(jnp.logical_not(mine))
                def _(j=j):
                    m.arrive(("o", j), oall.at[j])

            for _, own, copies in out_copies(m, range(1)):
                pl.when(jnp.logical_not(own))(copies[0].wait_send)

        stage.need(3)
        for_each(out_start)
        to_x(1, p.dg)
        to_y(1, p.dg)
        stage.need(1)
        token_grad(p.other)
        token_grad(p.dp)
        movers = [
            Mover(
                Place(u), names, send, recv, lambda: halves_of_rows(sib.at[0], 0), lambda: sib.at[0]
            )
            for u in range(4)
        ]
        lines = [
            line_reduce(m, "s", lambda i: part.at[i], out, sib, right, left) for m in movers
        ]
        for_each(lambda u: next(lines[u]))
        to_x(0, p.xn)
        to_y(0, p.yn)
        weight_grad(0, p.yn)
        weight_grad(1, p.xn)
        weight_grad(0, p.ctx)
        weight_grad(1, p.ctx)
        stage.need(5, 6)

        def rest(u):
            m = Mover(Place(u), names, send, recv)
            together(
                streams(
                    m, lines[u], tile, f_ref, in_ref, t_ref, out, gall, fall, gains,
                    gotx, goty, gotx2, goty2, away,
                )
            )
            m.finish()
            movers[u].finish()
            out_end(u)

        for_each(rest)
        common.finish()
        assert len(names) <= N_SEMS

    arrays = (grad_cat, w_all, scaled, gout, gffn, inputs, term)
    return staged_call(
        kernel,
        "last",
        [(array, i != 4) for i, array in enumerate(arrays)],
        [
            ((tokens, width), F32, True),
            ((8, rows, cols), BF16, False),
            ((4, out_rows, quarter), BF16, False),
            ((8, rows, ff2), BF16, False),
            ((8, width), F32, True),
        ],
        [
            ((2, 4, 4 * rows, cols), BF16),
            ((8, tokens, width), BF16),
            *[((4, tokens, width), BF16)] * 3,
            *[((2, 4, rows, cols), BF16)] * 2,
            *[((4, rows, cols), BF16)] * 2,
            ((7, 8, width), F32),
        ],
        2,
        (3, 0, 2),
    )


def local(
    hidden_in,
    cotangent,
    log_decay,
    w_query,
    w_key,
    w_value,
    w_swish,
    w_output,
    w_gate,
    w_up,
    w_down,
    gain_attn,
    gain_ffn,
):
    bf16, f32 = BF16, F32
    dp, ctx = lax.axis_index(DP), lax.axis_index(CTX)
    tokens = hidden_in.shape[1]
    width = hidden_in.shape[2]
    rows = w_query.shape[0]
    out_rows = w_output.shape[0]
    key, val, ff = KEY_DIM, VALUE_DIM, w_gate.shape[1] // 8

    gains = jnp.pad(jnp.stack([gain_attn, gain_ffn], axis=1), ((0, 0), (0, 30)))
    block = 4 * tokens
    (
        w_all, scaled_one, w_out, q, k, v, swish_pre, weights, mask, state_in, reach, tail, cum,
        gains, head_normed, head_inverse, gated, residual, scaled_two, top_all, w_gu, w_dn,
    ) = forward(
        hidden_in[0], cotangent[0], log_decay[0], w_down,
        w_query, w_key, w_value, w_swish, w_output, w_gate, w_up, gains,
    )
    grad_residual, grad_y, gain_two_term, grad_down, layer_part, ggu = feed_forward(
        scaled_two, top_all, w_gu, w_dn, residual, cotangent[0], gains
    )
    grad_cat, out_part, g_out, ggu = attention_back(
        grad_y,
        layer_part,
        ggu.reshape(2, 4, 4, rows, 2 * ff),
        w_out,
        gated,
        head_normed,
        head_inverse,
        swish_pre,
        q,
        k,
        v,
        weights,
        mask,
        state_in,
        reach,
        tail,
        cum,
    )
    gs1, gcat, g_out, ggu, gain_terms = last_exchange(
        grad_cat,
        w_all,
        scaled_one,
        g_out,
        ggu.reshape(8, rows, 2 * ff),
        hidden_in[0],
        gain_two_term,
    )
    (
        grad_query, grad_key, grad_value, grad_swish, grad_output, grad_gate, grad_up,
        layer_out, grad_input, grad_down, gain_one_term, gain_two_term,
    ) = finish(
        gcat, g_out, ggu, residual, out_part, grad_residual, gs1, hidden_in[0], gains, gain_terms, grad_down
    )
    return (
        layer_out[None],
        grad_input[None],
        grad_query,
        grad_key,
        grad_value,
        grad_swish,
        grad_output,
        grad_gate,
        grad_up,
        grad_down,
        gain_one_term[0],
        gain_two_term[0],
    )


def solution(mesh):
    shape = mesh.shape
    planned = (shape[DP], shape[CTX], shape[ULY]) == (2, 4, 4)
    tokens = P(DP, (CTX, ULY), None)
    weight = P(EVERYWHERE, None)
    gain = P(EVERYWHERE)
    return jax.shard_map(
        local if planned else local_any,
        mesh=mesh,
        in_specs=(tokens, tokens, P(DP, ULY, CTX), *[weight] * 8, gain, gain),
        out_specs=(tokens, tokens, *[weight] * 8, gain, gain),
        check_vma=False,
    )
```

```python
import functools
import math

import jax
import jax.numpy as jnp
from jax import lax
from jax.experimental import pallas as pl
from jax.experimental.pallas import tpu as pltpu
from jax.sharding import PartitionSpec as P

RETENTION_HEADS = 8
KEY_DIM = 256
VALUE_DIM = 432


EPSILON = 1e-06
DP, CTX, ULY = "dp", "ctx", "ulysses"
EVERYWHERE = (DP, CTX, ULY)


def entering(value, axis, join, neutral, backward):
    count, mine = (lax.axis_size(axis), lax.axis_index(axis))
    pieces = jax.tree.map(lambda part: lax.all_gather(part, axis), value)
    if backward:
        pieces = jax.tree.map(lambda part: part[::-1], pieces)
        mine = count - 1 - mine
    subtotal = jax.tree.map(
        lambda part, zero: jnp.full_like(part, 0) + jnp.asarray(zero, part.dtype), value, neutral
    )

    def step(position, subtotal):
        longer = join(subtotal, jax.tree.map(lambda part: part[position], pieces))
        return jax.tree.map(lambda new, old: jnp.where(position < mine, new, old), longer, subtotal)

    return lax.fori_loop(0, count - 1, step, subtotal)


def normalize(values):
    inverse = lax.rsqrt(jnp.mean(values * values, axis=-1, keepdims=True) + EPSILON)
    return (values * inverse, inverse)


def norm_back(grad_normed, normed, inverse):
    return inverse * (grad_normed - normed * jnp.mean(grad_normed * normed, axis=-1, keepdims=True))


def swish_slope(values):
    sigma = jax.nn.sigmoid(values)
    return sigma * (1.0 + values * (1.0 - sigma))


def carry_forward(earlier, later):
    return (earlier[0] * later[0], later[0][:, None, None] * earlier[1] + later[1])


def carry_backward(earlier, later):
    return (earlier[0] * later[0], later[1] + later[0][:, None, None] * earlier[1])


def running_sum(values):
    size = values.shape[-1]
    upper = lax.broadcasted_iota(jnp.int32, (size, size), 0) <= lax.broadcasted_iota(
        jnp.int32, (size, size), 1
    )
    return jnp.dot(values, upper.astype(jnp.float32), precision=lax.Precision.HIGHEST)


def matmul(left, right):
    return jnp.dot(left, right, preferred_element_type=jnp.float32)


def local_any(
    hidden_in,
    cotangent,
    log_decay,
    w_query,
    w_key,
    w_value,
    w_swish,
    w_output,
    w_gate,
    w_up,
    w_down,
    gain_attn,
    gain_ffn,
):
    highest = lax.Precision.HIGHEST
    query_full, key_full, value_full, swish_full, output_full, gain_one = (
        lax.all_gather(w_query, EVERYWHERE, axis=0, tiled=True),
        lax.all_gather(w_key, EVERYWHERE, axis=0, tiled=True),
        lax.all_gather(w_value, EVERYWHERE, axis=0, tiled=True),
        lax.all_gather(w_swish, EVERYWHERE, axis=0, tiled=True),
        lax.all_gather(w_output, EVERYWHERE, axis=0, tiled=True),
        lax.all_gather(gain_attn, EVERYWHERE, axis=0, tiled=True),
    )
    inputs = hidden_in[0].astype(jnp.float32)
    tokens = inputs.shape[0]
    normed_one, inverse_one = normalize(inputs)
    scaled_one = (normed_one * gain_one.astype(jnp.float32)).astype(jnp.bfloat16)
    queries = (
        matmul(scaled_one, query_full)
        .astype(jnp.bfloat16)
        .reshape(tokens, RETENTION_HEADS, KEY_DIM)
    )
    keys_tok = (
        matmul(scaled_one, key_full).astype(jnp.bfloat16).reshape(tokens, RETENTION_HEADS, KEY_DIM)
    )
    values_tok = (
        matmul(scaled_one, value_full)
        .astype(jnp.bfloat16)
        .reshape(tokens, RETENTION_HEADS, VALUE_DIM)
    )
    swish_pre = matmul(scaled_one, swish_full)
    head_q, head_k, head_v = (
        lax.all_to_all(queries, ULY, split_axis=1, concat_axis=0, tiled=True),
        lax.all_to_all(keys_tok, ULY, split_axis=1, concat_axis=0, tiled=True),
        lax.all_to_all(values_tok, ULY, split_axis=1, concat_axis=0, tiled=True),
    )
    block = head_q.shape[0]
    scale = 1.0 / math.sqrt(KEY_DIM)
    cumulative = running_sum(log_decay[0])
    later = lax.broadcasted_iota(jnp.int32, (block, block), 0) >= lax.broadcasted_iota(
        jnp.int32, (block, block), 1
    )
    gap = cumulative[:, :, None] - cumulative[:, None, :]
    mask = jnp.where(later[None], jnp.exp(jnp.minimum(gap, 0.0)), 0.0) * scale
    scores = jnp.einsum("thd,shd->hts", head_q, head_k, preferred_element_type=jnp.float32)
    weights = (scores * mask).astype(jnp.bfloat16)
    intra = jnp.einsum("hts,she->the", weights, head_v, preferred_element_type=jnp.float32)
    query_f = head_q.astype(jnp.float32)
    key_f = head_k.astype(jnp.float32)
    value_f = head_v.astype(jnp.float32)
    tail = jnp.exp(cumulative[:, -1:] - cumulative).T[:, :, None]
    reach = jnp.exp(cumulative).T[:, :, None]
    update = jnp.einsum("shd,she->hde", key_f * tail, value_f, precision=highest)
    block_decay = jnp.exp(cumulative[:, -1])
    identity = (jnp.ones_like(block_decay), jnp.zeros_like(update))
    _, state_in = entering((block_decay, update), CTX, carry_forward, identity, False)
    retained = intra + scale * reach * jnp.einsum(
        "thd,hde->the", query_f, state_in, precision=highest
    )
    head_normed, head_inverse = normalize(retained)
    head_out = head_normed.astype(jnp.bfloat16)
    token_out = lax.all_to_all(
        head_out, ULY, split_axis=0, concat_axis=1, tiled=True
    ).reshape(tokens, RETENTION_HEADS * VALUE_DIM)
    token_out_f = token_out.astype(jnp.float32)
    swish_act = jax.nn.silu(swish_pre)
    gated = (swish_act * token_out_f).astype(jnp.bfloat16)
    residual = inputs + matmul(gated, output_full)
    gate_full, up_full, down_full, gain_two = (
        lax.all_gather(w_gate, EVERYWHERE, axis=0, tiled=True),
        lax.all_gather(w_up, EVERYWHERE, axis=0, tiled=True),
        lax.all_gather(w_down, EVERYWHERE, axis=0, tiled=True),
        lax.all_gather(gain_ffn, EVERYWHERE, axis=0, tiled=True),
    )
    normed_two, inverse_two = normalize(residual)
    scaled_two = (normed_two * gain_two.astype(jnp.float32)).astype(jnp.bfloat16)
    gate_pre = matmul(scaled_two, gate_full)
    up_pre = matmul(scaled_two, up_full)
    product = (jax.nn.silu(gate_pre) * up_pre).astype(jnp.bfloat16)
    layer_out = residual + matmul(product, down_full)
    grad_top = cotangent[0].astype(jnp.float32)
    grad_top_low = grad_top.astype(jnp.bfloat16)
    grad_product = matmul(grad_top_low, down_full.T)
    grad_down_term = matmul(product.T, grad_top_low)
    grad_gate_pre = (grad_product * up_pre * swish_slope(gate_pre)).astype(jnp.bfloat16)
    grad_up_pre = (grad_product * jax.nn.silu(gate_pre)).astype(jnp.bfloat16)
    grad_gate_term = matmul(scaled_two.T, grad_gate_pre)
    grad_up_term = matmul(scaled_two.T, grad_up_pre)
    grad_scaled_two = matmul(grad_gate_pre, gate_full.T) + matmul(grad_up_pre, up_full.T)
    grad_gain_two = jnp.sum(grad_scaled_two * normed_two, axis=0)
    grad_residual = grad_top + norm_back(
        grad_scaled_two * gain_two.astype(jnp.float32), normed_two, inverse_two
    )
    grad_gate, grad_up, grad_down, grad_gain_ffn = (
        lax.psum_scatter(grad_gate_term, EVERYWHERE, scatter_dimension=0, tiled=True),
        lax.psum_scatter(grad_up_term, EVERYWHERE, scatter_dimension=0, tiled=True),
        lax.psum_scatter(grad_down_term, EVERYWHERE, scatter_dimension=0, tiled=True),
        lax.psum_scatter(grad_gain_two, EVERYWHERE, scatter_dimension=0, tiled=True),
    )
    grad_y = grad_residual.astype(jnp.bfloat16)
    grad_output_term = matmul(gated.T, grad_y)
    grad_gated = matmul(grad_y, output_full.T)
    grad_swish_pre = (grad_gated * token_out_f * swish_slope(swish_pre)).astype(jnp.bfloat16)
    grad_token_out = (
        (grad_gated * swish_act).astype(jnp.bfloat16).reshape(tokens, RETENTION_HEADS, VALUE_DIM)
    )
    grad_swish_term = matmul(scaled_one.T, grad_swish_pre)
    grad_head_out = lax.all_to_all(
        grad_token_out, ULY, split_axis=1, concat_axis=0, tiled=True
    ).astype(jnp.float32)
    grad_retained = norm_back(grad_head_out, head_normed, head_inverse).astype(jnp.bfloat16)
    grad_retained_f = grad_retained.astype(jnp.float32)
    grad_weights = jnp.einsum(
        "the,she->hts", grad_retained, head_v, preferred_element_type=jnp.float32
    )
    grad_scores = (grad_weights * mask).astype(jnp.bfloat16)
    grad_state_in = scale * jnp.einsum(
        "thd,the->hde", query_f * reach, grad_retained_f, precision=highest
    )
    _, grad_update = entering((block_decay, grad_state_in), CTX, carry_backward, identity, True)
    grad_head_q = jnp.einsum(
        "hts,shd->thd", grad_scores, head_k, preferred_element_type=jnp.float32
    ) + scale * reach * jnp.einsum("the,hde->thd", grad_retained_f, state_in, precision=highest)
    grad_head_k = jnp.einsum(
        "hts,thd->shd", grad_scores, head_q, preferred_element_type=jnp.float32
    ) + tail * jnp.einsum("she,hde->shd", value_f, grad_update, precision=highest)
    grad_head_v = jnp.einsum(
        "hts,the->she", weights, grad_retained, preferred_element_type=jnp.float32
    ) + tail * jnp.einsum("shd,hde->she", key_f, grad_update, precision=highest)
    grad_queries, grad_keys, grad_values = (
        lax.all_to_all(
            grad_head_q.astype(jnp.bfloat16), ULY, split_axis=0, concat_axis=1, tiled=True
        ),
        lax.all_to_all(
            grad_head_k.astype(jnp.bfloat16), ULY, split_axis=0, concat_axis=1, tiled=True
        ),
        lax.all_to_all(
            grad_head_v.astype(jnp.bfloat16), ULY, split_axis=0, concat_axis=1, tiled=True
        ),
    )
    grad_queries = grad_queries.reshape(tokens, RETENTION_HEADS * KEY_DIM)
    grad_keys = grad_keys.reshape(tokens, RETENTION_HEADS * KEY_DIM)
    grad_values = grad_values.reshape(tokens, RETENTION_HEADS * VALUE_DIM)
    grad_query_term = matmul(scaled_one.T, grad_queries)
    grad_key_term = matmul(scaled_one.T, grad_keys)
    grad_value_term = matmul(scaled_one.T, grad_values)
    grad_scaled_one = (
        matmul(grad_queries, query_full.T)
        + matmul(grad_keys, key_full.T)
        + matmul(grad_values, value_full.T)
        + matmul(grad_swish_pre, swish_full.T)
    )
    grad_gain_one = jnp.sum(grad_scaled_one * normed_one, axis=0)
    grad_input = grad_residual + norm_back(
        grad_scaled_one * gain_one.astype(jnp.float32), normed_one, inverse_one
    )
    grad_query, grad_key, grad_value, grad_swish, grad_output, grad_gain_attn = (
        lax.psum_scatter(
            grad_query_term, EVERYWHERE, scatter_dimension=0, tiled=True
        ),
        lax.psum_scatter(grad_key_term, EVERYWHERE, scatter_dimension=0, tiled=True),
        lax.psum_scatter(
            grad_value_term, EVERYWHERE, scatter_dimension=0, tiled=True
        ),
        lax.psum_scatter(
            grad_swish_term, EVERYWHERE, scatter_dimension=0, tiled=True
        ),
        lax.psum_scatter(
            grad_output_term, EVERYWHERE, scatter_dimension=0, tiled=True
        ),
        lax.psum_scatter(grad_gain_one, EVERYWHERE, scatter_dimension=0, tiled=True),
    )
    return (
        layer_out[None],
        grad_input[None],
        grad_query,
        grad_key,
        grad_value,
        grad_swish,
        grad_output,
        grad_gate,
        grad_up,
        grad_down,
        grad_gain_attn,
        grad_gain_ffn,
    )


MESH = pl.DeviceIdType.MESH
BF16, F32 = jnp.bfloat16, jnp.float32
HBM, VMEM = pltpu.HBM, pltpu.VMEM
N_SEMS = 160


def dot_t(left, right):
    return lax.dot_general(left, right, (((0,), (0,)), ((), ())), preferred_element_type=F32)


def dot_nt(left, right):
    return lax.dot_general(left, right, (((1,), (1,)), ((), ())), preferred_element_type=F32)


def pair_dot(left_axis, right_axis, left, right):
    dims = (((left_axis,), (right_axis,)), ((0,), (0,)))
    return lax.dot_general(left, right, dims, preferred_element_type=F32)


class Place:
    def __init__(self, uly):
        self.dp, self.ctx, self.uly = lax.axis_index(DP), lax.axis_index(CTX), uly
        odd = lax.rem(self.ctx, 2)
        self.xn = self.ctx + 1 - 2 * odd
        self.yn = lax.rem(self.ctx + 2, 4)
        self.dg = self.yn + 1 - 2 * odd
        self.other = 1 - self.dp

    def at(self, dp=None, ctx=None, uly=None):
        return (
            self.dp if dp is None else dp,
            self.ctx if ctx is None else ctx,
            self.uly if uly is None else uly,
        )


class Mover:
    def __init__(self, place, names, send, recv, like=None, like_whole=None):
        self.like, self.like_whole = like, like_whole
        self.place, self.names, self.send_sems, self.recv_sems = place, names, send, recv
        self.sent, self.whole = [], []

    def number(self, name):
        return self.names.setdefault(name, len(self.names))

    def remote(self, name, src, dst, device):
        k = self.number(name)
        return pltpu.make_async_remote_copy(
            src_ref=src,
            dst_ref=dst,
            send_sem=self.send_sems.at[k],
            recv_sem=self.recv_sems.at[k],
            device_id=device,
            device_id_type=MESH,
        )

    def send(self, name, src, dst, device):
        copy = self.remote(name, src, dst, device)
        copy.start()
        self.sent.append(copy if self.like is None else name)

    def send_whole(self, name, src, dst, device):
        copy = self.remote(name, src, dst, device)
        copy.start()
        self.whole.append((copy if self.like is None else None, name, None))

    def arrive(self, name, dst):
        self.remote(name, dst, dst, self.place.at(dp=self.place.other)).wait_recv()

    def local(self, name, src, dst):
        copy = pltpu.make_async_copy(src, dst, self.send_sems.at[self.number(name)])
        copy.start()
        return copy

    def finish(self):
        for copy, name, _ in self.whole:
            if self.like is not None:
                ref = self.like_whole()
                copy = self.remote(name, ref, ref, self.place.at(dp=self.place.other))
            copy.wait_send()
        for copy in self.sent:
            if self.like is not None:
                ref = self.like()
                copy = self.remote(copy, ref, ref, self.place.at(dp=self.place.other))
            copy.wait_send()


def greet(devices, meanwhile=None):
    barrier = pltpu.get_barrier_semaphore()
    for device in devices:
        pl.semaphore_signal(barrier, inc=1, device_id=device, device_id_type=MESH)
    if meanwhile is not None:
        meanwhile()
    pl.semaphore_wait(barrier, len(devices))


def together(streams):
    streams = list(streams)
    while streams:
        left = []
        for stream in streams:
            if next(stream, 0) is None:
                left.append(stream)
        streams = left


def later(stream, stages):
    for _ in range(stages):
        yield
    yield from stream


def add_up(dst, sources, step=32):
    if len(dst.shape) > 2:
        for i in range(dst.shape[0]):
            add_up(dst.at[i], [source.at[i] for source in sources], step)
        return
    rows, columns = dst.shape
    by_rows = rows % step == 0
    step = step if by_rows else 256

    def body(i, carry):
        part = pl.ds(pl.multiple_of(i * step, step), step)
        at = (part, slice(None)) if by_rows else (slice(None), part)
        total = sources[0][at].astype(F32)
        for source in sources[1:]:
            total = total + source[at].astype(F32)
        dst[at] = total.astype(dst.dtype)
        return carry

    lax.fori_loop(0, (rows if by_rows else columns) // step, body, 0)


def halves_of_rows(view, i):
    rows = view.shape[0] // 2
    return view.at[pl.ds(i * rows, rows)]


def halves_of_columns(view, i):
    columns = view.shape[1] // 2
    return view.at[:, pl.ds(i * columns, columns)]


def line_gather(m, tag, own, out, pause=1):
    p = m.place
    u = p.uly
    mine = out.at[p.dp * 4 + u]
    copy = m.local((tag, "="), own, mine)
    for i in range(2):
        src, dst = halves_of_rows(own, i), halves_of_rows(mine, i)
        if u < 3:
            m.send((tag, "r", u, i), src, dst, p.at(uly=u + 1))
        if u > 0:
            m.send((tag, "l", u, i), src, dst, p.at(uly=u - 1))
    m.send((tag, "c", u), own, mine, p.at(dp=p.other))
    for _ in range(pause):
        yield
    for d in range(1, 4):
        for i in range(2):
            for way, b, onward in (("r", u - d, u + 1), ("l", u + d, u - 1)):
                if 0 <= b <= 3:
                    half = halves_of_rows(out.at[p.dp * 4 + b], i)
                    m.arrive((tag, way, b, i), half)
                    if 0 <= onward <= 3:
                        m.send((tag, way, b, i), half, half, p.at(uly=onward))
        for b in (u - d, u + d):
            if 0 <= b <= 3:
                block = out.at[p.dp * 4 + b]
                m.send((tag, "c", b), block, block, p.at(dp=p.other))
        yield
    for b in range(4):
        m.arrive((tag, "c", b), out.at[p.other * 4 + b])
    copy.wait()


def plane_gather(m, tag, own, out, slot, halves, pair=True):
    p = m.place

    def half(c, i):
        return slot(out, p.dp, c, halves[i])

    mine = slot(out, p.dp, p.ctx, None)
    copy = m.local((tag, "="), own, mine)
    m.send((tag, "x"), own, mine, p.at(ctx=p.xn))
    m.send((tag, "y"), own, mine, p.at(ctx=p.yn))
    if pair:
        m.send((tag, "c", 0), own, mine, p.at(dp=p.other))
    yield
    block = slot(out, p.dp, p.xn, None)
    m.arrive((tag, "x"), block)
    m.send((tag, "z", 0), half(p.xn, 0), half(p.xn, 0), p.at(ctx=p.yn))
    if pair:
        m.send((tag, "c", 1), block, block, p.at(dp=p.other))
    block = slot(out, p.dp, p.yn, None)
    m.arrive((tag, "y"), block)
    m.send((tag, "z", 1), half(p.yn, 1), half(p.yn, 1), p.at(ctx=p.xn))
    if pair:
        m.send((tag, "c", 2), block, block, p.at(dp=p.other))
    yield
    for i in range(2):
        block = half(p.dg, i)
        m.arrive((tag, "z", i), block)
        if pair:
            m.send((tag, "c", 3 + i), block, block, p.at(dp=p.other))
    yield
    if pair:
        for i, c in enumerate((p.ctx, p.xn, p.yn)):
            m.arrive((tag, "c", i), slot(out, p.other, c, None))
        for i in range(2):
            m.arrive((tag, "c", 3 + i), slot(out, p.other, p.dg, halves[i]))
    copy.wait()


def line_reduce(m, tag, part, out, sib, right, left, cut=halves_of_rows):
    p = m.place
    u = p.uly
    order = (3, 0, 2, 1) if u < 2 else (0, 3, 1, 2)
    for b in order if sib is not None else ():
        m.send_whole((tag, "c", b), part(p.other * 4 + b), sib.at[b], p.at(dp=p.other))
    met = set()

    def meet(b, i):
        if sib is None:
            return [cut(part(b), i)]
        if b not in met:
            met.add(b)
            m.arrive((tag, "c", b), sib.at[b])
        return [cut(part(p.dp * 4 + b), i), cut(sib.at[b], i)]

    def onward(way, b, i, arrived, there):
        terms = meet(b, i)
        if arrived is not None:
            arrived = cut(arrived.at[b], i)
            m.arrive((tag, way, b, i), arrived)
            terms.append(arrived)
        if len(terms) > 1:
            add_up(terms[-1], terms)
        away = cut((right if way == "r" else left).at[b], i)
        m.send((tag, way, b, i), terms[-1], away, p.at(uly=there))

    for slot in range(3):
        for b in range(4):
            for i in range(2):
                if u < b and u + 3 - b == slot:
                    onward("r", b, i, right if u > 0 else None, u + 1)
        for b in range(4):
            for i in range(2):
                if u > b and 3 - u + b == slot:
                    onward("l", b, i, left if u < 3 else None, u - 1)
        yield
    for i in range(2):
        terms = meet(u, i)
        if u > 0:
            m.arrive((tag, "r", u, i), cut(right.at[u], i))
            terms.append(cut(right.at[u], i))
        if u < 3:
            m.arrive((tag, "l", u, i), cut(left.at[u], i))
            terms.append(cut(left.at[u], i))
        add_up(cut(out, i), terms)


def plane_reduce(m, tag, part, out, sib, sums, got, got2):
    p = m.place
    rows = out.shape[0]
    halves = (pl.ds(0, rows // 2), pl.ds(rows // 2, rows // 2))
    order = (p.dg, p.xn, p.yn, p.ctx)
    for i, c in enumerate(order):
        m.send((tag, "c", i), part.at[p.other * 4 + c], sib.at[c], p.at(dp=p.other))
    yield
    for i, c in enumerate(order):
        m.arrive((tag, "c", i), sib.at[c])
        add_up(sums.at[c], [part.at[p.dp * 4 + c], sib.at[c]])
        if i == 0:
            m.send((tag, "x", 1), sums.at[c, halves[0]], got.at[1, halves[0]], p.at(ctx=p.xn))
            m.send((tag, "y", 1), sums.at[c, halves[1]], got.at[1, halves[1]], p.at(ctx=p.yn))
        if i == 1:
            m.send((tag, "x", 0), sums.at[c, halves[0]], got.at[0, halves[0]], p.at(ctx=p.xn))
        if i == 2:
            m.send((tag, "y", 0), sums.at[c, halves[1]], got.at[0, halves[1]], p.at(ctx=p.yn))
    yield
    m.arrive((tag, "x", 1), got.at[1, halves[0]])
    add_up(got.at[1, halves[0]], [sums.at[p.yn, halves[0]], got.at[1, halves[0]]])
    m.send((tag, "y2"), got.at[1, halves[0]], got2.at[halves[0]], p.at(ctx=p.yn))
    m.arrive((tag, "y", 1), got.at[1, halves[1]])
    add_up(got.at[1, halves[1]], [sums.at[p.xn, halves[1]], got.at[1, halves[1]]])
    m.send((tag, "x2"), got.at[1, halves[1]], got2.at[halves[1]], p.at(ctx=p.xn))
    yield
    m.arrive((tag, "x", 0), got.at[0, halves[0]])
    m.arrive((tag, "y", 0), got.at[0, halves[1]])
    yield
    m.arrive((tag, "y2"), got2.at[halves[0]])
    m.arrive((tag, "x2"), got2.at[halves[1]])
    add_up(out, [sums.at[p.ctx], got.at[0], got2])


class Stage:
    def __init__(self, loads, stores, first):
        self.loads, self.stores, self.started = loads, stores, []
        for i in (*first, *(i for i in loads if i not in first)):
            loads[i].start()

    def need(self, *which):
        for i in which:
            self.loads.pop(i).wait()

    def put(self, *which):
        for i in which:
            copy = self.stores.pop(i)
            copy.start()
            self.started.append(copy)

    def end(self):
        self.need(*list(self.loads))
        self.put(*list(self.stores))
        for copy in self.started:
            copy.wait()


def staged_call(kernel, name, ins, outs, scratch, remote=None, first=()):
    in_held = [i for i, (_, held) in enumerate(ins) if held]
    out_held = [i for i, (_, _, held) in enumerate(outs) if held]

    def body(*refs):
        given, results = list(refs[: len(ins)]), list(refs[len(ins) : len(ins) + len(outs)])
        rest = refs[len(ins) + len(outs) :]
        held, own, sems = rest[: len(in_held) + len(out_held)], rest[len(in_held) + len(out_held) : -1], rest[-1]
        loads, stores = {}, {}
        for j, i in enumerate(in_held):
            loads[i] = pltpu.make_async_copy(given[i], held[j], sems.at[j])
            given[i] = held[j]
        for j, i in enumerate(out_held, len(in_held)):
            stores[i] = pltpu.make_async_copy(held[j], results[i], sems.at[j])
            results[i] = held[j]
        stage = Stage(loads, stores, first)
        kernel(stage, *given, *results, *own)
        stage.end()

    params = {} if remote is None else {"collective_id": remote, "has_side_effects": True}
    return pl.pallas_call(
        body,
        out_shape=[jax.ShapeDtypeStruct(shape, kind) for shape, kind, _ in outs],
        in_specs=[pl.BlockSpec(memory_space=HBM)] * len(ins),
        out_specs=[pl.BlockSpec(memory_space=HBM)] * len(outs),
        scratch_shapes=[
            *[pltpu.VMEM(ins[i][0].shape, ins[i][0].dtype) for i in in_held],
            *[pltpu.VMEM(*outs[i][:2]) for i in out_held],
            *[pltpu.VMEM(shape, kind) for shape, kind in scratch],
            *([pltpu.SemaphoreType.DMA((N_SEMS,))] * 2 if remote is not None else []),
            pltpu.SemaphoreType.DMA((len(in_held) + len(out_held),)),
        ],
        name=name,
        compiler_params=pltpu.CompilerParams(vmem_limit_bytes=62 << 20, **params),
    )(*[array for array, _ in ins])


def everyone(p):
    me = p.dp * 16 + p.ctx * 4 + p.uly
    found = []
    for k in range(1, 32):
        there = lax.rem(me + k, 32)
        found.append((lax.div(there, 16), lax.rem(lax.div(there, 4), 4), lax.rem(there, 4)))
    return found


def line_partners(p):
    found = [p.at(dp=p.other)]
    for d in range(1, 4):
        there = lax.rem(p.uly + d, 4)
        found += [p.at(uly=there), p.at(dp=p.other, uly=there)]
    return found


def plane_partners(p):
    return [p.at(dp=p.other), p.at(ctx=p.xn), p.at(ctx=p.yn)]


def token_slot(out, dp, c, part):
    view = out.at[dp * 4 + c]
    return view if part is None else view.at[part]


def state_slot(out, dp, c, part):
    view = out.at[c]
    return view if part is None else view.at[part]


def finish(heads, outg, slices, residual, layer_part, grad, grad_scaled, hidden, gains, terms, down):
    rows, (_, out_rows, quarter) = heads.shape[1], outg.shape
    tokens, width = hidden.shape
    key, val, ff = KEY_DIM, VALUE_DIM, slices.shape[2] // 2

    def kernel(
        stage, hs, og, sl, res, part, gr, gs, hid, gain, term, down_in, q, k, v, s, o, g, u, y, x, down_out, n1, n2
    ):
        stage.need(0, 1, 2)
        for d in range(2):
            for z in range(4):
                h, i = 2 * z + d, 4 * d + z
                at = 0
                for ref, w in ((q, key), (k, key), (v, val), (s, val)):
                    ref[:, h * w : (h + 1) * w] = hs[i, :, at : at + w].astype(F32)
                    at += w
        stage.put(0, 1, 2, 3)
        for i in range(8):
            g[:, i * ff : (i + 1) * ff] = sl[i, :, :ff].astype(F32)
            u[:, i * ff : (i + 1) * ff] = sl[i, :, ff:].astype(F32)
        stage.put(5, 6)
        for j in range(4):
            o[:, j * quarter : (j + 1) * quarter] = og[j].astype(F32)
        stage.put(4)
        stage.need(3, 4, 5, 6, 7, 8, 9)
        me = lax.axis_index(DP) * 16 + lax.axis_index(CTX) * 4 + lax.axis_index(ULY)
        pair = pl.ds(pl.multiple_of(lax.div(me, 2) * 2 * rows, 2 * rows), 2 * rows)
        own = jnp.where(lax.rem(me, 2) == 0, term[:, pair][:, :rows], term[:, pair][:, rows:])
        n1[...] = own[0:1]
        n2[...] = own[1:2]

        def body(i, carry):
            at = pl.ds(pl.multiple_of(i * 16, 16), 16)
            y[at, :] = res[at, :] + part[at, :]
            normed, inverse = normalize(hid[at, :].astype(F32))
            x[at, :] = gr[at, :] + norm_back(gs[at, :] * gain[0:1, :], normed, inverse)
            return carry

        lax.fori_loop(0, tokens // 16, body, 0)
        stage.put(7, 8)
        stage.need(10)
        down_out[...] = down_in[...]
        stage.put(9)

    widths = (8 * key, 8 * key, 8 * val, 8 * val, 4 * quarter, 8 * ff, 8 * ff)
    heights = (rows, rows, rows, rows, out_rows, rows, rows)
    arrays = (heads, outg, slices, residual, layer_part, grad, grad_scaled, hidden, gains, terms, down)
    shapes = [*zip(heights, widths), (tokens, width), (tokens, width), down.shape, (1, rows), (1, rows)]
    return staged_call(
        kernel,
        "finish",
        [(array, True) for array in arrays],
        [(shape, F32, True) for shape in shapes],
        [],
        first=(0, 2, 1),
    )


def line_spread(m, tag, own, slot):
    u = m.place.uly
    copy = m.local((tag, 8), own, slot(u))
    if u < 3:
        m.send((tag, "r", u), own, slot(u), m.place.at(uly=u + 1))
    if u > 0:
        m.send((tag, "l", u), own, slot(u), m.place.at(uly=u - 1))
    copy.wait()
    yield
    for d in range(1, 4):
        for way, b, onward in (("r", u - d, u + 1), ("l", u + d, u - 1)):
            if 0 <= b <= 3:
                m.arrive((tag, way, b), slot(b))
                if 0 <= onward <= 3:
                    m.send((tag, way, b), slot(b), slot(b), m.place.at(uly=onward))
        yield


def block_factors(cum, ctx, s, backward):
    count = cum.shape[1]
    lasts = [cum[4 * s + j : 4 * s + j + 1, count - 1 : count] for j in range(4)]
    found = []
    for j in range(4):
        total = jnp.zeros((1, 1), F32)
        for i in range(4):
            inside = ((i > ctx) & (i < j)) if backward else ((i > j) & (i < ctx))
            total = total + jnp.where(inside, lasts[i], 0.0)
        right = (j > ctx) if backward else (j < ctx)
        found.append(jnp.where(right, jnp.exp(total), 0.0))
    return found


def forward(hidden, cot, decay, w_down, w_query, w_key, w_value, w_swish, w_output, w_gate, w_up, gains):
    tokens, width = hidden.shape
    key, val = KEY_DIM, VALUE_DIM
    rows, cols = w_query.shape[0], 2 * key + 2 * val + gains.shape[1]
    out_rows, quarter = w_output.shape[0], width // 4
    ff = w_gate.shape[1] // 8
    ff2 = 2 * ff
    block, both = 4 * tokens, 8 * tokens
    half = block // 2
    scale = 1.0 / math.sqrt(key)
    at_s = 2 * key + val

    def start_streams(m, hid_ref, dec_ref, pk_ref, gu_ref, hall, dall, wall, gall):
        p = m.place
        u = p.uly

        def row(q, c, us):
            dp = p.dp if q == 0 else p.other
            at = (dp * 16 + c * 4 + us) * rows
            return wall.at[pl.ds(pl.multiple_of(at, rows), rows)]

        def attn():
            sources = sorted(
                ((q, us) for q in range(2) for us in range(4)), key=lambda s: (abs(s[1] - u), s[0])
            )
            copy = None
            for q, to in sources:
                dp = p.dp if q == 0 else p.other
                mine = row(0, p.ctx, u)
                src = pk_ref.at[dp * 4 + to]
                if (q, to) == (0, u):
                    copy = m.local("T", src, mine)
                else:
                    m.send(("t", q, u), src, mine, p.at(dp=dp, uly=to))
            yield
            relays = []
            for n, (q, us) in enumerate(sources):
                tile = row(q, p.ctx, us)
                if (q, us) == (0, u):
                    copy.wait()
                else:
                    m.arrive(("t", q, us), tile)
                m.send(("X", q, us), tile, tile, p.at(ctx=p.xn))
                m.send(("Y", q, us), tile, tile, p.at(ctx=p.yn))
                relays.append((q, us))
                if n >= 2:
                    yield
                    relay(*relays.pop(0))
            while relays:
                yield
                relay(*relays.pop(0))
            yield
            for q, us in sources:
                even = (q + us) % 2 == 0
                m.arrive(("Y" if even else "X", q, us), row(q, p.yn if even else p.xn, us))
                m.arrive(("Z", q, us), row(q, p.dg, us))

        def relay(q, us):
            if (q + us) % 2 == 0:
                tile = row(q, p.xn, us)
                m.arrive(("X", q, us), tile)
                m.send(("Z", q, us), tile, tile, p.at(ctx=p.yn))
            else:
                tile = row(q, p.yn, us)
                m.arrive(("Y", q, us), tile)
                m.send(("Z", q, us), tile, tile, p.at(ctx=p.xn))

        def feed():
            mine = gall.at[p.dp * 4 + p.ctx]
            copy = m.local("F", gu_ref.at[p.dp * 4 + p.ctx], mine)
            decays = m.local("D", dec_ref, dall.at[p.dp * 4 + p.ctx])
            spots = [(q, c, i) for i, c in enumerate((p.ctx, p.xn, p.yn, p.dg)) for q in range(2)][1:]
            for q, c, i in spots:
                dp = p.dp if q == 0 else p.other
                m.send(("d", q, i), dec_ref, dall.at[p.dp * 4 + p.ctx], p.at(dp=dp, ctx=c))
                m.send(("f", q, i), gu_ref.at[dp * 4 + c], mine, p.at(dp=dp, ctx=c))
            for _ in range(5):
                yield
            for q, c, i in spots:
                dp = p.dp if q == 0 else p.other
                m.arrive(("d", q, i), dall.at[dp * 4 + c])
                m.arrive(("f", q, i), gall.at[dp * 4 + c])
            copy.wait()
            decays.wait()

        return [
            attn(),
            later(line_gather(m, "h", hid_ref, hall, 6), 1),
            later(feed(), 2),
        ]

    def quarter_of(oall, part, c):
        return oall.at[part, :, pl.ds(pl.multiple_of(c * quarter, quarter), quarter)]

    def out_rows_go(m, ow_ref, oall):
        p = m.place
        u = p.uly
        head_dp, head_u = lax.rem(p.ctx, 2), p.dp * 2 + lax.div(p.ctx, 2)
        found = []
        for j in range(4):
            there = oall.at[u, :, pl.ds(j * quarter, quarter)]
            away = pltpu.make_async_remote_copy(
                src_ref=ow_ref.at[j],
                dst_ref=there,
                send_sem=m.send_sems.at[m.number(("S", j))],
                recv_sem=m.recv_sems.at[m.number(("o", u))],
                device_id=(head_dp, j, head_u),
                device_id_type=MESH,
            )
            here = (ow_ref.at[j], there, m.send_sems.at[m.number("O")])
            own = (head_dp == p.dp) & (p.ctx == j) & (head_u == u)
            found.append((own, away, here))
        return found

    def out_start(m, ow_ref, oall):
        for own, away, here in out_rows_go(m, ow_ref, oall):

            @pl.when(own)
            def _(here=here):
                copy = pltpu.make_async_copy(*here)
                copy.start()
                copy.wait()

            pl.when(jnp.logical_not(own))(away.start)

    def out_share(m, ow_ref, oall):
        p = m.place
        u = p.uly
        for us in range(4):
            mine = (u // 2 == p.dp) & (2 * (u % 2) + p.dp == p.ctx) & (us == u)

            @pl.when(jnp.logical_not(mine))
            def _(us=us):
                m.arrive(("o", us), quarter_of(oall, us, p.ctx))

        mine = quarter_of(oall, pl.ds(0, 4), p.ctx)
        m.send("ox", mine, mine, p.at(ctx=p.xn))
        m.send("oy", mine, mine, p.at(ctx=p.yn))
        for own, away, _ in out_rows_go(m, ow_ref, oall):
            pl.when(jnp.logical_not(own))(away.wait_send)

    def out_relay(m, oall):
        p = m.place
        low, high = pl.ds(0, 2), pl.ds(2, 2)
        m.arrive("ox", quarter_of(oall, pl.ds(0, 4), p.xn))
        m.send("o0", quarter_of(oall, low, p.xn), quarter_of(oall, low, p.xn), p.at(ctx=p.yn))
        m.arrive("oy", quarter_of(oall, pl.ds(0, 4), p.yn))
        m.send("o1", quarter_of(oall, high, p.yn), quarter_of(oall, high, p.yn), p.at(ctx=p.xn))

    def out_end(m, oall):
        p = m.place
        m.arrive("o0", quarter_of(oall, pl.ds(0, 2), p.dg))
        m.arrive("o1", quarter_of(oall, pl.ds(2, 2), p.dg))

    def kernel(
        stage, hid_ref, cot_ref, dec_ref, wd_ref, wq_ref, wk_ref, wv_ref, ws_ref, wo_ref, wg_ref, wu_ref, n_ref,
        w_all, s1_all, w2d, q_ref, k_ref, v_ref, sw_ref, w_ref, mask_ref, st_ref, reach_ref, tail_ref, cum_ref,
        gain_ref, hn_ref, hi_ref, ga_ref, res_ref, s2_all, top_all, gu_all, wd_all,
        pk_ref, ow_ref, gu_ref, wall, s1, oall, dall, gall, dec8, cols8, upd, upds, ret, part, sib, right, left, s2, send, recv,
    ):
        uly = lax.axis_index(ULY)
        names = {}
        place = Place(uly)

        def pack():
            stage.need(*range(4, 12))
            for d in range(2):
                for z in range(4):
                    h, i = 2 * z + d, 4 * d + z
                    at = 0
                    for ref, w in ((wq_ref, key), (wk_ref, key), (wv_ref, val), (ws_ref, val)):
                        pk_ref[i, :, at : at + w] = ref[:, h * w : (h + 1) * w]
                        at += w
                    pk_ref[i, :, at:] = n_ref[...]
            for i in range(8):
                gu_ref[i, :, :ff] = wg_ref[:, i * ff : (i + 1) * ff]
                gu_ref[i, :, ff:] = wu_ref[:, i * ff : (i + 1) * ff]
            for j in range(4):
                ow_ref[j] = wo_ref[:, j * quarter : (j + 1) * quarter]

        greet(everyone(place), pack)
        stage.need(0)
        common = Mover(place, names, send, recv)
        ctx = place.ctx

        def for_each(body):
            for u in range(4):
                pl.when(uly == u)(functools.partial(body, u))

        spread = []
        for u in range(4):
            for tag, own, slot in (
                ("g", gall, lambda b: gu_all.at[:, b]),
                ("e", wd_ref, lambda b: wd_all.at[b]),
            ):
                m = Mover(Place(u), names, send, recv, lambda slot=slot: slot(0))
                spread.append((u, m, line_spread(m, tag, own, slot)))

        def spread_on(u):
            for v, _, stream in spread:
                if u == v:
                    next(stream, 0)

        def first(u):
            m = Mover(Place(u), names, send, recv)

            def spread_stage():
                out_start(Mover(Place(u), names, send, recv), ow_ref, oall)
                spread_on(u)
                yield

            together(
                [
                    *start_streams(m, hid_ref, dec_ref, pk_ref, gu_ref, s1, dall, wall, gall),
                    later(spread_stage(), 8),
                ]
            )
            m.finish()

        for_each(first)
        keep = [common.local("w", wall, w_all)]

        table = wall[:, cols - 128 : cols].astype(F32).T
        first_gain = 128 - 32
        gain_ref[...] = table[first_gain : first_gain + 8]

        def norm_one(i, carry):
            b, at = lax.div(i, 4), pl.ds(pl.multiple_of(lax.rem(i, 4) * 32, 32), 32)
            normed, _ = normalize(s1[b, at, :].astype(F32))
            s1[b, at, :] = (normed * gain_ref[0:1, :]).astype(BF16)
            return carry

        lax.fori_loop(0, 32, norm_one, 0)
        keep.append(common.local("W", s1, s1_all))

        for i in range(8):
            dec8[i : i + 1, :] = dall[i, pl.ds(place.dp, 1), :]
        upper = lax.broadcasted_iota(jnp.int32, (block, block), 0) <= lax.broadcasted_iota(
            jnp.int32, (block, block), 1
        )
        cum_ref[...] = jnp.dot(
            dec8[...], upper.astype(F32), precision=lax.Precision.HIGHEST, preferred_element_type=F32
        )
        for s in range(2):
            dec8[s : s + 1, :] = cum_ref[pl.ds(4 * s + ctx, 1), :]
        cols8[...] = dec8[...].T
        for s in range(2):
            column = cols8[:, s : s + 1]
            reach_ref[s] = jnp.exp(column) * scale
            tail_ref[s] = jnp.exp(dec8[s : s + 1, block - 1 : block] - column)

        whole = [
            Mover(Place(u), names, send, recv, lambda: quarter_of(oall, pl.ds(0, 4), 0))
            for u in range(4)
        ]
        for_each(lambda u: out_share(whole[u], ow_ref, oall))

        for s in range(2):
            lhs = s1[4 * s : 4 * s + 4].reshape(block, width)
            q_ref[s] = matmul(lhs, wall[:, :key]).astype(BF16)
            k_ref[s] = matmul(lhs, wall[:, key : 2 * key]).astype(BF16)
            rest = matmul(lhs, wall[:, 2 * key :])
            v_ref[s] = rest[:, :val].astype(BF16)
            sw_ref[pl.ds(s * block, block), :] = rest[:, val : 2 * val]
        out_relay(common, oall)
        for s in range(2):
            k_tail = (k_ref[s].astype(F32) * tail_ref[s]).astype(BF16)
            upd[s] = dot_t(k_tail, v_ref[s]).astype(BF16)
        states = plane_gather(
            common, "t", upd, upds, state_slot, (pl.ds(0, 1), pl.ds(1, 1)), pair=False
        )
        next(states)

        def intra(c, carry):
            s, h = lax.div(c, 2), lax.rem(c, 2)
            at = pl.ds(pl.multiple_of(h * half, half), half)
            here = pl.ds(pl.multiple_of(c * half, half), half)
            gap = cols8[at, :]
            column = jnp.where(s == 0, gap[:, 0:1], gap[:, 1:2])
            gap = column - dec8[pl.ds(s, 1), :]
            t = lax.broadcasted_iota(jnp.int32, (half, block), 0) + h * half
            later_on = t >= lax.broadcasted_iota(jnp.int32, (half, block), 1)
            mask = jnp.where(later_on, jnp.exp(jnp.minimum(gap, 0.0)), 0.0) * scale
            mask_ref[s, at, :] = mask
            weights = (dot_nt(q_ref[s, at, :], k_ref[s]) * mask).astype(BF16)
            w_ref[s, at, :] = weights
            ret[here, :] = matmul(weights, v_ref[s])
            return carry

        lax.fori_loop(0, 2, intra, 0)
        for_each(spread_on)
        next(states)
        lax.fori_loop(2, 4, intra, 0)
        out_end(common, oall)
        for i in range(4):
            w2d[i * out_rows : (i + 1) * out_rows, :] = oall[i]
        for _ in states:
            pass
        for s in range(2):
            factors = block_factors(cum_ref, ctx, s, False)
            total = factors[0] * upds[0, s].astype(F32)
            for j in range(1, 4):
                total = total + factors[j] * upds[j, s].astype(F32)
            st_ref[s] = total.astype(BF16)

        def outer(c, carry):
            s, h = lax.div(c, 2), lax.rem(c, 2)
            at = pl.ds(pl.multiple_of(h * half, half), half)
            here = pl.ds(pl.multiple_of(c * half, half), half)
            retained = ret[here, :] + reach_ref[s, at, :] * matmul(q_ref[s, at, :], st_ref[s])
            normed, inverse = normalize(retained)
            hn_ref[here, :] = normed
            hi_ref[here, :] = inverse
            pre = sw_ref[here, :]
            gated = (pre * jax.nn.sigmoid(pre) * normed.astype(BF16).astype(F32)).astype(BF16)
            ga_ref[here, :] = gated
            for n in range(4):
                cut = pl.ds(n * quarter, quarter)
                value = matmul(gated, w2d[:, cut]).astype(BF16)
                part[pl.ds(2 * c, 2), :, cut] = value.reshape(2, tokens, quarter)
            return carry

        lax.fori_loop(0, 4, outer, 0)
        stage.put(*range(2, 17))

        def reduce(u):
            m = Mover(Place(u), names, send, recv)
            low = tokens // 2

            def spread_stage():
                spread_on(u)
                yield

            together(
                [
                    line_reduce(m, "s", lambda i: part.at[i], res_ref, sib, right, left),
                    plane_gather(
                        m, "C", cot_ref, top_all, token_slot, (pl.ds(0, low), pl.ds(low, low))
                    ),
                    later(spread_stage(), 2),
                ]
            )
            m.finish()

        for_each(reduce)

        def norm_two(i, carry):
            at = pl.ds(pl.multiple_of(i * 16, 16), 16)
            residual = hid_ref[at, :].astype(F32) + res_ref[at, :]
            res_ref[at, :] = residual
            normed, _ = normalize(residual)
            s2[at, :] = (normed * gain_ref[1:2, :]).astype(BF16)
            return carry

        lax.fori_loop(0, tokens // 16, norm_two, 0)
        low = tokens // 2
        for _ in plane_gather(
            common, "k", s2, s2_all, token_slot, (pl.ds(0, low), pl.ds(low, low))
        ):
            pass

        def last(u):
            spread_on(u)
            whole[u].finish()
            for v, m, _ in spread:
                if u == v:
                    m.finish()

        for_each(last)
        for copy in keep:
            copy.wait()
        common.finish()
        assert len(names) <= N_SEMS

    return staged_call(
        kernel,
        "forward",
        [
            (hidden, True), (cot, False), (decay, False), (w_down, False), (w_query, True), (w_key, True),
            (w_value, True), (w_swish, True), (w_output, True), (w_gate, True), (w_up, True), (gains, True),
        ],
        [
            ((width, cols), BF16, False),
            ((8, tokens, width), BF16, False),
            ((4 * out_rows, width), BF16, True),
            ((2, block, key), BF16, True),
            ((2, block, key), BF16, True),
            ((2, block, val), BF16, True),
            ((both, val), F32, True),
            ((2, block, block), BF16, True),
            ((2, block, block), F32, True),
            ((2, key, val), BF16, True),
            ((2, block, 1), F32, True),
            ((2, block, 1), F32, True),
            ((8, block), F32, True),
            ((8, width), F32, True),
            ((both, val), F32, True),
            ((both, 1), F32, True),
            ((both, val), BF16, True),
            ((tokens, width), F32, True),
            ((8, tokens, width), BF16, False),
            ((8, tokens, width), BF16, False),
            ((8, 4, rows, ff2), BF16, False),
            ((4, out_rows, width), BF16, False),
        ],
        [
            ((8, rows, cols), BF16),
            ((4, out_rows, quarter), BF16),
            ((8, rows, ff2), BF16),
            ((width, cols), BF16),
            ((8, tokens, width), BF16),
            ((4, out_rows, width), BF16),
            ((8, 2, block), F32),
            ((8, rows, ff2), BF16),
            ((8, block), F32),
            ((block, 8), F32),
            ((2, key, val), BF16),
            ((4, 2, key, val), BF16),
            ((both, val), F32),
            ((8, tokens, width), BF16),
            ((4, tokens, width), BF16),
            ((4, tokens, width), BF16),
            ((4, tokens, width), BF16),
            ((tokens, width), BF16),
        ],
        1,
    )


def feed_forward(scaled, top, w_gu, w_dn, residual, cot, gains):
    _, tokens, width = scaled.shape
    out_rows = w_dn.shape[1]
    rows, ff2 = w_gu.shape[2:]
    ff = ff2 // 2
    block = 4 * tokens

    def kernel(
        stage, s2_ref, top_ref, gu_ref, wd_ref, res_ref, cot_ref, gain_ref, grad, grad_low, term, dout, lo, ggu,
        w_d, prod, grad_gu, part, down, total, sib, sums, got, got2, right, left, send, recv,
    ):
        uly = lax.axis_index(ULY)
        names = {}
        p = Place(uly)
        greet(line_partners(p) + plane_partners(p)[1:])
        common = Mover(p, names, send, recv)
        movers = [
            Mover(Place(u), names, send, recv, lambda: halves_of_columns(right.at[0], 0))
            for u in range(4)
        ]
        lines = [
            line_reduce(m, "d", lambda b: down.at[b], dout, None, right, left, halves_of_columns)
            for m in movers
        ]

        def for_each(body):
            for u in range(4):
                pl.when(uly == u)(functools.partial(body, u))

        stage.need(0, 2)

        def weights():
            return gu_ref[...].reshape(32 * rows, ff2)

        def tokens_of(s):
            here = pl.ds(pl.multiple_of(s * block, block), block)
            lhs = s2_ref[pl.ds(4 * s, 4)].reshape(block, width)
            pre = matmul(lhs, weights())
            gate_pre, up_pre = pre[:, :ff], pre[:, ff:]
            if 1 in stage.loads:
                stage.need(1, 3)
                for i in range(4):
                    w_d[i * out_rows : (i + 1) * out_rows, :] = wd_ref[i]
            grad_product = dot_nt(top_ref[pl.ds(4 * s, 4)].reshape(block, width), w_d[...])
            sigma = jax.nn.sigmoid(gate_pre)
            act = gate_pre * sigma
            prod[here, :] = (act * up_pre).astype(BF16)
            slope = sigma * (1.0 + gate_pre * (1.0 - sigma))
            grad_gu[here, :ff] = (grad_product * up_pre * slope).astype(BF16)
            grad_gu[here, ff:] = (grad_product * act).astype(BF16)

        def tokens_back(s):
            here = pl.ds(pl.multiple_of(s * block, block), block)

            value = dot_nt(grad_gu[here, :], weights()).astype(BF16)
            part[pl.ds(4 * s, 4)] = value.reshape(4, tokens, width)

        reduced = plane_reduce(common, "s", part, total, sib, sums, got, got2)
        tokens_of(p.other)
        tokens_of(p.dp)

        def down_grad(n, carry):
            at = pl.ds(pl.multiple_of(n * 512, 512), 512)
            value = dot_t(prod[...], top_ref[:, :, at].reshape(2 * block, 512)).astype(BF16)
            for i in range(4):
                down[i, :, at] = value[i * out_rows : (i + 1) * out_rows]
            return carry

        lax.fori_loop(0, width // 512, down_grad, 0)
        for_each(lambda u: next(lines[u]))
        tokens_back(p.other)
        next(reduced)
        tokens_back(p.dp)
        next(reduced)
        for_each(lambda u: next(lines[u]))

        def up_grad(n, carry):
            at = pl.ds(pl.multiple_of(n * 4 * rows, 4 * rows), 4 * rows)
            value = dot_t(s2_ref[:, :, at].reshape(2 * block, 4 * rows), grad_gu[...])
            ggu[n] = value.astype(BF16).reshape(4, rows, ff2)
            return carry

        lax.fori_loop(0, 8, up_grad, 0)
        stage.put(5)
        for_each(lambda u: next(lines[u]))
        next(reduced)

        def out_part(n, carry):
            at = pl.ds(pl.multiple_of(n * 512, 512), 512)
            value = matmul(prod[...], w_d[:, at]).astype(BF16)
            lo[:, :, at] = value.reshape(8, tokens, 512)
            return carry

        lax.fori_loop(0, width // 512, out_part, 0)
        stage.put(4)
        for _ in reduced:
            pass
        stage.need(4, 5, 6)

        def back(i, carry):
            at = pl.ds(pl.multiple_of(i * 16, 16), 16)
            normed, inverse = normalize(res_ref[at, :])
            scaled_grad = total[at, :]
            value = cot_ref[at, :].astype(F32) + norm_back(
                scaled_grad * gain_ref[1:2, :], normed, inverse
            )
            grad[at, :] = value
            grad_low[at, :] = value.astype(BF16)
            return carry + jnp.sum(scaled_grad * normed, axis=0, keepdims=True)

        term[...] = lax.fori_loop(0, tokens // 16, back, jnp.zeros((1, width), F32))

        def last(u):
            for _ in lines[u]:
                pass
            movers[u].finish()

        for_each(last)
        common.finish()
        assert len(names) <= N_SEMS

    return staged_call(
        kernel,
        "feed_forward",
        [(array, True) for array in (scaled, top, w_gu, w_dn, residual, cot, gains)],
        [
            ((tokens, width), F32, True),
            ((tokens, width), BF16, True),
            ((1, width), F32, True),
            ((out_rows, width), F32, True),
            ((8, tokens, width), BF16, True),
            ((8, 4, rows, ff2), BF16, True),
        ],
        [
            ((4 * out_rows, width), BF16),
            ((2 * block, ff), BF16),
            ((2 * block, ff2), BF16),
            ((8, tokens, width), BF16),
            ((4, out_rows, width), BF16),
            ((tokens, width), F32),
            ((4, tokens, width), BF16),
            ((4, tokens, width), BF16),
            ((2, tokens, width), BF16),
            ((tokens, width), BF16),
            ((4, out_rows, width), BF16),
            ((4, out_rows, width), BF16),
        ],
        3,
        (0, 2),
    )


def attention_back(
    own, lo, ggu, w_out, gated, normed, inverse, swish, q, k, v, weights, mask, state_in, reach, tail, cum
):
    tokens, width = own.shape
    both, val = gated.shape
    block, key = q.shape[1:]
    rows, cols = ggu.shape[3:]
    piece = w_out.shape[0] // 4
    half = block // 2
    at_v, at_s = 2 * key, 2 * key + val

    def kernel(
        stage, own_ref, lo_ref, g_ref, wo_ref, ga_ref, hn_ref, hi_ref, sw_ref, q_ref, k_ref, v_ref, w_ref, mask_ref, st_ref,
        reach_ref, tail_ref, cum_ref, cat_ref, total, osum, gsum,
        gout, oxs, oys, ox2, oy2, gy, gr, gs, gq, gk, gv, gst, gsts, sib, chip, got, got2, right, left, send, recv,
    ):
        uly = lax.axis_index(ULY)
        names = {}
        place = Place(uly)
        greet(line_partners(place) + plane_partners(place)[1:])
        stage.need(0, 1, 2)
        common = Mover(place, names, send, recv)
        movers = [Mover(Place(u), names, send, recv, lambda: right.at[0, 0]) for u in range(4)]
        ways = [
            line_reduce(
                movers[u],
                "f",
                lambda b: g_ref.at[:, :, b],
                gsum,
                None,
                right,
                left,
                lambda view, i: view.at[i],
            )
            for u in range(4)
        ]

        def for_each(body):
            for u in range(4):
                pl.when(uly == u)(functools.partial(body, u))

        def first(u):
            def sums():
                yield
                next(ways[u])
                yield
                yield
                next(ways[u])

            m = Mover(Place(u), names, send, recv)
            together(
                [
                    plane_reduce(m, "s", lo_ref, total, sib, chip, got, got2),
                    sums(),
                    line_gather(m, "k", own_ref, gy),
                ]
            )
            m.finish()

        for_each(first)

        stage.put(1)
        stage.need(*range(3, 17))

        def chunk(c):
            return pl.ds(pl.multiple_of(c * half, half), half)

        def gradients(c, carry):
            at = chunk(c)
            grad = gy[pl.ds(2 * c, 2)].reshape(half, width)
            gg = dot_nt(grad, wo_ref[...])
            pre = sw_ref[at, :]
            sigma = jax.nn.sigmoid(pre)
            head = hn_ref[at, :]
            low = head.astype(BF16).astype(F32)
            cat_ref[at, at_s : at_s + val] = (
                gg * low * (sigma * (1.0 + pre * (1.0 - sigma)))
            ).astype(BF16)
            gh = (gg * (pre * sigma)).astype(BF16).astype(F32)
            mean = jnp.mean(gh * head, axis=-1, keepdims=True)
            grad_retained = (hi_ref[at, :] * (gh - head * mean)).astype(BF16)
            gr[at, :] = grad_retained
            s = lax.div(c, 2)
            part = pl.ds(pl.multiple_of(lax.rem(c, 2) * half, half), half)
            gs[at, :] = (dot_nt(grad_retained, v_ref[s]) * mask_ref[s, part, :]).astype(BF16)
            return carry

        lax.fori_loop(0, both // half, gradients, 0)
        for s in range(2):
            at = pl.ds(s * block, block)
            reached = (q_ref[s].astype(F32) * reach_ref[s]).astype(BF16)
            gst[s] = dot_t(reached, gr[at, :]).astype(BF16)
        states = plane_gather(
            common, "t", gst, gsts, state_slot, (pl.ds(0, 1), pl.ds(1, 1)), pair=False
        )
        next(states)
        for_each(lambda u: next(ways[u]))

        for s in range(2):
            at = pl.ds(s * block, block)
            gq[at, :] = jnp.dot(gs[at, :], k_ref[s], preferred_element_type=F32)
            gk[at, :] = dot_t(gs[at, :], q_ref[s])
        def out_grad(n, carry):
            at = pl.ds(pl.multiple_of(n * 512, 512), 512)
            grad = gy[:, :, at].reshape(both, 512)
            value = dot_t(ga_ref[...], grad).astype(BF16)
            for i in range(4):
                gout[i, :, at] = value[i * piece : (i + 1) * piece]
            return carry

        lax.fori_loop(0, width // 512, out_grad, 0)
        next(states)

        quarter = width // 4

        def column(part, c):
            return gout.at[part, :, pl.ds(pl.multiple_of(c * quarter, quarter), quarter)]

        for i, (cx, cy) in ((1, (place.dg, place.dg)), (0, (place.xn, place.yn))):
            common.send(("ox", i), column(pl.ds(0, 2), cx), oxs.at[i], place.at(ctx=place.xn))
            common.send(("oy", i), column(pl.ds(2, 2), cy), oys.at[i], place.at(ctx=place.yn))
        for s in range(2):
            at = pl.ds(s * block, block)
            gv[at, :] = dot_t(w_ref[s], gr[at, :])
        for _ in states:
            pass
        for s in range(2):
            at = pl.ds(s * block, block)
            factors = block_factors(cum_ref, place.ctx, s, True)
            update = factors[0] * gsts[0, s].astype(F32)
            for j in range(1, 4):
                update = update + factors[j] * gsts[j, s].astype(F32)
            update = update.astype(BF16)
            grad = gr[at, :]
            cat_ref[at, :key] = (gq[at, :] + reach_ref[s] * dot_nt(grad, st_ref[s])).astype(BF16)
            cat_ref[at, key:at_v] = (gk[at, :] + tail_ref[s] * dot_nt(v_ref[s], update)).astype(BF16)
            cat_ref[at, at_v:at_s] = (
                gv[at, :] + tail_ref[s] * jnp.dot(k_ref[s], update, preferred_element_type=F32)
            ).astype(BF16)
        stage.put(0)
        common.arrive(("ox", 1), oxs.at[1])
        common.arrive(("oy", 1), oys.at[1])
        for t in range(2):
            add_up(oxs.at[1, t], [column(t, place.yn), oxs.at[1, t]])
            add_up(oys.at[1, t], [column(2 + t, place.xn), oys.at[1, t]])
        common.send("oy2", oxs.at[1], oy2, place.at(ctx=place.yn))
        common.send("ox2", oys.at[1], ox2, place.at(ctx=place.xn))

        def last(u):
            for _ in ways[u]:
                pass
            movers[u].finish()

        for_each(last)
        for name, ref in ((("ox", 0), oxs.at[0]), (("oy", 0), oys.at[0]), ("oy2", oy2), ("ox2", ox2)):
            common.arrive(name, ref)
        for us in range(4):
            got, got2 = (oxs, oy2) if us < 2 else (oys, ox2)
            add_up(osum.at[us], [column(us, place.ctx), got.at[0, us % 2], got2.at[us % 2]])
        common.finish()
        assert len(names) <= N_SEMS

    arrays = (own, lo, ggu, w_out, gated, normed, inverse, swish, q, k, v, weights, mask, state_in, reach, tail, cum)
    return staged_call(
        kernel,
        "attention_back",
        [(array, True) for array in arrays],
        [
            ((both, 2 * key + 2 * val), BF16, True),
            ((tokens, width), F32, True),
            ((4, piece, width // 4), BF16, True),
            ((2, 4, rows, cols), BF16, True),
        ],
        [
            ((4, piece, width), BF16),
            *[((2, 2, piece, width // 4), BF16)] * 2,
            *[((2, piece, width // 4), BF16)] * 2,
            ((8, tokens, width), BF16),
            ((both, val), BF16),
            ((both, block), BF16),
            ((both, key), F32),
            ((both, key), F32),
            ((both, val), F32),
            ((2, key, val), BF16),
            ((4, 2, key, val), BF16),
            ((4, tokens, width), BF16),
            ((4, tokens, width), BF16),
            ((2, tokens, width), BF16),
            ((tokens, width), BF16),
            ((4, 2, 4, rows, cols), BF16),
            ((4, 2, 4, rows, cols), BF16),
        ],
        7,
    )


def last_exchange(grad_cat, w_all, scaled, gout, gffn, inputs, term):
    tokens, width = inputs.shape
    both, cols = grad_cat.shape
    block = both // 2
    out_rows, quarter = gout.shape[1:]
    rows, ff2 = gffn.shape[1:]

    def streams(
        m, line, tile, f_ref, in_ref, t_ref, out, gall, fall, gains, gotx, goty, gotx2, goty2, away,
    ):
        p = m.place
        u = p.uly

        def attn():
            for t in range(4):
                m.arrive(("gx", 1, t), gotx.at[1, t])
                add_up(gotx.at[1, t], [tile(0, p.yn, t), gotx.at[1, t]])
                m.send(("gy2", t), gotx.at[1, t], goty2.at[t], p.at(ctx=p.yn))
                m.arrive(("gy", 1, t), goty.at[1, t])
                add_up(goty.at[1, t], [tile(1, p.xn, t), goty.at[1, t]])
                m.send(("gx2", t), goty.at[1, t], gotx2.at[t], p.at(ctx=p.xn))
            yield
            yield
            for t in range(4):
                for dp, got, got2, tags in (
                    (0, gotx, goty2, ("gx", "gy2")),
                    (1, goty, gotx2, ("gy", "gx2")),
                ):
                    m.arrive((tags[0], 0, t), got.at[0, t])
                    m.arrive((tags[1], t), got2.at[t])
                    add_up(got.at[0, t], [tile(dp, p.ctx, t), got.at[0, t], got2.at[t]])
                    there = gall.at[p.dp * 4 + u]
                    if t == u:

                        @pl.when(p.dp == dp)
                        def _(got=got, there=there):
                            here = pltpu.make_async_copy(
                                got.at[0, u], there, m.send_sems.at[m.number("G")]
                            )
                            here.start()
                            here.wait()

                        @pl.when(p.dp != dp)
                        def _(got=got, there=there, dp=dp):
                            m.remote(
                                ("gc", u), got.at[0, u], there, (dp, p.ctx, u)
                            ).start()
                    else:
                        k = m.number(("gs", dp, t))
                        copies = []
                        for q in range(2):
                            copies.append(
                                pltpu.make_async_remote_copy(
                                    src_ref=got.at[0, t],
                                    dst_ref=there,
                                    send_sem=m.send_sems.at[k],
                                    recv_sem=m.recv_sems.at[m.number(("g", q, u))],
                                    device_id=(dp, p.ctx, t),
                                    device_id_type=MESH,
                                )
                            )
                        pl.when(p.dp == dp)(copies[0].start)
                        pl.when(p.dp != dp)(copies[1].start)
                        m.sent.append(copies[0])
            for _ in range(6):
                yield
            m.remote(("gc", u), gotx.at[0, u], gotx.at[0, u], p.at(dp=p.other)).wait_send()
            m.arrive(("gc", u), gall.at[p.other * 4 + u])
            for us in range(4):
                if us != u:
                    m.arrive(("g", 0, us), gall.at[p.dp * 4 + us])
                    m.arrive(("g", 1, us), gall.at[p.other * 4 + us])

        def feed():
            mine = fall.at[p.dp * 4 + p.ctx]
            copy = m.local("F", f_ref.at[p.dp * 4 + p.ctx], mine)
            spots = [(q, c, i) for i, c in enumerate((p.ctx, p.xn, p.yn, p.dg)) for q in range(2)][1:]
            for q, c, i in spots:
                dp = p.dp if q == 0 else p.other
                m.send(("f", q, i), f_ref.at[dp * 4 + c], mine, p.at(dp=dp, ctx=c))
            for _ in range(4):
                yield
            for q, c, i in spots:
                dp = p.dp if q == 0 else p.other
                m.arrive(("f", q, i), fall.at[dp * 4 + c])
            copy.wait()

        def tokens_stream():
            yield from line

            def body(i, total):
                at = pl.ds(pl.multiple_of(i * 16, 16), 16)
                values = in_ref[at, :].astype(F32)
                normed, _ = normalize(values)
                return total + jnp.sum(out[at, :] * normed, axis=0, keepdims=True)

            total = lax.fori_loop(0, tokens // 16, body, jnp.zeros((1, width), F32))
            row = lax.broadcasted_iota(jnp.int32, (8, width), 0)
            gains[...] = jnp.where(
                row == 0,
                jnp.broadcast_to(total, (8, width)),
                jnp.where(row == 1, jnp.broadcast_to(t_ref[...], (8, width)), 0.0),
            )
            for i, device in enumerate((p.at(dp=p.other), p.at(ctx=p.xn), p.at(ctx=p.yn))):
                m.remote(("n", i), gains, away.at[i], device).start()
                yield
                m.remote(("n", i), gains, away.at[i], device).wait()
                gains[...] = gains[...] + away[i]
            copies = [
                m.remote(("N", u, other), gains, away.at[3 + u], p.at(uly=other))
                for other in range(4)
                if other != u
            ]
            for copy in copies:
                copy.start()
            yield
            mine = gains[...]
            for other in range(4):
                if other != u:
                    m.arrive(("N", other, u), away.at[3 + other])
                    mine = mine + away[3 + other]
            for copy in copies:
                copy.wait_send()
            gains[...] = mine

        return [
            attn(),
            tokens_stream(),
            later(feed(), 3),
        ]

    def kernel(
        stage, cat_ref, wa_ref, s1_ref, o_ref, f_ref, in_ref, t_ref, out, gall, oall, fall, gains,
        grads, part, sib, right, left, gotx, goty, gotx2, goty2, away, send, recv,
    ):
        uly = lax.axis_index(ULY)
        names = {}
        p = Place(uly)
        greet(everyone(p))
        stage.need(0, 2)
        common = Mover(p, names, send, recv)

        def for_each(body):
            for u in range(4):
                pl.when(uly == u)(functools.partial(body, u))

        def tile(dp, c, t):
            return grads.at[dp, c, pl.ds(t * rows, rows)]

        def weight_grad(dp, c):
            at = pl.ds(pl.multiple_of((dp * 4 + c) * 4 * rows, 4 * rows), 4 * rows)
            grads[dp, c] = dot_t(s1_ref[:, :, at].reshape(both, 4 * rows), cat_ref[...]).astype(BF16)

        def token_grad(s):
            rows_s = pl.ds(pl.multiple_of(s * block, block), block)
            value = dot_nt(cat_ref[rows_s, :], wa_ref[:, :cols]).astype(BF16)
            part[pl.ds(4 * s, 4)] = value.reshape(4, tokens, width)

        def to_x(i, c):
            weight_grad(0, c)
            for t in range(4):
                common.send(("gx", i, t), tile(0, c, t), gotx.at[i, t], p.at(ctx=p.xn))

        def to_y(i, c):
            weight_grad(1, c)
            for t in range(4):
                common.send(("gy", i, t), tile(1, c, t), goty.at[i, t], p.at(ctx=p.yn))

        def out_copies(m, senders):
            at = m.place
            home_dp, home_ctx = at.uly // 2, 2 * (at.uly % 2) + at.dp
            found = []
            for us in range(4):
                own = (home_dp == at.dp) & (home_ctx == at.ctx) & (us == at.uly)
                copies = [
                    pltpu.make_async_remote_copy(
                        src_ref=o_ref.at[us],
                        dst_ref=oall.at[at.ctx],
                        send_sem=m.send_sems.at[m.number(("os", us))],
                        recv_sem=m.recv_sems.at[m.number(("o", j))],
                        device_id=(home_dp, home_ctx, us),
                        device_id_type=MESH,
                    )
                    for j in senders
                ]
                found.append((us, own, copies))
            return found

        def out_start(u):
            m = Mover(Place(u), names, send, recv)
            for us, own, copies in out_copies(m, range(4)):

                @pl.when(own)
                def _(us=us):
                    here = pltpu.make_async_copy(
                        o_ref.at[us], oall.at[p.ctx], send.at[m.number("O")]
                    )
                    here.start()
                    here.wait()

                for j, copy in enumerate(copies):
                    pl.when(jnp.logical_not(own) & (p.ctx == j))(copy.start)

        def out_end(u):
            m = Mover(Place(u), names, send, recv)
            head_dp, head_u = lax.rem(p.ctx, 2), p.dp * 2 + lax.div(p.ctx, 2)
            for j in range(4):
                mine = (head_dp == p.dp) & (p.ctx == j) & (head_u == u)

                @pl.when(jnp.logical_not(mine))
                def _(j=j):
                    m.arrive(("o", j), oall.at[j])

            for _, own, copies in out_copies(m, range(1)):
                pl.when(jnp.logical_not(own))(copies[0].wait_send)

        stage.need(3)
        for_each(out_start)
        to_x(1, p.dg)
        to_y(1, p.dg)
        stage.need(1)
        token_grad(p.other)
        token_grad(p.dp)
        movers = [
            Mover(
                Place(u), names, send, recv, lambda: halves_of_rows(sib.at[0], 0), lambda: sib.at[0]
            )
            for u in range(4)
        ]
        lines = [
            line_reduce(m, "s", lambda i: part.at[i], out, sib, right, left) for m in movers
        ]
        for_each(lambda u: next(lines[u]))
        to_x(0, p.xn)
        to_y(0, p.yn)
        weight_grad(0, p.yn)
        weight_grad(1, p.xn)
        weight_grad(0, p.ctx)
        weight_grad(1, p.ctx)
        stage.need(5, 6)

        def rest(u):
            m = Mover(Place(u), names, send, recv)
            together(
                streams(
                    m, lines[u], tile, f_ref, in_ref, t_ref, out, gall, fall, gains,
                    gotx, goty, gotx2, goty2, away,
                )
            )
            m.finish()
            movers[u].finish()
            out_end(u)

        for_each(rest)
        common.finish()
        assert len(names) <= N_SEMS

    arrays = (grad_cat, w_all, scaled, gout, gffn, inputs, term)
    return staged_call(
        kernel,
        "last",
        [(array, i != 4) for i, array in enumerate(arrays)],
        [
            ((tokens, width), F32, True),
            ((8, rows, cols), BF16, False),
            ((4, out_rows, quarter), BF16, False),
            ((8, rows, ff2), BF16, False),
            ((8, width), F32, True),
        ],
        [
            ((2, 4, 4 * rows, cols), BF16),
            ((8, tokens, width), BF16),
            *[((4, tokens, width), BF16)] * 3,
            *[((2, 4, rows, cols), BF16)] * 2,
            *[((4, rows, cols), BF16)] * 2,
            ((7, 8, width), F32),
        ],
        2,
        (3, 0, 2),
    )


def local(
    hidden_in,
    cotangent,
    log_decay,
    w_query,
    w_key,
    w_value,
    w_swish,
    w_output,
    w_gate,
    w_up,
    w_down,
    gain_attn,
    gain_ffn,
):
    bf16, f32 = BF16, F32
    dp, ctx = lax.axis_index(DP), lax.axis_index(CTX)
    tokens = hidden_in.shape[1]
    width = hidden_in.shape[2]
    rows = w_query.shape[0]
    out_rows = w_output.shape[0]
    key, val, ff = KEY_DIM, VALUE_DIM, w_gate.shape[1] // 8

    gains = jnp.pad(jnp.stack([gain_attn, gain_ffn], axis=1), ((0, 0), (0, 30)))
    block = 4 * tokens
    (
        w_all, scaled_one, w_out, q, k, v, swish_pre, weights, mask, state_in, reach, tail, cum,
        gains, head_normed, head_inverse, gated, residual, scaled_two, top_all, w_gu, w_dn,
    ) = forward(
        hidden_in[0], cotangent[0], log_decay[0], w_down,
        w_query, w_key, w_value, w_swish, w_output, w_gate, w_up, gains,
    )
    grad_residual, grad_y, gain_two_term, grad_down, layer_part, ggu = feed_forward(
        scaled_two, top_all, w_gu, w_dn, residual, cotangent[0], gains
    )
    grad_cat, out_part, g_out, ggu = attention_back(
        grad_y,
        layer_part,
        ggu.reshape(2, 4, 4, rows, 2 * ff),
        w_out,
        gated,
        head_normed,
        head_inverse,
        swish_pre,
        q,
        k,
        v,
        weights,
        mask,
        state_in,
        reach,
        tail,
        cum,
    )
    gs1, gcat, g_out, ggu, gain_terms = last_exchange(
        grad_cat,
        w_all,
        scaled_one,
        g_out,
        ggu.reshape(8, rows, 2 * ff),
        hidden_in[0],
        gain_two_term,
    )
    (
        grad_query, grad_key, grad_value, grad_swish, grad_output, grad_gate, grad_up,
        layer_out, grad_input, grad_down, gain_one_term, gain_two_term,
    ) = finish(
        gcat, g_out, ggu, residual, out_part, grad_residual, gs1, hidden_in[0], gains, gain_terms, grad_down
    )
    return (
        layer_out[None],
        grad_input[None],
        grad_query,
        grad_key,
        grad_value,
        grad_swish,
        grad_output,
        grad_gate,
        grad_up,
        grad_down,
        gain_one_term[0],
        gain_two_term[0],
    )


def solution(mesh):
    shape = mesh.shape
    planned = (shape[DP], shape[CTX], shape[ULY]) == (2, 4, 4)
    tokens = P(DP, (CTX, ULY), None)
    weight = P(EVERYWHERE, None)
    gain = P(EVERYWHERE)
    return jax.shard_map(
        local if planned else local_any,
        mesh=mesh,
        in_specs=(tokens, tokens, P(DP, ULY, CTX), *[weight] * 8, gain, gain),
        out_specs=(tokens, tokens, *[weight] * 8, gain, gain),
        check_vma=False,
    )
```

```python
import functools
import math

import jax
import jax.numpy as jnp
from jax import lax
from jax.experimental import pallas as pl
from jax.experimental.pallas import tpu as pltpu
from jax.sharding import PartitionSpec as P

RETENTION_HEADS = 8
KEY_DIM = 256
VALUE_DIM = 432


EPSILON = 1e-06
DP, CTX, ULY = "dp", "ctx", "ulysses"
EVERYWHERE = (DP, CTX, ULY)


def entering(value, axis, join, neutral, backward):
    count, mine = (lax.axis_size(axis), lax.axis_index(axis))
    pieces = jax.tree.map(lambda part: lax.all_gather(part, axis), value)
    if backward:
        pieces = jax.tree.map(lambda part: part[::-1], pieces)
        mine = count - 1 - mine
    subtotal = jax.tree.map(
        lambda part, zero: jnp.full_like(part, 0) + jnp.asarray(zero, part.dtype), value, neutral
    )

    def step(position, subtotal):
        longer = join(subtotal, jax.tree.map(lambda part: part[position], pieces))
        return jax.tree.map(lambda new, old: jnp.where(position < mine, new, old), longer, subtotal)

    return lax.fori_loop(0, count - 1, step, subtotal)


def normalize(values):
    inverse = lax.rsqrt(jnp.mean(values * values, axis=-1, keepdims=True) + EPSILON)
    return (values * inverse, inverse)


def norm_back(grad_normed, normed, inverse):
    return inverse * (grad_normed - normed * jnp.mean(grad_normed * normed, axis=-1, keepdims=True))


def swish_slope(values):
    sigma = jax.nn.sigmoid(values)
    return sigma * (1.0 + values * (1.0 - sigma))


def carry_forward(earlier, later):
    return (earlier[0] * later[0], later[0][:, None, None] * earlier[1] + later[1])


def carry_backward(earlier, later):
    return (earlier[0] * later[0], later[1] + later[0][:, None, None] * earlier[1])


def running_sum(values):
    size = values.shape[-1]
    upper = lax.broadcasted_iota(jnp.int32, (size, size), 0) <= lax.broadcasted_iota(
        jnp.int32, (size, size), 1
    )
    return jnp.dot(values, upper.astype(jnp.float32), precision=lax.Precision.HIGHEST)


def matmul(left, right):
    return jnp.dot(left, right, preferred_element_type=jnp.float32)


def local_any(
    hidden_in,
    cotangent,
    log_decay,
    w_query,
    w_key,
    w_value,
    w_swish,
    w_output,
    w_gate,
    w_up,
    w_down,
    gain_attn,
    gain_ffn,
):
    highest = lax.Precision.HIGHEST
    query_full, key_full, value_full, swish_full, output_full, gain_one = (
        lax.all_gather(w_query, EVERYWHERE, axis=0, tiled=True),
        lax.all_gather(w_key, EVERYWHERE, axis=0, tiled=True),
        lax.all_gather(w_value, EVERYWHERE, axis=0, tiled=True),
        lax.all_gather(w_swish, EVERYWHERE, axis=0, tiled=True),
        lax.all_gather(w_output, EVERYWHERE, axis=0, tiled=True),
        lax.all_gather(gain_attn, EVERYWHERE, axis=0, tiled=True),
    )
    inputs = hidden_in[0].astype(jnp.float32)
    tokens = inputs.shape[0]
    normed_one, inverse_one = normalize(inputs)
    scaled_one = (normed_one * gain_one.astype(jnp.float32)).astype(jnp.bfloat16)
    queries = (
        matmul(scaled_one, query_full)
        .astype(jnp.bfloat16)
        .reshape(tokens, RETENTION_HEADS, KEY_DIM)
    )
    keys_tok = (
        matmul(scaled_one, key_full).astype(jnp.bfloat16).reshape(tokens, RETENTION_HEADS, KEY_DIM)
    )
    values_tok = (
        matmul(scaled_one, value_full)
        .astype(jnp.bfloat16)
        .reshape(tokens, RETENTION_HEADS, VALUE_DIM)
    )
    swish_pre = matmul(scaled_one, swish_full)
    head_q, head_k, head_v = (
        lax.all_to_all(queries, ULY, split_axis=1, concat_axis=0, tiled=True),
        lax.all_to_all(keys_tok, ULY, split_axis=1, concat_axis=0, tiled=True),
        lax.all_to_all(values_tok, ULY, split_axis=1, concat_axis=0, tiled=True),
    )
    block = head_q.shape[0]
    scale = 1.0 / math.sqrt(KEY_DIM)
    cumulative = running_sum(log_decay[0])
    later = lax.broadcasted_iota(jnp.int32, (block, block), 0) >= lax.broadcasted_iota(
        jnp.int32, (block, block), 1
    )
    gap = cumulative[:, :, None] - cumulative[:, None, :]
    mask = jnp.where(later[None], jnp.exp(jnp.minimum(gap, 0.0)), 0.0) * scale
    scores = jnp.einsum("thd,shd->hts", head_q, head_k, preferred_element_type=jnp.float32)
    weights = (scores * mask).astype(jnp.bfloat16)
    intra = jnp.einsum("hts,she->the", weights, head_v, preferred_element_type=jnp.float32)
    query_f = head_q.astype(jnp.float32)
    key_f = head_k.astype(jnp.float32)
    value_f = head_v.astype(jnp.float32)
    tail = jnp.exp(cumulative[:, -1:] - cumulative).T[:, :, None]
    reach = jnp.exp(cumulative).T[:, :, None]
    update = jnp.einsum("shd,she->hde", key_f * tail, value_f, precision=highest)
    block_decay = jnp.exp(cumulative[:, -1])
    identity = (jnp.ones_like(block_decay), jnp.zeros_like(update))
    _, state_in = entering((block_decay, update), CTX, carry_forward, identity, False)
    retained = intra + scale * reach * jnp.einsum(
        "thd,hde->the", query_f, state_in, precision=highest
    )
    head_normed, head_inverse = normalize(retained)
    head_out = head_normed.astype(jnp.bfloat16)
    token_out = lax.all_to_all(
        head_out, ULY, split_axis=0, concat_axis=1, tiled=True
    ).reshape(tokens, RETENTION_HEADS * VALUE_DIM)
    token_out_f = token_out.astype(jnp.float32)
    swish_act = jax.nn.silu(swish_pre)
    gated = (swish_act * token_out_f).astype(jnp.bfloat16)
    residual = inputs + matmul(gated, output_full)
    gate_full, up_full, down_full, gain_two = (
        lax.all_gather(w_gate, EVERYWHERE, axis=0, tiled=True),
        lax.all_gather(w_up, EVERYWHERE, axis=0, tiled=True),
        lax.all_gather(w_down, EVERYWHERE, axis=0, tiled=True),
        lax.all_gather(gain_ffn, EVERYWHERE, axis=0, tiled=True),
    )
    normed_two, inverse_two = normalize(residual)
    scaled_two = (normed_two * gain_two.astype(jnp.float32)).astype(jnp.bfloat16)
    gate_pre = matmul(scaled_two, gate_full)
    up_pre = matmul(scaled_two, up_full)
    product = (jax.nn.silu(gate_pre) * up_pre).astype(jnp.bfloat16)
    layer_out = residual + matmul(product, down_full)
    grad_top = cotangent[0].astype(jnp.float32)
    grad_top_low = grad_top.astype(jnp.bfloat16)
    grad_product = matmul(grad_top_low, down_full.T)
    grad_down_term = matmul(product.T, grad_top_low)
    grad_gate_pre = (grad_product * up_pre * swish_slope(gate_pre)).astype(jnp.bfloat16)
    grad_up_pre = (grad_product * jax.nn.silu(gate_pre)).astype(jnp.bfloat16)
    grad_gate_term = matmul(scaled_two.T, grad_gate_pre)
    grad_up_term = matmul(scaled_two.T, grad_up_pre)
    grad_scaled_two = matmul(grad_gate_pre, gate_full.T) + matmul(grad_up_pre, up_full.T)
    grad_gain_two = jnp.sum(grad_scaled_two * normed_two, axis=0)
    grad_residual = grad_top + norm_back(
        grad_scaled_two * gain_two.astype(jnp.float32), normed_two, inverse_two
    )
    grad_gate, grad_up, grad_down, grad_gain_ffn = (
        lax.psum_scatter(grad_gate_term, EVERYWHERE, scatter_dimension=0, tiled=True),
        lax.psum_scatter(grad_up_term, EVERYWHERE, scatter_dimension=0, tiled=True),
        lax.psum_scatter(grad_down_term, EVERYWHERE, scatter_dimension=0, tiled=True),
        lax.psum_scatter(grad_gain_two, EVERYWHERE, scatter_dimension=0, tiled=True),
    )
    grad_y = grad_residual.astype(jnp.bfloat16)
    grad_output_term = matmul(gated.T, grad_y)
    grad_gated = matmul(grad_y, output_full.T)
    grad_swish_pre = (grad_gated * token_out_f * swish_slope(swish_pre)).astype(jnp.bfloat16)
    grad_token_out = (
        (grad_gated * swish_act).astype(jnp.bfloat16).reshape(tokens, RETENTION_HEADS, VALUE_DIM)
    )
    grad_swish_term = matmul(scaled_one.T, grad_swish_pre)
    grad_head_out = lax.all_to_all(
        grad_token_out, ULY, split_axis=1, concat_axis=0, tiled=True
    ).astype(jnp.float32)
    grad_retained = norm_back(grad_head_out, head_normed, head_inverse).astype(jnp.bfloat16)
    grad_retained_f = grad_retained.astype(jnp.float32)
    grad_weights = jnp.einsum(
        "the,she->hts", grad_retained, head_v, preferred_element_type=jnp.float32
    )
    grad_scores = (grad_weights * mask).astype(jnp.bfloat16)
    grad_state_in = scale * jnp.einsum(
        "thd,the->hde", query_f * reach, grad_retained_f, precision=highest
    )
    _, grad_update = entering((block_decay, grad_state_in), CTX, carry_backward, identity, True)
    grad_head_q = jnp.einsum(
        "hts,shd->thd", grad_scores, head_k, preferred_element_type=jnp.float32
    ) + scale * reach * jnp.einsum("the,hde->thd", grad_retained_f, state_in, precision=highest)
    grad_head_k = jnp.einsum(
        "hts,thd->shd", grad_scores, head_q, preferred_element_type=jnp.float32
    ) + tail * jnp.einsum("she,hde->shd", value_f, grad_update, precision=highest)
    grad_head_v = jnp.einsum(
        "hts,the->she", weights, grad_retained, preferred_element_type=jnp.float32
    ) + tail * jnp.einsum("shd,hde->she", key_f, grad_update, precision=highest)
    grad_queries, grad_keys, grad_values = (
        lax.all_to_all(
            grad_head_q.astype(jnp.bfloat16), ULY, split_axis=0, concat_axis=1, tiled=True
        ),
        lax.all_to_all(
            grad_head_k.astype(jnp.bfloat16), ULY, split_axis=0, concat_axis=1, tiled=True
        ),
        lax.all_to_all(
            grad_head_v.astype(jnp.bfloat16), ULY, split_axis=0, concat_axis=1, tiled=True
        ),
    )
    grad_queries = grad_queries.reshape(tokens, RETENTION_HEADS * KEY_DIM)
    grad_keys = grad_keys.reshape(tokens, RETENTION_HEADS * KEY_DIM)
    grad_values = grad_values.reshape(tokens, RETENTION_HEADS * VALUE_DIM)
    grad_query_term = matmul(scaled_one.T, grad_queries)
    grad_key_term = matmul(scaled_one.T, grad_keys)
    grad_value_term = matmul(scaled_one.T, grad_values)
    grad_scaled_one = (
        matmul(grad_queries, query_full.T)
        + matmul(grad_keys, key_full.T)
        + matmul(grad_values, value_full.T)
        + matmul(grad_swish_pre, swish_full.T)
    )
    grad_gain_one = jnp.sum(grad_scaled_one * normed_one, axis=0)
    grad_input = grad_residual + norm_back(
        grad_scaled_one * gain_one.astype(jnp.float32), normed_one, inverse_one
    )
    grad_query, grad_key, grad_value, grad_swish, grad_output, grad_gain_attn = (
        lax.psum_scatter(
            grad_query_term, EVERYWHERE, scatter_dimension=0, tiled=True
        ),
        lax.psum_scatter(grad_key_term, EVERYWHERE, scatter_dimension=0, tiled=True),
        lax.psum_scatter(
            grad_value_term, EVERYWHERE, scatter_dimension=0, tiled=True
        ),
        lax.psum_scatter(
            grad_swish_term, EVERYWHERE, scatter_dimension=0, tiled=True
        ),
        lax.psum_scatter(
            grad_output_term, EVERYWHERE, scatter_dimension=0, tiled=True
        ),
        lax.psum_scatter(grad_gain_one, EVERYWHERE, scatter_dimension=0, tiled=True),
    )
    return (
        layer_out[None],
        grad_input[None],
        grad_query,
        grad_key,
        grad_value,
        grad_swish,
        grad_output,
        grad_gate,
        grad_up,
        grad_down,
        grad_gain_attn,
        grad_gain_ffn,
    )


MESH = pl.DeviceIdType.MESH
BF16, F32 = jnp.bfloat16, jnp.float32
HBM, VMEM = pltpu.HBM, pltpu.VMEM
N_SEMS = 160


def dot_t(left, right):
    return lax.dot_general(left, right, (((0,), (0,)), ((), ())), preferred_element_type=F32)


def dot_nt(left, right):
    return lax.dot_general(left, right, (((1,), (1,)), ((), ())), preferred_element_type=F32)


def pair_dot(left_axis, right_axis, left, right):
    dims = (((left_axis,), (right_axis,)), ((0,), (0,)))
    return lax.dot_general(left, right, dims, preferred_element_type=F32)


class Place:
    def __init__(self, uly):
        self.dp, self.ctx, self.uly = lax.axis_index(DP), lax.axis_index(CTX), uly
        odd = lax.rem(self.ctx, 2)
        self.xn = self.ctx + 1 - 2 * odd
        self.yn = lax.rem(self.ctx + 2, 4)
        self.dg = self.yn + 1 - 2 * odd
        self.other = 1 - self.dp

    def at(self, dp=None, ctx=None, uly=None):
        return (
            self.dp if dp is None else dp,
            self.ctx if ctx is None else ctx,
            self.uly if uly is None else uly,
        )


class Mover:
    def __init__(self, place, names, send, recv, like=None, like_whole=None):
        self.like, self.like_whole = like, like_whole
        self.place, self.names, self.send_sems, self.recv_sems = place, names, send, recv
        self.sent, self.whole = [], []

    def number(self, name):
        return self.names.setdefault(name, len(self.names))

    def remote(self, name, src, dst, device):
        k = self.number(name)
        return pltpu.make_async_remote_copy(
            src_ref=src,
            dst_ref=dst,
            send_sem=self.send_sems.at[k],
            recv_sem=self.recv_sems.at[k],
            device_id=device,
            device_id_type=MESH,
        )

    def send(self, name, src, dst, device):
        copy = self.remote(name, src, dst, device)
        copy.start()
        self.sent.append(copy if self.like is None else name)

    def send_whole(self, name, src, dst, device):
        copy = self.remote(name, src, dst, device)
        copy.start()
        self.whole.append((copy if self.like is None else None, name, None))

    def arrive(self, name, dst):
        self.remote(name, dst, dst, self.place.at(dp=self.place.other)).wait_recv()

    def local(self, name, src, dst):
        copy = pltpu.make_async_copy(src, dst, self.send_sems.at[self.number(name)])
        copy.start()
        return copy

    def finish(self):
        for copy, name, _ in self.whole:
            if self.like is not None:
                ref = self.like_whole()
                copy = self.remote(name, ref, ref, self.place.at(dp=self.place.other))
            copy.wait_send()
        for copy in self.sent:
            if self.like is not None:
                ref = self.like()
                copy = self.remote(copy, ref, ref, self.place.at(dp=self.place.other))
            copy.wait_send()


def greet(devices, meanwhile=None):
    barrier = pltpu.get_barrier_semaphore()
    for device in devices:
        pl.semaphore_signal(barrier, inc=1, device_id=device, device_id_type=MESH)
    if meanwhile is not None:
        meanwhile()
    pl.semaphore_wait(barrier, len(devices))


def together(streams):
    streams = list(streams)
    while streams:
        left = []
        for stream in streams:
            if next(stream, 0) is None:
                left.append(stream)
        streams = left


def later(stream, stages):
    for _ in range(stages):
        yield
    yield from stream


def add_up(dst, sources, step=32):
    if len(dst.shape) > 2:
        for i in range(dst.shape[0]):
            add_up(dst.at[i], [source.at[i] for source in sources], step)
        return
    rows, columns = dst.shape
    by_rows = rows % step == 0
    step = step if by_rows else 256

    def body(i, carry):
        part = pl.ds(pl.multiple_of(i * step, step), step)
        at = (part, slice(None)) if by_rows else (slice(None), part)
        total = sources[0][at].astype(F32)
        for source in sources[1:]:
            total = total + source[at].astype(F32)
        dst[at] = total.astype(dst.dtype)
        return carry

    lax.fori_loop(0, (rows if by_rows else columns) // step, body, 0)


def halves_of_rows(view, i):
    rows = view.shape[0] // 2
    return view.at[pl.ds(i * rows, rows)]


def halves_of_columns(view, i):
    columns = view.shape[1] // 2
    return view.at[:, pl.ds(i * columns, columns)]


def line_gather(m, tag, own, out, pause=1):
    p = m.place
    u = p.uly
    mine = out.at[p.dp * 4 + u]
    copy = m.local((tag, "="), own, mine)
    for i in range(2):
        src, dst = halves_of_rows(own, i), halves_of_rows(mine, i)
        if u < 3:
            m.send((tag, "r", u, i), src, dst, p.at(uly=u + 1))
        if u > 0:
            m.send((tag, "l", u, i), src, dst, p.at(uly=u - 1))
    m.send((tag, "c", u), own, mine, p.at(dp=p.other))
    for _ in range(pause):
        yield
    for d in range(1, 4):
        for i in range(2):
            for way, b, onward in (("r", u - d, u + 1), ("l", u + d, u - 1)):
                if 0 <= b <= 3:
                    half = halves_of_rows(out.at[p.dp * 4 + b], i)
                    m.arrive((tag, way, b, i), half)
                    if 0 <= onward <= 3:
                        m.send((tag, way, b, i), half, half, p.at(uly=onward))
        for b in (u - d, u + d):
            if 0 <= b <= 3:
                block = out.at[p.dp * 4 + b]
                m.send((tag, "c", b), block, block, p.at(dp=p.other))
        yield
    for b in range(4):
        m.arrive((tag, "c", b), out.at[p.other * 4 + b])
    copy.wait()


def plane_gather(m, tag, own, out, slot, halves, pair=True):
    p = m.place

    def half(c, i):
        return slot(out, p.dp, c, halves[i])

    mine = slot(out, p.dp, p.ctx, None)
    copy = m.local((tag, "="), own, mine)
    m.send((tag, "x"), own, mine, p.at(ctx=p.xn))
    m.send((tag, "y"), own, mine, p.at(ctx=p.yn))
    if pair:
        m.send((tag, "c", 0), own, mine, p.at(dp=p.other))
    yield
    block = slot(out, p.dp, p.xn, None)
    m.arrive((tag, "x"), block)
    m.send((tag, "z", 0), half(p.xn, 0), half(p.xn, 0), p.at(ctx=p.yn))
    if pair:
        m.send((tag, "c", 1), block, block, p.at(dp=p.other))
    block = slot(out, p.dp, p.yn, None)
    m.arrive((tag, "y"), block)
    m.send((tag, "z", 1), half(p.yn, 1), half(p.yn, 1), p.at(ctx=p.xn))
    if pair:
        m.send((tag, "c", 2), block, block, p.at(dp=p.other))
    yield
    for i in range(2):
        block = half(p.dg, i)
        m.arrive((tag, "z", i), block)
        if pair:
            m.send((tag, "c", 3 + i), block, block, p.at(dp=p.other))
    yield
    if pair:
        for i, c in enumerate((p.ctx, p.xn, p.yn)):
            m.arrive((tag, "c", i), slot(out, p.other, c, None))
        for i in range(2):
            m.arrive((tag, "c", 3 + i), slot(out, p.other, p.dg, halves[i]))
    copy.wait()


def line_reduce(m, tag, part, out, sib, right, left, cut=halves_of_rows):
    p = m.place
    u = p.uly
    order = (3, 0, 2, 1) if u < 2 else (0, 3, 1, 2)
    for b in order if sib is not None else ():
        m.send_whole((tag, "c", b), part(p.other * 4 + b), sib.at[b], p.at(dp=p.other))
    met = set()

    def meet(b, i):
        if sib is None:
            return [cut(part(b), i)]
        if b not in met:
            met.add(b)
            m.arrive((tag, "c", b), sib.at[b])
        return [cut(part(p.dp * 4 + b), i), cut(sib.at[b], i)]

    def onward(way, b, i, arrived, there):
        terms = meet(b, i)
        if arrived is not None:
            arrived = cut(arrived.at[b], i)
            m.arrive((tag, way, b, i), arrived)
            terms.append(arrived)
        if len(terms) > 1:
            add_up(terms[-1], terms)
        away = cut((right if way == "r" else left).at[b], i)
        m.send((tag, way, b, i), terms[-1], away, p.at(uly=there))

    for slot in range(3):
        for b in range(4):
            for i in range(2):
                if u < b and u + 3 - b == slot:
                    onward("r", b, i, right if u > 0 else None, u + 1)
        for b in range(4):
            for i in range(2):
                if u > b and 3 - u + b == slot:
                    onward("l", b, i, left if u < 3 else None, u - 1)
        yield
    for i in range(2):
        terms = meet(u, i)
        if u > 0:
            m.arrive((tag, "r", u, i), cut(right.at[u], i))
            terms.append(cut(right.at[u], i))
        if u < 3:
            m.arrive((tag, "l", u, i), cut(left.at[u], i))
            terms.append(cut(left.at[u], i))
        add_up(cut(out, i), terms)


def plane_reduce(m, tag, part, out, sib, sums, got, got2):
    p = m.place
    rows = out.shape[0]
    halves = (pl.ds(0, rows // 2), pl.ds(rows // 2, rows // 2))
    order = (p.dg, p.xn, p.yn, p.ctx)
    for i, c in enumerate(order):
        m.send((tag, "c", i), part.at[p.other * 4 + c], sib.at[c], p.at(dp=p.other))
    yield
    for i, c in enumerate(order):
        m.arrive((tag, "c", i), sib.at[c])
        add_up(sums.at[c], [part.at[p.dp * 4 + c], sib.at[c]])
        if i == 0:
            m.send((tag, "x", 1), sums.at[c, halves[0]], got.at[1, halves[0]], p.at(ctx=p.xn))
            m.send((tag, "y", 1), sums.at[c, halves[1]], got.at[1, halves[1]], p.at(ctx=p.yn))
        if i == 1:
            m.send((tag, "x", 0), sums.at[c, halves[0]], got.at[0, halves[0]], p.at(ctx=p.xn))
        if i == 2:
            m.send((tag, "y", 0), sums.at[c, halves[1]], got.at[0, halves[1]], p.at(ctx=p.yn))
    yield
    m.arrive((tag, "x", 1), got.at[1, halves[0]])
    add_up(got.at[1, halves[0]], [sums.at[p.yn, halves[0]], got.at[1, halves[0]]])
    m.send((tag, "y2"), got.at[1, halves[0]], got2.at[halves[0]], p.at(ctx=p.yn))
    m.arrive((tag, "y", 1), got.at[1, halves[1]])
    add_up(got.at[1, halves[1]], [sums.at[p.xn, halves[1]], got.at[1, halves[1]]])
    m.send((tag, "x2"), got.at[1, halves[1]], got2.at[halves[1]], p.at(ctx=p.xn))
    yield
    m.arrive((tag, "x", 0), got.at[0, halves[0]])
    m.arrive((tag, "y", 0), got.at[0, halves[1]])
    yield
    m.arrive((tag, "y2"), got2.at[halves[0]])
    m.arrive((tag, "x2"), got2.at[halves[1]])
    add_up(out, [sums.at[p.ctx], got.at[0], got2])


class Stage:
    def __init__(self, loads, stores, first):
        self.loads, self.stores, self.started = loads, stores, []
        for i in (*first, *(i for i in loads if i not in first)):
            loads[i].start()

    def need(self, *which):
        for i in which:
            self.loads.pop(i).wait()

    def put(self, *which):
        for i in which:
            copy = self.stores.pop(i)
            copy.start()
            self.started.append(copy)

    def end(self):
        self.need(*list(self.loads))
        self.put(*list(self.stores))
        for copy in self.started:
            copy.wait()


def staged_call(kernel, name, ins, outs, scratch, remote=None, first=()):
    in_held = [i for i, (_, held) in enumerate(ins) if held]
    out_held = [i for i, (_, _, held) in enumerate(outs) if held]

    def body(*refs):
        given, results = list(refs[: len(ins)]), list(refs[len(ins) : len(ins) + len(outs)])
        rest = refs[len(ins) + len(outs) :]
        held, own, sems = rest[: len(in_held) + len(out_held)], rest[len(in_held) + len(out_held) : -1], rest[-1]
        loads, stores = {}, {}
        for j, i in enumerate(in_held):
            loads[i] = pltpu.make_async_copy(given[i], held[j], sems.at[j])
            given[i] = held[j]
        for j, i in enumerate(out_held, len(in_held)):
            stores[i] = pltpu.make_async_copy(held[j], results[i], sems.at[j])
            results[i] = held[j]
        stage = Stage(loads, stores, first)
        kernel(stage, *given, *results, *own)
        stage.end()

    params = {} if remote is None else {"collective_id": remote, "has_side_effects": True}
    return pl.pallas_call(
        body,
        out_shape=[jax.ShapeDtypeStruct(shape, kind) for shape, kind, _ in outs],
        in_specs=[pl.BlockSpec(memory_space=HBM)] * len(ins),
        out_specs=[pl.BlockSpec(memory_space=HBM)] * len(outs),
        scratch_shapes=[
            *[pltpu.VMEM(ins[i][0].shape, ins[i][0].dtype) for i in in_held],
            *[pltpu.VMEM(*outs[i][:2]) for i in out_held],
            *[pltpu.VMEM(shape, kind) for shape, kind in scratch],
            *([pltpu.SemaphoreType.DMA((N_SEMS,))] * 2 if remote is not None else []),
            pltpu.SemaphoreType.DMA((len(in_held) + len(out_held),)),
        ],
        name=name,
        compiler_params=pltpu.CompilerParams(vmem_limit_bytes=62 << 20, **params),
    )(*[array for array, _ in ins])


def everyone(p):
    me = p.dp * 16 + p.ctx * 4 + p.uly
    found = []
    for k in range(1, 32):
        there = lax.rem(me + k, 32)
        found.append((lax.div(there, 16), lax.rem(lax.div(there, 4), 4), lax.rem(there, 4)))
    return found


def line_partners(p):
    found = [p.at(dp=p.other)]
    for d in range(1, 4):
        there = lax.rem(p.uly + d, 4)
        found += [p.at(uly=there), p.at(dp=p.other, uly=there)]
    return found


def plane_partners(p):
    return [p.at(dp=p.other), p.at(ctx=p.xn), p.at(ctx=p.yn)]


def token_slot(out, dp, c, part):
    view = out.at[dp * 4 + c]
    return view if part is None else view.at[part]


def state_slot(out, dp, c, part):
    view = out.at[c]
    return view if part is None else view.at[part]


def finish(heads, outg, slices, residual, layer_part, grad, grad_scaled, hidden, gains, terms, down):
    rows, (_, out_rows, quarter) = heads.shape[1], outg.shape
    tokens, width = hidden.shape
    key, val, ff = KEY_DIM, VALUE_DIM, slices.shape[2] // 2

    def kernel(
        stage, hs, og, sl, res, part, gr, gs, hid, gain, term, down_in, q, k, v, s, o, g, u, y, x, down_out, n1, n2
    ):
        stage.need(0, 1, 2)
        for d in range(2):
            for z in range(4):
                h, i = 2 * z + d, 4 * d + z
                at = 0
                for ref, w in ((q, key), (k, key), (v, val), (s, val)):
                    ref[:, h * w : (h + 1) * w] = hs[i, :, at : at + w].astype(F32)
                    at += w
        stage.put(0, 1, 2, 3)
        for i in range(8):
            g[:, i * ff : (i + 1) * ff] = sl[i, :, :ff].astype(F32)
            u[:, i * ff : (i + 1) * ff] = sl[i, :, ff:].astype(F32)
        stage.put(5, 6)
        for j in range(4):
            o[:, j * quarter : (j + 1) * quarter] = og[j].astype(F32)
        stage.put(4)
        stage.need(3, 4, 5, 6, 7, 8, 9)
        me = lax.axis_index(DP) * 16 + lax.axis_index(CTX) * 4 + lax.axis_index(ULY)
        pair = pl.ds(pl.multiple_of(lax.div(me, 2) * 2 * rows, 2 * rows), 2 * rows)
        own = jnp.where(lax.rem(me, 2) == 0, term[:, pair][:, :rows], term[:, pair][:, rows:])
        n1[...] = own[0:1]
        n2[...] = own[1:2]

        def body(i, carry):
            at = pl.ds(pl.multiple_of(i * 16, 16), 16)
            y[at, :] = res[at, :] + part[at, :]
            normed, inverse = normalize(hid[at, :].astype(F32))
            x[at, :] = gr[at, :] + norm_back(gs[at, :] * gain[0:1, :], normed, inverse)
            return carry

        lax.fori_loop(0, tokens // 16, body, 0)
        stage.put(7, 8)
        stage.need(10)
        down_out[...] = down_in[...]
        stage.put(9)

    widths = (8 * key, 8 * key, 8 * val, 8 * val, 4 * quarter, 8 * ff, 8 * ff)
    heights = (rows, rows, rows, rows, out_rows, rows, rows)
    arrays = (heads, outg, slices, residual, layer_part, grad, grad_scaled, hidden, gains, terms, down)
    shapes = [*zip(heights, widths), (tokens, width), (tokens, width), down.shape, (1, rows), (1, rows)]
    return staged_call(
        kernel,
        "finish",
        [(array, True) for array in arrays],
        [(shape, F32, True) for shape in shapes],
        [],
        first=(0, 2, 1),
    )


def line_spread(m, tag, own, slot):
    u = m.place.uly
    copy = m.local((tag, 8), own, slot(u))
    if u < 3:
        m.send((tag, "r", u), own, slot(u), m.place.at(uly=u + 1))
    if u > 0:
        m.send((tag, "l", u), own, slot(u), m.place.at(uly=u - 1))
    copy.wait()
    yield
    for d in range(1, 4):
        for way, b, onward in (("r", u - d, u + 1), ("l", u + d, u - 1)):
            if 0 <= b <= 3:
                m.arrive((tag, way, b), slot(b))
                if 0 <= onward <= 3:
                    m.send((tag, way, b), slot(b), slot(b), m.place.at(uly=onward))
        yield


def block_factors(cum, ctx, s, backward):
    count = cum.shape[1]
    lasts = [cum[4 * s + j : 4 * s + j + 1, count - 1 : count] for j in range(4)]
    found = []
    for j in range(4):
        total = jnp.zeros((1, 1), F32)
        for i in range(4):
            inside = ((i > ctx) & (i < j)) if backward else ((i > j) & (i < ctx))
            total = total + jnp.where(inside, lasts[i], 0.0)
        right = (j > ctx) if backward else (j < ctx)
        found.append(jnp.where(right, jnp.exp(total), 0.0))
    return found


def forward(hidden, cot, decay, w_down, w_query, w_key, w_value, w_swish, w_output, w_gate, w_up, gains):
    tokens, width = hidden.shape
    key, val = KEY_DIM, VALUE_DIM
    rows, cols = w_query.shape[0], 2 * key + 2 * val + gains.shape[1]
    out_rows, quarter = w_output.shape[0], width // 4
    ff = w_gate.shape[1] // 8
    ff2 = 2 * ff
    block, both = 4 * tokens, 8 * tokens
    half = block // 2
    scale = 1.0 / math.sqrt(key)
    at_s = 2 * key + val

    def start_streams(m, hid_ref, dec_ref, pk_ref, gu_ref, hall, dall, wall, gall):
        p = m.place
        u = p.uly

        def row(q, c, us):
            dp = p.dp if q == 0 else p.other
            at = (dp * 16 + c * 4 + us) * rows
            return wall.at[pl.ds(pl.multiple_of(at, rows), rows)]

        def attn():
            sources = sorted(
                ((q, us) for q in range(2) for us in range(4)), key=lambda s: (abs(s[1] - u), s[0])
            )
            copy = None
            for q, to in sources:
                dp = p.dp if q == 0 else p.other
                mine = row(0, p.ctx, u)
                src = pk_ref.at[dp * 4 + to]
                if (q, to) == (0, u):
                    copy = m.local("T", src, mine)
                else:
                    m.send(("t", q, u), src, mine, p.at(dp=dp, uly=to))
            yield
            relays = []
            for n, (q, us) in enumerate(sources):
                tile = row(q, p.ctx, us)
                if (q, us) == (0, u):
                    copy.wait()
                else:
                    m.arrive(("t", q, us), tile)
                m.send(("X", q, us), tile, tile, p.at(ctx=p.xn))
                m.send(("Y", q, us), tile, tile, p.at(ctx=p.yn))
                relays.append((q, us))
                if n >= 2:
                    yield
                    relay(*relays.pop(0))
            while relays:
                yield
                relay(*relays.pop(0))
            yield
            for q, us in sources:
                even = (q + us) % 2 == 0
                m.arrive(("Y" if even else "X", q, us), row(q, p.yn if even else p.xn, us))
                m.arrive(("Z", q, us), row(q, p.dg, us))

        def relay(q, us):
            if (q + us) % 2 == 0:
                tile = row(q, p.xn, us)
                m.arrive(("X", q, us), tile)
                m.send(("Z", q, us), tile, tile, p.at(ctx=p.yn))
            else:
                tile = row(q, p.yn, us)
                m.arrive(("Y", q, us), tile)
                m.send(("Z", q, us), tile, tile, p.at(ctx=p.xn))

        def feed():
            mine = gall.at[p.dp * 4 + p.ctx]
            copy = m.local("F", gu_ref.at[p.dp * 4 + p.ctx], mine)
            decays = m.local("D", dec_ref, dall.at[p.dp * 4 + p.ctx])
            spots = [(q, c, i) for i, c in enumerate((p.ctx, p.xn, p.yn, p.dg)) for q in range(2)][1:]
            for q, c, i in spots:
                dp = p.dp if q == 0 else p.other
                m.send(("d", q, i), dec_ref, dall.at[p.dp * 4 + p.ctx], p.at(dp=dp, ctx=c))
                m.send(("f", q, i), gu_ref.at[dp * 4 + c], mine, p.at(dp=dp, ctx=c))
            for _ in range(5):
                yield
            for q, c, i in spots:
                dp = p.dp if q == 0 else p.other
                m.arrive(("d", q, i), dall.at[dp * 4 + c])
                m.arrive(("f", q, i), gall.at[dp * 4 + c])
            copy.wait()
            decays.wait()

        return [
            attn(),
            later(line_gather(m, "h", hid_ref, hall, 6), 1),
            later(feed(), 2),
        ]

    def quarter_of(oall, part, c):
        return oall.at[part, :, pl.ds(pl.multiple_of(c * quarter, quarter), quarter)]

    def out_rows_go(m, ow_ref, oall):
        p = m.place
        u = p.uly
        head_dp, head_u = lax.rem(p.ctx, 2), p.dp * 2 + lax.div(p.ctx, 2)
        found = []
        for j in range(4):
            there = oall.at[u, :, pl.ds(j * quarter, quarter)]
            away = pltpu.make_async_remote_copy(
                src_ref=ow_ref.at[j],
                dst_ref=there,
                send_sem=m.send_sems.at[m.number(("S", j))],
                recv_sem=m.recv_sems.at[m.number(("o", u))],
                device_id=(head_dp, j, head_u),
                device_id_type=MESH,
            )
            here = (ow_ref.at[j], there, m.send_sems.at[m.number("O")])
            own = (head_dp == p.dp) & (p.ctx == j) & (head_u == u)
            found.append((own, away, here))
        return found

    def out_start(m, ow_ref, oall):
        for own, away, here in out_rows_go(m, ow_ref, oall):

            @pl.when(own)
            def _(here=here):
                copy = pltpu.make_async_copy(*here)
                copy.start()
                copy.wait()

            pl.when(jnp.logical_not(own))(away.start)

    def out_share(m, ow_ref, oall):
        p = m.place
        u = p.uly
        for us in range(4):
            mine = (u // 2 == p.dp) & (2 * (u % 2) + p.dp == p.ctx) & (us == u)

            @pl.when(jnp.logical_not(mine))
            def _(us=us):
                m.arrive(("o", us), quarter_of(oall, us, p.ctx))

        mine = quarter_of(oall, pl.ds(0, 4), p.ctx)
        m.send("ox", mine, mine, p.at(ctx=p.xn))
        m.send("oy", mine, mine, p.at(ctx=p.yn))
        for own, away, _ in out_rows_go(m, ow_ref, oall):
            pl.when(jnp.logical_not(own))(away.wait_send)

    def out_relay(m, oall):
        p = m.place
        low, high = pl.ds(0, 2), pl.ds(2, 2)
        m.arrive("ox", quarter_of(oall, pl.ds(0, 4), p.xn))
        m.send("o0", quarter_of(oall, low, p.xn), quarter_of(oall, low, p.xn), p.at(ctx=p.yn))
        m.arrive("oy", quarter_of(oall, pl.ds(0, 4), p.yn))
        m.send("o1", quarter_of(oall, high, p.yn), quarter_of(oall, high, p.yn), p.at(ctx=p.xn))

    def out_end(m, oall):
        p = m.place
        m.arrive("o0", quarter_of(oall, pl.ds(0, 2), p.dg))
        m.arrive("o1", quarter_of(oall, pl.ds(2, 2), p.dg))

    def kernel(
        stage, hid_ref, cot_ref, dec_ref, wd_ref, wq_ref, wk_ref, wv_ref, ws_ref, wo_ref, wg_ref, wu_ref, n_ref,
        w_all, s1_all, w2d, q_ref, k_ref, v_ref, sw_ref, w_ref, mask_ref, st_ref, reach_ref, tail_ref, cum_ref,
        gain_ref, hn_ref, hi_ref, ga_ref, res_ref, s2_all, top_all, gu_all, wd_all,
        pk_ref, ow_ref, gu_ref, wall, s1, oall, dall, gall, dec8, cols8, upd, upds, ret, part, sib, right, left, s2, send, recv,
    ):
        uly = lax.axis_index(ULY)
        names = {}
        place = Place(uly)

        def pack():
            stage.need(*range(4, 12))
            for d in range(2):
                for z in range(4):
                    h, i = 2 * z + d, 4 * d + z
                    at = 0
                    for ref, w in ((wq_ref, key), (wk_ref, key), (wv_ref, val), (ws_ref, val)):
                        pk_ref[i, :, at : at + w] = ref[:, h * w : (h + 1) * w]
                        at += w
                    pk_ref[i, :, at:] = n_ref[...]
            for i in range(8):
                gu_ref[i, :, :ff] = wg_ref[:, i * ff : (i + 1) * ff]
                gu_ref[i, :, ff:] = wu_ref[:, i * ff : (i + 1) * ff]
            for j in range(4):
                ow_ref[j] = wo_ref[:, j * quarter : (j + 1) * quarter]

        greet(everyone(place), pack)
        stage.need(0)
        common = Mover(place, names, send, recv)
        ctx = place.ctx

        def for_each(body):
            for u in range(4):
                pl.when(uly == u)(functools.partial(body, u))

        spread = []
        for u in range(4):
            for tag, own, slot in (
                ("g", gall, lambda b: gu_all.at[:, b]),
                ("e", wd_ref, lambda b: wd_all.at[b]),
            ):
                m = Mover(Place(u), names, send, recv, lambda slot=slot: slot(0))
                spread.append((u, m, line_spread(m, tag, own, slot)))

        def spread_on(u):
            for v, _, stream in spread:
                if u == v:
                    next(stream, 0)

        def first(u):
            m = Mover(Place(u), names, send, recv)

            def spread_stage():
                out_start(Mover(Place(u), names, send, recv), ow_ref, oall)
                spread_on(u)
                yield

            together(
                [
                    *start_streams(m, hid_ref, dec_ref, pk_ref, gu_ref, s1, dall, wall, gall),
                    later(spread_stage(), 8),
                ]
            )
            m.finish()

        for_each(first)
        keep = [common.local("w", wall, w_all)]

        table = wall[:, cols - 128 : cols].astype(F32).T
        first_gain = 128 - 32
        gain_ref[...] = table[first_gain : first_gain + 8]

        def norm_one(i, carry):
            b, at = lax.div(i, 4), pl.ds(pl.multiple_of(lax.rem(i, 4) * 32, 32), 32)
            normed, _ = normalize(s1[b, at, :].astype(F32))
            s1[b, at, :] = (normed * gain_ref[0:1, :]).astype(BF16)
            return carry

        lax.fori_loop(0, 32, norm_one, 0)
        keep.append(common.local("W", s1, s1_all))

        for i in range(8):
            dec8[i : i + 1, :] = dall[i, pl.ds(place.dp, 1), :]
        upper = lax.broadcasted_iota(jnp.int32, (block, block), 0) <= lax.broadcasted_iota(
            jnp.int32, (block, block), 1
        )
        cum_ref[...] = jnp.dot(
            dec8[...], upper.astype(F32), precision=lax.Precision.HIGHEST, preferred_element_type=F32
        )
        for s in range(2):
            dec8[s : s + 1, :] = cum_ref[pl.ds(4 * s + ctx, 1), :]
        cols8[...] = dec8[...].T
        for s in range(2):
            column = cols8[:, s : s + 1]
            reach_ref[s] = jnp.exp(column) * scale
            tail_ref[s] = jnp.exp(dec8[s : s + 1, block - 1 : block] - column)

        whole = [
            Mover(Place(u), names, send, recv, lambda: quarter_of(oall, pl.ds(0, 4), 0))
            for u in range(4)
        ]
        for_each(lambda u: out_share(whole[u], ow_ref, oall))

        for s in range(2):
            lhs = s1[4 * s : 4 * s + 4].reshape(block, width)
            q_ref[s] = matmul(lhs, wall[:, :key]).astype(BF16)
            k_ref[s] = matmul(lhs, wall[:, key : 2 * key]).astype(BF16)
            rest = matmul(lhs, wall[:, 2 * key :])
            v_ref[s] = rest[:, :val].astype(BF16)
            sw_ref[pl.ds(s * block, block), :] = rest[:, val : 2 * val]
        out_relay(common, oall)
        for s in range(2):
            k_tail = (k_ref[s].astype(F32) * tail_ref[s]).astype(BF16)
            upd[s] = dot_t(k_tail, v_ref[s]).astype(BF16)
        states = plane_gather(
            common, "t", upd, upds, state_slot, (pl.ds(0, 1), pl.ds(1, 1)), pair=False
        )
        next(states)

        def intra(c, carry):
            s, h = lax.div(c, 2), lax.rem(c, 2)
            at = pl.ds(pl.multiple_of(h * half, half), half)
            here = pl.ds(pl.multiple_of(c * half, half), half)
            gap = cols8[at, :]
            column = jnp.where(s == 0, gap[:, 0:1], gap[:, 1:2])
            gap = column - dec8[pl.ds(s, 1), :]
            t = lax.broadcasted_iota(jnp.int32, (half, block), 0) + h * half
            later_on = t >= lax.broadcasted_iota(jnp.int32, (half, block), 1)
            mask = jnp.where(later_on, jnp.exp(jnp.minimum(gap, 0.0)), 0.0) * scale
            mask_ref[s, at, :] = mask
            weights = (dot_nt(q_ref[s, at, :], k_ref[s]) * mask).astype(BF16)
            w_ref[s, at, :] = weights
            ret[here, :] = matmul(weights, v_ref[s])
            return carry

        lax.fori_loop(0, 2, intra, 0)
        for_each(spread_on)
        next(states)
        lax.fori_loop(2, 4, intra, 0)
        out_end(common, oall)
        for i in range(4):
            w2d[i * out_rows : (i + 1) * out_rows, :] = oall[i]
        for _ in states:
            pass
        for s in range(2):
            factors = block_factors(cum_ref, ctx, s, False)
            total = factors[0] * upds[0, s].astype(F32)
            for j in range(1, 4):
                total = total + factors[j] * upds[j, s].astype(F32)
            st_ref[s] = total.astype(BF16)

        def outer(c, carry):
            s, h = lax.div(c, 2), lax.rem(c, 2)
            at = pl.ds(pl.multiple_of(h * half, half), half)
            here = pl.ds(pl.multiple_of(c * half, half), half)
            retained = ret[here, :] + reach_ref[s, at, :] * matmul(q_ref[s, at, :], st_ref[s])
            normed, inverse = normalize(retained)
            hn_ref[here, :] = normed
            hi_ref[here, :] = inverse
            pre = sw_ref[here, :]
            gated = (pre * jax.nn.sigmoid(pre) * normed.astype(BF16).astype(F32)).astype(BF16)
            ga_ref[here, :] = gated
            for n in range(4):
                cut = pl.ds(n * quarter, quarter)
                value = matmul(gated, w2d[:, cut]).astype(BF16)
                part[pl.ds(2 * c, 2), :, cut] = value.reshape(2, tokens, quarter)
            return carry

        lax.fori_loop(0, 4, outer, 0)
        stage.put(*range(2, 17))

        def reduce(u):
            m = Mover(Place(u), names, send, recv)
            low = tokens // 2

            def spread_stage():
                spread_on(u)
                yield

            together(
                [
                    line_reduce(m, "s", lambda i: part.at[i], res_ref, sib, right, left),
                    plane_gather(
                        m, "C", cot_ref, top_all, token_slot, (pl.ds(0, low), pl.ds(low, low))
                    ),
                    later(spread_stage(), 2),
                ]
            )
            m.finish()

        for_each(reduce)

        def norm_two(i, carry):
            at = pl.ds(pl.multiple_of(i * 16, 16), 16)
            residual = hid_ref[at, :].astype(F32) + res_ref[at, :]
            res_ref[at, :] = residual
            normed, _ = normalize(residual)
            s2[at, :] = (normed * gain_ref[1:2, :]).astype(BF16)
            return carry

        lax.fori_loop(0, tokens // 16, norm_two, 0)
        low = tokens // 2
        for _ in plane_gather(
            common, "k", s2, s2_all, token_slot, (pl.ds(0, low), pl.ds(low, low))
        ):
            pass

        def last(u):
            spread_on(u)
            whole[u].finish()
            for v, m, _ in spread:
                if u == v:
                    m.finish()

        for_each(last)
        for copy in keep:
            copy.wait()
        common.finish()
        assert len(names) <= N_SEMS

    return staged_call(
        kernel,
        "forward",
        [
            (hidden, True), (cot, False), (decay, False), (w_down, False), (w_query, True), (w_key, True),
            (w_value, True), (w_swish, True), (w_output, True), (w_gate, True), (w_up, True), (gains, True),
        ],
        [
            ((width, cols), BF16, False),
            ((8, tokens, width), BF16, False),
            ((4 * out_rows, width), BF16, True),
            ((2, block, key), BF16, True),
            ((2, block, key), BF16, True),
            ((2, block, val), BF16, True),
            ((both, val), F32, True),
            ((2, block, block), BF16, True),
            ((2, block, block), F32, True),
            ((2, key, val), BF16, True),
            ((2, block, 1), F32, True),
            ((2, block, 1), F32, True),
            ((8, block), F32, True),
            ((8, width), F32, True),
            ((both, val), F32, True),
            ((both, 1), F32, True),
            ((both, val), BF16, True),
            ((tokens, width), F32, True),
            ((8, tokens, width), BF16, False),
            ((8, tokens, width), BF16, False),
            ((8, 4, rows, ff2), BF16, False),
            ((4, out_rows, width), BF16, False),
        ],
        [
            ((8, rows, cols), BF16),
            ((4, out_rows, quarter), BF16),
            ((8, rows, ff2), BF16),
            ((width, cols), BF16),
            ((8, tokens, width), BF16),
            ((4, out_rows, width), BF16),
            ((8, 2, block), F32),
            ((8, rows, ff2), BF16),
            ((8, block), F32),
            ((block, 8), F32),
            ((2, key, val), BF16),
            ((4, 2, key, val), BF16),
            ((both, val), F32),
            ((8, tokens, width), BF16),
            ((4, tokens, width), BF16),
            ((4, tokens, width), BF16),
            ((4, tokens, width), BF16),
            ((tokens, width), BF16),
        ],
        1,
    )


def feed_forward(scaled, top, w_gu, w_dn, residual, cot, gains):
    _, tokens, width = scaled.shape
    out_rows = w_dn.shape[1]
    rows, ff2 = w_gu.shape[2:]
    ff = ff2 // 2
    block = 4 * tokens

    def kernel(
        stage, s2_ref, top_ref, gu_ref, wd_ref, res_ref, cot_ref, gain_ref, grad, grad_low, term, dout, lo, ggu,
        w_d, prod, grad_gu, part, down, total, sib, sums, got, got2, right, left, send, recv,
    ):
        uly = lax.axis_index(ULY)
        names = {}
        p = Place(uly)
        greet(line_partners(p) + plane_partners(p)[1:])
        common = Mover(p, names, send, recv)
        movers = [
            Mover(Place(u), names, send, recv, lambda: halves_of_columns(right.at[0], 0))
            for u in range(4)
        ]
        lines = [
            line_reduce(m, "d", lambda b: down.at[b], dout, None, right, left, halves_of_columns)
            for m in movers
        ]

        def for_each(body):
            for u in range(4):
                pl.when(uly == u)(functools.partial(body, u))

        stage.need(0, 2)

        def weights():
            return gu_ref[...].reshape(32 * rows, ff2)

        def tokens_of(s):
            here = pl.ds(pl.multiple_of(s * block, block), block)
            lhs = s2_ref[pl.ds(4 * s, 4)].reshape(block, width)
            pre = matmul(lhs, weights())
            gate_pre, up_pre = pre[:, :ff], pre[:, ff:]
            if 1 in stage.loads:
                stage.need(1, 3)
                for i in range(4):
                    w_d[i * out_rows : (i + 1) * out_rows, :] = wd_ref[i]
            grad_product = dot_nt(top_ref[pl.ds(4 * s, 4)].reshape(block, width), w_d[...])
            sigma = jax.nn.sigmoid(gate_pre)
            act = gate_pre * sigma
            prod[here, :] = (act * up_pre).astype(BF16)
            slope = sigma * (1.0 + gate_pre * (1.0 - sigma))
            grad_gu[here, :ff] = (grad_product * up_pre * slope).astype(BF16)
            grad_gu[here, ff:] = (grad_product * act).astype(BF16)

        def tokens_back(s):
            here = pl.ds(pl.multiple_of(s * block, block), block)

            value = dot_nt(grad_gu[here, :], weights()).astype(BF16)
            part[pl.ds(4 * s, 4)] = value.reshape(4, tokens, width)

        reduced = plane_reduce(common, "s", part, total, sib, sums, got, got2)
        tokens_of(p.other)
        tokens_of(p.dp)

        def down_grad(n, carry):
            at = pl.ds(pl.multiple_of(n * 512, 512), 512)
            value = dot_t(prod[...], top_ref[:, :, at].reshape(2 * block, 512)).astype(BF16)
            for i in range(4):
                down[i, :, at] = value[i * out_rows : (i + 1) * out_rows]
            return carry

        lax.fori_loop(0, width // 512, down_grad, 0)
        for_each(lambda u: next(lines[u]))
        tokens_back(p.other)
        next(reduced)
        tokens_back(p.dp)
        next(reduced)
        for_each(lambda u: next(lines[u]))

        def up_grad(n, carry):
            at = pl.ds(pl.multiple_of(n * 4 * rows, 4 * rows), 4 * rows)
            value = dot_t(s2_ref[:, :, at].reshape(2 * block, 4 * rows), grad_gu[...])
            ggu[n] = value.astype(BF16).reshape(4, rows, ff2)
            return carry

        lax.fori_loop(0, 8, up_grad, 0)
        stage.put(5)
        for_each(lambda u: next(lines[u]))
        next(reduced)

        def out_part(n, carry):
            at = pl.ds(pl.multiple_of(n * 512, 512), 512)
            value = matmul(prod[...], w_d[:, at]).astype(BF16)
            lo[:, :, at] = value.reshape(8, tokens, 512)
            return carry

        lax.fori_loop(0, width // 512, out_part, 0)
        stage.put(4)
        for _ in reduced:
            pass
        stage.need(4, 5, 6)

        def back(i, carry):
            at = pl.ds(pl.multiple_of(i * 16, 16), 16)
            normed, inverse = normalize(res_ref[at, :])
            scaled_grad = total[at, :]
            value = cot_ref[at, :].astype(F32) + norm_back(
                scaled_grad * gain_ref[1:2, :], normed, inverse
            )
            grad[at, :] = value
            grad_low[at, :] = value.astype(BF16)
            return carry + jnp.sum(scaled_grad * normed, axis=0, keepdims=True)

        term[...] = lax.fori_loop(0, tokens // 16, back, jnp.zeros((1, width), F32))

        def last(u):
            for _ in lines[u]:
                pass
            movers[u].finish()

        for_each(last)
        common.finish()
        assert len(names) <= N_SEMS

    return staged_call(
        kernel,
        "feed_forward",
        [(array, True) for array in (scaled, top, w_gu, w_dn, residual, cot, gains)],
        [
            ((tokens, width), F32, True),
            ((tokens, width), BF16, True),
            ((1, width), F32, True),
            ((out_rows, width), F32, True),
            ((8, tokens, width), BF16, True),
            ((8, 4, rows, ff2), BF16, True),
        ],
        [
            ((4 * out_rows, width), BF16),
            ((2 * block, ff), BF16),
            ((2 * block, ff2), BF16),
            ((8, tokens, width), BF16),
            ((4, out_rows, width), BF16),
            ((tokens, width), F32),
            ((4, tokens, width), BF16),
            ((4, tokens, width), BF16),
            ((2, tokens, width), BF16),
            ((tokens, width), BF16),
            ((4, out_rows, width), BF16),
            ((4, out_rows, width), BF16),
        ],
        3,
        (0, 2),
    )


def attention_back(
    own, lo, ggu, w_out, gated, normed, inverse, swish, q, k, v, weights, mask, state_in, reach, tail, cum
):
    tokens, width = own.shape
    both, val = gated.shape
    block, key = q.shape[1:]
    rows, cols = ggu.shape[3:]
    piece = w_out.shape[0] // 4
    half = block // 2
    at_v, at_s = 2 * key, 2 * key + val

    def kernel(
        stage, own_ref, lo_ref, g_ref, wo_ref, ga_ref, hn_ref, hi_ref, sw_ref, q_ref, k_ref, v_ref, w_ref, mask_ref, st_ref,
        reach_ref, tail_ref, cum_ref, cat_ref, total, osum, gsum,
        gout, oxs, oys, ox2, oy2, gy, gr, gs, gq, gk, gv, gst, gsts, sib, chip, got, got2, right, left, send, recv,
    ):
        uly = lax.axis_index(ULY)
        names = {}
        place = Place(uly)
        greet(line_partners(place) + plane_partners(place)[1:])
        stage.need(0, 1, 2)
        common = Mover(place, names, send, recv)
        movers = [Mover(Place(u), names, send, recv, lambda: right.at[0, 0]) for u in range(4)]
        ways = [
            line_reduce(
                movers[u],
                "f",
                lambda b: g_ref.at[:, :, b],
                gsum,
                None,
                right,
                left,
                lambda view, i: view.at[i],
            )
            for u in range(4)
        ]

        def for_each(body):
            for u in range(4):
                pl.when(uly == u)(functools.partial(body, u))

        def first(u):
            def sums():
                yield
                next(ways[u])
                yield
                yield
                next(ways[u])

            m = Mover(Place(u), names, send, recv)
            together(
                [
                    plane_reduce(m, "s", lo_ref, total, sib, chip, got, got2),
                    sums(),
                    line_gather(m, "k", own_ref, gy),
                ]
            )
            m.finish()

        for_each(first)

        stage.put(1)
        stage.need(*range(3, 17))

        def chunk(c):
            return pl.ds(pl.multiple_of(c * half, half), half)

        def gradients(c, carry):
            at = chunk(c)
            grad = gy[pl.ds(2 * c, 2)].reshape(half, width)
            gg = dot_nt(grad, wo_ref[...])
            pre = sw_ref[at, :]
            sigma = jax.nn.sigmoid(pre)
            head = hn_ref[at, :]
            low = head.astype(BF16).astype(F32)
            cat_ref[at, at_s : at_s + val] = (
                gg * low * (sigma * (1.0 + pre * (1.0 - sigma)))
            ).astype(BF16)
            gh = (gg * (pre * sigma)).astype(BF16).astype(F32)
            mean = jnp.mean(gh * head, axis=-1, keepdims=True)
            grad_retained = (hi_ref[at, :] * (gh - head * mean)).astype(BF16)
            gr[at, :] = grad_retained
            s = lax.div(c, 2)
            part = pl.ds(pl.multiple_of(lax.rem(c, 2) * half, half), half)
            gs[at, :] = (dot_nt(grad_retained, v_ref[s]) * mask_ref[s, part, :]).astype(BF16)
            return carry

        lax.fori_loop(0, both // half, gradients, 0)
        for s in range(2):
            at = pl.ds(s * block, block)
            reached = (q_ref[s].astype(F32) * reach_ref[s]).astype(BF16)
            gst[s] = dot_t(reached, gr[at, :]).astype(BF16)
        states = plane_gather(
            common, "t", gst, gsts, state_slot, (pl.ds(0, 1), pl.ds(1, 1)), pair=False
        )
        next(states)
        for_each(lambda u: next(ways[u]))

        for s in range(2):
            at = pl.ds(s * block, block)
            gq[at, :] = jnp.dot(gs[at, :], k_ref[s], preferred_element_type=F32)
            gk[at, :] = dot_t(gs[at, :], q_ref[s])
        def out_grad(n, carry):
            at = pl.ds(pl.multiple_of(n * 512, 512), 512)
            grad = gy[:, :, at].reshape(both, 512)
            value = dot_t(ga_ref[...], grad).astype(BF16)
            for i in range(4):
                gout[i, :, at] = value[i * piece : (i + 1) * piece]
            return carry

        lax.fori_loop(0, width // 512, out_grad, 0)
        next(states)

        quarter = width // 4

        def column(part, c):
            return gout.at[part, :, pl.ds(pl.multiple_of(c * quarter, quarter), quarter)]

        for i, (cx, cy) in ((1, (place.dg, place.dg)), (0, (place.xn, place.yn))):
            common.send(("ox", i), column(pl.ds(0, 2), cx), oxs.at[i], place.at(ctx=place.xn))
            common.send(("oy", i), column(pl.ds(2, 2), cy), oys.at[i], place.at(ctx=place.yn))
        for s in range(2):
            at = pl.ds(s * block, block)
            gv[at, :] = dot_t(w_ref[s], gr[at, :])
        for _ in states:
            pass
        for s in range(2):
            at = pl.ds(s * block, block)
            factors = block_factors(cum_ref, place.ctx, s, True)
            update = factors[0] * gsts[0, s].astype(F32)
            for j in range(1, 4):
                update = update + factors[j] * gsts[j, s].astype(F32)
            update = update.astype(BF16)
            grad = gr[at, :]
            cat_ref[at, :key] = (gq[at, :] + reach_ref[s] * dot_nt(grad, st_ref[s])).astype(BF16)
            cat_ref[at, key:at_v] = (gk[at, :] + tail_ref[s] * dot_nt(v_ref[s], update)).astype(BF16)
            cat_ref[at, at_v:at_s] = (
                gv[at, :] + tail_ref[s] * jnp.dot(k_ref[s], update, preferred_element_type=F32)
            ).astype(BF16)
        stage.put(0)
        common.arrive(("ox", 1), oxs.at[1])
        common.arrive(("oy", 1), oys.at[1])
        for t in range(2):
            add_up(oxs.at[1, t], [column(t, place.yn), oxs.at[1, t]])
            add_up(oys.at[1, t], [column(2 + t, place.xn), oys.at[1, t]])
        common.send("oy2", oxs.at[1], oy2, place.at(ctx=place.yn))
        common.send("ox2", oys.at[1], ox2, place.at(ctx=place.xn))

        def last(u):
            for _ in ways[u]:
                pass
            movers[u].finish()

        for name, ref in ((("ox", 0), oxs.at[0]), (("oy", 0), oys.at[0]), ("oy2", oy2), ("ox2", ox2)):
            common.arrive(name, ref)
        for us in range(4):
            got, got2 = (oxs, oy2) if us < 2 else (oys, ox2)
            add_up(osum.at[us], [column(us, place.ctx), got.at[0, us % 2], got2.at[us % 2]])
        stage.put(2)
        for_each(last)
        common.finish()
        assert len(names) <= N_SEMS

    arrays = (own, lo, ggu, w_out, gated, normed, inverse, swish, q, k, v, weights, mask, state_in, reach, tail, cum)
    return staged_call(
        kernel,
        "attention_back",
        [(array, True) for array in arrays],
        [
            ((both, 2 * key + 2 * val), BF16, True),
            ((tokens, width), F32, True),
            ((4, piece, width // 4), BF16, True),
            ((2, 4, rows, cols), BF16, True),
        ],
        [
            ((4, piece, width), BF16),
            *[((2, 2, piece, width // 4), BF16)] * 2,
            *[((2, piece, width // 4), BF16)] * 2,
            ((8, tokens, width), BF16),
            ((both, val), BF16),
            ((both, block), BF16),
            ((both, key), F32),
            ((both, key), F32),
            ((both, val), F32),
            ((2, key, val), BF16),
            ((4, 2, key, val), BF16),
            ((4, tokens, width), BF16),
            ((4, tokens, width), BF16),
            ((2, tokens, width), BF16),
            ((tokens, width), BF16),
            ((4, 2, 4, rows, cols), BF16),
            ((4, 2, 4, rows, cols), BF16),
        ],
        7,
    )


def last_exchange(grad_cat, w_all, scaled, gout, gffn, inputs, term):
    tokens, width = inputs.shape
    both, cols = grad_cat.shape
    block = both // 2
    out_rows, quarter = gout.shape[1:]
    rows, ff2 = gffn.shape[1:]

    def streams(
        m, line, tile, f_ref, in_ref, t_ref, out, gall, fall, gains, gotx, goty, gotx2, goty2, away,
    ):
        p = m.place
        u = p.uly

        def attn():
            for t in range(4):
                m.arrive(("gx", 1, t), gotx.at[1, t])
                add_up(gotx.at[1, t], [tile(0, p.yn, t), gotx.at[1, t]])
                m.send(("gy2", t), gotx.at[1, t], goty2.at[t], p.at(ctx=p.yn))
                m.arrive(("gy", 1, t), goty.at[1, t])
                add_up(goty.at[1, t], [tile(1, p.xn, t), goty.at[1, t]])
                m.send(("gx2", t), goty.at[1, t], gotx2.at[t], p.at(ctx=p.xn))
            yield
            yield
            for t in range(4):
                for dp, got, got2, tags in (
                    (0, gotx, goty2, ("gx", "gy2")),
                    (1, goty, gotx2, ("gy", "gx2")),
                ):
                    m.arrive((tags[0], 0, t), got.at[0, t])
                    m.arrive((tags[1], t), got2.at[t])
                    add_up(got.at[0, t], [tile(dp, p.ctx, t), got.at[0, t], got2.at[t]])
                    there = gall.at[p.dp * 4 + u]
                    if t == u:

                        @pl.when(p.dp == dp)
                        def _(got=got, there=there):
                            here = pltpu.make_async_copy(
                                got.at[0, u], there, m.send_sems.at[m.number("G")]
                            )
                            here.start()
                            here.wait()

                        @pl.when(p.dp != dp)
                        def _(got=got, there=there, dp=dp):
                            m.remote(
                                ("gc", u), got.at[0, u], there, (dp, p.ctx, u)
                            ).start()
                    else:
                        k = m.number(("gs", dp, t))
                        copies = []
                        for q in range(2):
                            copies.append(
                                pltpu.make_async_remote_copy(
                                    src_ref=got.at[0, t],
                                    dst_ref=there,
                                    send_sem=m.send_sems.at[k],
                                    recv_sem=m.recv_sems.at[m.number(("g", q, u))],
                                    device_id=(dp, p.ctx, t),
                                    device_id_type=MESH,
                                )
                            )
                        pl.when(p.dp == dp)(copies[0].start)
                        pl.when(p.dp != dp)(copies[1].start)
                        m.sent.append(copies[0])
            for _ in range(6):
                yield
            m.remote(("gc", u), gotx.at[0, u], gotx.at[0, u], p.at(dp=p.other)).wait_send()
            m.arrive(("gc", u), gall.at[p.other * 4 + u])
            for us in range(4):
                if us != u:
                    m.arrive(("g", 0, us), gall.at[p.dp * 4 + us])
                    m.arrive(("g", 1, us), gall.at[p.other * 4 + us])

        def feed():
            mine = fall.at[p.dp * 4 + p.ctx]
            copy = m.local("F", f_ref.at[p.dp * 4 + p.ctx], mine)
            spots = [(q, c, i) for i, c in enumerate((p.ctx, p.xn, p.yn, p.dg)) for q in range(2)][1:]
            for q, c, i in spots:
                dp = p.dp if q == 0 else p.other
                m.send(("f", q, i), f_ref.at[dp * 4 + c], mine, p.at(dp=dp, ctx=c))
            for _ in range(4):
                yield
            for q, c, i in spots:
                dp = p.dp if q == 0 else p.other
                m.arrive(("f", q, i), fall.at[dp * 4 + c])
            copy.wait()

        def tokens_stream():
            yield from line

            def body(i, total):
                at = pl.ds(pl.multiple_of(i * 16, 16), 16)
                values = in_ref[at, :].astype(F32)
                normed, _ = normalize(values)
                return total + jnp.sum(out[at, :] * normed, axis=0, keepdims=True)

            total = lax.fori_loop(0, tokens // 16, body, jnp.zeros((1, width), F32))
            row = lax.broadcasted_iota(jnp.int32, (8, width), 0)
            gains[...] = jnp.where(
                row == 0,
                jnp.broadcast_to(total, (8, width)),
                jnp.where(row == 1, jnp.broadcast_to(t_ref[...], (8, width)), 0.0),
            )
            for i, device in enumerate((p.at(dp=p.other), p.at(ctx=p.xn), p.at(ctx=p.yn))):
                m.remote(("n", i), gains, away.at[i], device).start()
                yield
                m.remote(("n", i), gains, away.at[i], device).wait()
                gains[...] = gains[...] + away[i]
            copies = [
                m.remote(("N", u, other), gains, away.at[3 + u], p.at(uly=other))
                for other in range(4)
                if other != u
            ]
            for copy in copies:
                copy.start()
            yield
            mine = gains[...]
            for other in range(4):
                if other != u:
                    m.arrive(("N", other, u), away.at[3 + other])
                    mine = mine + away[3 + other]
            for copy in copies:
                copy.wait_send()
            gains[...] = mine

        return [
            attn(),
            tokens_stream(),
            later(feed(), 3),
        ]

    def kernel(
        stage, cat_ref, wa_ref, s1_ref, o_ref, f_ref, in_ref, t_ref, out, gall, oall, fall, gains,
        grads, part, sib, right, left, gotx, goty, gotx2, goty2, away, send, recv,
    ):
        uly = lax.axis_index(ULY)
        names = {}
        p = Place(uly)
        greet(everyone(p))
        stage.need(0, 2)
        common = Mover(p, names, send, recv)

        def for_each(body):
            for u in range(4):
                pl.when(uly == u)(functools.partial(body, u))

        def tile(dp, c, t):
            return grads.at[dp, c, pl.ds(t * rows, rows)]

        def weight_grad(dp, c):
            at = pl.ds(pl.multiple_of((dp * 4 + c) * 4 * rows, 4 * rows), 4 * rows)
            grads[dp, c] = dot_t(s1_ref[:, :, at].reshape(both, 4 * rows), cat_ref[...]).astype(BF16)

        def token_grad(s):
            rows_s = pl.ds(pl.multiple_of(s * block, block), block)
            value = dot_nt(cat_ref[rows_s, :], wa_ref[:, :cols]).astype(BF16)
            part[pl.ds(4 * s, 4)] = value.reshape(4, tokens, width)

        def to_x(i, c):
            weight_grad(0, c)
            for t in range(4):
                common.send(("gx", i, t), tile(0, c, t), gotx.at[i, t], p.at(ctx=p.xn))

        def to_y(i, c):
            weight_grad(1, c)
            for t in range(4):
                common.send(("gy", i, t), tile(1, c, t), goty.at[i, t], p.at(ctx=p.yn))

        def out_copies(m, senders):
            at = m.place
            home_dp, home_ctx = at.uly // 2, 2 * (at.uly % 2) + at.dp
            found = []
            for us in range(4):
                own = (home_dp == at.dp) & (home_ctx == at.ctx) & (us == at.uly)
                copies = [
                    pltpu.make_async_remote_copy(
                        src_ref=o_ref.at[us],
                        dst_ref=oall.at[at.ctx],
                        send_sem=m.send_sems.at[m.number(("os", us))],
                        recv_sem=m.recv_sems.at[m.number(("o", j))],
                        device_id=(home_dp, home_ctx, us),
                        device_id_type=MESH,
                    )
                    for j in senders
                ]
                found.append((us, own, copies))
            return found

        def out_start(u):
            m = Mover(Place(u), names, send, recv)
            for us, own, copies in out_copies(m, range(4)):

                @pl.when(own)
                def _(us=us):
                    here = pltpu.make_async_copy(
                        o_ref.at[us], oall.at[p.ctx], send.at[m.number("O")]
                    )
                    here.start()
                    here.wait()

                for j, copy in enumerate(copies):
                    pl.when(jnp.logical_not(own) & (p.ctx == j))(copy.start)

        def out_end(u):
            m = Mover(Place(u), names, send, recv)
            head_dp, head_u = lax.rem(p.ctx, 2), p.dp * 2 + lax.div(p.ctx, 2)
            for j in range(4):
                mine = (head_dp == p.dp) & (p.ctx == j) & (head_u == u)

                @pl.when(jnp.logical_not(mine))
                def _(j=j):
                    m.arrive(("o", j), oall.at[j])

            for _, own, copies in out_copies(m, range(1)):
                pl.when(jnp.logical_not(own))(copies[0].wait_send)

        stage.need(3)
        for_each(out_start)
        to_x(1, p.dg)
        to_y(1, p.dg)
        stage.need(1)
        token_grad(p.other)
        token_grad(p.dp)
        movers = [
            Mover(
                Place(u), names, send, recv, lambda: halves_of_rows(sib.at[0], 0), lambda: sib.at[0]
            )
            for u in range(4)
        ]
        lines = [
            line_reduce(m, "s", lambda i: part.at[i], out, sib, right, left) for m in movers
        ]
        for_each(lambda u: next(lines[u]))
        to_x(0, p.xn)
        to_y(0, p.yn)
        weight_grad(0, p.yn)
        weight_grad(1, p.xn)
        weight_grad(0, p.ctx)
        weight_grad(1, p.ctx)
        stage.need(5, 6)

        def rest(u):
            m = Mover(Place(u), names, send, recv)
            together(
                streams(
                    m, lines[u], tile, f_ref, in_ref, t_ref, out, gall, fall, gains,
                    gotx, goty, gotx2, goty2, away,
                )
            )
            m.finish()
            movers[u].finish()
            out_end(u)

        for_each(rest)
        common.finish()
        assert len(names) <= N_SEMS

    arrays = (grad_cat, w_all, scaled, gout, gffn, inputs, term)
    return staged_call(
        kernel,
        "last",
        [(array, i != 4) for i, array in enumerate(arrays)],
        [
            ((tokens, width), F32, True),
            ((8, rows, cols), BF16, False),
            ((4, out_rows, quarter), BF16, False),
            ((8, rows, ff2), BF16, False),
            ((8, width), F32, True),
        ],
        [
            ((2, 4, 4 * rows, cols), BF16),
            ((8, tokens, width), BF16),
            *[((4, tokens, width), BF16)] * 3,
            *[((2, 4, rows, cols), BF16)] * 2,
            *[((4, rows, cols), BF16)] * 2,
            ((7, 8, width), F32),
        ],
        2,
        (3, 0, 2),
    )


def local(
    hidden_in,
    cotangent,
    log_decay,
    w_query,
    w_key,
    w_value,
    w_swish,
    w_output,
    w_gate,
    w_up,
    w_down,
    gain_attn,
    gain_ffn,
):
    bf16, f32 = BF16, F32
    dp, ctx = lax.axis_index(DP), lax.axis_index(CTX)
    tokens = hidden_in.shape[1]
    width = hidden_in.shape[2]
    rows = w_query.shape[0]
    out_rows = w_output.shape[0]
    key, val, ff = KEY_DIM, VALUE_DIM, w_gate.shape[1] // 8

    gains = jnp.pad(jnp.stack([gain_attn, gain_ffn], axis=1), ((0, 0), (0, 30)))
    block = 4 * tokens
    (
        w_all, scaled_one, w_out, q, k, v, swish_pre, weights, mask, state_in, reach, tail, cum,
        gains, head_normed, head_inverse, gated, residual, scaled_two, top_all, w_gu, w_dn,
    ) = forward(
        hidden_in[0], cotangent[0], log_decay[0], w_down,
        w_query, w_key, w_value, w_swish, w_output, w_gate, w_up, gains,
    )
    grad_residual, grad_y, gain_two_term, grad_down, layer_part, ggu = feed_forward(
        scaled_two, top_all, w_gu, w_dn, residual, cotangent[0], gains
    )
    grad_cat, out_part, g_out, ggu = attention_back(
        grad_y,
        layer_part,
        ggu.reshape(2, 4, 4, rows, 2 * ff),
        w_out,
        gated,
        head_normed,
        head_inverse,
        swish_pre,
        q,
        k,
        v,
        weights,
        mask,
        state_in,
        reach,
        tail,
        cum,
    )
    gs1, gcat, g_out, ggu, gain_terms = last_exchange(
        grad_cat,
        w_all,
        scaled_one,
        g_out,
        ggu.reshape(8, rows, 2 * ff),
        hidden_in[0],
        gain_two_term,
    )
    (
        grad_query, grad_key, grad_value, grad_swish, grad_output, grad_gate, grad_up,
        layer_out, grad_input, grad_down, gain_one_term, gain_two_term,
    ) = finish(
        gcat, g_out, ggu, residual, out_part, grad_residual, gs1, hidden_in[0], gains, gain_terms, grad_down
    )
    return (
        layer_out[None],
        grad_input[None],
        grad_query,
        grad_key,
        grad_value,
        grad_swish,
        grad_output,
        grad_gate,
        grad_up,
        grad_down,
        gain_one_term[0],
        gain_two_term[0],
    )


def solution(mesh):
    shape = mesh.shape
    planned = (shape[DP], shape[CTX], shape[ULY]) == (2, 4, 4)
    tokens = P(DP, (CTX, ULY), None)
    weight = P(EVERYWHERE, None)
    gain = P(EVERYWHERE)
    return jax.shard_map(
        local if planned else local_any,
        mesh=mesh,
        in_specs=(tokens, tokens, P(DP, ULY, CTX), *[weight] * 8, gain, gain),
        out_specs=(tokens, tokens, *[weight] * 8, gain, gain),
        check_vma=False,
    )
```
